32 devices in a mesh: seq: 8 (over z, y), batch: 4 (over x, core).
Axes of the slice: x: 2, y: 2, z: 4, core: 2. Of those that a mesh axis runs over, the one named last changes fastest.
Arguments:
- tokens: bfloat16 [4, 2048, 1024], P('batch', 'seq'), may hold values from -6 to 6
- w_query: float32 [1024, 1024], P('batch', 'seq'), may hold values from -0.1875 to 0.1875
- w_key: float32 [1024, 1024], P('batch', 'seq'), may hold values from -0.1875 to 0.1875
- w_value: float32 [1024, 1024], P('batch', 'seq'), may hold values from -0.1875 to 0.1875
- w_out: float32 [1024, 1024], P('batch', 'seq'), may hold values from -0.75 to 0.75
- w_ada: float32 [1024, 6144], P('batch', 'seq'), may hold values from -0.375 to 0.375
- w_up: float32 [1024, 2048], P('batch', 'seq'), may hold values from -0.1875 to 0.1875
- w_down: float32 [2048, 1024], P('batch', 'seq'), may hold values from -0.125 to 0.125
- segments: int32 [4, 2048], P('batch', 'seq'), may hold values from 0 to 15, as said below
- validity: int32 [4, 2048], P('batch', 'seq'), may hold values from 0 to 1, as said below
- timesteps: int32 [4, 16], P('batch'), may hold values from 0 to 999
- cotangent: bfloat16 [4, 2048, 1024], P('batch', 'seq'), may hold values from -6 to 6
Outputs:
- output: bfloat16 [4, 2048, 1024], P('batch', 'seq')
- grad_tokens: bfloat16 [4, 2048, 1024], P('batch', 'seq')
- grad_query: float32 [1024, 1024], P('batch', 'seq')
- grad_key: float32 [1024, 1024], P('batch', 'seq')
- grad_value: float32 [1024, 1024], P('batch', 'seq')
- grad_out: float32 [1024, 1024], P('batch', 'seq')
- grad_ada: float32 [1024, 6144], P('batch', 'seq')
- grad_up: float32 [1024, 2048], P('batch', 'seq')
- grad_down: float32 [2048, 1024], P('batch', 'seq')
The draws below stay inside these ranges and needn't reach their ends.
Inputs may be any that keep to these rules, and one draw needn't show every extreme that they name: `segments`: in each replica one clip, drawn from the seed, holds the first rows of every device's 256 frames; the other clips' frames follow in order of clip id; every clip that has frames has frames with validity 1. `validity`: frames with 0 belong to the clip that spans every device.
All inputs are finite; a program needn't handle non-finite values.
Results may differ from the reference program's by a relative error of at most 0.018.
The reference program's roundings to bfloat16 on the way count: a program that leaves them out, or rounds other values in their place, can miss the bound.
Values may be sent and summed in bfloat16 or wider, within the bound.
No kernel may reach another device: no remote copies, remote signals or barrier semaphores. Data moves between devices by JAX's collectives and lax.ppermute only.
A program may use at most 320 MiB of HBM per device.

```python
import math
import jax
import jax.numpy as jnp
from jax import lax

D = 1024
HEADS = 16
HEAD = 64
FF = 2048
CLIPS = 16
TOK_DEV = 256
FRAMES = 2048
REPL = 4


def pack_layout(key):
    subkeys = jax.random.split(key, 4)
    device_count = FRAMES // TOK_DEV
    long_id = jax.random.randint(subkeys[0], (REPL, 1, 1), 0, CLIPS)
    long_rows = jax.random.randint(subkeys[1], (REPL, device_count, 1), TOK_DEV // 2, 3 * TOK_DEV // 4 + 1)
    pad_rows = jax.random.randint(subkeys[2], (REPL, device_count, 1), 1, TOK_DEV // 8 + 2)
    raw_ids = jnp.sort(jax.random.randint(subkeys[3], (REPL, FRAMES), 0, CLIPS - 1), axis=1)
    raw_ids = raw_ids.at[:, :TOK_DEV].set(0).at[:, FRAMES - 1].set(CLIPS - 2)
    raw_ids = raw_ids.reshape(REPL, device_count, TOK_DEV)
    short_ids = raw_ids + (raw_ids >= long_id).astype(jnp.int32)
    row_index = jnp.arange(TOK_DEV, dtype=jnp.int32)[None, None, :]
    in_long = row_index < long_rows
    segment = jnp.where(in_long, long_id, short_ids).reshape(REPL, FRAMES)
    padding = in_long & (row_index >= long_rows - pad_rows)
    valid_rows = jnp.where(padding, 0, 1).reshape(REPL, FRAMES)
    return (segment.astype(jnp.int32), valid_rows.astype(jnp.int32))


def draw_segments(key, part):
    return pack_layout(key)[0]


def draw_validity(key, part):
    return pack_layout(key)[1]


def place_ends(values, rng, low, high):
    longest = values.shape.index(max(values.shape))
    spots = []
    for shift in (0, 1):
        where = [jax.random.randint(jax.random.fold_in(rng, axis), (), 0, length) for axis, length in enumerate(values.shape)]
        where[longest] = (where[longest] + shift) % values.shape[longest]
        spots.append(tuple(where))
    return values.at[spots[0]].set(low).at[spots[1]].set(high)


def block_scale(stream_key, extent, cuts, low, high):
    def one(dim, blocks):
        steps = jax.random.uniform(jax.random.fold_in(jax.random.fold_in(stream_key, 6), dim), (blocks,), jnp.float32, low / len(cuts), high / len(cuts))
        return jnp.repeat(jnp.exp(steps), extent[dim] // blocks).reshape((-1,) + (1,) * (len(extent) - dim - 1))

    loudness = one(*cuts[0])
    for cut in cuts[1:]:
        loudness = loudness * one(*cut)
    return loudness


def noise(key, dims, spread, limit, shards=(), held_as=jnp.bfloat16):
    values = jax.random.normal(key, dims, jnp.float32) * spread
    if len(shards) > 0:
        values = block_scale(key, dims, shards, -0.22, 0.18) * values
    return jnp.clip(values, min=-limit, max=limit).astype(held_as)


def setup_inputs(seed: int = 0) -> dict:
    splits = jax.random.split(jax.random.key(seed), 13)
    tokens = noise(splits[0], (REPL, FRAMES, D), 1.0, 6.0, ((0, 4), (1, 8)))
    w_query = noise(splits[1], (D, D), D ** -0.5, 0.1875, ((0, 4), (1, 8)), jnp.float32)
    w_key = noise(splits[2], (D, D), D ** -0.5, 0.1875, ((0, 4), (1, 8)), jnp.float32)
    w_value = noise(splits[3], (D, D), D ** -0.5, 0.1875, ((0, 4), (1, 8)), jnp.float32)
    w_out = noise(splits[4], (D, D), (D // 16) ** -0.5, 0.75, ((0, 4), (1, 8)), jnp.float32)
    w_ada = noise(splits[5], (D, 6 * D), (D // 4) ** -0.5, 0.375, ((0, 4), (1, 8)), jnp.float32)
    w_up = noise(splits[6], (D, FF), D ** -0.5, 0.1875, ((0, 4), (1, 8)), jnp.float32)
    w_down = noise(splits[7], (FF, D), FF ** -0.5, 0.125, ((0, 4), (1, 8)), jnp.float32)
    segments = draw_segments(jax.random.fold_in(splits[12], 71), 0)
    validity = draw_validity(jax.random.fold_in(splits[12], 71), 0)
    timesteps = place_ends(jax.random.randint(splits[10], (REPL, CLIPS), 0, 1000), jax.random.fold_in(splits[10], 1), 0, 999).astype(jnp.int32)
    cotangent = noise(splits[11], (REPL, FRAMES, D), 1.0, 6.0, ((0, 4), (1, 8)))
    return dict(tokens=tokens, w_query=w_query, w_key=w_key, w_value=w_value, w_out=w_out, w_ada=w_ada, w_up=w_up, w_down=w_down, segments=segments, validity=validity, timesteps=timesteps, cotangent=cotangent)


@jax.custom_vjp
def low(v):
    return lax.optimization_barrier(v.astype(jnp.bfloat16)).astype(jnp.float32)

@jax.custom_vjp
def low_back(v):
    return v

def low_keep(v):
    return (low(v), None)

def low_pass(kept, grad):
    return (grad,)

def back_keep(v):
    return (v, None)

def back_low(kept, grad):
    return (low(grad),)
low.defvjp(low_keep, low_pass)
low_back.defvjp(back_keep, back_low)

def time_embedding(timestep_row):
    half_width = D // 2
    frequency = jnp.exp(-math.log(10000.0) * jnp.arange(half_width, dtype=jnp.float32) / half_width)
    angle = timestep_row.astype(jnp.float32)[:, None] * frequency[None, :]
    return jnp.concatenate([jnp.sin(angle), jnp.cos(angle)], axis=1)

def rotate_pairs(vectors, position, direction):
    half_size = vectors.shape[-1] // 2
    frequency = jnp.exp(-math.log(10000.0) * jnp.arange(half_size, dtype=jnp.float32) / half_size)
    angle = position[:, None] * frequency[None, :]
    cosine = jnp.cos(angle)[:, None, :]
    sine = jnp.sin(angle)[:, None, :] * direction
    first_half = vectors[..., :half_size]
    second_half = vectors[..., half_size:]
    return jnp.concatenate([first_half * cosine - second_half * sine, second_half * cosine + first_half * sine], axis=-1)

def normalize(inputs):
    centered = inputs - lax.optimization_barrier(jnp.mean(inputs, axis=-1, keepdims=True))
    inverse = lax.rsqrt(lax.optimization_barrier(jnp.mean(centered * centered, axis=-1, keepdims=True)) + 1e-06)
    return centered * inverse

def frame_positions(segment):
    member = (segment[:, None] == jnp.arange(CLIPS, dtype=jnp.int32)[None, :]).astype(jnp.int32)
    before = jnp.cumsum(member, axis=0) - member
    return lax.optimization_barrier(jnp.sum(before * member, axis=1)).astype(jnp.float32)

def layer_forward(inputs, w_query, w_key, w_value, w_out, w_ada, w_up, w_down, segment, valid_row, timestep_row):
    highest = lax.Precision.HIGHEST
    query_low = low(w_query)
    key_low = low(w_key)
    value_low = low(w_value)
    out_low = low(w_out)
    ada_low = low(w_ada)
    up_low = low(w_up)
    down_low = low(w_down)
    frame_count = inputs.shape[0]
    silu_time = low(jax.nn.silu(time_embedding(timestep_row)))
    modulation = jnp.take(jnp.dot(silu_time, ada_low, precision=highest), segment, axis=0)
    shift_attn, scale_attn, gate_attn, shift_ffn, scale_ffn, gate_ffn = jnp.split(modulation, 6, axis=1)
    position = frame_positions(segment)
    attn_input = low(normalize(inputs) * (1.0 + scale_attn) + shift_attn)
    query_lin = low_back(jnp.dot(attn_input, query_low, precision=highest)).reshape(frame_count, HEADS, HEAD)
    queries = low(rotate_pairs(query_lin, position, 1.0))
    key_lin = low_back(jnp.dot(attn_input, key_low, precision=highest)).reshape(frame_count, HEADS, HEAD)
    key_rows = low(rotate_pairs(key_lin, position, 1.0))
    values = low(low_back(jnp.dot(attn_input, value_low, precision=highest))).reshape(frame_count, HEADS, HEAD)
    key_codes = jnp.where(valid_row == 1, segment, -1)
    block_rows = math.gcd(frame_count, 512)
    block_count = frame_count // block_rows

    def attend(query_block):
        block_queries, block_segments = query_block
        scores = low_back(jnp.einsum('qhe,khe->hqk', block_queries, key_rows, precision=highest) * 0.125)
        allowed = (block_segments[:, None] == key_codes[None, :])[None]
        largest = lax.optimization_barrier(jnp.max(jnp.where(allowed, scores, -1e+30), axis=2, keepdims=True))
        weights = jnp.where(allowed, jnp.exp(scores - largest), 0.0)
        probabilities = weights / lax.optimization_barrier(jnp.sum(weights, axis=2, keepdims=True))
        return jnp.einsum('hqk,khe->qhe', probabilities, values, precision=highest)
    attended = lax.map(jax.checkpoint(attend), (queries.reshape(block_count, block_rows, HEADS, HEAD), segment.reshape(block_count, block_rows)))
    attended = attended.reshape(frame_count, D)
    attn_branch = low_back(jnp.dot(low(low_back(attended)), out_low, precision=highest))
    middle = inputs + gate_attn * attn_branch
    ffn_input = low(normalize(middle) * (1.0 + scale_ffn) + shift_ffn)
    hidden = low_back(jnp.dot(ffn_input, up_low, precision=highest))
    activated = low(jax.nn.gelu(hidden, approximate=True))
    ffn_branch = low_back(jnp.dot(activated, down_low, precision=highest))
    return middle + gate_ffn * ffn_branch

def reference(tokens, w_query, w_key, w_value, w_out, w_ada, w_up, w_down, segments, validity, timesteps, cotangent):
    outputs = []
    input_grads = []
    weight_sums = None
    for replica in range(REPL):

        def bound(inputs, wq_arg, wk_arg, wv_arg, wo_arg, wa_arg, wu_arg, wd_arg):
            return layer_forward(inputs, wq_arg, wk_arg, wv_arg, wo_arg, wa_arg, wu_arg, wd_arg, segments[replica], validity[replica], timesteps[replica])
        result, pull = jax.vjp(bound, tokens[replica].astype(jnp.float32), w_query.astype(jnp.float32), w_key.astype(jnp.float32), w_value.astype(jnp.float32), w_out.astype(jnp.float32), w_ada.astype(jnp.float32), w_up.astype(jnp.float32), w_down.astype(jnp.float32))
        grads = pull(cotangent[replica].astype(jnp.float32))
        outputs.append(result.astype(jnp.bfloat16))
        input_grads.append(grads[0].astype(jnp.bfloat16))
        if weight_sums is None:
            weight_sums = tuple(grads[1:])
        else:
            weight_sums = jax.tree.map(lambda left, right: left + right, weight_sums, tuple(grads[1:]))
    return (jnp.stack(outputs), jnp.stack(input_grads), weight_sums[0], weight_sums[1], weight_sums[2], weight_sums[3], weight_sums[4], weight_sums[5], weight_sums[6])
```

```python
from functools import partial
import math

import jax
import jax.numpy as jnp
from jax import lax
from jax.experimental import pallas as pl
from jax.experimental.pallas import tpu as pltpu
from jax.sharding import PartitionSpec as P

D = 1024
HEADS = 16
HEAD = 64
CLIPS = 16


def carried_in(part, axis, combine, identity):
    place = lax.axis_index(axis)
    gathered = lax.all_gather(part, axis)
    state = jnp.zeros_like(part) + jnp.asarray(identity, part.dtype)

    def one(step, state):
        return combine(state, lax.dynamic_index_in_dim(gathered, step, 0, False))

    return lax.fori_loop(0, place, one, state)


def matmul(left, right):
    return jnp.dot(left, right, preferred_element_type=jnp.float32)


def time_embedding(timestep_row):
    half_width = D // 2
    frequency = jnp.exp(-math.log(10000.0) * jnp.arange(half_width, dtype=jnp.float32) / half_width)
    angle = timestep_row.astype(jnp.float32)[:, None] * frequency[None, :]
    return jnp.concatenate([jnp.sin(angle), jnp.cos(angle)], axis=1)


def rotate_pairs(vectors, position, direction):
    half_size = vectors.shape[-1] // 2
    frequency = jnp.exp(-math.log(10000.0) * jnp.arange(half_size, dtype=jnp.float32) / half_size)
    angle = position[:, None] * frequency[None, :]
    cosine = jnp.cos(angle)[:, None, :]
    sine = jnp.sin(angle)[:, None, :] * direction
    first_half = vectors[..., :half_size]
    second_half = vectors[..., half_size:]
    return jnp.concatenate(
        [first_half * cosine - second_half * sine, second_half * cosine + first_half * sine],
        axis=-1,
    )


def normalize(inputs):
    centered = inputs - jnp.mean(inputs, axis=-1, keepdims=True)
    inverse = lax.rsqrt(jnp.mean(centered * centered, axis=-1, keepdims=True) + 1e-06)
    return (centered * inverse, inverse)


def norm_backward(grad_normed, normed, inverse):
    mean_grad = jnp.mean(grad_normed, axis=-1, keepdims=True)
    mean_mixed = jnp.mean(grad_normed * normed, axis=-1, keepdims=True)
    return inverse * (grad_normed - mean_grad - normed * mean_mixed)


def add_counts(earlier, later):
    return earlier + later


def block_rows_for(row_count):
    chosen = 1
    for candidate in range(1, 513):
        if row_count % candidate == 0:
            chosen = candidate
    return chosen


def stack_blocks(shard_piece):
    row_count = shard_piece[0].shape[0]
    block_rows = block_rows_for(row_count)
    block_count = row_count // block_rows
    return (
        shard_piece[0].reshape(block_count, block_rows, HEADS, HEAD),
        shard_piece[1].reshape(block_count, block_rows, HEADS, HEAD),
        shard_piece[2].reshape(block_count, block_rows),
    )


def forward_block(carried, key_block, queries, query_codes):
    running_max, running_sum, accumulated = carried
    key_rows, values, key_codes = key_block
    scores = (
        jnp.einsum("qhe,khe->hqk", queries, key_rows, preferred_element_type=jnp.float32) * 0.125
    )
    allowed = (query_codes[:, None] == key_codes.astype(jnp.float32)[None, :])[None]
    masked = jnp.where(allowed, scores, -1e30)
    new_max = jnp.maximum(running_max, jnp.max(masked, axis=2))
    rescale = jnp.exp(running_max - new_max)
    weights = jnp.where(allowed, jnp.exp(masked - new_max[:, :, None]), 0.0)
    running_sum = running_sum * rescale + jnp.sum(weights, axis=2)
    product = jnp.einsum(
        "hqk,khe->qhe", weights, values.astype(jnp.float32), precision=lax.Precision.HIGHEST
    )
    accumulated = accumulated * rescale.T[:, :, None] + product
    return (new_max, running_sum, accumulated)


def block_grads(key_block, queries, query_codes, grad_attn, log_total, delta_rows):
    key_rows, values, key_codes = key_block
    scores = (
        jnp.einsum("qhe,khe->hqk", queries, key_rows, preferred_element_type=jnp.float32) * 0.125
    )
    allowed = (query_codes[:, None] == key_codes.astype(jnp.float32)[None, :])[None]
    probabilities = jnp.exp(jnp.where(allowed, scores, -1e30) - log_total[:, :, None])
    grad_probs = jnp.einsum("qhe,khe->hqk", grad_attn, values, preferred_element_type=jnp.float32)
    grad_scores = (probabilities * (grad_probs - delta_rows[:, :, None])).astype(jnp.bfloat16)
    return (probabilities, grad_scores)


def body(
    tokens,
    w_query,
    w_key,
    w_value,
    w_out,
    w_ada,
    w_up,
    w_down,
    segments,
    validity,
    timesteps,
    cotangent,
):
    inputs = tokens[0].astype(jnp.float32)
    segment = segments[0]
    valid_row = validity[0]
    timestep_row = timesteps[0]
    grad_output = cotangent[0].astype(jnp.float32)
    frame_count = inputs.shape[0]
    highest = lax.Precision.HIGHEST
    cols_q, cols_k, cols_v, cols_o, cols_a, cols_u, cols_d = (
        lax.all_gather(w_query.astype(jnp.bfloat16), "seq", axis=1, tiled=True),
        lax.all_gather(w_key.astype(jnp.bfloat16), "seq", axis=1, tiled=True),
        lax.all_gather(w_value.astype(jnp.bfloat16), "seq", axis=1, tiled=True),
        lax.all_gather(w_out.astype(jnp.bfloat16), "seq", axis=1, tiled=True),
        lax.all_gather(w_ada.astype(jnp.bfloat16), "seq", axis=1, tiled=True),
        lax.all_gather(w_up.astype(jnp.bfloat16), "seq", axis=1, tiled=True),
        lax.all_gather(w_down.astype(jnp.bfloat16), "seq", axis=1, tiled=True),
    )
    full_q, full_k, full_v, full_o, full_a, full_u, full_d = (
        lax.all_gather(cols_q, "batch", axis=0, tiled=True),
        lax.all_gather(cols_k, "batch", axis=0, tiled=True),
        lax.all_gather(cols_v, "batch", axis=0, tiled=True),
        lax.all_gather(cols_o, "batch", axis=0, tiled=True),
        lax.all_gather(cols_a, "batch", axis=0, tiled=True),
        lax.all_gather(cols_u, "batch", axis=0, tiled=True),
        lax.all_gather(cols_d, "batch", axis=0, tiled=True),
    )
    silu_time = jax.nn.silu(time_embedding(timestep_row)).astype(jnp.bfloat16)
    emb_rows = matmul(silu_time, full_a)
    member = segment[:, None] == jnp.arange(CLIPS, dtype=jnp.int32)[None, :]
    one_hot = member.astype(jnp.float32)
    counted = member.astype(jnp.int32)
    modulation = jnp.dot(one_hot, emb_rows, precision=highest)
    shift_attn, scale_attn, gate_attn, shift_ffn, scale_ffn, gate_ffn = jnp.split(
        modulation, 6, axis=1
    )
    offsets = carried_in(
        jnp.sum(counted, axis=0), "seq", add_counts, jnp.zeros((CLIPS,), jnp.int32)
    )
    before = jnp.cumsum(counted, axis=0) - counted + offsets[None, :]
    position = jnp.sum(before * counted, axis=1).astype(jnp.float32)
    normed, inverse = normalize(inputs)
    attn_input = (normed * (1.0 + scale_attn) + shift_attn).astype(jnp.bfloat16)
    queries = rotate_pairs(
        matmul(attn_input, full_q).reshape(frame_count, HEADS, HEAD), position, 1.0
    ).astype(jnp.bfloat16)
    key_flat = (
        rotate_pairs(matmul(attn_input, full_k).reshape(frame_count, HEADS, HEAD), position, 1.0)
        .astype(jnp.bfloat16)
        .reshape(frame_count, D)
    )
    value_flat = matmul(attn_input, full_v).astype(jnp.bfloat16)
    key_codes = jnp.where(valid_row == 1, segment, -1).astype(jnp.bfloat16)
    query_codes = segment.astype(jnp.float32)
    start_state = (
        jnp.full((HEADS, frame_count), -1e30, jnp.float32),
        jnp.zeros((HEADS, frame_count), jnp.float32),
        jnp.zeros((frame_count, HEADS, HEAD), jnp.float32),
    )

    def step(state, key_block):
        return (forward_block(state, key_block, queries, query_codes), None)

    running_max, running_sum, accumulated = lax.scan(
        step,
        start_state,
        stack_blocks(
            (
                lax.all_gather(key_flat, "seq", axis=0, tiled=True),
                lax.all_gather(value_flat, "seq", axis=0, tiled=True),
                lax.all_gather(key_codes, "seq", axis=0, tiled=True),
            )
        ),
    )[0]
    attended = accumulated / running_sum.T[:, :, None]
    log_total = running_max + jnp.log(running_sum)
    attended_low = attended.reshape(frame_count, D).astype(jnp.bfloat16)
    attn_branch = matmul(attended_low, full_o)
    middle = inputs + gate_attn * attn_branch
    normed_mid, inverse_mid = normalize(middle)
    ffn_input = (normed_mid * (1.0 + scale_ffn) + shift_ffn).astype(jnp.bfloat16)
    hidden = matmul(ffn_input, full_u)
    activated, gelu_pull = jax.vjp(partial(jax.nn.gelu, approximate=True), hidden)
    activated_low = activated.astype(jnp.bfloat16)
    ffn_branch = matmul(activated_low, full_d)
    result = middle + gate_ffn * ffn_branch
    back_q, back_k, back_v, back_o, back_u, back_d = (
        full_q,
        full_k,
        full_v,
        full_o,
        full_u,
        full_d,
    )
    grad_gate_ffn = grad_output * ffn_branch
    g_ffn = (grad_output * gate_ffn).astype(jnp.bfloat16)
    grad_down_local = matmul(activated_low.T, g_ffn)
    grad_activated = matmul(g_ffn, back_d.T)
    g_hidden = gelu_pull(grad_activated)[0].astype(jnp.bfloat16)
    grad_up_local = matmul(ffn_input.T, g_hidden)
    grad_ffn_input = matmul(g_hidden, back_u.T)
    grad_middle = grad_output + norm_backward(
        grad_ffn_input * (1.0 + scale_ffn), normed_mid, inverse_mid
    )
    grad_scale_ffn = grad_ffn_input * normed_mid
    grad_gate_attn = grad_middle * attn_branch
    g_attn = (grad_middle * gate_attn).astype(jnp.bfloat16)
    grad_out_local = matmul(attended_low.T, g_attn)
    grad_attn = matmul(g_attn, back_o.T).astype(jnp.bfloat16).reshape(frame_count, HEADS, HEAD)
    delta_rows = jnp.einsum("qhe,qhe->hq", grad_attn.astype(jnp.float32), attended)
    zero_query = jnp.zeros((frame_count, HEADS, HEAD), jnp.float32)
    gathered = (
        lax.all_gather(key_flat, "seq", axis=0, tiled=True),
        lax.all_gather(value_flat, "seq", axis=0, tiled=True),
        lax.all_gather(key_codes, "seq", axis=0, tiled=True),
    )
    pack_rows = gathered[0].shape[0]
    grad_attn_wide = grad_attn.astype(jnp.float32)

    def joint_step(total_grad, key_block):
        probabilities, grad_scores = block_grads(
            key_block, queries, query_codes, grad_attn, log_total, delta_rows
        )
        total_grad = total_grad + 0.125 * jnp.einsum(
            "hqk,khe->qhe", grad_scores, key_block[0], preferred_element_type=jnp.float32
        )
        grad_keys = 0.125 * jnp.einsum(
            "hqk,qhe->khe", grad_scores, queries, preferred_element_type=jnp.float32
        )
        grad_values = jnp.einsum("hqk,qhe->khe", probabilities, grad_attn_wide, precision=highest)
        return (total_grad, (grad_keys, grad_values))

    grad_queries_rot, both_grads = lax.scan(joint_step, zero_query, stack_blocks(gathered))
    key_value_terms = jnp.concatenate(
        [both_grads[0].reshape(pack_rows, D), both_grads[1].reshape(pack_rows, D)], axis=1
    )
    key_value_grad = lax.psum_scatter(key_value_terms, "seq", scatter_dimension=0, tiled=True)
    g_query = (
        rotate_pairs(grad_queries_rot, position, -1.0).reshape(frame_count, D).astype(jnp.bfloat16)
    )
    g_key = (
        rotate_pairs(key_value_grad[:, :D].reshape(frame_count, HEADS, HEAD), position, -1.0)
        .reshape(frame_count, D)
        .astype(jnp.bfloat16)
    )
    g_value = key_value_grad[:, D:].astype(jnp.bfloat16)
    grad_query_local = matmul(attn_input.T, g_query)
    grad_key_local = matmul(attn_input.T, g_key)
    grad_value_local = matmul(attn_input.T, g_value)
    grad_attn_input = (
        matmul(g_query, back_q.T) + matmul(g_key, back_k.T) + matmul(g_value, back_v.T)
    )
    grad_inputs = grad_middle + norm_backward(grad_attn_input * (1.0 + scale_attn), normed, inverse)
    grad_modulation = jnp.concatenate(
        [
            grad_attn_input,
            grad_attn_input * normed,
            grad_gate_attn,
            grad_ffn_input,
            grad_scale_ffn,
            grad_gate_ffn,
        ],
        axis=1,
    )
    grad_emb = jnp.dot(one_hot.T, grad_modulation, precision=highest)
    grad_ada_local = jnp.dot(silu_time.astype(jnp.float32).T, grad_emb, precision=highest)
    part_q, part_k, part_v, part_o, part_a, part_u, part_d = (
        lax.psum_scatter(grad_query_local, "seq", scatter_dimension=1, tiled=True),
        lax.psum_scatter(grad_key_local, "seq", scatter_dimension=1, tiled=True),
        lax.psum_scatter(grad_value_local, "seq", scatter_dimension=1, tiled=True),
        lax.psum_scatter(grad_out_local, "seq", scatter_dimension=1, tiled=True),
        lax.psum_scatter(grad_ada_local, "seq", scatter_dimension=1, tiled=True),
        lax.psum_scatter(grad_up_local, "seq", scatter_dimension=1, tiled=True),
        lax.psum_scatter(grad_down_local, "seq", scatter_dimension=1, tiled=True),
    )
    final_q, final_k, final_v, final_o, final_a, final_u, final_d = (
        lax.psum_scatter(
            part_q.astype(jnp.bfloat16), "batch", scatter_dimension=0, tiled=True
        ).astype(jnp.float32),
        lax.psum_scatter(
            part_k.astype(jnp.bfloat16), "batch", scatter_dimension=0, tiled=True
        ).astype(jnp.float32),
        lax.psum_scatter(
            part_v.astype(jnp.bfloat16), "batch", scatter_dimension=0, tiled=True
        ).astype(jnp.float32),
        lax.psum_scatter(
            part_o.astype(jnp.bfloat16), "batch", scatter_dimension=0, tiled=True
        ).astype(jnp.float32),
        lax.psum_scatter(
            part_a.astype(jnp.bfloat16), "batch", scatter_dimension=0, tiled=True
        ).astype(jnp.float32),
        lax.psum_scatter(
            part_u.astype(jnp.bfloat16), "batch", scatter_dimension=0, tiled=True
        ).astype(jnp.float32),
        lax.psum_scatter(
            part_d.astype(jnp.bfloat16), "batch", scatter_dimension=0, tiled=True
        ).astype(jnp.float32),
    )
    return (
        result.astype(jnp.bfloat16)[None],
        grad_inputs.astype(jnp.bfloat16)[None],
        final_q,
        final_k,
        final_v,
        final_o,
        final_a,
        final_u,
        final_d,
    )


TWO = 2 * HEAD
ROWS = 256
BIG = 1e30
SEQ = 8
REPLICAS = 4


def swap(part, axis, distance):
    size = SEQ if axis == "seq" else REPLICAS
    return lax.ppermute(part, axis, [(i, i ^ distance) for i in range(size)])


def along_line(part, step):
    pairs = [
        (z * 2 + y, (z + step) * 2 + y) for z in range(4) for y in range(2) if 0 <= z + step < 4
    ]
    return lax.ppermute(part, "seq", pairs)


def gather_rows(part):
    place = lax.axis_index("seq")
    z, y = place // 2, place % 2
    right, left = [part], [part]
    for _ in range(3):
        right.append(along_line(right[-1], 1))
        left.append(along_line(left[-1], -1))
    line = [part] + [jnp.where(z >= k, right[k], left[4 - k]) for k in range(1, 4)]
    other = [swap(chunk, "seq", 1) for chunk in line]
    line, other = jnp.stack(line[::-1] * 2), jnp.stack(other[::-1] * 2)
    line = lax.dynamic_slice_in_dim(line, 3 - z, 4, 0)
    other = lax.dynamic_slice_in_dim(other, 3 - z, 4, 0)
    pair = jnp.stack([jnp.where(y == 0, line, other), jnp.where(y == 0, other, line)], axis=1)
    return pair.reshape((SEQ * part.shape[0],) + part.shape[1:])


def exchange(blocks):
    return lax.all_to_all(blocks, "seq", 0, 0, tiled=True)


def sum_over_replicas(grad):
    place = lax.axis_index("batch")
    x, core = place // 2, place % 2
    rows, cols = grad.shape[0] // REPLICAS, grad.shape[1]
    parts = grad.reshape(2, 2, rows, cols)
    keep = lax.dynamic_index_in_dim(parts, core, 1, False)
    send = lax.dynamic_index_in_dim(parts, 1 - core, 1, False)
    both = (
        keep.astype(jnp.float32) + swap(send.astype(jnp.bfloat16), "batch", 1).astype(jnp.float32)
    ).astype(jnp.bfloat16)
    keep = lax.dynamic_index_in_dim(both, x, 0, False)
    send = lax.dynamic_index_in_dim(both, 1 - x, 0, False)
    return keep.astype(jnp.float32) + swap(send, "batch", 2).astype(jnp.float32)


def sum_over_frames(part):
    place = lax.axis_index("seq")
    rows, cols = part.shape[0], part.shape[1] // SEQ
    blocks = part.astype(jnp.bfloat16).reshape(rows, SEQ, cols)
    total = lax.dynamic_index_in_dim(part.reshape(rows, SEQ, cols), place, 1, False)
    for k in range(1, SEQ):
        sent = swap(lax.dynamic_index_in_dim(blocks, place ^ k, 1, False), "seq", k)
        total = total + sent.astype(jnp.float32)
    return total


def turn(vectors, cosine, sine):
    lane = lax.broadcasted_iota(jnp.int32, vectors.shape, 1)
    first = (lane % HEAD) < HEAD // 2
    partner = jnp.where(
        first,
        pltpu.roll(vectors, TWO - HEAD // 2, 1),
        pltpu.roll(vectors, HEAD // 2, 1),
    )
    return vectors * cosine + partner * jnp.where(first, -sine, sine)


def of_head(vectors, head):
    lane = lax.broadcasted_iota(jnp.int32, vectors.shape, 1)
    return jnp.where(lane // HEAD == head, vectors, jnp.zeros_like(vectors))


def dot_t(left, right):
    return lax.dot_general(
        left, right, (((1,), (1,)), ((), ())), preferred_element_type=jnp.float32
    )


def project_kernel(x_ref, member_ref, bar_ref, cos_ref, sin_ref, emb_ref, w_ref,
                   input_ref, q_ref, k_ref, kt_ref, v_ref, vt_ref):
    rows = x_ref[...].astype(jnp.float32)
    centered = rows - jnp.mean(rows, axis=1, keepdims=True)
    inverse = lax.rsqrt(jnp.mean(centered * centered, axis=1, keepdims=True) + 1e-06)
    modulation = matmul(member_ref[...], emb_ref[...])
    low = (centered * inverse * (1.0 + modulation[:, D:]) + modulation[:, :D]).astype(jnp.bfloat16)
    input_ref[...] = low
    product = matmul(low, w_ref[...])
    cosine, sine = cos_ref[...], sin_ref[...]
    keys = turn(product[:, TWO:2 * TWO], cosine, sine)
    values = product[:, 2 * TWO:]
    q_ref[...] = turn(product[:, :TWO], cosine, sine).astype(jnp.bfloat16)
    k_ref[:, :TWO] = keys.astype(jnp.bfloat16)
    k_ref[:, TWO:] = bar_ref[...]
    kt_ref[...] = keys.T.astype(jnp.bfloat16)
    v_ref[...] = values.astype(jnp.bfloat16)
    vt_ref[...] = values.T.astype(jnp.bfloat16)


def rows_spec(width):
    return pl.BlockSpec((ROWS, width), lambda i: (i, 0))


def cols_spec(height):
    return pl.BlockSpec((height, ROWS), lambda i: (0, i))


def whole_spec(height, width):
    return pl.BlockSpec((height, width), lambda i: (0, 0))


def params(mib):
    return pltpu.CompilerParams(
        dimension_semantics=("arbitrary",), vmem_limit_bytes=mib * 1024 * 1024
    )


def project(x, member, bar, cosine, sine, emb, weights):
    frames = x.shape[0]
    low = jnp.bfloat16
    return pl.pallas_call(
        project_kernel,
        grid=(frames // ROWS,),
        in_specs=[rows_spec(D), rows_spec(TWO), rows_spec(TWO), rows_spec(TWO), rows_spec(TWO),
                  whole_spec(TWO, 2 * D), whole_spec(D, 3 * TWO)],
        out_specs=[rows_spec(D), rows_spec(TWO), rows_spec(2 * TWO), cols_spec(TWO),
                   rows_spec(TWO), cols_spec(TWO)],
        out_shape=[
            jax.ShapeDtypeStruct((frames, D), low),
            jax.ShapeDtypeStruct((frames, TWO), low),
            jax.ShapeDtypeStruct((frames, 2 * TWO), low),
            jax.ShapeDtypeStruct((TWO, frames), low),
            jax.ShapeDtypeStruct((frames, TWO), low),
            jax.ShapeDtypeStruct((TWO, frames), low),
        ],
        compiler_params=params(40),
        name="project",
    )(x, member, bar, cosine, sine, emb, weights)


def attend_kernel(q_ref, member_ref, k_ref, vt_ref, att_ref, low_ref, log_ref, score_ref):
    frames = k_ref.shape[0]
    step = min(frames, 512)
    queries = q_ref[...] * 0.125
    member = member_ref[...]
    halves = []
    for head in range(2):
        wide = jnp.concatenate([of_head(queries, head), member], axis=1)
        largest = jnp.full((1, ROWS), -BIG, jnp.float32)
        for start in range(0, frames, step):
            scores = dot_t(k_ref[start:start + step, :], wide)
            score_ref[start:start + step, :] = scores
            largest = jnp.maximum(largest, jnp.max(scores, axis=0, keepdims=True))
        total = jnp.zeros((1, ROWS), jnp.float32)
        out = jnp.zeros((TWO, ROWS), jnp.float32)
        for start in range(0, frames, step):
            weights = jnp.exp(score_ref[start:start + step, :] - largest)
            total = total + jnp.sum(weights, axis=0, keepdims=True)
            out = out + matmul(vt_ref[:, start:start + step], weights.astype(jnp.bfloat16))
        halves.append(out[head * HEAD:(head + 1) * HEAD, :] / total)
        log_ref[head:head + 1, :] = largest + jnp.log(total)
    attended = jnp.concatenate(halves, axis=0).T
    att_ref[...] = attended
    low_ref[...] = attended.astype(jnp.bfloat16)


def attend(q, member, k, vt):
    frames = q.shape[0]
    return pl.pallas_call(
        attend_kernel,
        grid=(frames // ROWS,),
        in_specs=[rows_spec(TWO), rows_spec(TWO), whole_spec(frames, 2 * TWO),
                  whole_spec(TWO, frames)],
        out_specs=[rows_spec(TWO), rows_spec(TWO), cols_spec(8)],
        out_shape=[
            jax.ShapeDtypeStruct((frames, TWO), jnp.float32),
            jax.ShapeDtypeStruct((frames, TWO), jnp.bfloat16),
            jax.ShapeDtypeStruct((8, frames), jnp.float32),
        ],
        scratch_shapes=[pltpu.VMEM((frames, ROWS), jnp.float32)],
        compiler_params=params(40),
        name="attend",
    )(q, member, k, vt)


def attend_back_kernel(q_ref, member_ref, grad_ref, att_ref, log_ref, cos_ref, sin_ref, cos_all_ref,
                       sin_all_ref, k_ref, kt_ref, v_ref, gq_ref, gk_ref, gv_ref, dk_ref, dv_ref):
    block = pl.program_id(0)
    frames = k_ref.shape[0]
    step = min(frames, 512)

    @pl.when(block == 0)
    def _():
        dk_ref[...] = jnp.zeros_like(dk_ref)
        dv_ref[...] = jnp.zeros_like(dv_ref)

    queries = q_ref[...] * 0.125
    member = member_ref[...]
    grad = grad_ref[...]
    mixed = (grad.astype(jnp.float32) * att_ref[...]).T
    halves = []
    wides, grads, deltas = [], [], []
    for head in range(2):
        wides.append(jnp.concatenate([of_head(queries, head), member], axis=1))
        grads.append(of_head(grad, head))
        deltas.append(jnp.sum(mixed[head * HEAD:(head + 1) * HEAD, :], axis=0, keepdims=True))
    totals = [jnp.zeros((TWO, ROWS), jnp.float32) for _ in range(2)]
    for start in range(0, frames, step):
        part = slice(start, start + step)
        dk = dk_ref[part, :]
        dv = dv_ref[part, :]
        for head in range(2):
            scores = dot_t(k_ref[part, :], wides[head])
            weights = jnp.exp(scores - log_ref[head:head + 1, :])
            grad_weights = dot_t(v_ref[part, :], grads[head])
            grad_scores = (weights * (grad_weights - deltas[head])).astype(jnp.bfloat16)
            dv = dv + matmul(weights.astype(jnp.bfloat16), grads[head])
            dk = dk + matmul(grad_scores, wides[head][:, :TWO])
            totals[head] = totals[head] + matmul(kt_ref[:, part], grad_scores)
        dk_ref[part, :] = dk
        dv_ref[part, :] = dv
    dq = jnp.concatenate([totals[0][:HEAD, :], totals[1][HEAD:, :]], axis=0).T * 0.125
    gq_ref[...] = turn(dq, cos_ref[...], -sin_ref[...]).astype(jnp.bfloat16)

    @pl.when(block == pl.num_programs(0) - 1)
    def _():
        gk_ref[...] = turn(dk_ref[...], cos_all_ref[...], -sin_all_ref[...]).astype(jnp.bfloat16)
        gv_ref[...] = dv_ref[...].astype(jnp.bfloat16)


def attend_back(q, member, grad, att, log_total, cosine, sine, k, kt, v):
    frames = q.shape[0]
    pair = jax.ShapeDtypeStruct((frames, TWO), jnp.bfloat16)
    return pl.pallas_call(
        attend_back_kernel,
        grid=(frames // ROWS,),
        in_specs=[rows_spec(TWO), rows_spec(TWO), rows_spec(TWO), rows_spec(TWO), cols_spec(8),
                  rows_spec(TWO), rows_spec(TWO), whole_spec(frames, TWO), whole_spec(frames, TWO),
                  whole_spec(frames, 2 * TWO), whole_spec(TWO, frames), whole_spec(frames, TWO)],
        out_specs=[rows_spec(TWO), whole_spec(frames, TWO), whole_spec(frames, TWO)],
        out_shape=[pair, pair, pair],
        scratch_shapes=[pltpu.VMEM((frames, TWO), jnp.float32),
                        pltpu.VMEM((frames, TWO), jnp.float32)],
        compiler_params=params(48),
        name="attend_back",
    )(q, member, grad, att, log_total, cosine, sine, cosine, sine, k, kt, v)


def three_terms(values):
    high = lax.reduce_precision(values, 8, 7)
    middle = lax.reduce_precision(values - high, 8, 7)
    return [high, middle, values - high - middle]


def body_fast(
    tokens, w_query, w_key, w_value, w_out, w_ada, w_up, w_down,
    segments, validity, timesteps, cotangent,
):
    highest = lax.Precision.HIGHEST
    low = jnp.bfloat16
    replica = lax.axis_index("batch")
    inputs = tokens[0].astype(jnp.float32)
    grad_output = cotangent[0].astype(jnp.float32)
    frame_count = inputs.shape[0]
    frames = frame_count * SEQ
    segment = segments[0]

    x_all = gather_rows(tokens[0])
    codes = lax.all_gather(segment * 2 + (validity[0] == 1), "seq", axis=0, tiled=True)
    clip = codes // 2
    clips = jnp.arange(CLIPS, dtype=jnp.int32)
    member_all = clip[:, None] == clips[None, :]
    counted = member_all.astype(jnp.int32)
    before = jnp.cumsum(counted, axis=0) - counted
    position = jnp.sum(before * counted, axis=1).astype(jnp.float32)
    half = HEAD // 2
    frequency = jnp.exp(-math.log(10000.0) * jnp.arange(half, dtype=jnp.float32) / half)
    angle = position[:, None] * frequency[None, :]
    cosine = jnp.tile(jnp.cos(angle), (1, 4))
    sine = jnp.tile(jnp.sin(angle), (1, 4))
    spread = member_all.astype(low)
    member = jnp.concatenate([spread] * 3 + [jnp.zeros((frames, TWO - 3 * CLIPS), low)], axis=1)
    allowed = jnp.where((codes % 2 == 1)[:, None], member_all, False)
    bar = jnp.concatenate(
        [jnp.where(allowed, 0.0, -BIG).astype(low), jnp.zeros((frames, TWO - CLIPS), low)], axis=1
    )

    times = lax.all_gather(timesteps[0], "batch", axis=0, tiled=True)
    silu_all = jax.nn.silu(time_embedding(times)).astype(low)
    wide = w_ada.shape[0]
    silu_part = lax.dynamic_slice_in_dim(silu_all, replica * wide, wide, 1)
    emb_part = matmul(silu_part, w_ada.astype(low)).reshape(REPLICAS, CLIPS, -1)
    emb_cols = jnp.sum(lax.all_to_all(emb_part, "batch", 0, 0, tiled=True), axis=0)
    emb = exchange(jnp.broadcast_to(emb_cols[None], (SEQ,) + emb_cols.shape))
    emb = emb.transpose(1, 0, 2).reshape(CLIPS, -1)
    emb_terms = jnp.concatenate(
        [t.astype(low) for t in three_terms(emb[:, :2 * D])]
        + [jnp.zeros((TWO - 3 * CLIPS, 2 * D), low)], axis=0
    )

    heads_w = jnp.concatenate([w_query, w_key, w_value], axis=1).astype(low)
    heads_w = lax.all_gather(heads_w, "batch", axis=0, tiled=True)

    def whole(weight):
        gathered = lax.all_gather(weight.astype(low), ("batch", "seq"), axis=0)
        rows, cols = weight.shape
        return gathered.reshape(REPLICAS, SEQ, rows, cols).transpose(0, 2, 1, 3).reshape(
            REPLICAS * rows, SEQ * cols
        )

    full_o, full_u, full_d = whole(w_out), whole(w_up), whole(w_down)
    full_q, full_k, full_v = whole(w_query), whole(w_key), whole(w_value)

    attn_input, q, k, kt, v, vt = project(x_all, member, bar, cosine, sine, emb_terms, heads_w)
    attended, attended_low, log_total = attend(q, member, k, vt)
    mine = exchange(attended_low.reshape(SEQ, frame_count, TWO))
    mine = mine.transpose(1, 0, 2).reshape(frame_count, D)

    one_hot = (segment[:, None] == clips[None, :]).astype(jnp.float32)
    modulation = jnp.dot(one_hot, emb, precision=highest)
    shift_attn, scale_attn, gate_attn, shift_ffn, scale_ffn, gate_ffn = jnp.split(
        modulation, 6, axis=1
    )
    attn_branch = matmul(mine, full_o)
    middle = inputs + gate_attn * attn_branch
    normed_mid, inverse_mid = normalize(middle)
    ffn_input = (normed_mid * (1.0 + scale_ffn) + shift_ffn).astype(low)
    hidden = matmul(ffn_input, full_u)
    activated, gelu_pull = jax.vjp(partial(jax.nn.gelu, approximate=True), hidden)
    activated_low = activated.astype(low)
    ffn_branch = matmul(activated_low, full_d)
    result = middle + gate_ffn * ffn_branch
    grad_gate_ffn = grad_output * ffn_branch
    g_ffn = (grad_output * gate_ffn).astype(low)
    grad_down_local = matmul(activated_low.T, g_ffn).astype(low)
    grad_activated = matmul(g_ffn, full_d.T)
    g_hidden = gelu_pull(grad_activated)[0].astype(low)
    grad_up_local = matmul(ffn_input.T, g_hidden).astype(low)
    grad_ffn_input = matmul(g_hidden, full_u.T)
    grad_middle = grad_output + norm_backward(
        grad_ffn_input * (1.0 + scale_ffn), normed_mid, inverse_mid
    )
    grad_scale_ffn = grad_ffn_input * normed_mid
    grad_gate_attn = grad_middle * attn_branch
    g_attn = (grad_middle * gate_attn).astype(low)
    grad_out_local = matmul(mine.T, g_attn).astype(low)
    grad_attn = matmul(g_attn, full_o.T).astype(low)

    final_d = sum_over_frames(sum_over_replicas(grad_down_local))
    final_u = sum_over_frames(sum_over_replicas(grad_up_local))
    final_o = sum_over_frames(sum_over_replicas(grad_out_local))

    grad_heads = exchange(grad_attn.reshape(frame_count, SEQ, TWO).transpose(1, 0, 2))
    grad_heads = grad_heads.reshape(frames, TWO)
    g_query, g_key, g_value = attend_back(
        q, member, grad_heads, attended, log_total, cosine, sine, k, kt, v
    )
    g_heads = jnp.concatenate([g_query, g_key, g_value], axis=1)
    grad_heads_w = matmul(attn_input.T, g_heads).astype(low)
    own = exchange(g_heads.reshape(SEQ, frame_count, 3 * TWO)).reshape(SEQ, frame_count, 3, TWO)
    own = own.transpose(2, 1, 0, 3).reshape(3, frame_count, D)
    final_heads = sum_over_replicas(grad_heads_w)

    grad_attn_input = (
        matmul(own[0], full_q.T) + matmul(own[1], full_k.T) + matmul(own[2], full_v.T)
    )
    normed, inverse = normalize(inputs)
    grad_inputs = grad_middle + norm_backward(grad_attn_input * (1.0 + scale_attn), normed, inverse)
    grad_modulation = jnp.concatenate(
        [
            grad_attn_input,
            grad_attn_input * normed,
            grad_gate_attn,
            grad_ffn_input,
            grad_scale_ffn,
            grad_gate_ffn,
        ],
        axis=1,
    )
    grad_emb = jnp.dot(one_hot.T, grad_modulation, precision=highest)
    grad_emb = grad_emb.reshape(CLIPS, SEQ, -1).transpose(1, 0, 2)
    grad_emb = jnp.sum(exchange(grad_emb), axis=0)
    grad_emb = lax.all_gather(grad_emb, "batch", axis=0, tiled=True)
    final_a = jnp.dot(silu_part.astype(jnp.float32).T, grad_emb, precision=highest)
    head_cols = w_query.shape[1]
    return (
        result.astype(low)[None],
        grad_inputs.astype(low)[None],
        final_heads[:, :head_cols],
        final_heads[:, head_cols:2 * head_cols],
        final_heads[:, 2 * head_cols:],
        final_o,
        final_a,
        final_u,
        final_d,
    )


def solution(mesh):
    fits = mesh.shape["seq"] == SEQ and mesh.shape["batch"] == REPLICAS
    chosen = body_fast if fits else body
    return jax.shard_map(
        chosen,
        mesh=mesh,
        in_specs=(
            P("batch", "seq", None),
            P("batch", "seq"),
            P("batch", "seq"),
            P("batch", "seq"),
            P("batch", "seq"),
            P("batch", "seq"),
            P("batch", "seq"),
            P("batch", "seq"),
            P("batch", "seq"),
            P("batch", "seq"),
            P("batch", None),
            P("batch", "seq", None),
        ),
        out_specs=(
            P("batch", "seq", None),
            P("batch", "seq", None),
            P("batch", "seq"),
            P("batch", "seq"),
            P("batch", "seq"),
            P("batch", "seq"),
            P("batch", "seq"),
            P("batch", "seq"),
            P("batch", "seq"),
        ),
        check_vma=False,
    )
```

```python
from functools import partial
import math

import jax
import jax.numpy as jnp
from jax import lax
from jax.experimental import pallas as pl
from jax.experimental.pallas import tpu as pltpu
from jax.sharding import PartitionSpec as P

D = 1024
HEADS = 16
HEAD = 64
CLIPS = 16


def carried_in(part, axis, combine, identity):
    place = lax.axis_index(axis)
    gathered = lax.all_gather(part, axis)
    state = jnp.zeros_like(part) + jnp.asarray(identity, part.dtype)

    def one(step, state):
        return combine(state, lax.dynamic_index_in_dim(gathered, step, 0, False))

    return lax.fori_loop(0, place, one, state)


def matmul(left, right):
    return jnp.dot(left, right, preferred_element_type=jnp.float32)


def time_embedding(timestep_row):
    half_width = D // 2
    frequency = jnp.exp(-math.log(10000.0) * jnp.arange(half_width, dtype=jnp.float32) / half_width)
    angle = timestep_row.astype(jnp.float32)[:, None] * frequency[None, :]
    return jnp.concatenate([jnp.sin(angle), jnp.cos(angle)], axis=1)


def rotate_pairs(vectors, position, direction):
    half_size = vectors.shape[-1] // 2
    frequency = jnp.exp(-math.log(10000.0) * jnp.arange(half_size, dtype=jnp.float32) / half_size)
    angle = position[:, None] * frequency[None, :]
    cosine = jnp.cos(angle)[:, None, :]
    sine = jnp.sin(angle)[:, None, :] * direction
    first_half = vectors[..., :half_size]
    second_half = vectors[..., half_size:]
    return jnp.concatenate(
        [first_half * cosine - second_half * sine, second_half * cosine + first_half * sine],
        axis=-1,
    )


def normalize(inputs):
    centered = inputs - jnp.mean(inputs, axis=-1, keepdims=True)
    inverse = lax.rsqrt(jnp.mean(centered * centered, axis=-1, keepdims=True) + 1e-06)
    return (centered * inverse, inverse)


def norm_backward(grad_normed, normed, inverse):
    mean_grad = jnp.mean(grad_normed, axis=-1, keepdims=True)
    mean_mixed = jnp.mean(grad_normed * normed, axis=-1, keepdims=True)
    return inverse * (grad_normed - mean_grad - normed * mean_mixed)


def add_counts(earlier, later):
    return earlier + later


def block_rows_for(row_count):
    chosen = 1
    for candidate in range(1, 513):
        if row_count % candidate == 0:
            chosen = candidate
    return chosen


def stack_blocks(shard_piece):
    row_count = shard_piece[0].shape[0]
    block_rows = block_rows_for(row_count)
    block_count = row_count // block_rows
    return (
        shard_piece[0].reshape(block_count, block_rows, HEADS, HEAD),
        shard_piece[1].reshape(block_count, block_rows, HEADS, HEAD),
        shard_piece[2].reshape(block_count, block_rows),
    )


def forward_block(carried, key_block, queries, query_codes):
    running_max, running_sum, accumulated = carried
    key_rows, values, key_codes = key_block
    scores = (
        jnp.einsum("qhe,khe->hqk", queries, key_rows, preferred_element_type=jnp.float32) * 0.125
    )
    allowed = (query_codes[:, None] == key_codes.astype(jnp.float32)[None, :])[None]
    masked = jnp.where(allowed, scores, -1e30)
    new_max = jnp.maximum(running_max, jnp.max(masked, axis=2))
    rescale = jnp.exp(running_max - new_max)
    weights = jnp.where(allowed, jnp.exp(masked - new_max[:, :, None]), 0.0)
    running_sum = running_sum * rescale + jnp.sum(weights, axis=2)
    product = jnp.einsum(
        "hqk,khe->qhe", weights, values.astype(jnp.float32), precision=lax.Precision.HIGHEST
    )
    accumulated = accumulated * rescale.T[:, :, None] + product
    return (new_max, running_sum, accumulated)


def block_grads(key_block, queries, query_codes, grad_attn, log_total, delta_rows):
    key_rows, values, key_codes = key_block
    scores = (
        jnp.einsum("qhe,khe->hqk", queries, key_rows, preferred_element_type=jnp.float32) * 0.125
    )
    allowed = (query_codes[:, None] == key_codes.astype(jnp.float32)[None, :])[None]
    probabilities = jnp.exp(jnp.where(allowed, scores, -1e30) - log_total[:, :, None])
    grad_probs = jnp.einsum("qhe,khe->hqk", grad_attn, values, preferred_element_type=jnp.float32)
    grad_scores = (probabilities * (grad_probs - delta_rows[:, :, None])).astype(jnp.bfloat16)
    return (probabilities, grad_scores)


def body(
    tokens,
    w_query,
    w_key,
    w_value,
    w_out,
    w_ada,
    w_up,
    w_down,
    segments,
    validity,
    timesteps,
    cotangent,
):
    inputs = tokens[0].astype(jnp.float32)
    segment = segments[0]
    valid_row = validity[0]
    timestep_row = timesteps[0]
    grad_output = cotangent[0].astype(jnp.float32)
    frame_count = inputs.shape[0]
    highest = lax.Precision.HIGHEST
    cols_q, cols_k, cols_v, cols_o, cols_a, cols_u, cols_d = (
        lax.all_gather(w_query.astype(jnp.bfloat16), "seq", axis=1, tiled=True),
        lax.all_gather(w_key.astype(jnp.bfloat16), "seq", axis=1, tiled=True),
        lax.all_gather(w_value.astype(jnp.bfloat16), "seq", axis=1, tiled=True),
        lax.all_gather(w_out.astype(jnp.bfloat16), "seq", axis=1, tiled=True),
        lax.all_gather(w_ada.astype(jnp.bfloat16), "seq", axis=1, tiled=True),
        lax.all_gather(w_up.astype(jnp.bfloat16), "seq", axis=1, tiled=True),
        lax.all_gather(w_down.astype(jnp.bfloat16), "seq", axis=1, tiled=True),
    )
    full_q, full_k, full_v, full_o, full_a, full_u, full_d = (
        lax.all_gather(cols_q, "batch", axis=0, tiled=True),
        lax.all_gather(cols_k, "batch", axis=0, tiled=True),
        lax.all_gather(cols_v, "batch", axis=0, tiled=True),
        lax.all_gather(cols_o, "batch", axis=0, tiled=True),
        lax.all_gather(cols_a, "batch", axis=0, tiled=True),
        lax.all_gather(cols_u, "batch", axis=0, tiled=True),
        lax.all_gather(cols_d, "batch", axis=0, tiled=True),
    )
    silu_time = jax.nn.silu(time_embedding(timestep_row)).astype(jnp.bfloat16)
    emb_rows = matmul(silu_time, full_a)
    member = segment[:, None] == jnp.arange(CLIPS, dtype=jnp.int32)[None, :]
    one_hot = member.astype(jnp.float32)
    counted = member.astype(jnp.int32)
    modulation = jnp.dot(one_hot, emb_rows, precision=highest)
    shift_attn, scale_attn, gate_attn, shift_ffn, scale_ffn, gate_ffn = jnp.split(
        modulation, 6, axis=1
    )
    offsets = carried_in(
        jnp.sum(counted, axis=0), "seq", add_counts, jnp.zeros((CLIPS,), jnp.int32)
    )
    before = jnp.cumsum(counted, axis=0) - counted + offsets[None, :]
    position = jnp.sum(before * counted, axis=1).astype(jnp.float32)
    normed, inverse = normalize(inputs)
    attn_input = (normed * (1.0 + scale_attn) + shift_attn).astype(jnp.bfloat16)
    queries = rotate_pairs(
        matmul(attn_input, full_q).reshape(frame_count, HEADS, HEAD), position, 1.0
    ).astype(jnp.bfloat16)
    key_flat = (
        rotate_pairs(matmul(attn_input, full_k).reshape(frame_count, HEADS, HEAD), position, 1.0)
        .astype(jnp.bfloat16)
        .reshape(frame_count, D)
    )
    value_flat = matmul(attn_input, full_v).astype(jnp.bfloat16)
    key_codes = jnp.where(valid_row == 1, segment, -1).astype(jnp.bfloat16)
    query_codes = segment.astype(jnp.float32)
    start_state = (
        jnp.full((HEADS, frame_count), -1e30, jnp.float32),
        jnp.zeros((HEADS, frame_count), jnp.float32),
        jnp.zeros((frame_count, HEADS, HEAD), jnp.float32),
    )

    def step(state, key_block):
        return (forward_block(state, key_block, queries, query_codes), None)

    running_max, running_sum, accumulated = lax.scan(
        step,
        start_state,
        stack_blocks(
            (
                lax.all_gather(key_flat, "seq", axis=0, tiled=True),
                lax.all_gather(value_flat, "seq", axis=0, tiled=True),
                lax.all_gather(key_codes, "seq", axis=0, tiled=True),
            )
        ),
    )[0]
    attended = accumulated / running_sum.T[:, :, None]
    log_total = running_max + jnp.log(running_sum)
    attended_low = attended.reshape(frame_count, D).astype(jnp.bfloat16)
    attn_branch = matmul(attended_low, full_o)
    middle = inputs + gate_attn * attn_branch
    normed_mid, inverse_mid = normalize(middle)
    ffn_input = (normed_mid * (1.0 + scale_ffn) + shift_ffn).astype(jnp.bfloat16)
    hidden = matmul(ffn_input, full_u)
    activated, gelu_pull = jax.vjp(partial(jax.nn.gelu, approximate=True), hidden)
    activated_low = activated.astype(jnp.bfloat16)
    ffn_branch = matmul(activated_low, full_d)
    result = middle + gate_ffn * ffn_branch
    back_q, back_k, back_v, back_o, back_u, back_d = (
        full_q,
        full_k,
        full_v,
        full_o,
        full_u,
        full_d,
    )
    grad_gate_ffn = grad_output * ffn_branch
    g_ffn = (grad_output * gate_ffn).astype(jnp.bfloat16)
    grad_down_local = matmul(activated_low.T, g_ffn)
    grad_activated = matmul(g_ffn, back_d.T)
    g_hidden = gelu_pull(grad_activated)[0].astype(jnp.bfloat16)
    grad_up_local = matmul(ffn_input.T, g_hidden)
    grad_ffn_input = matmul(g_hidden, back_u.T)
    grad_middle = grad_output + norm_backward(
        grad_ffn_input * (1.0 + scale_ffn), normed_mid, inverse_mid
    )
    grad_scale_ffn = grad_ffn_input * normed_mid
    grad_gate_attn = grad_middle * attn_branch
    g_attn = (grad_middle * gate_attn).astype(jnp.bfloat16)
    grad_out_local = matmul(attended_low.T, g_attn)
    grad_attn = matmul(g_attn, back_o.T).astype(jnp.bfloat16).reshape(frame_count, HEADS, HEAD)
    delta_rows = jnp.einsum("qhe,qhe->hq", grad_attn.astype(jnp.float32), attended)
    zero_query = jnp.zeros((frame_count, HEADS, HEAD), jnp.float32)
    gathered = (
        lax.all_gather(key_flat, "seq", axis=0, tiled=True),
        lax.all_gather(value_flat, "seq", axis=0, tiled=True),
        lax.all_gather(key_codes, "seq", axis=0, tiled=True),
    )
    pack_rows = gathered[0].shape[0]
    grad_attn_wide = grad_attn.astype(jnp.float32)

    def joint_step(total_grad, key_block):
        probabilities, grad_scores = block_grads(
            key_block, queries, query_codes, grad_attn, log_total, delta_rows
        )
        total_grad = total_grad + 0.125 * jnp.einsum(
            "hqk,khe->qhe", grad_scores, key_block[0], preferred_element_type=jnp.float32
        )
        grad_keys = 0.125 * jnp.einsum(
            "hqk,qhe->khe", grad_scores, queries, preferred_element_type=jnp.float32
        )
        grad_values = jnp.einsum("hqk,qhe->khe", probabilities, grad_attn_wide, precision=highest)
        return (total_grad, (grad_keys, grad_values))

    grad_queries_rot, both_grads = lax.scan(joint_step, zero_query, stack_blocks(gathered))
    key_value_terms = jnp.concatenate(
        [both_grads[0].reshape(pack_rows, D), both_grads[1].reshape(pack_rows, D)], axis=1
    )
    key_value_grad = lax.psum_scatter(key_value_terms, "seq", scatter_dimension=0, tiled=True)
    g_query = (
        rotate_pairs(grad_queries_rot, position, -1.0).reshape(frame_count, D).astype(jnp.bfloat16)
    )
    g_key = (
        rotate_pairs(key_value_grad[:, :D].reshape(frame_count, HEADS, HEAD), position, -1.0)
        .reshape(frame_count, D)
        .astype(jnp.bfloat16)
    )
    g_value = key_value_grad[:, D:].astype(jnp.bfloat16)
    grad_query_local = matmul(attn_input.T, g_query)
    grad_key_local = matmul(attn_input.T, g_key)
    grad_value_local = matmul(attn_input.T, g_value)
    grad_attn_input = (
        matmul(g_query, back_q.T) + matmul(g_key, back_k.T) + matmul(g_value, back_v.T)
    )
    grad_inputs = grad_middle + norm_backward(grad_attn_input * (1.0 + scale_attn), normed, inverse)
    grad_modulation = jnp.concatenate(
        [
            grad_attn_input,
            grad_attn_input * normed,
            grad_gate_attn,
            grad_ffn_input,
            grad_scale_ffn,
            grad_gate_ffn,
        ],
        axis=1,
    )
    grad_emb = jnp.dot(one_hot.T, grad_modulation, precision=highest)
    grad_ada_local = jnp.dot(silu_time.astype(jnp.float32).T, grad_emb, precision=highest)
    part_q, part_k, part_v, part_o, part_a, part_u, part_d = (
        lax.psum_scatter(grad_query_local, "seq", scatter_dimension=1, tiled=True),
        lax.psum_scatter(grad_key_local, "seq", scatter_dimension=1, tiled=True),
        lax.psum_scatter(grad_value_local, "seq", scatter_dimension=1, tiled=True),
        lax.psum_scatter(grad_out_local, "seq", scatter_dimension=1, tiled=True),
        lax.psum_scatter(grad_ada_local, "seq", scatter_dimension=1, tiled=True),
        lax.psum_scatter(grad_up_local, "seq", scatter_dimension=1, tiled=True),
        lax.psum_scatter(grad_down_local, "seq", scatter_dimension=1, tiled=True),
    )
    final_q, final_k, final_v, final_o, final_a, final_u, final_d = (
        lax.psum_scatter(
            part_q.astype(jnp.bfloat16), "batch", scatter_dimension=0, tiled=True
        ).astype(jnp.float32),
        lax.psum_scatter(
            part_k.astype(jnp.bfloat16), "batch", scatter_dimension=0, tiled=True
        ).astype(jnp.float32),
        lax.psum_scatter(
            part_v.astype(jnp.bfloat16), "batch", scatter_dimension=0, tiled=True
        ).astype(jnp.float32),
        lax.psum_scatter(
            part_o.astype(jnp.bfloat16), "batch", scatter_dimension=0, tiled=True
        ).astype(jnp.float32),
        lax.psum_scatter(
            part_a.astype(jnp.bfloat16), "batch", scatter_dimension=0, tiled=True
        ).astype(jnp.float32),
        lax.psum_scatter(
            part_u.astype(jnp.bfloat16), "batch", scatter_dimension=0, tiled=True
        ).astype(jnp.float32),
        lax.psum_scatter(
            part_d.astype(jnp.bfloat16), "batch", scatter_dimension=0, tiled=True
        ).astype(jnp.float32),
    )
    return (
        result.astype(jnp.bfloat16)[None],
        grad_inputs.astype(jnp.bfloat16)[None],
        final_q,
        final_k,
        final_v,
        final_o,
        final_a,
        final_u,
        final_d,
    )


TWO = 2 * HEAD
ROWS = 256
BIG = 1e30
SEQ = 8
REPLICAS = 4
VMEM_MIB = 60


def swap(part, axis, distance):
    size = SEQ if axis == "seq" else REPLICAS
    return lax.ppermute(part, axis, [(i, i ^ distance) for i in range(size)])


def exchange(blocks):
    return lax.all_to_all(blocks, "seq", 0, 0, tiled=True)


def sum_over_replicas(grad):
    place = lax.axis_index("batch")
    x, core = place // 2, place % 2
    rows, cols = grad.shape[0] // REPLICAS, grad.shape[1]
    parts = grad.reshape(2, 2, rows, cols)
    keep = lax.dynamic_index_in_dim(parts, core, 1, False)
    send = lax.dynamic_index_in_dim(parts, 1 - core, 1, False)
    both = (
        keep.astype(jnp.float32) + swap(send.astype(jnp.bfloat16), "batch", 1).astype(jnp.float32)
    ).astype(jnp.bfloat16)
    keep = lax.dynamic_index_in_dim(both, x, 0, False)
    send = lax.dynamic_index_in_dim(both, 1 - x, 0, False)
    return keep.astype(jnp.float32) + swap(send, "batch", 2).astype(jnp.float32)


def along_z(part):
    total = part[0].astype(jnp.float32)
    for k in range(1, 4):
        total = total + swap(part[k], "seq", 2 * k).astype(jnp.float32)
    return total


def turn(vectors, cosine, sine):
    lane = lax.broadcasted_iota(jnp.int32, vectors.shape, 1)
    first = (lane % HEAD) < HEAD // 2
    partner = jnp.where(
        first,
        pltpu.roll(vectors, TWO - HEAD // 2, 1),
        pltpu.roll(vectors, HEAD // 2, 1),
    )
    return vectors * cosine + partner * jnp.where(first, -sine, sine)


def of_head(vectors, head):
    lane = lax.broadcasted_iota(jnp.int32, vectors.shape, 1)
    return jnp.where(lane // HEAD == head, vectors, jnp.zeros_like(vectors))


def dot_t(left, right):
    return lax.dot_general(
        left, right, (((1,), (1,)), ((), ())), preferred_element_type=jnp.float32
    )


def project_kernel(place_ref, a_ref, b_ref, c_ref, d_ref, member_ref, bar_ref, cos_ref, sin_ref,
                   emb_ref, w_ref, *refs):
    x_ref, input_ref, q_ref, k_ref, kt_ref, v_ref, vt_ref, chunk_ref = refs[-8:]
    for step, ref in enumerate((a_ref, b_ref, c_ref, d_ref)):

        @pl.when(pl.program_id(0) == step)
        def _():
            chunk_ref[...] = ref[...]

    chunk = chunk_ref[...]
    x_ref[...] = chunk
    normed, _ = standardize(chunk.astype(jnp.float32))
    modulation = matmul(member_ref[...], emb_ref[...])
    low = (normed * (1.0 + modulation[:, D:]) + modulation[:, :D]).astype(jnp.bfloat16)
    input_ref[...] = low
    weight = jnp.concatenate([w_ref[b ^ place_ref[1]] for b in range(REPLICAS)], axis=0)
    product = matmul(low, weight)
    cosine, sine = cos_ref[...], sin_ref[...]
    keys = turn(product[:, TWO:2 * TWO], cosine, sine)
    values = product[:, 2 * TWO:]
    q_ref[...] = turn(product[:, :TWO], cosine, sine).astype(jnp.bfloat16)
    k_ref[:, :TWO] = keys.astype(jnp.bfloat16)
    k_ref[:, TWO:] = bar_ref[...]
    kt_ref[...] = keys.T.astype(jnp.bfloat16)
    v_ref[...] = values.astype(jnp.bfloat16)
    vt_ref[...] = values.T.astype(jnp.bfloat16)


def rows_spec(width):
    return pl.BlockSpec((ROWS, width), lambda i: (i, 0))


def cols_spec(height):
    return pl.BlockSpec((height, ROWS), lambda i: (0, i))


def whole_spec(height, width):
    return pl.BlockSpec((height, width), lambda i: (0, 0))


def params(mib):
    return pltpu.CompilerParams(
        dimension_semantics=("arbitrary",), vmem_limit_bytes=mib * 1024 * 1024
    )


def cost(micros):
    return pl.CostEstimate(
        flops=int(micros * 1e9), bytes_accessed=int(micros * 3e6), transcendentals=0
    )


def project(place, odd, chunks, member, bar, cosine, sine, emb, weights, earlier):
    frames = member.shape[0]
    low = jnp.bfloat16

    def rows(width):
        return pl.BlockSpec((ROWS, width), lambda i, p: ((2 * i + odd) ^ p[0], 0))

    def cols(height):
        return pl.BlockSpec((height, ROWS), lambda i, p: (0, (2 * i + odd) ^ p[0]))

    def whole(height, width):
        return pl.BlockSpec((height, width), lambda i, p: (0, 0))

    inputs = [place, *chunks, member, bar, cosine, sine, emb, weights, *earlier]
    first = len(inputs) - len(earlier)
    return pl.pallas_call(
        project_kernel,
        grid_spec=pltpu.PrefetchScalarGridSpec(
            num_scalar_prefetch=1,
            grid=(4,),
            in_specs=[whole(ROWS, D)] * 4 + [rows(TWO)] * 4
            + [whole(TWO, 2 * D),
               pl.BlockSpec((REPLICAS, ROWS, 3 * TWO), lambda i, p: (0, 0, 0))]
            + [pl.BlockSpec(memory_space=pl.ANY)] * len(earlier),
            out_specs=[rows(D), rows(D), rows(TWO), rows(2 * TWO), cols(TWO), rows(TWO),
                       cols(TWO)],
            scratch_shapes=[pltpu.VMEM((ROWS, D), low)],
        ),
        out_shape=[
            jax.ShapeDtypeStruct((frames, D), low),
            jax.ShapeDtypeStruct((frames, D), low),
            jax.ShapeDtypeStruct((frames, TWO), low),
            jax.ShapeDtypeStruct((frames, 2 * TWO), low),
            jax.ShapeDtypeStruct((TWO, frames), low),
            jax.ShapeDtypeStruct((frames, TWO), low),
            jax.ShapeDtypeStruct((TWO, frames), low),
        ],
        input_output_aliases={first + i: i for i in range(len(earlier))},
        compiler_params=params(VMEM_MIB),
        cost_estimate=cost(5),
        name="project",
    )(*inputs)


def attend_kernel(q_ref, member_ref, k_ref, vt_ref, att_ref, low_ref, log_ref, score_ref):
    frames = k_ref.shape[0]
    step = min(frames, 512)
    queries = q_ref[...] * 0.125
    member = member_ref[...]
    halves = []
    for head in range(2):
        wide = jnp.concatenate([of_head(queries, head), member], axis=1)
        largest = jnp.full((1, ROWS), -BIG, jnp.float32)
        for start in range(0, frames, step):
            scores = dot_t(k_ref[start:start + step, :], wide)
            score_ref[start:start + step, :] = scores
            largest = jnp.maximum(largest, jnp.max(scores, axis=0, keepdims=True))
        total = jnp.zeros((1, ROWS), jnp.float32)
        out = jnp.zeros((TWO, ROWS), jnp.float32)
        for start in range(0, frames, step):
            weights = jnp.exp(score_ref[start:start + step, :] - largest)
            total = total + jnp.sum(weights, axis=0, keepdims=True)
            out = out + matmul(vt_ref[:, start:start + step], weights.astype(jnp.bfloat16))
        halves.append(out[head * HEAD:(head + 1) * HEAD, :] / total)
        log_ref[head:head + 1, :] = largest + jnp.log(total)
    attended = jnp.concatenate(halves, axis=0).T
    att_ref[...] = attended
    low_ref[...] = attended.astype(jnp.bfloat16)


def attend(q, member, k, vt):
    frames = q.shape[0]
    return pl.pallas_call(
        attend_kernel,
        grid=(frames // ROWS,),
        in_specs=[rows_spec(TWO), rows_spec(TWO), whole_spec(frames, 2 * TWO),
                  whole_spec(TWO, frames)],
        out_specs=[rows_spec(TWO), rows_spec(TWO), cols_spec(8)],
        out_shape=[
            jax.ShapeDtypeStruct((frames, TWO), jnp.float32),
            jax.ShapeDtypeStruct((frames, TWO), jnp.bfloat16),
            jax.ShapeDtypeStruct((8, frames), jnp.float32),
        ],
        scratch_shapes=[pltpu.VMEM((frames, ROWS), jnp.float32)],
        compiler_params=params(VMEM_MIB),
        cost_estimate=cost(18),
        name="attend",
    )(q, member, k, vt)


def attend_back_kernel(q_ref, member_ref, grad_ref, att_ref, log_ref, cos_ref, sin_ref, cos_all_ref,
                       sin_all_ref, k_ref, kt_ref, v_ref, g_ref, dk_ref, dv_ref):
    block = pl.program_id(0)
    frames = k_ref.shape[0]
    step = min(frames, 512)

    @pl.when(block == 0)
    def _():
        dk_ref[...] = jnp.zeros_like(dk_ref)
        dv_ref[...] = jnp.zeros_like(dv_ref)

    queries = q_ref[...] * 0.125
    member = member_ref[...]
    grad = grad_ref[...]
    mixed = (grad.astype(jnp.float32) * att_ref[...]).T
    halves = []
    wides, grads, deltas = [], [], []
    for head in range(2):
        wides.append(jnp.concatenate([of_head(queries, head), member], axis=1))
        grads.append(of_head(grad, head))
        deltas.append(jnp.sum(mixed[head * HEAD:(head + 1) * HEAD, :], axis=0, keepdims=True))
    totals = [jnp.zeros((TWO, ROWS), jnp.float32) for _ in range(2)]
    for start in range(0, frames, step):
        part = slice(start, start + step)
        dk = dk_ref[part, :]
        dv = dv_ref[part, :]
        for head in range(2):
            scores = dot_t(k_ref[part, :], wides[head])
            weights = jnp.exp(scores - log_ref[head:head + 1, :])
            grad_weights = dot_t(v_ref[part, :], grads[head])
            grad_scores = (weights * (grad_weights - deltas[head])).astype(jnp.bfloat16)
            dv = dv + matmul(weights.astype(jnp.bfloat16), grads[head])
            dk = dk + matmul(grad_scores, wides[head][:, :TWO])
            totals[head] = totals[head] + matmul(kt_ref[:, part], grad_scores)
        dk_ref[part, :] = dk
        dv_ref[part, :] = dv
    dq = jnp.concatenate([totals[0][:HEAD, :], totals[1][HEAD:, :]], axis=0).T * 0.125
    here = pl.ds(pl.multiple_of(block * ROWS, ROWS), ROWS)
    g_ref[here, :TWO] = turn(dq, cos_ref[...], -sin_ref[...]).astype(jnp.bfloat16)

    @pl.when(block == pl.num_programs(0) - 1)
    def _():
        turned = turn(dk_ref[...], cos_all_ref[...], -sin_all_ref[...])
        g_ref[:, TWO:2 * TWO] = turned.astype(jnp.bfloat16)
        g_ref[:, 2 * TWO:] = dv_ref[...].astype(jnp.bfloat16)


def attend_back(q, member, grad, att, log_total, cosine, sine, k, kt, v):
    frames = q.shape[0]
    return pl.pallas_call(
        attend_back_kernel,
        grid=(frames // ROWS,),
        in_specs=[rows_spec(TWO), rows_spec(TWO), rows_spec(TWO), rows_spec(TWO), cols_spec(8),
                  rows_spec(TWO), rows_spec(TWO), whole_spec(frames, TWO), whole_spec(frames, TWO),
                  whole_spec(frames, 2 * TWO), whole_spec(TWO, frames), whole_spec(frames, TWO)],
        out_specs=whole_spec(frames, 3 * TWO),
        out_shape=jax.ShapeDtypeStruct((frames, 3 * TWO), jnp.bfloat16),
        scratch_shapes=[pltpu.VMEM((frames, TWO), jnp.float32),
                        pltpu.VMEM((frames, TWO), jnp.float32)],
        compiler_params=params(VMEM_MIB),
        cost_estimate=cost(27),
        name="attend_back",
    )(q, member, grad, att, log_total, cosine, sine, cosine, sine, k, kt, v)


def three_terms(values):
    high = lax.reduce_precision(values, 8, 7)
    middle = lax.reduce_precision(values - high, 8, 7)
    return [high, middle, values - high - middle]


def standardize(rows):
    centered = rows - jnp.mean(rows, axis=1, keepdims=True)
    inverse = lax.rsqrt(jnp.mean(centered * centered, axis=1, keepdims=True) + 1e-06)
    return centered * inverse, inverse


def sum_of_clips(clip_ref, values):
    ids = lax.broadcasted_iota(jnp.int32, (CLIPS, clip_ref.shape[1]), 0)
    chosen = jnp.where(clip_ref[...] == ids, 1.0, 0.0).astype(jnp.bfloat16)
    high = values.astype(jnp.bfloat16)
    rest = values - high.astype(jnp.float32)
    middle = rest.astype(jnp.bfloat16)
    last = (rest - middle.astype(jnp.float32)).astype(jnp.bfloat16)
    return matmul(chosen, high) + matmul(chosen, middle) + matmul(chosen, last)


def beside(ref, tiles, rows):
    return jnp.concatenate([ref[tile, rows, :] for tile in tiles], axis=1)


def middle_kernel(mine_ref, x_ref, cot_ref, member_ref, clip_ref, emb_ref, tiles_ref,
                  result_ref, grad_middle_ref, grad_att_ref, grad_emb_ref, left_ref, right_ref,
                  out_ref, up_ref, down_ref, sems, branch_ref, low_ref, act_ref, slope_ref,
                  wide_ref):
    low = jnp.bfloat16
    act_t_ref, ffn_t_ref = left_ref.at[:2 * D], left_ref.at[2 * D:3 * D]
    mine_t_ref = left_ref.at[3 * D:]
    g_ffn_ref, g_attn_ref = right_ref.at[:, :D], right_ref.at[:, 3 * D:]
    g_hidden_ref = right_ref.at[:, D:3 * D]
    pieces = ((out_ref, 0, 256), (up_ref, 256, 512), (down_ref, 768, 512))
    copies = [
        pltpu.make_async_copy(tiles_ref.at[:, pl.ds(start, size), :], ref, sems.at[i])
        for i, (ref, start, size) in enumerate(pieces)
    ]
    for copy in copies:
        copy.start()
    member = member_ref[...]

    def modulation(index):
        return matmul(member, emb_ref[:, index * D:(index + 1) * D])

    def cols(n, width=256):
        return pl.ds(pl.multiple_of(n * width, width), width)

    every = slice(None)
    mine = jnp.concatenate([mine_ref[j] for j in range(SEQ)], axis=1)
    low_ref[...] = mine
    mine_t_ref[...] = mine.T
    gate_attn = modulation(2)
    copies[0].wait()

    @pl.loop(0, 4)
    def _(n):
        total = jnp.zeros((ROWS, 256), jnp.float32)
        for b in range(REPLICAS):
            weight = beside(out_ref, [8 * b + 2 * n, 8 * b + 2 * n + 1], every)
            total = total + matmul(low_ref[:, 256 * b:256 * b + 256], weight)
        branch_ref[:, cols(n)] = total

    branch = branch_ref[...]
    middle = x_ref[...].astype(jnp.float32) + gate_attn * branch
    normed, inverse = standardize(middle)
    scale_ffn = modulation(4)
    ffn_input = normed * (1.0 + scale_ffn) + modulation(3)
    low_ref[...] = ffn_input.astype(low)
    ffn_t_ref[...] = ffn_input.T.astype(low)
    gate_ffn = modulation(5)
    cot = cot_ref[...].astype(jnp.float32)
    g_ffn_ref[...] = (cot * gate_ffn).astype(low)
    copies[1].wait()

    @pl.loop(0, 8)
    def _(n):
        hidden = jnp.zeros((ROWS, 256), jnp.float32)
        for b in range(REPLICAS):
            tile = 8 * b + n
            weight = jnp.concatenate([up_ref[tile, :256, :], up_ref[tile, 256:, :]], axis=1)
            hidden = hidden + matmul(low_ref[:, 256 * b:256 * b + 256], weight)
        root = math.sqrt(2.0 / math.pi)
        squared = hidden * hidden
        bent = jnp.tanh(root * (hidden + 0.044715 * (squared * hidden)))
        half = 0.5 * (1.0 + bent)
        activated = hidden * half
        slope = half + 0.5 * hidden * (1.0 - bent * bent) * (
            root * (1.0 + (3.0 * 0.044715) * squared)
        )
        act_ref[:, cols(n)] = activated.astype(low)
        act_t_ref[cols(n), :] = activated.T.astype(low)
        slope_ref[:, cols(n)] = slope

    copies[2].wait()

    @pl.loop(0, 4)
    def _(n):
        total = jnp.zeros((ROWS, 256), jnp.float32)
        for b in range(REPLICAS):
            weight = beside(down_ref, [8 * b + 2 * n, 8 * b + 2 * n + 1], every)
            total = total + matmul(act_ref[:, 512 * b:512 * b + 512], weight)
        wide_ref[:, cols(n)] = total

    ffn_branch = wide_ref[...]
    result_ref[...] = (middle + gate_ffn * ffn_branch).astype(low)
    grad_emb_ref[:, 3 * D:] = sum_of_clips(clip_ref, cot * ffn_branch)

    @pl.loop(0, REPLICAS)
    def _(b):
        weight = beside(down_ref, [8 * b + s for s in range(SEQ)], every)
        grad = dot_t(g_ffn_ref[...], weight)
        here = cols(b, 512)
        g_hidden_ref[:, here] = (grad * slope_ref[:, here]).astype(low)

    @pl.loop(0, REPLICAS)
    def _(b):
        weight = jnp.concatenate(
            [up_ref[8 * b + s, 256 * k:256 * k + 256, :] for s in range(SEQ) for k in range(2)],
            axis=1,
        )
        wide_ref[:, cols(b)] = dot_t(g_hidden_ref[...], weight)

    grad_ffn_input = wide_ref[...]
    grad_emb_ref[:, D:2 * D] = sum_of_clips(clip_ref, grad_ffn_input)
    grad_emb_ref[:, 2 * D:3 * D] = sum_of_clips(clip_ref, grad_ffn_input * normed)
    spread = grad_ffn_input * (1.0 + scale_ffn)
    grad_middle = cot + inverse * (
        spread
        - jnp.mean(spread, axis=1, keepdims=True)
        - normed * jnp.mean(spread * normed, axis=1, keepdims=True)
    )
    grad_middle_ref[...] = grad_middle
    grad_emb_ref[:, :D] = sum_of_clips(clip_ref, grad_middle * branch)
    g_attn_ref[...] = (grad_middle * gate_attn).astype(low)

    @pl.loop(0, REPLICAS)
    def _(b):
        weight = beside(out_ref, [8 * b + s for s in range(SEQ)], every)
        grad = dot_t(g_attn_ref[...], weight).astype(low)
        grad_att_ref[2 * b] = grad[:, :TWO]
        grad_att_ref[2 * b + 1] = grad[:, TWO:]


def middle_part(mine, x, cot, member, clip_row, emb, tiles):
    low = jnp.bfloat16
    shapes = [
        ((ROWS, D), low), ((ROWS, D), jnp.float32), ((SEQ, ROWS, TWO), low),
        ((CLIPS, 4 * D), jnp.float32),
        ((4 * D, ROWS), low), ((ROWS, 4 * D), low),
    ]
    vmem = pl.BlockSpec(memory_space=pltpu.VMEM)
    return pl.pallas_call(
        middle_kernel,
        in_specs=[vmem] * 6 + [pl.BlockSpec(memory_space=pl.ANY)],
        out_specs=[vmem] * len(shapes),
        out_shape=[jax.ShapeDtypeStruct(shape, dtype) for shape, dtype in shapes],
        scratch_shapes=[
            pltpu.VMEM((32, 256, 128), low),
            pltpu.VMEM((32, 512, 128), low),
            pltpu.VMEM((32, 512, 128), low),
            pltpu.SemaphoreType.DMA((3,)),
            pltpu.VMEM((ROWS, D), jnp.float32),
            pltpu.VMEM((ROWS, D), low),
            pltpu.VMEM((ROWS, 2 * D), low),
            pltpu.VMEM((ROWS, 2 * D), jnp.float32),
            pltpu.VMEM((ROWS, D), jnp.float32),
        ],
        compiler_params=pltpu.CompilerParams(vmem_limit_bytes=VMEM_MIB * 1024 * 1024),
        cost_estimate=cost(20),
        name="middle",
    )(mine, x, cot, member, clip_row, emb, tiles)


def weight_grads_kernel(place_ref, down_l, up_l, out_l, right_ref, down_o, up_o, out_o, other_ref,
                        away_d_ref, keep_d_ref, away_u_ref, keep_u_ref):
    low = jnp.bfloat16
    z, y = place_ref[2] // 2, place_ref[2] % 2
    lefts = [
        jnp.concatenate([mine[...], other[...]], axis=1)
        for mine, other in ((down_l, down_o), (up_l, up_o), (out_l, out_o))
    ]

    def product(left, first, block):
        here = pl.ds(pl.multiple_of(first + 256 * block, 256), 256)
        right = jnp.concatenate([right_ref[:, here], other_ref[:, here]], axis=0)
        return matmul(left, right).astype(low)

    def fill(down_ref):
        for k in range(4):
            block = z ^ k
            grad = product(lefts[0], 0, block)
            down_ref[4 * y + k] = grad[:, :128]
            down_ref[4 - 4 * y + k] = grad[:, 128:]
            grad = product(lefts[2], 3 * D, block)
            keep_u_ref[0, k, :256, :] = jnp.where(y == 0, grad[:, :128], grad[:, 128:])
            away_u_ref[0, k, :256, :] = jnp.where(y == 0, grad[:, 128:], grad[:, :128])
            for side, ref in enumerate((keep_u_ref, away_u_ref)):
                grad = product(lefts[1], D, 2 * block + (y ^ side))
                ref[0, k, 256:512, :] = grad[:, :128]
                ref[0, k, 512:, :] = grad[:, 128:]

    @pl.when(pl.program_id(0) == 0)
    def _():
        fill(away_d_ref)

    @pl.when(pl.program_id(0) == 1)
    def _():
        fill(keep_d_ref)


def weight_grads(place, left, right, other_left, other_right):
    low = jnp.bfloat16

    def target(i, p):
        return 2 * jnp.where(i == 0, 1 - p[0], p[0]) + p[1]

    down = pl.BlockSpec((512, ROWS), lambda i, p: (target(i, p), 0))
    up = pl.BlockSpec((256, ROWS), lambda i, p: (8 + target(i, p), 0))
    out = pl.BlockSpec((256, ROWS), lambda i, p: (12 + target(i, p), 0))
    wide = pl.BlockSpec((ROWS, 4 * D), lambda i, p: (0, 0))
    whole = pl.BlockSpec((SEQ, 512, 128), lambda i, p: (0, 0, 0))
    part = pl.BlockSpec((1, 4, 768, 128), lambda i, p: (1 - i, 0, 0, 0))
    return pl.pallas_call(
        weight_grads_kernel,
        grid_spec=pltpu.PrefetchScalarGridSpec(
            num_scalar_prefetch=1,
            grid=(2,),
            in_specs=[down, up, out, wide] * 2,
            out_specs=[whole, whole, part, part],
        ),
        out_shape=[jax.ShapeDtypeStruct((SEQ, 512, 128), low)] * 2
        + [jax.ShapeDtypeStruct((2, 4, 768, 128), low)] * 2,
        compiler_params=params(VMEM_MIB),
        cost_estimate=cost(9),
        name="weight_grads",
    )(place, left, left, left, right, other_left, other_left, other_left, other_right)


def last_kernel(place_ref, own_ref, x_ref, grad_middle_ref, member_ref, clip_ref, emb_ref, *refs):
    *tile_refs, out_ref, grad_emb_ref, wide_ref = refs
    grads = jnp.concatenate([own_ref[place_ref[2] ^ s] for s in range(SEQ)], axis=1)

    def tile(apart, s):
        index = apart * SEQ + (s % 2) * 4 + s // 2
        for ref in tile_refs:
            if index < ref.shape[0]:
                return ref[index]
            index -= ref.shape[0]

    for apart in range(REPLICAS):
        weight = jnp.concatenate(
            [
                tile(apart, s)[256 * k:256 * k + 256, :]
                for s in range(SEQ)
                for k in range(3)
            ],
            axis=1,
        )
        b = (2 * place_ref[0] + place_ref[1]) ^ ((apart % 2) * 2 + apart // 2)
        wide_ref[:, pl.ds(pl.multiple_of(b * 256, 256), 256)] = dot_t(grads, weight)

    normed, inverse = standardize(x_ref[...].astype(jnp.float32))
    grad_input = wide_ref[...]
    grad_emb_ref[:, :D] = sum_of_clips(clip_ref, grad_input)
    grad_emb_ref[:, D:] = sum_of_clips(clip_ref, grad_input * normed)
    spread = grad_input * (1.0 + matmul(member_ref[...], emb_ref[:, D:2 * D]))
    grad = grad_middle_ref[...] + inverse * (
        spread
        - jnp.mean(spread, axis=1, keepdims=True)
        - normed * jnp.mean(spread * normed, axis=1, keepdims=True)
    )
    out_ref[...] = grad.astype(jnp.bfloat16)


def last_part(place, own, x, grad_middle, member, clip_row, emb, tiles):
    vmem = pl.BlockSpec(memory_space=pltpu.VMEM)
    return pl.pallas_call(
        last_kernel,
        in_specs=[pl.BlockSpec(memory_space=pltpu.SMEM)] + [vmem] * (6 + len(tiles)),
        out_specs=[vmem, vmem],
        out_shape=[
            jax.ShapeDtypeStruct((ROWS, D), jnp.bfloat16),
            jax.ShapeDtypeStruct((CLIPS, 2 * D), jnp.float32),
        ],
        scratch_shapes=[pltpu.VMEM((ROWS, D), jnp.float32)],
        compiler_params=pltpu.CompilerParams(vmem_limit_bytes=30 * 1024 * 1024),
        cost_estimate=cost(4),
        name="last",
    )(place, own, x, grad_middle, member, clip_row, emb, *tiles)


def after(value, *others):
    return lax.optimization_barrier((value,) + others)[0]


def together(*values):
    return lax.optimization_barrier(values)


def plus(*terms):
    total = terms[0].astype(jnp.float32)
    for term in terms[1:]:
        total = total + term.astype(jnp.float32)
    return total


def clip_lanes(clip, terms):
    lane = jnp.arange(TWO, dtype=jnp.int32)[None, :]
    return (clip[:, None] == lane % CLIPS) & (lane < terms * CLIPS)


def body_fast(
    tokens, w_query, w_key, w_value, w_out, w_ada, w_up, w_down,
    segments, validity, timesteps, cotangent,
):
    highest = lax.Precision.HIGHEST
    low = jnp.bfloat16
    wide = jnp.float32
    replica = lax.axis_index("batch")
    x = tokens[0]
    frame_count = x.shape[0]
    frames = frame_count * SEQ
    segment = segments[0]

    mine_w = jnp.concatenate(
        [w_out, w_up[:, :128], w_up[:, 128:], w_down], axis=0
    ).astype(low)
    tiles = lax.all_gather(mine_w, ("batch", "seq"), axis=0)

    own_codes = segment * 2 + (validity[0] == 1)
    codes = exchange(jnp.broadcast_to(own_codes[None], (SEQ, frame_count))).reshape(frames)
    times = lax.all_gather(timesteps[0], "batch", axis=0, tiled=True)
    silu_all = jax.nn.silu(time_embedding(times)).astype(low)
    depth = w_ada.shape[0]
    silu_part = lax.dynamic_slice_in_dim(silu_all, replica * depth, depth, 1)
    emb_part = matmul(silu_part, w_ada.astype(low)).reshape(REPLICAS, CLIPS, -1)
    emb_cols = lax.all_to_all(emb_part, "batch", 0, 0, tiled=True)
    start = after(x, emb_part, codes)
    z1, z2, y0 = swap(start, "seq", 2), swap(start, "seq", 4), swap(start, "seq", 1)
    emb_cols = jnp.sum(emb_cols, axis=0)
    emb = exchange(jnp.broadcast_to(emb_cols[None], (SEQ,) + emb_cols.shape))
    z1 = after(z1, emb_cols)
    y1 = swap(z1, "seq", 1)
    z2 = after(z2, emb_cols)
    y2, z3 = swap(z2, "seq", 1), swap(z2, "seq", 2)
    heads_w = jnp.concatenate([w_query, w_key, w_value], axis=1).astype(low)
    heads_w = jnp.stack([heads_w, swap(heads_w, "batch", 1)])
    heads_w = jnp.concatenate([heads_w, swap(after(heads_w, z1), "batch", 2)])
    codes = after(codes, z2)
    clip = codes // 2
    tri = jnp.arange(frame_count)[:, None] > jnp.arange(frame_count)[None, :]
    ids = jnp.arange(CLIPS, dtype=jnp.int32)
    one_hot = (clip.reshape(SEQ, frame_count)[:, :, None] == ids).astype(low)
    within = jnp.einsum("ij,njc->nic", tri.astype(low), one_hot, preferred_element_type=wide)
    counts = jnp.sum(one_hot.astype(wide), axis=1)
    offsets = jnp.cumsum(counts, axis=0) - counts
    position = jnp.sum(one_hot.astype(wide) * (within + offsets[:, None, :]), axis=2)
    half = HEAD // 2
    frequency = jnp.exp(-math.log(10000.0) * jnp.arange(half, dtype=wide) / half)
    angle = position.reshape(frames)[:, None] * jnp.tile(frequency, 4)[None, :]
    cosine, sine = jnp.cos(angle), jnp.sin(angle)
    member = clip_lanes(clip, 3).astype(low)
    allowed = clip_lanes(jnp.where(codes % 2 == 1, clip, -1), 1)
    inside = jnp.arange(TWO, dtype=jnp.int32)[None, :] < CLIPS
    bar = jnp.where(inside & ~allowed, -BIG, 0.0).astype(low)
    z3 = after(z3, member, bar, cosine, sine, heads_w)
    y3 = swap(z3, "seq", 1)
    mine_h = jnp.concatenate([w_query, w_key, w_value], axis=0).astype(low)
    mine_h = after(mine_h, z3)
    tiles_z = [swap(mine_h, "seq", 2 * k) for k in range(1, 4)]
    line, other = (x, z1, z2, z3), (y0, y1, y2, y3)
    emb = after(emb, z3)
    emb = emb.transpose(1, 0, 2).reshape(CLIPS, -1)
    emb = jnp.concatenate(
        [t.astype(low) for t in three_terms(emb)] + [jnp.zeros((TWO - 3 * CLIPS, 6 * D), low)],
        axis=0,
    )

    seat = lax.axis_index("seq").astype(jnp.int32)
    tables = (member, bar, cosine, sine, emb[:, :2 * D], heads_w)
    places = jnp.stack([seat, replica.astype(jnp.int32)])
    earlier = project(places, 0, line, *tables, ())
    *other, tiles_1, tiles_2, tiles_3 = together(*other, *tiles_z)
    tiles_z = [tiles_1, tiles_2, tiles_3]
    x_all, attn_input, q, k, kt, v, vt = project(places, 1, other, *tables, earlier)
    tiles_z = jnp.stack([mine_h] + tiles_z)
    tiles_y = swap(tiles_z, "seq", 1)
    attended, attended_low, log_total = attend(after(q, tiles_z), member, k, vt)
    attended_low, tiles_y = together(attended_low, tiles_y)
    tiles_zy = jnp.concatenate([tiles_z, tiles_y])
    tiles_x = swap(tiles_zy, "batch", 2)
    mine = exchange(attended_low.reshape(SEQ, frame_count, TWO))
    mine = after(mine, tiles_zy)

    own_member = clip_lanes(segment, 3).astype(low)
    result, grad_middle, grad_att, grad_emb, left, right = middle_part(
        mine, x, cotangent[0], own_member, segment[None, :], emb, tiles
    )
    place = jnp.stack([replica // 2, replica % 2, seat]).astype(jnp.int32)
    left, tiles_x = together(left, tiles_x)
    other_left, other_right = swap(left, "batch", 1), swap(right, "batch", 1)
    away_d, keep_d, away_u, keep_u = weight_grads(place, left, right, other_left, other_right)
    grad_heads = exchange(grad_att).reshape(frames, TWO)
    grad_heads, away_d, away_u = together(grad_heads, away_d, away_u)
    from_x = swap(away_d, "batch", 2)
    from_y = swap(away_u, "seq", 1)
    tiles_zyx = jnp.concatenate([tiles_zy, tiles_x])
    grad_heads = after(grad_heads, tiles_zyx)
    tiles_c = swap(tiles_zyx, "batch", 1)

    g_heads = attend_back(
        q, member, grad_heads, attended, log_total, cosine, sine, k, kt, v
    )
    own = exchange(g_heads.reshape(SEQ, frame_count, 3 * TWO))
    from_x, from_y, tiles_c = after(from_x, g_heads), after(from_y, g_heads), after(tiles_c, g_heads)
    near_d = plus(keep_d, from_x)
    from_y_d = swap(near_d[4:].astype(low), "seq", 1)
    near_u = plus(keep_u, from_y)
    from_x_u = swap(near_u[1].astype(low), "batch", 2)
    part_d = plus(near_d[:4], from_y_d).astype(low)
    part_u = after(plus(near_u[0], from_x_u).astype(low), own)
    final_d = along_z(part_d)
    final_uo = along_z(part_u)
    final_o = final_uo[:256]
    final_u = jnp.concatenate([final_uo[256:512], final_uo[512:]], axis=1)

    grad_heads_w = matmul(attn_input.T, g_heads).astype(low)
    final_heads = sum_over_replicas(grad_heads_w)
    grad_tokens, late = last_part(
        place, own, x, grad_middle, own_member, segment[None, :], emb,
        (tiles_zyx, tiles_c),
    )
    grad_emb = jnp.concatenate([late, grad_emb], axis=1)
    grad_emb = grad_emb.reshape(CLIPS, SEQ, -1).transpose(1, 0, 2)
    grad_emb = jnp.sum(exchange(grad_emb), axis=0)
    grad_emb = lax.all_gather(grad_emb, "batch", axis=0, tiled=True)
    final_a = jnp.dot(silu_part.astype(wide).T, grad_emb, precision=highest)
    width = w_query.shape[1]
    return (
        result[None],
        grad_tokens[None],
        final_heads[:, :width],
        final_heads[:, width:2 * width],
        final_heads[:, 2 * width:],
        final_o,
        final_a,
        final_u,
        final_d,
    )


def solution(mesh):
    fits = mesh.shape["seq"] == SEQ and mesh.shape["batch"] == REPLICAS
    chosen = body_fast if fits else body
    return jax.shard_map(
        chosen,
        mesh=mesh,
        in_specs=(
            P("batch", "seq", None),
            P("batch", "seq"),
            P("batch", "seq"),
            P("batch", "seq"),
            P("batch", "seq"),
            P("batch", "seq"),
            P("batch", "seq"),
            P("batch", "seq"),
            P("batch", "seq"),
            P("batch", "seq"),
            P("batch", None),
            P("batch", "seq", None),
        ),
        out_specs=(
            P("batch", "seq", None),
            P("batch", "seq", None),
            P("batch", "seq"),
            P("batch", "seq"),
            P("batch", "seq"),
            P("batch", "seq"),
            P("batch", "seq"),
            P("batch", "seq"),
            P("batch", "seq"),
        ),
        check_vma=False,
    )
```

```python
from functools import partial
import math

import jax
import jax.numpy as jnp
from jax import lax
from jax.experimental import pallas as pl
from jax.experimental.pallas import tpu as pltpu
from jax.sharding import PartitionSpec as P

D = 1024
HEADS = 16
HEAD = 64
CLIPS = 16


def carried_in(part, axis, combine, identity):
    place = lax.axis_index(axis)
    gathered = lax.all_gather(part, axis)
    state = jnp.zeros_like(part) + jnp.asarray(identity, part.dtype)

    def one(step, state):
        return combine(state, lax.dynamic_index_in_dim(gathered, step, 0, False))

    return lax.fori_loop(0, place, one, state)


def matmul(left, right):
    return jnp.dot(left, right, preferred_element_type=jnp.float32)


def time_embedding(timestep_row):
    half_width = D // 2
    frequency = jnp.exp(-math.log(10000.0) * jnp.arange(half_width, dtype=jnp.float32) / half_width)
    angle = timestep_row.astype(jnp.float32)[:, None] * frequency[None, :]
    return jnp.concatenate([jnp.sin(angle), jnp.cos(angle)], axis=1)


def rotate_pairs(vectors, position, direction):
    half_size = vectors.shape[-1] // 2
    frequency = jnp.exp(-math.log(10000.0) * jnp.arange(half_size, dtype=jnp.float32) / half_size)
    angle = position[:, None] * frequency[None, :]
    cosine = jnp.cos(angle)[:, None, :]
    sine = jnp.sin(angle)[:, None, :] * direction
    first_half = vectors[..., :half_size]
    second_half = vectors[..., half_size:]
    return jnp.concatenate(
        [first_half * cosine - second_half * sine, second_half * cosine + first_half * sine],
        axis=-1,
    )


def normalize(inputs):
    centered = inputs - jnp.mean(inputs, axis=-1, keepdims=True)
    inverse = lax.rsqrt(jnp.mean(centered * centered, axis=-1, keepdims=True) + 1e-06)
    return (centered * inverse, inverse)


def norm_backward(grad_normed, normed, inverse):
    mean_grad = jnp.mean(grad_normed, axis=-1, keepdims=True)
    mean_mixed = jnp.mean(grad_normed * normed, axis=-1, keepdims=True)
    return inverse * (grad_normed - mean_grad - normed * mean_mixed)


def add_counts(earlier, later):
    return earlier + later


def block_rows_for(row_count):
    chosen = 1
    for candidate in range(1, 513):
        if row_count % candidate == 0:
            chosen = candidate
    return chosen


def stack_blocks(shard_piece):
    row_count = shard_piece[0].shape[0]
    block_rows = block_rows_for(row_count)
    block_count = row_count // block_rows
    return (
        shard_piece[0].reshape(block_count, block_rows, HEADS, HEAD),
        shard_piece[1].reshape(block_count, block_rows, HEADS, HEAD),
        shard_piece[2].reshape(block_count, block_rows),
    )


def forward_block(carried, key_block, queries, query_codes):
    running_max, running_sum, accumulated = carried
    key_rows, values, key_codes = key_block
    scores = (
        jnp.einsum("qhe,khe->hqk", queries, key_rows, preferred_element_type=jnp.float32) * 0.125
    )
    allowed = (query_codes[:, None] == key_codes.astype(jnp.float32)[None, :])[None]
    masked = jnp.where(allowed, scores, -1e30)
    new_max = jnp.maximum(running_max, jnp.max(masked, axis=2))
    rescale = jnp.exp(running_max - new_max)
    weights = jnp.where(allowed, jnp.exp(masked - new_max[:, :, None]), 0.0)
    running_sum = running_sum * rescale + jnp.sum(weights, axis=2)
    product = jnp.einsum(
        "hqk,khe->qhe", weights, values.astype(jnp.float32), precision=lax.Precision.HIGHEST
    )
    accumulated = accumulated * rescale.T[:, :, None] + product
    return (new_max, running_sum, accumulated)


def block_grads(key_block, queries, query_codes, grad_attn, log_total, delta_rows):
    key_rows, values, key_codes = key_block
    scores = (
        jnp.einsum("qhe,khe->hqk", queries, key_rows, preferred_element_type=jnp.float32) * 0.125
    )
    allowed = (query_codes[:, None] == key_codes.astype(jnp.float32)[None, :])[None]
    probabilities = jnp.exp(jnp.where(allowed, scores, -1e30) - log_total[:, :, None])
    grad_probs = jnp.einsum("qhe,khe->hqk", grad_attn, values, preferred_element_type=jnp.float32)
    grad_scores = (probabilities * (grad_probs - delta_rows[:, :, None])).astype(jnp.bfloat16)
    return (probabilities, grad_scores)


def body(
    tokens,
    w_query,
    w_key,
    w_value,
    w_out,
    w_ada,
    w_up,
    w_down,
    segments,
    validity,
    timesteps,
    cotangent,
):
    inputs = tokens[0].astype(jnp.float32)
    segment = segments[0]
    valid_row = validity[0]
    timestep_row = timesteps[0]
    grad_output = cotangent[0].astype(jnp.float32)
    frame_count = inputs.shape[0]
    highest = lax.Precision.HIGHEST
    cols_q, cols_k, cols_v, cols_o, cols_a, cols_u, cols_d = (
        lax.all_gather(w_query.astype(jnp.bfloat16), "seq", axis=1, tiled=True),
        lax.all_gather(w_key.astype(jnp.bfloat16), "seq", axis=1, tiled=True),
        lax.all_gather(w_value.astype(jnp.bfloat16), "seq", axis=1, tiled=True),
        lax.all_gather(w_out.astype(jnp.bfloat16), "seq", axis=1, tiled=True),
        lax.all_gather(w_ada.astype(jnp.bfloat16), "seq", axis=1, tiled=True),
        lax.all_gather(w_up.astype(jnp.bfloat16), "seq", axis=1, tiled=True),
        lax.all_gather(w_down.astype(jnp.bfloat16), "seq", axis=1, tiled=True),
    )
    full_q, full_k, full_v, full_o, full_a, full_u, full_d = (
        lax.all_gather(cols_q, "batch", axis=0, tiled=True),
        lax.all_gather(cols_k, "batch", axis=0, tiled=True),
        lax.all_gather(cols_v, "batch", axis=0, tiled=True),
        lax.all_gather(cols_o, "batch", axis=0, tiled=True),
        lax.all_gather(cols_a, "batch", axis=0, tiled=True),
        lax.all_gather(cols_u, "batch", axis=0, tiled=True),
        lax.all_gather(cols_d, "batch", axis=0, tiled=True),
    )
    silu_time = jax.nn.silu(time_embedding(timestep_row)).astype(jnp.bfloat16)
    emb_rows = matmul(silu_time, full_a)
    member = segment[:, None] == jnp.arange(CLIPS, dtype=jnp.int32)[None, :]
    one_hot = member.astype(jnp.float32)
    counted = member.astype(jnp.int32)
    modulation = jnp.dot(one_hot, emb_rows, precision=highest)
    shift_attn, scale_attn, gate_attn, shift_ffn, scale_ffn, gate_ffn = jnp.split(
        modulation, 6, axis=1
    )
    offsets = carried_in(
        jnp.sum(counted, axis=0), "seq", add_counts, jnp.zeros((CLIPS,), jnp.int32)
    )
    before = jnp.cumsum(counted, axis=0) - counted + offsets[None, :]
    position = jnp.sum(before * counted, axis=1).astype(jnp.float32)
    normed, inverse = normalize(inputs)
    attn_input = (normed * (1.0 + scale_attn) + shift_attn).astype(jnp.bfloat16)
    queries = rotate_pairs(
        matmul(attn_input, full_q).reshape(frame_count, HEADS, HEAD), position, 1.0
    ).astype(jnp.bfloat16)
    key_flat = (
        rotate_pairs(matmul(attn_input, full_k).reshape(frame_count, HEADS, HEAD), position, 1.0)
        .astype(jnp.bfloat16)
        .reshape(frame_count, D)
    )
    value_flat = matmul(attn_input, full_v).astype(jnp.bfloat16)
    key_codes = jnp.where(valid_row == 1, segment, -1).astype(jnp.bfloat16)
    query_codes = segment.astype(jnp.float32)
    start_state = (
        jnp.full((HEADS, frame_count), -1e30, jnp.float32),
        jnp.zeros((HEADS, frame_count), jnp.float32),
        jnp.zeros((frame_count, HEADS, HEAD), jnp.float32),
    )

    def step(state, key_block):
        return (forward_block(state, key_block, queries, query_codes), None)

    running_max, running_sum, accumulated = lax.scan(
        step,
        start_state,
        stack_blocks(
            (
                lax.all_gather(key_flat, "seq", axis=0, tiled=True),
                lax.all_gather(value_flat, "seq", axis=0, tiled=True),
                lax.all_gather(key_codes, "seq", axis=0, tiled=True),
            )
        ),
    )[0]
    attended = accumulated / running_sum.T[:, :, None]
    log_total = running_max + jnp.log(running_sum)
    attended_low = attended.reshape(frame_count, D).astype(jnp.bfloat16)
    attn_branch = matmul(attended_low, full_o)
    middle = inputs + gate_attn * attn_branch
    normed_mid, inverse_mid = normalize(middle)
    ffn_input = (normed_mid * (1.0 + scale_ffn) + shift_ffn).astype(jnp.bfloat16)
    hidden = matmul(ffn_input, full_u)
    activated, gelu_pull = jax.vjp(partial(jax.nn.gelu, approximate=True), hidden)
    activated_low = activated.astype(jnp.bfloat16)
    ffn_branch = matmul(activated_low, full_d)
    result = middle + gate_ffn * ffn_branch
    back_q, back_k, back_v, back_o, back_u, back_d = (
        full_q,
        full_k,
        full_v,
        full_o,
        full_u,
        full_d,
    )
    grad_gate_ffn = grad_output * ffn_branch
    g_ffn = (grad_output * gate_ffn).astype(jnp.bfloat16)
    grad_down_local = matmul(activated_low.T, g_ffn)
    grad_activated = matmul(g_ffn, back_d.T)
    g_hidden = gelu_pull(grad_activated)[0].astype(jnp.bfloat16)
    grad_up_local = matmul(ffn_input.T, g_hidden)
    grad_ffn_input = matmul(g_hidden, back_u.T)
    grad_middle = grad_output + norm_backward(
        grad_ffn_input * (1.0 + scale_ffn), normed_mid, inverse_mid
    )
    grad_scale_ffn = grad_ffn_input * normed_mid
    grad_gate_attn = grad_middle * attn_branch
    g_attn = (grad_middle * gate_attn).astype(jnp.bfloat16)
    grad_out_local = matmul(attended_low.T, g_attn)
    grad_attn = matmul(g_attn, back_o.T).astype(jnp.bfloat16).reshape(frame_count, HEADS, HEAD)
    delta_rows = jnp.einsum("qhe,qhe->hq", grad_attn.astype(jnp.float32), attended)
    zero_query = jnp.zeros((frame_count, HEADS, HEAD), jnp.float32)
    gathered = (
        lax.all_gather(key_flat, "seq", axis=0, tiled=True),
        lax.all_gather(value_flat, "seq", axis=0, tiled=True),
        lax.all_gather(key_codes, "seq", axis=0, tiled=True),
    )
    pack_rows = gathered[0].shape[0]
    grad_attn_wide = grad_attn.astype(jnp.float32)

    def joint_step(total_grad, key_block):
        probabilities, grad_scores = block_grads(
            key_block, queries, query_codes, grad_attn, log_total, delta_rows
        )
        total_grad = total_grad + 0.125 * jnp.einsum(
            "hqk,khe->qhe", grad_scores, key_block[0], preferred_element_type=jnp.float32
        )
        grad_keys = 0.125 * jnp.einsum(
            "hqk,qhe->khe", grad_scores, queries, preferred_element_type=jnp.float32
        )
        grad_values = jnp.einsum("hqk,qhe->khe", probabilities, grad_attn_wide, precision=highest)
        return (total_grad, (grad_keys, grad_values))

    grad_queries_rot, both_grads = lax.scan(joint_step, zero_query, stack_blocks(gathered))
    key_value_terms = jnp.concatenate(
        [both_grads[0].reshape(pack_rows, D), both_grads[1].reshape(pack_rows, D)], axis=1
    )
    key_value_grad = lax.psum_scatter(key_value_terms, "seq", scatter_dimension=0, tiled=True)
    g_query = (
        rotate_pairs(grad_queries_rot, position, -1.0).reshape(frame_count, D).astype(jnp.bfloat16)
    )
    g_key = (
        rotate_pairs(key_value_grad[:, :D].reshape(frame_count, HEADS, HEAD), position, -1.0)
        .reshape(frame_count, D)
        .astype(jnp.bfloat16)
    )
    g_value = key_value_grad[:, D:].astype(jnp.bfloat16)
    grad_query_local = matmul(attn_input.T, g_query)
    grad_key_local = matmul(attn_input.T, g_key)
    grad_value_local = matmul(attn_input.T, g_value)
    grad_attn_input = (
        matmul(g_query, back_q.T) + matmul(g_key, back_k.T) + matmul(g_value, back_v.T)
    )
    grad_inputs = grad_middle + norm_backward(grad_attn_input * (1.0 + scale_attn), normed, inverse)
    grad_modulation = jnp.concatenate(
        [
            grad_attn_input,
            grad_attn_input * normed,
            grad_gate_attn,
            grad_ffn_input,
            grad_scale_ffn,
            grad_gate_ffn,
        ],
        axis=1,
    )
    grad_emb = jnp.dot(one_hot.T, grad_modulation, precision=highest)
    grad_ada_local = jnp.dot(silu_time.astype(jnp.float32).T, grad_emb, precision=highest)
    part_q, part_k, part_v, part_o, part_a, part_u, part_d = (
        lax.psum_scatter(grad_query_local, "seq", scatter_dimension=1, tiled=True),
        lax.psum_scatter(grad_key_local, "seq", scatter_dimension=1, tiled=True),
        lax.psum_scatter(grad_value_local, "seq", scatter_dimension=1, tiled=True),
        lax.psum_scatter(grad_out_local, "seq", scatter_dimension=1, tiled=True),
        lax.psum_scatter(grad_ada_local, "seq", scatter_dimension=1, tiled=True),
        lax.psum_scatter(grad_up_local, "seq", scatter_dimension=1, tiled=True),
        lax.psum_scatter(grad_down_local, "seq", scatter_dimension=1, tiled=True),
    )
    final_q, final_k, final_v, final_o, final_a, final_u, final_d = (
        lax.psum_scatter(
            part_q.astype(jnp.bfloat16), "batch", scatter_dimension=0, tiled=True
        ).astype(jnp.float32),
        lax.psum_scatter(
            part_k.astype(jnp.bfloat16), "batch", scatter_dimension=0, tiled=True
        ).astype(jnp.float32),
        lax.psum_scatter(
            part_v.astype(jnp.bfloat16), "batch", scatter_dimension=0, tiled=True
        ).astype(jnp.float32),
        lax.psum_scatter(
            part_o.astype(jnp.bfloat16), "batch", scatter_dimension=0, tiled=True
        ).astype(jnp.float32),
        lax.psum_scatter(
            part_a.astype(jnp.bfloat16), "batch", scatter_dimension=0, tiled=True
        ).astype(jnp.float32),
        lax.psum_scatter(
            part_u.astype(jnp.bfloat16), "batch", scatter_dimension=0, tiled=True
        ).astype(jnp.float32),
        lax.psum_scatter(
            part_d.astype(jnp.bfloat16), "batch", scatter_dimension=0, tiled=True
        ).astype(jnp.float32),
    )
    return (
        result.astype(jnp.bfloat16)[None],
        grad_inputs.astype(jnp.bfloat16)[None],
        final_q,
        final_k,
        final_v,
        final_o,
        final_a,
        final_u,
        final_d,
    )


TWO = 2 * HEAD
ROWS = 256
BIG = 1e30
SEQ = 8
REPLICAS = 4
VMEM_MIB = 60


def swap(part, axis, distance):
    size = SEQ if axis == "seq" else REPLICAS
    return lax.ppermute(part, axis, [(i, i ^ distance) for i in range(size)])


def exchange(blocks):
    return lax.all_to_all(blocks, "seq", 0, 0, tiled=True)


def turn(vectors, cosine, sine):
    lane = lax.broadcasted_iota(jnp.int32, vectors.shape, 1)
    first = (lane % HEAD) < HEAD // 2
    partner = jnp.where(
        first,
        pltpu.roll(vectors, TWO - HEAD // 2, 1),
        pltpu.roll(vectors, HEAD // 2, 1),
    )
    return vectors * cosine + partner * jnp.where(first, -sine, sine)


def of_head(vectors, head):
    lane = lax.broadcasted_iota(jnp.int32, vectors.shape, 1)
    return jnp.where(lane // HEAD == head, vectors, jnp.zeros_like(vectors))


def dot_t(left, right):
    return lax.dot_general(
        left, right, (((1,), (1,)), ((), ())), preferred_element_type=jnp.float32
    )


def project_kernel(place_ref, a_ref, b_ref, c_ref, d_ref, member_ref, bar_ref, cos_ref, sin_ref,
                   emb_ref, w_ref, *refs):
    x_ref, input_ref, q_ref, k_ref, kt_ref, v_ref, vt_ref, chunk_ref = refs[-8:]
    for step, ref in enumerate((a_ref, b_ref, c_ref, d_ref)):

        @pl.when(pl.program_id(0) == step)
        def _():
            chunk_ref[...] = ref[...]

    chunk = chunk_ref[...]
    x_ref[...] = chunk
    normed, _ = standardize(chunk.astype(jnp.float32))
    modulation = matmul(member_ref[...], emb_ref[...])
    low = (normed * (1.0 + modulation[:, D:]) + modulation[:, :D]).astype(jnp.bfloat16)
    input_ref[...] = low
    weight = jnp.concatenate([w_ref[b ^ place_ref[1]] for b in range(REPLICAS)], axis=0)
    product = matmul(low, weight)
    cosine, sine = cos_ref[...], sin_ref[...]
    keys = turn(product[:, TWO:2 * TWO], cosine, sine)
    values = product[:, 2 * TWO:]
    q_ref[...] = turn(product[:, :TWO], cosine, sine).astype(jnp.bfloat16)
    k_ref[:, :TWO] = keys.astype(jnp.bfloat16)
    k_ref[:, TWO:] = bar_ref[...]
    kt_ref[...] = keys.T.astype(jnp.bfloat16)
    v_ref[...] = values.astype(jnp.bfloat16)
    vt_ref[...] = values.T.astype(jnp.bfloat16)


def rows_spec(width):
    return pl.BlockSpec((ROWS, width), lambda i: (i, 0))


def cols_spec(height):
    return pl.BlockSpec((height, ROWS), lambda i: (0, i))


def whole_spec(height, width):
    return pl.BlockSpec((height, width), lambda i: (0, 0))


def params(mib):
    return pltpu.CompilerParams(
        dimension_semantics=("arbitrary",), vmem_limit_bytes=mib * 1024 * 1024
    )


def cost(micros):
    return pl.CostEstimate(
        flops=int(micros * 1e9), bytes_accessed=int(micros * 3e6), transcendentals=0
    )


def project(place, odd, chunks, member, bar, cosine, sine, emb, weights, earlier):
    frames = member.shape[0]
    low = jnp.bfloat16

    def rows(width):
        return pl.BlockSpec((ROWS, width), lambda i, p: ((2 * i + odd) ^ p[0], 0))

    def cols(height):
        return pl.BlockSpec((height, ROWS), lambda i, p: (0, (2 * i + odd) ^ p[0]))

    def whole(height, width):
        return pl.BlockSpec((height, width), lambda i, p: (0, 0))

    inputs = [place, *chunks, member, bar, cosine, sine, emb, weights, *earlier]
    first = len(inputs) - len(earlier)
    return pl.pallas_call(
        project_kernel,
        grid_spec=pltpu.PrefetchScalarGridSpec(
            num_scalar_prefetch=1,
            grid=(4,),
            in_specs=[whole(ROWS, D)] * 4 + [rows(TWO)] * 4
            + [whole(TWO, 2 * D),
               pl.BlockSpec((REPLICAS, ROWS, 3 * TWO), lambda i, p: (0, 0, 0))]
            + [pl.BlockSpec(memory_space=pl.ANY)] * len(earlier),
            out_specs=[rows(D), rows(D), rows(TWO), rows(2 * TWO), cols(TWO), rows(TWO),
                       cols(TWO)],
            scratch_shapes=[pltpu.VMEM((ROWS, D), low)],
        ),
        out_shape=[
            jax.ShapeDtypeStruct((frames, D), low),
            jax.ShapeDtypeStruct((frames, D), low),
            jax.ShapeDtypeStruct((frames, TWO), low),
            jax.ShapeDtypeStruct((frames, 2 * TWO), low),
            jax.ShapeDtypeStruct((TWO, frames), low),
            jax.ShapeDtypeStruct((frames, TWO), low),
            jax.ShapeDtypeStruct((TWO, frames), low),
        ],
        input_output_aliases={first + i: i for i in range(len(earlier))},
        compiler_params=params(VMEM_MIB),
        cost_estimate=cost(2),
        name="project",
    )(*inputs)


def attend_kernel(q_ref, member_ref, k_ref, vt_ref, att_ref, low_ref, log_ref, score_ref):
    frames = k_ref.shape[0]
    step = min(frames, 512)
    queries = q_ref[...] * 0.125
    member = member_ref[...]
    halves = []
    for head in range(2):
        wide = jnp.concatenate([of_head(queries, head), member], axis=1)
        largest = jnp.full((1, ROWS), -BIG, jnp.float32)
        for start in range(0, frames, step):
            scores = dot_t(k_ref[start:start + step, :], wide)
            score_ref[start:start + step, :] = scores
            largest = jnp.maximum(largest, jnp.max(scores, axis=0, keepdims=True))
        total = jnp.zeros((1, ROWS), jnp.float32)
        out = jnp.zeros((TWO, ROWS), jnp.float32)
        for start in range(0, frames, step):
            weights = jnp.exp(score_ref[start:start + step, :] - largest)
            total = total + jnp.sum(weights, axis=0, keepdims=True)
            out = out + matmul(vt_ref[:, start:start + step], weights.astype(jnp.bfloat16))
        halves.append(out[head * HEAD:(head + 1) * HEAD, :] / total)
        log_ref[head:head + 1, :] = largest + jnp.log(total)
    attended = jnp.concatenate(halves, axis=0).T
    att_ref[...] = attended
    low_ref[...] = attended.astype(jnp.bfloat16)


def attend(q, member, k, vt):
    frames = q.shape[0]
    return pl.pallas_call(
        attend_kernel,
        grid=(frames // ROWS,),
        in_specs=[rows_spec(TWO), rows_spec(TWO), whole_spec(frames, 2 * TWO),
                  whole_spec(TWO, frames)],
        out_specs=[rows_spec(TWO), rows_spec(TWO), cols_spec(8)],
        out_shape=[
            jax.ShapeDtypeStruct((frames, TWO), jnp.float32),
            jax.ShapeDtypeStruct((frames, TWO), jnp.bfloat16),
            jax.ShapeDtypeStruct((8, frames), jnp.float32),
        ],
        scratch_shapes=[pltpu.VMEM((frames, ROWS), jnp.float32)],
        compiler_params=params(VMEM_MIB),
        cost_estimate=cost(18),
        name="attend",
    )(q, member, k, vt)


def attend_back_kernel(q_ref, member_ref, grad_ref, att_ref, log_ref, cos_ref, sin_ref, cos_all_ref,
                       sin_all_ref, k_ref, kt_ref, v_ref, g_ref, dk_ref, dv_ref):
    block = pl.program_id(0)
    frames = k_ref.shape[0]
    step = min(frames, 512)

    @pl.when(block == 0)
    def _():
        dk_ref[...] = jnp.zeros_like(dk_ref)
        dv_ref[...] = jnp.zeros_like(dv_ref)

    queries = q_ref[...] * 0.125
    member = member_ref[...]
    grad = grad_ref[...]
    mixed = (grad.astype(jnp.float32) * att_ref[...]).T
    halves = []
    wides, grads, deltas = [], [], []
    for head in range(2):
        wides.append(jnp.concatenate([of_head(queries, head), member], axis=1))
        grads.append(of_head(grad, head))
        deltas.append(jnp.sum(mixed[head * HEAD:(head + 1) * HEAD, :], axis=0, keepdims=True))
    totals = [jnp.zeros((TWO, ROWS), jnp.float32) for _ in range(2)]
    for start in range(0, frames, step):
        part = slice(start, start + step)
        dk = dk_ref[part, :]
        dv = dv_ref[part, :]
        for head in range(2):
            scores = dot_t(k_ref[part, :], wides[head])
            weights = jnp.exp(scores - log_ref[head:head + 1, :])
            grad_weights = dot_t(v_ref[part, :], grads[head])
            grad_scores = (weights * (grad_weights - deltas[head])).astype(jnp.bfloat16)
            dv = dv + matmul(weights.astype(jnp.bfloat16), grads[head])
            dk = dk + matmul(grad_scores, wides[head][:, :TWO])
            totals[head] = totals[head] + matmul(kt_ref[:, part], grad_scores)
        dk_ref[part, :] = dk
        dv_ref[part, :] = dv
    dq = jnp.concatenate([totals[0][:HEAD, :], totals[1][HEAD:, :]], axis=0).T * 0.125
    here = pl.ds(pl.multiple_of(block * ROWS, ROWS), ROWS)
    g_ref[here, :TWO] = turn(dq, cos_ref[...], -sin_ref[...]).astype(jnp.bfloat16)

    @pl.when(block == pl.num_programs(0) - 1)
    def _():
        turned = turn(dk_ref[...], cos_all_ref[...], -sin_all_ref[...])
        g_ref[:, TWO:2 * TWO] = turned.astype(jnp.bfloat16)
        g_ref[:, 2 * TWO:] = dv_ref[...].astype(jnp.bfloat16)


def attend_back(q, member, grad, att, log_total, cosine, sine, k, kt, v):
    frames = q.shape[0]
    return pl.pallas_call(
        attend_back_kernel,
        grid=(frames // ROWS,),
        in_specs=[rows_spec(TWO), rows_spec(TWO), rows_spec(TWO), rows_spec(TWO), cols_spec(8),
                  rows_spec(TWO), rows_spec(TWO), whole_spec(frames, TWO), whole_spec(frames, TWO),
                  whole_spec(frames, 2 * TWO), whole_spec(TWO, frames), whole_spec(frames, TWO)],
        out_specs=whole_spec(frames, 3 * TWO),
        out_shape=jax.ShapeDtypeStruct((frames, 3 * TWO), jnp.bfloat16),
        scratch_shapes=[pltpu.VMEM((frames, TWO), jnp.float32),
                        pltpu.VMEM((frames, TWO), jnp.float32)],
        compiler_params=params(VMEM_MIB),
        cost_estimate=cost(27),
        name="attend_back",
    )(q, member, grad, att, log_total, cosine, sine, cosine, sine, k, kt, v)


def three_terms(values):
    high = lax.reduce_precision(values, 8, 7)
    middle = lax.reduce_precision(values - high, 8, 7)
    return [high, middle, values - high - middle]


def standardize(rows):
    centered = rows - jnp.mean(rows, axis=1, keepdims=True)
    inverse = lax.rsqrt(jnp.mean(centered * centered, axis=1, keepdims=True) + 1e-06)
    return centered * inverse, inverse


def sum_of_clips(clip_ref, values):
    ids = lax.broadcasted_iota(jnp.int32, (CLIPS, clip_ref.shape[1]), 0)
    chosen = jnp.where(clip_ref[...] == ids, 1.0, 0.0).astype(jnp.bfloat16)
    high = values.astype(jnp.bfloat16)
    rest = values - high.astype(jnp.float32)
    middle = rest.astype(jnp.bfloat16)
    last = (rest - middle.astype(jnp.float32)).astype(jnp.bfloat16)
    return matmul(chosen, high) + matmul(chosen, middle) + matmul(chosen, last)


def beside(ref, tiles, rows):
    return jnp.concatenate([ref[tile, rows, :] for tile in tiles], axis=1)


def tile_index(away, apart):
    return 16 * (away % 2) + 8 * (away // 2) + 4 * (apart % 2) + apart // 2


def middle_kernel(mine_ref, x_ref, cot_ref, member_ref, clip_ref, emb_ref, *refs):
    *tile_refs, result_ref, grad_middle_ref, grad_att_ref, grad_emb_ref, left_ref, right_ref = refs[:-9]
    out_ref, up_ref, down_ref, sems, branch_ref, low_ref, act_ref, slope_ref, wide_ref = refs[-9:]
    low = jnp.bfloat16
    act_t_ref, ffn_t_ref = left_ref.at[:2 * D], left_ref.at[2 * D:3 * D]
    mine_t_ref = left_ref.at[3 * D:]
    g_ffn_ref, g_attn_ref = right_ref.at[:, :D], right_ref.at[:, 3 * D:]
    g_hidden_ref = right_ref.at[:, D:3 * D]
    pieces = ((out_ref, 0, 256), (up_ref, 256, 512), (down_ref, 768, 512))
    for i, (ref, start, size) in enumerate(pieces):
        first = 0
        for tile_ref in tile_refs:
            count = tile_ref.shape[0]
            pltpu.make_async_copy(
                tile_ref.at[:, pl.ds(start, size), :], ref.at[pl.ds(first, count)], sems.at[i]
            ).start()
            first += count
    copies = [
        pltpu.make_async_copy(ref, ref, sems.at[i]) for i, (ref, _, _) in enumerate(pieces)
    ]

    def tile(b, s):
        return SEQ * b + s

    member = member_ref[...]

    def modulation(index):
        return matmul(member, emb_ref[:, index * D:(index + 1) * D])

    def cols(n, width=256):
        return pl.ds(pl.multiple_of(n * width, width), width)

    every = slice(None)
    mine = jnp.concatenate([mine_ref[j] for j in range(SEQ)], axis=1)
    low_ref[...] = mine
    mine_t_ref[...] = mine.T
    gate_attn = modulation(2)
    copies[0].wait()

    @pl.loop(0, 4)
    def _(n):
        total = jnp.zeros((ROWS, 256), jnp.float32)
        for b in range(REPLICAS):
            weight = beside(out_ref, [tile(b, 2 * n), tile(b, 2 * n + 1)], every)
            total = total + matmul(low_ref[:, 256 * b:256 * b + 256], weight)
        branch_ref[:, cols(n)] = total

    branch = branch_ref[...]
    middle = x_ref[...].astype(jnp.float32) + gate_attn * branch
    normed, inverse = standardize(middle)
    scale_ffn = modulation(4)
    ffn_input = normed * (1.0 + scale_ffn) + modulation(3)
    low_ref[...] = ffn_input.astype(low)
    ffn_t_ref[...] = ffn_input.T.astype(low)
    gate_ffn = modulation(5)
    cot = cot_ref[...].astype(jnp.float32)
    g_ffn_ref[...] = (cot * gate_ffn).astype(low)
    copies[1].wait()

    @pl.loop(0, 8)
    def _(n):
        hidden = jnp.zeros((ROWS, 256), jnp.float32)
        for b in range(REPLICAS):
            index = tile(b, n)
            weight = jnp.concatenate([up_ref[index, :256, :], up_ref[index, 256:, :]], axis=1)
            hidden = hidden + matmul(low_ref[:, 256 * b:256 * b + 256], weight)
        root = math.sqrt(2.0 / math.pi)
        squared = hidden * hidden
        bent = jnp.tanh(root * (hidden + 0.044715 * (squared * hidden)))
        half = 0.5 * (1.0 + bent)
        activated = hidden * half
        slope = half + 0.5 * hidden * (1.0 - bent * bent) * (
            root * (1.0 + (3.0 * 0.044715) * squared)
        )
        act_ref[:, cols(n)] = activated.astype(low)
        act_t_ref[cols(n), :] = activated.T.astype(low)
        slope_ref[:, cols(n)] = slope

    copies[2].wait()

    @pl.loop(0, 4)
    def _(n):
        total = jnp.zeros((ROWS, 256), jnp.float32)
        for b in range(REPLICAS):
            weight = beside(down_ref, [tile(b, 2 * n), tile(b, 2 * n + 1)], every)
            total = total + matmul(act_ref[:, 512 * b:512 * b + 512], weight)
        wide_ref[:, cols(n)] = total

    ffn_branch = wide_ref[...]
    result_ref[...] = (middle + gate_ffn * ffn_branch).astype(low)
    grad_emb_ref[:, 3 * D:] = sum_of_clips(clip_ref, cot * ffn_branch)

    @pl.loop(0, REPLICAS)
    def _(b):
        weight = beside(down_ref, [tile(b, s) for s in range(SEQ)], every)
        grad = dot_t(g_ffn_ref[...], weight)
        here = cols(b, 512)
        g_hidden_ref[:, here] = (grad * slope_ref[:, here]).astype(low)

    @pl.loop(0, REPLICAS)
    def _(b):
        weight = jnp.concatenate(
            [up_ref[tile(b, s), 256 * k:256 * k + 256, :] for s in range(SEQ) for k in range(2)],
            axis=1,
        )
        wide_ref[:, cols(b)] = dot_t(g_hidden_ref[...], weight)

    grad_ffn_input = wide_ref[...]
    grad_emb_ref[:, D:2 * D] = sum_of_clips(clip_ref, grad_ffn_input)
    grad_emb_ref[:, 2 * D:3 * D] = sum_of_clips(clip_ref, grad_ffn_input * normed)
    spread = grad_ffn_input * (1.0 + scale_ffn)
    grad_middle = cot + inverse * (
        spread
        - jnp.mean(spread, axis=1, keepdims=True)
        - normed * jnp.mean(spread * normed, axis=1, keepdims=True)
    )
    grad_middle_ref[...] = grad_middle
    grad_emb_ref[:, :D] = sum_of_clips(clip_ref, grad_middle * branch)
    g_attn_ref[...] = (grad_middle * gate_attn).astype(low)

    @pl.loop(0, REPLICAS)
    def _(b):
        weight = beside(out_ref, [tile(b, s) for s in range(SEQ)], every)
        grad = dot_t(g_attn_ref[...], weight).astype(low)
        grad_att_ref[2 * b] = grad[:, :TWO]
        grad_att_ref[2 * b + 1] = grad[:, TWO:]


def middle_part(mine, x, cot, member, clip_row, emb, tiles):
    low = jnp.bfloat16
    shapes = [
        ((ROWS, D), low), ((ROWS, D), jnp.float32), ((SEQ, ROWS, TWO), low),
        ((CLIPS, 4 * D), jnp.float32),
        ((4 * D, ROWS), low), ((ROWS, 4 * D), low),
    ]
    vmem = pl.BlockSpec(memory_space=pltpu.VMEM)
    return pl.pallas_call(
        middle_kernel,
        in_specs=[vmem] * 6 + [pl.BlockSpec(memory_space=pl.ANY)] * len(tiles),
        out_specs=[vmem] * len(shapes),
        out_shape=[jax.ShapeDtypeStruct(shape, dtype) for shape, dtype in shapes],
        scratch_shapes=[
            pltpu.VMEM((32, 256, 128), low),
            pltpu.VMEM((32, 512, 128), low),
            pltpu.VMEM((32, 512, 128), low),
            pltpu.SemaphoreType.DMA((3,)),
            pltpu.VMEM((ROWS, D), jnp.float32),
            pltpu.VMEM((ROWS, D), low),
            pltpu.VMEM((ROWS, 2 * D), low),
            pltpu.VMEM((ROWS, 2 * D), jnp.float32),
            pltpu.VMEM((ROWS, D), jnp.float32),
        ],
        compiler_params=pltpu.CompilerParams(vmem_limit_bytes=VMEM_MIB * 1024 * 1024),
        cost_estimate=cost(20),
        name="middle",
    )(mine, x, cot, member, clip_row, emb, *tiles)


def weight_grads_kernel(place_ref, down_l, up_l, out_l, right_ref, down_o, up_o, out_o, other_ref,
                        away_d_ref, keep_d_ref, away_u_ref, keep_u_ref):
    low = jnp.bfloat16
    z, y = place_ref[2] // 2, place_ref[2] % 2
    lefts = [
        jnp.concatenate([mine[...], other[...]], axis=1)
        for mine, other in ((down_l, down_o), (up_l, up_o), (out_l, out_o))
    ]

    def product(left, first, block):
        here = pl.ds(pl.multiple_of(first + 256 * block, 256), 256)
        right = jnp.concatenate([right_ref[:, here], other_ref[:, here]], axis=0)
        return matmul(left, right).astype(low)

    def fill(down_ref):
        for k in range(4):
            block = z ^ k
            grad = product(lefts[0], 0, block)
            down_ref[4 * y + k] = grad[:, :128]
            down_ref[4 - 4 * y + k] = grad[:, 128:]
            grad = product(lefts[2], 3 * D, block)
            keep_u_ref[0, k, :256, :] = jnp.where(y == 0, grad[:, :128], grad[:, 128:])
            away_u_ref[0, k, :256, :] = jnp.where(y == 0, grad[:, 128:], grad[:, :128])
            for side, ref in enumerate((keep_u_ref, away_u_ref)):
                grad = product(lefts[1], D, 2 * block + (y ^ side))
                ref[0, k, 256:512, :] = grad[:, :128]
                ref[0, k, 512:, :] = grad[:, 128:]

    @pl.when(pl.program_id(0) == 0)
    def _():
        fill(away_d_ref)

    @pl.when(pl.program_id(0) == 1)
    def _():
        fill(keep_d_ref)


def weight_grads(place, left, right, other_left, other_right):
    low = jnp.bfloat16

    def target(i, p):
        return 2 * jnp.where(i == 0, 1 - p[0], p[0]) + p[1]

    down = pl.BlockSpec((512, ROWS), lambda i, p: (target(i, p), 0))
    up = pl.BlockSpec((256, ROWS), lambda i, p: (8 + target(i, p), 0))
    out = pl.BlockSpec((256, ROWS), lambda i, p: (12 + target(i, p), 0))
    wide = pl.BlockSpec((ROWS, 4 * D), lambda i, p: (0, 0))
    whole = pl.BlockSpec((SEQ, 512, 128), lambda i, p: (0, 0, 0))
    part = pl.BlockSpec((1, 4, 768, 128), lambda i, p: (1 - i, 0, 0, 0))
    return pl.pallas_call(
        weight_grads_kernel,
        grid_spec=pltpu.PrefetchScalarGridSpec(
            num_scalar_prefetch=1,
            grid=(2,),
            in_specs=[down, up, out, wide] * 2,
            out_specs=[whole, whole, part, part],
        ),
        out_shape=[jax.ShapeDtypeStruct((SEQ, 512, 128), low)] * 2
        + [jax.ShapeDtypeStruct((2, 4, 768, 128), low)] * 2,
        compiler_params=params(VMEM_MIB),
        cost_estimate=cost(9),
        name="weight_grads",
    )(place, left, left, left, right, other_left, other_left, other_left, other_right)


def clip_grads_kernel(place_ref, x_ref, clip_ref, g_ref, w_ref, out_ref):
    @pl.when(pl.program_id(0) == 0)
    def _():
        out_ref[...] = jnp.zeros_like(out_ref)

    normed, _ = standardize(x_ref[...].astype(jnp.float32))
    grad = jnp.concatenate(
        [dot_t(g_ref[...], w_ref[b ^ place_ref[1]]) for b in range(REPLICAS)], axis=1
    )
    out_ref[:, :D] += sum_of_clips(clip_ref, grad)
    out_ref[:, D:] += sum_of_clips(clip_ref, grad * normed)


def clip_grads(places, x, clip_row, g_heads, heads_w):
    frames = x.shape[0]
    return pl.pallas_call(
        clip_grads_kernel,
        grid=(frames // ROWS,),
        in_specs=[pl.BlockSpec(memory_space=pltpu.SMEM), rows_spec(D), cols_spec(1),
                  rows_spec(3 * TWO),
                  pl.BlockSpec((REPLICAS, ROWS, 3 * TWO), lambda i: (0, 0, 0))],
        out_specs=whole_spec(CLIPS, 2 * D),
        out_shape=jax.ShapeDtypeStruct((CLIPS, 2 * D), jnp.float32),
        compiler_params=params(VMEM_MIB),
        cost_estimate=cost(9),
        name="clip_grads",
    )(places, x, clip_row, g_heads, heads_w)


def last_kernel(place_ref, own_ref, x_ref, grad_middle_ref, member_ref, emb_ref, *refs):
    *tile_refs, out_ref, wide_ref = refs
    grads = jnp.concatenate([own_ref[place_ref[2] ^ s] for s in range(SEQ)], axis=1)

    def tile(away, apart):
        index = tile_index(away, apart)
        for ref in tile_refs:
            if index < ref.shape[0]:
                return ref[index, ref.shape[1] - 768:, :]
            index -= ref.shape[0]

    for away in range(REPLICAS):
        weight = jnp.concatenate(
            [
                tile(away, s)[256 * k:256 * k + 256, :]
                for s in range(SEQ)
                for k in range(3)
            ],
            axis=1,
        )
        b = (2 * place_ref[0] + place_ref[1]) ^ away
        wide_ref[:, pl.ds(pl.multiple_of(b * 256, 256), 256)] = dot_t(grads, weight)

    normed, inverse = standardize(x_ref[...].astype(jnp.float32))
    spread = wide_ref[...] * (1.0 + matmul(member_ref[...], emb_ref[:, D:2 * D]))
    grad = grad_middle_ref[...] + inverse * (
        spread
        - jnp.mean(spread, axis=1, keepdims=True)
        - normed * jnp.mean(spread * normed, axis=1, keepdims=True)
    )
    out_ref[...] = grad.astype(jnp.bfloat16)


def last_part(place, own, x, grad_middle, member, emb, tiles):
    vmem = pl.BlockSpec(memory_space=pltpu.VMEM)
    return pl.pallas_call(
        last_kernel,
        in_specs=[pl.BlockSpec(memory_space=pltpu.SMEM)] + [vmem] * (5 + len(tiles)),
        out_specs=vmem,
        out_shape=jax.ShapeDtypeStruct((ROWS, D), jnp.bfloat16),
        scratch_shapes=[pltpu.VMEM((ROWS, D), jnp.float32)],
        compiler_params=pltpu.CompilerParams(vmem_limit_bytes=30 * 1024 * 1024),
        cost_estimate=cost(4),
        name="last",
    )(place, own, x, grad_middle, member, emb, *tiles)


def after(value, *others):
    return lax.optimization_barrier((value,) + others)[0]


def together(*values):
    return lax.optimization_barrier(values)


def plus(*terms):
    total = terms[0].astype(jnp.float32)
    for term in terms[1:]:
        total = total + term.astype(jnp.float32)
    return total


def clip_lanes(clip, terms):
    lane = jnp.arange(TWO, dtype=jnp.int32)[None, :]
    return (clip[:, None] == lane % CLIPS) & (lane < terms * CLIPS)


def body_fast(
    tokens, w_query, w_key, w_value, w_out, w_ada, w_up, w_down,
    segments, validity, timesteps, cotangent,
):
    highest = lax.Precision.HIGHEST
    low = jnp.bfloat16
    wide = jnp.float32
    replica = lax.axis_index("batch")
    x = tokens[0]
    frame_count = x.shape[0]
    frames = frame_count * SEQ
    segment = segments[0]

    seat = lax.axis_index("seq").astype(jnp.int32)
    z, y = seat // 2, seat % 2
    place = jnp.stack([replica // 2, replica % 2, seat]).astype(jnp.int32)
    mine_w = jnp.concatenate([w_out, w_up[:, :128], w_up[:, 128:], w_down], axis=0).astype(low)

    z1, z2, y0 = swap(x, "seq", 2), swap(x, "seq", 4), swap(x, "seq", 1)
    times = lax.all_gather(timesteps[0], "batch", axis=0, tiled=True)
    silu_all = jax.nn.silu(time_embedding(times)).astype(low)
    depth = w_ada.shape[0]
    silu_part = lax.dynamic_slice_in_dim(silu_all, replica * depth, depth, 1)
    emb_part = matmul(silu_part, w_ada.astype(low)).reshape(REPLICAS, CLIPS, -1)
    emb_cols = lax.all_to_all(emb_part, "batch", 0, 0, tiled=True)
    emb_cols = jnp.sum(emb_cols, axis=0)
    own_codes = (segment * 2 + (validity[0] == 1)).astype(wide)
    cols = emb_cols.shape[1]
    own_codes = jnp.pad(own_codes, (0, 8 * cols - frame_count)).reshape(8, cols)
    packed = jnp.concatenate([emb_cols, own_codes])
    packed = jnp.broadcast_to(packed[None], (SEQ,) + packed.shape)
    heads_w = jnp.concatenate([w_query, w_key, w_value], axis=1).astype(low)
    heads_w = jnp.stack([heads_w, swap(heads_w, "batch", 1)])
    z1, z2, y0, packed, heads_w, mine_w = together(z1, z2, y0, packed, heads_w, mine_w)
    tiles_w = (lax.all_gather(mine_w, ("batch", "seq"), axis=0),)
    packed = exchange(packed)
    z3 = swap(z2, "seq", 2)
    y1, y2 = swap(z1, "seq", 1), swap(z2, "seq", 1)
    heads_x = swap(heads_w, "batch", 2)
    z3, y1, y2, heads_x = together(z3, y1, y2, heads_x)
    y3 = swap(z3, "seq", 1)
    heads_w = jnp.concatenate([heads_w, heads_x])
    emb = packed[:, :CLIPS]
    codes = packed[:, CLIPS:].reshape(SEQ, -1)[:, :frame_count].reshape(frames).astype(jnp.int32)
    clip = codes // 2
    clip_row = clip[None, :]
    tri = jnp.arange(frame_count)[:, None] > jnp.arange(frame_count)[None, :]
    ids = jnp.arange(CLIPS, dtype=jnp.int32)
    one_hot = (clip.reshape(SEQ, frame_count)[:, :, None] == ids).astype(low)
    within = jnp.einsum("ij,njc->nic", tri.astype(low), one_hot, preferred_element_type=wide)
    counts = jnp.sum(one_hot.astype(wide), axis=1)
    offsets = jnp.cumsum(counts, axis=0) - counts
    position = jnp.sum(one_hot.astype(wide) * (within + offsets[:, None, :]), axis=2)
    half = HEAD // 2
    frequency = jnp.exp(-math.log(10000.0) * jnp.arange(half, dtype=wide) / half)
    angle = position.reshape(frames)[:, None] * jnp.tile(frequency, 4)[None, :]
    cosine, sine = jnp.cos(angle), jnp.sin(angle)
    member = clip_lanes(clip, 3).astype(low)
    allowed = clip_lanes(jnp.where(codes % 2 == 1, clip, -1), 1)
    inside = jnp.arange(TWO, dtype=jnp.int32)[None, :] < CLIPS
    bar = jnp.where(inside & ~allowed, -BIG, 0.0).astype(low)
    emb = after(emb, heads_w, member, cosine)
    emb = emb.transpose(1, 0, 2).reshape(CLIPS, -1)
    emb = jnp.concatenate(
        [t.astype(low) for t in three_terms(emb)] + [jnp.zeros((TWO - 3 * CLIPS, 6 * D), low)],
        axis=0,
    )

    tables = (member, bar, cosine, sine, emb[:, :2 * D], heads_w)
    places = jnp.stack([seat, replica.astype(jnp.int32)])
    earlier = project(places, 0, (x, z1, z2, z3), *tables, ())
    y3, earlier = together(y3, earlier)
    mine_h = jnp.concatenate([w_query, w_key, w_value], axis=0).astype(low)
    mine_h = after(mine_h, y3)
    x_all, attn_input, q, k, kt, v, vt = project(places, 1, (y0, y1, y2, y3), *tables, earlier)
    h_z1, h_z2 = swap(mine_h, "seq", 2), swap(mine_h, "seq", 4)
    attended, attended_low, log_total = attend(q, member, k, vt)
    attended_low, h_z1, h_z2 = together(attended_low, h_z1, h_z2)
    h_z3 = swap(h_z2, "seq", 2)
    mine = exchange(attended_low.reshape(SEQ, frame_count, TWO))
    mine, h_z3 = together(mine, h_z3)
    h_z = jnp.stack([mine_h, h_z1, h_z2, h_z3])
    h_y, h_x = swap(h_z, "seq", 1), swap(h_z, "batch", 2)

    own_member = clip_lanes(segment, 3).astype(low)
    result, grad_middle, grad_att, grad_emb, left, right = middle_part(
        mine, x, cotangent[0], own_member, segment[None, :], emb, tiles_w
    )
    left, h_y, h_x = together(left, h_y, h_x)
    h_yx = swap(h_y, "batch", 2)
    other_left, other_right = swap(left, "batch", 1), swap(right, "batch", 1)
    away_d, keep_d, away_u, keep_u = weight_grads(place, left, right, other_left, other_right)
    grad_heads = exchange(grad_att).reshape(frames, TWO)
    grad_heads, away_d, away_u = together(grad_heads, away_d, away_u)
    from_x = swap(away_d, "batch", 2)
    from_y = swap(away_u, "seq", 1)

    g_heads = attend_back(
        q, member, grad_heads, attended, log_total, cosine, sine, k, kt, v
    )
    own = exchange(g_heads.reshape(SEQ, frame_count, 3 * TWO))
    near_d = plus(keep_d, after(from_x, g_heads))
    from_y_d = swap(near_d[4:].astype(low), "seq", 1)
    near_u = plus(keep_u, after(from_y, near_d, h_yx))
    from_x_u = swap(near_u[1].astype(low), "batch", 2)
    g_heads = after(g_heads, near_d, near_u)
    late = clip_grads(places, x_all, clip_row, g_heads, heads_w)
    grad_heads_w = matmul(attn_input.T, g_heads).astype(low).reshape(2, 2, ROWS, 3 * TWO)
    h_first = jnp.concatenate([after(h_z, near_u), h_y, h_x])
    h_first_core = swap(h_first, "batch", 1)
    late, grad_heads_w, from_y_d, from_x_u, h_first, h_first_core = together(
        late, grad_heads_w, from_y_d, from_x_u, h_first, h_first_core
    )
    part = jnp.concatenate(
        [plus(near_u[0], from_x_u).astype(low), plus(near_d[:4], from_y_d).astype(low)], axis=1
    )
    late, own = together(late, own)
    grad_emb = jnp.concatenate([late, grad_emb], axis=1)
    grad_emb = grad_emb.reshape(CLIPS, 4, 2, -1).transpose(2, 1, 0, 3)
    keep_e = lax.dynamic_index_in_dim(grad_emb, y, 0, False)
    other_e = swap(lax.dynamic_index_in_dim(grad_emb, 1 - y, 0, False), "seq", 1)
    x_place, core_place = replica // 2, replica % 2
    grad_emb = keep_e + other_e
    from_z_e = [
        swap(lax.dynamic_index_in_dim(grad_emb, z ^ k, 0, False), "seq", 2 * k) for k in range(1, 4)
    ]
    grad_emb = plus(lax.dynamic_index_in_dim(grad_emb, z, 0, False), *from_z_e)
    keep_h = lax.dynamic_index_in_dim(grad_heads_w, core_place, 1, False)
    other_h = swap(lax.dynamic_index_in_dim(grad_heads_w, 1 - core_place, 1, False), "batch", 1)
    h_yx_core = swap(after(h_yx, part), "batch", 1)
    from_z = [swap(part[k], "seq", 2 * k) for k in range(1, 4)]
    both_h = plus(keep_h, other_h).astype(low)
    away_h = swap(lax.dynamic_index_in_dim(both_h, 1 - x_place, 0, False), "batch", 2)

    grad_tokens = last_part(place, own, x, grad_middle, own_member, emb,
        (h_first, h_yx, h_first_core, h_yx_core),
    )
    grad_emb = lax.all_gather(grad_emb, "batch", axis=0, tiled=True)
    final_a = jnp.dot(silu_part.astype(wide).T, grad_emb, precision=highest)
    grad_tokens, final_a, away_h, *from_z = together(grad_tokens, final_a, away_h, *from_z)
    final_heads = plus(lax.dynamic_index_in_dim(both_h, x_place, 0, False), away_h)
    total = plus(part[0], *from_z)
    final_uo, final_d = total[:768], total[768:]
    final_o = final_uo[:256]
    final_u = jnp.concatenate([final_uo[256:512], final_uo[512:]], axis=1)
    width = w_query.shape[1]
    return (
        result[None],
        grad_tokens[None],
        final_heads[:, :width],
        final_heads[:, width:2 * width],
        final_heads[:, 2 * width:],
        final_o,
        final_a,
        final_u,
        final_d,
    )


def solution(mesh):
    fits = mesh.shape["seq"] == SEQ and mesh.shape["batch"] == REPLICAS
    chosen = body_fast if fits else body
    return jax.shard_map(
        chosen,
        mesh=mesh,
        in_specs=(
            P("batch", "seq", None),
            P("batch", "seq"),
            P("batch", "seq"),
            P("batch", "seq"),
            P("batch", "seq"),
            P("batch", "seq"),
            P("batch", "seq"),
            P("batch", "seq"),
            P("batch", "seq"),
            P("batch", "seq"),
            P("batch", None),
            P("batch", "seq", None),
        ),
        out_specs=(
            P("batch", "seq", None),
            P("batch", "seq", None),
            P("batch", "seq"),
            P("batch", "seq"),
            P("batch", "seq"),
            P("batch", "seq"),
            P("batch", "seq"),
            P("batch", "seq"),
            P("batch", "seq"),
        ),
        check_vma=False,
    )
```

```python
from functools import partial
import math

import jax
import jax.numpy as jnp
from jax import lax
from jax.experimental import pallas as pl
from jax.experimental.pallas import tpu as pltpu
from jax.sharding import PartitionSpec as P

D = 1024
HEADS = 16
HEAD = 64
CLIPS = 16


def carried_in(part, axis, combine, identity):
    place = lax.axis_index(axis)
    gathered = lax.all_gather(part, axis)
    state = jnp.zeros_like(part) + jnp.asarray(identity, part.dtype)

    def one(step, state):
        return combine(state, lax.dynamic_index_in_dim(gathered, step, 0, False))

    return lax.fori_loop(0, place, one, state)


def matmul(left, right):
    return jnp.dot(left, right, preferred_element_type=jnp.float32)


def time_embedding(timestep_row):
    half_width = D // 2
    frequency = jnp.exp(-math.log(10000.0) * jnp.arange(half_width, dtype=jnp.float32) / half_width)
    angle = timestep_row.astype(jnp.float32)[:, None] * frequency[None, :]
    return jnp.concatenate([jnp.sin(angle), jnp.cos(angle)], axis=1)


def rotate_pairs(vectors, position, direction):
    half_size = vectors.shape[-1] // 2
    frequency = jnp.exp(-math.log(10000.0) * jnp.arange(half_size, dtype=jnp.float32) / half_size)
    angle = position[:, None] * frequency[None, :]
    cosine = jnp.cos(angle)[:, None, :]
    sine = jnp.sin(angle)[:, None, :] * direction
    first_half = vectors[..., :half_size]
    second_half = vectors[..., half_size:]
    return jnp.concatenate(
        [first_half * cosine - second_half * sine, second_half * cosine + first_half * sine],
        axis=-1,
    )


def normalize(inputs):
    centered = inputs - jnp.mean(inputs, axis=-1, keepdims=True)
    inverse = lax.rsqrt(jnp.mean(centered * centered, axis=-1, keepdims=True) + 1e-06)
    return (centered * inverse, inverse)


def norm_backward(grad_normed, normed, inverse):
    mean_grad = jnp.mean(grad_normed, axis=-1, keepdims=True)
    mean_mixed = jnp.mean(grad_normed * normed, axis=-1, keepdims=True)
    return inverse * (grad_normed - mean_grad - normed * mean_mixed)


def add_counts(earlier, later):
    return earlier + later


def block_rows_for(row_count):
    chosen = 1
    for candidate in range(1, 513):
        if row_count % candidate == 0:
            chosen = candidate
    return chosen


def stack_blocks(shard_piece):
    row_count = shard_piece[0].shape[0]
    block_rows = block_rows_for(row_count)
    block_count = row_count // block_rows
    return (
        shard_piece[0].reshape(block_count, block_rows, HEADS, HEAD),
        shard_piece[1].reshape(block_count, block_rows, HEADS, HEAD),
        shard_piece[2].reshape(block_count, block_rows),
    )


def forward_block(carried, key_block, queries, query_codes):
    running_max, running_sum, accumulated = carried
    key_rows, values, key_codes = key_block
    scores = (
        jnp.einsum("qhe,khe->hqk", queries, key_rows, preferred_element_type=jnp.float32) * 0.125
    )
    allowed = (query_codes[:, None] == key_codes.astype(jnp.float32)[None, :])[None]
    masked = jnp.where(allowed, scores, -1e30)
    new_max = jnp.maximum(running_max, jnp.max(masked, axis=2))
    rescale = jnp.exp(running_max - new_max)
    weights = jnp.where(allowed, jnp.exp(masked - new_max[:, :, None]), 0.0)
    running_sum = running_sum * rescale + jnp.sum(weights, axis=2)
    product = jnp.einsum(
        "hqk,khe->qhe", weights, values.astype(jnp.float32), precision=lax.Precision.HIGHEST
    )
    accumulated = accumulated * rescale.T[:, :, None] + product
    return (new_max, running_sum, accumulated)


def block_grads(key_block, queries, query_codes, grad_attn, log_total, delta_rows):
    key_rows, values, key_codes = key_block
    scores = (
        jnp.einsum("qhe,khe->hqk", queries, key_rows, preferred_element_type=jnp.float32) * 0.125
    )
    allowed = (query_codes[:, None] == key_codes.astype(jnp.float32)[None, :])[None]
    probabilities = jnp.exp(jnp.where(allowed, scores, -1e30) - log_total[:, :, None])
    grad_probs = jnp.einsum("qhe,khe->hqk", grad_attn, values, preferred_element_type=jnp.float32)
    grad_scores = (probabilities * (grad_probs - delta_rows[:, :, None])).astype(jnp.bfloat16)
    return (probabilities, grad_scores)


def body(
    tokens,
    w_query,
    w_key,
    w_value,
    w_out,
    w_ada,
    w_up,
    w_down,
    segments,
    validity,
    timesteps,
    cotangent,
):
    inputs = tokens[0].astype(jnp.float32)
    segment = segments[0]
    valid_row = validity[0]
    timestep_row = timesteps[0]
    grad_output = cotangent[0].astype(jnp.float32)
    frame_count = inputs.shape[0]
    highest = lax.Precision.HIGHEST
    cols_q, cols_k, cols_v, cols_o, cols_a, cols_u, cols_d = (
        lax.all_gather(w_query.astype(jnp.bfloat16), "seq", axis=1, tiled=True),
        lax.all_gather(w_key.astype(jnp.bfloat16), "seq", axis=1, tiled=True),
        lax.all_gather(w_value.astype(jnp.bfloat16), "seq", axis=1, tiled=True),
        lax.all_gather(w_out.astype(jnp.bfloat16), "seq", axis=1, tiled=True),
        lax.all_gather(w_ada.astype(jnp.bfloat16), "seq", axis=1, tiled=True),
        lax.all_gather(w_up.astype(jnp.bfloat16), "seq", axis=1, tiled=True),
        lax.all_gather(w_down.astype(jnp.bfloat16), "seq", axis=1, tiled=True),
    )
    full_q, full_k, full_v, full_o, full_a, full_u, full_d = (
        lax.all_gather(cols_q, "batch", axis=0, tiled=True),
        lax.all_gather(cols_k, "batch", axis=0, tiled=True),
        lax.all_gather(cols_v, "batch", axis=0, tiled=True),
        lax.all_gather(cols_o, "batch", axis=0, tiled=True),
        lax.all_gather(cols_a, "batch", axis=0, tiled=True),
        lax.all_gather(cols_u, "batch", axis=0, tiled=True),
        lax.all_gather(cols_d, "batch", axis=0, tiled=True),
    )
    silu_time = jax.nn.silu(time_embedding(timestep_row)).astype(jnp.bfloat16)
    emb_rows = matmul(silu_time, full_a)
    member = segment[:, None] == jnp.arange(CLIPS, dtype=jnp.int32)[None, :]
    one_hot = member.astype(jnp.float32)
    counted = member.astype(jnp.int32)
    modulation = jnp.dot(one_hot, emb_rows, precision=highest)
    shift_attn, scale_attn, gate_attn, shift_ffn, scale_ffn, gate_ffn = jnp.split(
        modulation, 6, axis=1
    )
    offsets = carried_in(
        jnp.sum(counted, axis=0), "seq", add_counts, jnp.zeros((CLIPS,), jnp.int32)
    )
    before = jnp.cumsum(counted, axis=0) - counted + offsets[None, :]
    position = jnp.sum(before * counted, axis=1).astype(jnp.float32)
    normed, inverse = normalize(inputs)
    attn_input = (normed * (1.0 + scale_attn) + shift_attn).astype(jnp.bfloat16)
    queries = rotate_pairs(
        matmul(attn_input, full_q).reshape(frame_count, HEADS, HEAD), position, 1.0
    ).astype(jnp.bfloat16)
    key_flat = (
        rotate_pairs(matmul(attn_input, full_k).reshape(frame_count, HEADS, HEAD), position, 1.0)
        .astype(jnp.bfloat16)
        .reshape(frame_count, D)
    )
    value_flat = matmul(attn_input, full_v).astype(jnp.bfloat16)
    key_codes = jnp.where(valid_row == 1, segment, -1).astype(jnp.bfloat16)
    query_codes = segment.astype(jnp.float32)
    start_state = (
        jnp.full((HEADS, frame_count), -1e30, jnp.float32),
        jnp.zeros((HEADS, frame_count), jnp.float32),
        jnp.zeros((frame_count, HEADS, HEAD), jnp.float32),
    )

    def step(state, key_block):
        return (forward_block(state, key_block, queries, query_codes), None)

    running_max, running_sum, accumulated = lax.scan(
        step,
        start_state,
        stack_blocks(
            (
                lax.all_gather(key_flat, "seq", axis=0, tiled=True),
                lax.all_gather(value_flat, "seq", axis=0, tiled=True),
                lax.all_gather(key_codes, "seq", axis=0, tiled=True),
            )
        ),
    )[0]
    attended = accumulated / running_sum.T[:, :, None]
    log_total = running_max + jnp.log(running_sum)
    attended_low = attended.reshape(frame_count, D).astype(jnp.bfloat16)
    attn_branch = matmul(attended_low, full_o)
    middle = inputs + gate_attn * attn_branch
    normed_mid, inverse_mid = normalize(middle)
    ffn_input = (normed_mid * (1.0 + scale_ffn) + shift_ffn).astype(jnp.bfloat16)
    hidden = matmul(ffn_input, full_u)
    activated, gelu_pull = jax.vjp(partial(jax.nn.gelu, approximate=True), hidden)
    activated_low = activated.astype(jnp.bfloat16)
    ffn_branch = matmul(activated_low, full_d)
    result = middle + gate_ffn * ffn_branch
    back_q, back_k, back_v, back_o, back_u, back_d = (
        full_q,
        full_k,
        full_v,
        full_o,
        full_u,
        full_d,
    )
    grad_gate_ffn = grad_output * ffn_branch
    g_ffn = (grad_output * gate_ffn).astype(jnp.bfloat16)
    grad_down_local = matmul(activated_low.T, g_ffn)
    grad_activated = matmul(g_ffn, back_d.T)
    g_hidden = gelu_pull(grad_activated)[0].astype(jnp.bfloat16)
    grad_up_local = matmul(ffn_input.T, g_hidden)
    grad_ffn_input = matmul(g_hidden, back_u.T)
    grad_middle = grad_output + norm_backward(
        grad_ffn_input * (1.0 + scale_ffn), normed_mid, inverse_mid
    )
    grad_scale_ffn = grad_ffn_input * normed_mid
    grad_gate_attn = grad_middle * attn_branch
    g_attn = (grad_middle * gate_attn).astype(jnp.bfloat16)
    grad_out_local = matmul(attended_low.T, g_attn)
    grad_attn = matmul(g_attn, back_o.T).astype(jnp.bfloat16).reshape(frame_count, HEADS, HEAD)
    delta_rows = jnp.einsum("qhe,qhe->hq", grad_attn.astype(jnp.float32), attended)
    zero_query = jnp.zeros((frame_count, HEADS, HEAD), jnp.float32)
    gathered = (
        lax.all_gather(key_flat, "seq", axis=0, tiled=True),
        lax.all_gather(value_flat, "seq", axis=0, tiled=True),
        lax.all_gather(key_codes, "seq", axis=0, tiled=True),
    )
    pack_rows = gathered[0].shape[0]
    grad_attn_wide = grad_attn.astype(jnp.float32)

    def joint_step(total_grad, key_block):
        probabilities, grad_scores = block_grads(
            key_block, queries, query_codes, grad_attn, log_total, delta_rows
        )
        total_grad = total_grad + 0.125 * jnp.einsum(
            "hqk,khe->qhe", grad_scores, key_block[0], preferred_element_type=jnp.float32
        )
        grad_keys = 0.125 * jnp.einsum(
            "hqk,qhe->khe", grad_scores, queries, preferred_element_type=jnp.float32
        )
        grad_values = jnp.einsum("hqk,qhe->khe", probabilities, grad_attn_wide, precision=highest)
        return (total_grad, (grad_keys, grad_values))

    grad_queries_rot, both_grads = lax.scan(joint_step, zero_query, stack_blocks(gathered))
    key_value_terms = jnp.concatenate(
        [both_grads[0].reshape(pack_rows, D), both_grads[1].reshape(pack_rows, D)], axis=1
    )
    key_value_grad = lax.psum_scatter(key_value_terms, "seq", scatter_dimension=0, tiled=True)
    g_query = (
        rotate_pairs(grad_queries_rot, position, -1.0).reshape(frame_count, D).astype(jnp.bfloat16)
    )
    g_key = (
        rotate_pairs(key_value_grad[:, :D].reshape(frame_count, HEADS, HEAD), position, -1.0)
        .reshape(frame_count, D)
        .astype(jnp.bfloat16)
    )
    g_value = key_value_grad[:, D:].astype(jnp.bfloat16)
    grad_query_local = matmul(attn_input.T, g_query)
    grad_key_local = matmul(attn_input.T, g_key)
    grad_value_local = matmul(attn_input.T, g_value)
    grad_attn_input = (
        matmul(g_query, back_q.T) + matmul(g_key, back_k.T) + matmul(g_value, back_v.T)
    )
    grad_inputs = grad_middle + norm_backward(grad_attn_input * (1.0 + scale_attn), normed, inverse)
    grad_modulation = jnp.concatenate(
        [
            grad_attn_input,
            grad_attn_input * normed,
            grad_gate_attn,
            grad_ffn_input,
            grad_scale_ffn,
            grad_gate_ffn,
        ],
        axis=1,
    )
    grad_emb = jnp.dot(one_hot.T, grad_modulation, precision=highest)
    grad_ada_local = jnp.dot(silu_time.astype(jnp.float32).T, grad_emb, precision=highest)
    part_q, part_k, part_v, part_o, part_a, part_u, part_d = (
        lax.psum_scatter(grad_query_local, "seq", scatter_dimension=1, tiled=True),
        lax.psum_scatter(grad_key_local, "seq", scatter_dimension=1, tiled=True),
        lax.psum_scatter(grad_value_local, "seq", scatter_dimension=1, tiled=True),
        lax.psum_scatter(grad_out_local, "seq", scatter_dimension=1, tiled=True),
        lax.psum_scatter(grad_ada_local, "seq", scatter_dimension=1, tiled=True),
        lax.psum_scatter(grad_up_local, "seq", scatter_dimension=1, tiled=True),
        lax.psum_scatter(grad_down_local, "seq", scatter_dimension=1, tiled=True),
    )
    final_q, final_k, final_v, final_o, final_a, final_u, final_d = (
        lax.psum_scatter(
            part_q.astype(jnp.bfloat16), "batch", scatter_dimension=0, tiled=True
        ).astype(jnp.float32),
        lax.psum_scatter(
            part_k.astype(jnp.bfloat16), "batch", scatter_dimension=0, tiled=True
        ).astype(jnp.float32),
        lax.psum_scatter(
            part_v.astype(jnp.bfloat16), "batch", scatter_dimension=0, tiled=True
        ).astype(jnp.float32),
        lax.psum_scatter(
            part_o.astype(jnp.bfloat16), "batch", scatter_dimension=0, tiled=True
        ).astype(jnp.float32),
        lax.psum_scatter(
            part_a.astype(jnp.bfloat16), "batch", scatter_dimension=0, tiled=True
        ).astype(jnp.float32),
        lax.psum_scatter(
            part_u.astype(jnp.bfloat16), "batch", scatter_dimension=0, tiled=True
        ).astype(jnp.float32),
        lax.psum_scatter(
            part_d.astype(jnp.bfloat16), "batch", scatter_dimension=0, tiled=True
        ).astype(jnp.float32),
    )
    return (
        result.astype(jnp.bfloat16)[None],
        grad_inputs.astype(jnp.bfloat16)[None],
        final_q,
        final_k,
        final_v,
        final_o,
        final_a,
        final_u,
        final_d,
    )


TWO = 2 * HEAD
ROWS = 256
BIG = 1e30
SEQ = 8
REPLICAS = 4
VMEM_MIB = 60
BLOCK = 512


def swap(part, axis, distance):
    size = SEQ if axis == "seq" else REPLICAS
    return lax.ppermute(part, axis, [(i, i ^ distance) for i in range(size)])


def exchange(blocks):
    return lax.all_to_all(blocks, "seq", 0, 0, tiled=True)


def turn(vectors, cosine, sine):
    lane = lax.broadcasted_iota(jnp.int32, vectors.shape, 1)
    first = (lane % HEAD) < HEAD // 2
    partner = jnp.where(
        first,
        pltpu.roll(vectors, TWO - HEAD // 2, 1),
        pltpu.roll(vectors, HEAD // 2, 1),
    )
    return vectors * cosine + partner * jnp.where(first, -sine, sine)


def of_head(vectors, head):
    lane = lax.broadcasted_iota(jnp.int32, vectors.shape, 1)
    return jnp.where(lane // HEAD == head, vectors, jnp.zeros_like(vectors))


def dot_t(left, right):
    return lax.dot_general(
        left, right, (((1,), (1,)), ((), ())), preferred_element_type=jnp.float32
    )


def project_kernel(place_ref, a_ref, b_ref, c_ref, d_ref, member_ref, bar_ref, cos_ref, sin_ref,
                   emb_ref, w_ref, *refs):
    x_ref, input_ref, q_ref, k_ref, kt_ref, v_ref, vt_ref, chunk_ref = refs[-8:]
    for step, ref in enumerate((a_ref, b_ref, c_ref, d_ref)):

        @pl.when(pl.program_id(0) == step)
        def _():
            chunk_ref[...] = ref[...]

    chunk = chunk_ref[...]
    x_ref[...] = chunk
    normed, _ = standardize(chunk.astype(jnp.float32))
    modulation = matmul(member_ref[...], emb_ref[...])
    low = (normed * (1.0 + modulation[:, D:]) + modulation[:, :D]).astype(jnp.bfloat16)
    input_ref[...] = low
    weight = jnp.concatenate([w_ref[b ^ place_ref[1]] for b in range(REPLICAS)], axis=0)
    product = matmul(low, weight)
    cosine, sine = cos_ref[...], sin_ref[...]
    keys = turn(product[:, TWO:2 * TWO], cosine, sine)
    values = product[:, 2 * TWO:]
    q_ref[...] = turn(product[:, :TWO], cosine, sine).astype(jnp.bfloat16)
    k_ref[:, :TWO] = keys.astype(jnp.bfloat16)
    k_ref[:, TWO:] = bar_ref[...]
    kt_ref[...] = keys.T.astype(jnp.bfloat16)
    v_ref[...] = values.astype(jnp.bfloat16)
    vt_ref[...] = values.T.astype(jnp.bfloat16)


def rows_spec(width):
    return pl.BlockSpec((ROWS, width), lambda i: (i, 0))


def cols_spec(height):
    return pl.BlockSpec((height, ROWS), lambda i: (0, i))


def whole_spec(height, width):
    return pl.BlockSpec((height, width), lambda i: (0, 0))


def params(mib):
    return pltpu.CompilerParams(
        dimension_semantics=("arbitrary",), vmem_limit_bytes=mib * 1024 * 1024
    )


def cost(micros):
    return pl.CostEstimate(
        flops=int(micros * 1e9), bytes_accessed=int(micros * 3e6), transcendentals=0
    )


def project(place, odd, chunks, member, bar, cosine, sine, emb, weights, earlier):
    frames = member.shape[0]
    low = jnp.bfloat16

    def rows(width):
        return pl.BlockSpec((ROWS, width), lambda i, p: ((2 * i + odd) ^ p[0], 0))

    def cols(height):
        return pl.BlockSpec((height, ROWS), lambda i, p: (0, (2 * i + odd) ^ p[0]))

    def whole(height, width):
        return pl.BlockSpec((height, width), lambda i, p: (0, 0))

    inputs = [place, *chunks, member, bar, cosine, sine, emb, weights, *earlier]
    first = len(inputs) - len(earlier)
    return pl.pallas_call(
        project_kernel,
        grid_spec=pltpu.PrefetchScalarGridSpec(
            num_scalar_prefetch=1,
            grid=(4,),
            in_specs=[whole(ROWS, D)] * 4 + [rows(TWO)] * 4
            + [whole(TWO, 2 * D),
               pl.BlockSpec((REPLICAS, ROWS, 3 * TWO), lambda i, p: (0, 0, 0))]
            + [pl.BlockSpec(memory_space=pl.ANY)] * len(earlier),
            out_specs=[rows(D), rows(D), rows(TWO), rows(2 * TWO), cols(TWO), rows(TWO),
                       cols(TWO)],
            scratch_shapes=[pltpu.VMEM((ROWS, D), low)],
        ),
        out_shape=[
            jax.ShapeDtypeStruct((frames, D), low),
            jax.ShapeDtypeStruct((frames, D), low),
            jax.ShapeDtypeStruct((frames, TWO), low),
            jax.ShapeDtypeStruct((frames, 2 * TWO), low),
            jax.ShapeDtypeStruct((TWO, frames), low),
            jax.ShapeDtypeStruct((frames, TWO), low),
            jax.ShapeDtypeStruct((TWO, frames), low),
        ],
        input_output_aliases={first + i: i for i in range(len(earlier))},
        compiler_params=params(30),
        cost_estimate=cost(2),
        name="project",
    )(*inputs)


def attend_kernel(q_ref, member_ref, k_ref, vt_ref, att_ref, low_ref, log_ref, *score_refs):
    frames = k_ref.shape[0]
    step = min(frames, 1024)
    queries = q_ref[...] * 0.125
    member = member_ref[...]
    bests, halves = [], []
    for head, score_ref in enumerate(score_refs):
        wide = jnp.concatenate([of_head(queries, head), member], axis=1)
        largest = jnp.full((1, BLOCK), -BIG, jnp.float32)
        for start in range(0, frames, step):
            scores = dot_t(k_ref[start:start + step, :], wide)
            score_ref[start:start + step, :] = scores
            largest = jnp.maximum(largest, jnp.max(scores, axis=0, keepdims=True))
        bests.append(largest)
    for head, score_ref in enumerate(score_refs):
        total = jnp.zeros((1, BLOCK), jnp.float32)
        out = jnp.zeros((TWO, BLOCK), jnp.float32)
        for start in range(0, frames, step):
            weights = jnp.exp(score_ref[start:start + step, :] - bests[head])
            total = total + jnp.sum(weights, axis=0, keepdims=True)
            out = out + matmul(vt_ref[:, start:start + step], weights.astype(jnp.bfloat16))
        halves.append(out[head * HEAD:(head + 1) * HEAD, :] / total)
        log_ref[head:head + 1, :] = bests[head] + jnp.log(total)
    attended = jnp.concatenate(halves, axis=0).T
    att_ref[...] = attended
    low_ref[...] = attended.astype(jnp.bfloat16)


def block_spec(width):
    return pl.BlockSpec((BLOCK, width), lambda i: (i, 0))


def attend(q, member, k, vt):
    frames = q.shape[0]
    return pl.pallas_call(
        attend_kernel,
        grid=(frames // BLOCK,),
        in_specs=[block_spec(TWO), block_spec(TWO), whole_spec(frames, 2 * TWO),
                  whole_spec(TWO, frames)],
        out_specs=[block_spec(TWO), block_spec(TWO), pl.BlockSpec((8, BLOCK), lambda i: (0, i))],
        out_shape=[
            jax.ShapeDtypeStruct((frames, TWO), jnp.float32),
            jax.ShapeDtypeStruct((frames, TWO), jnp.bfloat16),
            jax.ShapeDtypeStruct((8, frames), jnp.float32),
        ],
        scratch_shapes=[pltpu.VMEM((frames, BLOCK), jnp.float32)] * 2,
        compiler_params=params(26),
        cost_estimate=cost(18),
        name="attend",
    )(q, member, k, vt)


def attend_back_kernel(q_ref, member_ref, grad_ref, att_ref, log_ref, cos_ref, sin_ref, cos_all_ref,
                       sin_all_ref, k_ref, kt_ref, v_ref, g_ref, dk_ref, dv_ref):
    block = pl.program_id(0)
    frames = k_ref.shape[0]
    step = min(frames, 1024)

    @pl.when(block == 0)
    def _():
        dk_ref[...] = jnp.zeros_like(dk_ref)
        dv_ref[...] = jnp.zeros_like(dv_ref)

    queries = q_ref[...] * 0.125
    member = member_ref[...]
    grad = grad_ref[...]
    mixed = (grad.astype(jnp.float32) * att_ref[...]).T
    heads = [of_head(queries, head) for head in range(2)]
    wides = [jnp.concatenate([part, member], axis=1) for part in heads]
    grads = [of_head(grad, head) for head in range(2)]
    rows = [slice(head * HEAD, (head + 1) * HEAD) for head in range(2)]
    deltas = [jnp.sum(mixed[here, :], axis=0, keepdims=True) for here in rows]
    queries, grad = jnp.concatenate(heads, axis=0), jnp.concatenate(grads, axis=0)
    totals = [jnp.zeros((HEAD, BLOCK), jnp.float32) for _ in range(2)]
    for start in range(0, frames, step):
        part = slice(start, start + step)
        low_weights, low_grads = [], []
        for head in range(2):
            scores = dot_t(k_ref[part, :], wides[head])
            weights = jnp.exp(scores - log_ref[head:head + 1, :])
            grad_weights = dot_t(v_ref[part, :], grads[head])
            grad_scores = (weights * (grad_weights - deltas[head])).astype(jnp.bfloat16)
            totals[head] = totals[head] + matmul(kt_ref[rows[head], part], grad_scores)
            low_weights.append(weights.astype(jnp.bfloat16))
            low_grads.append(grad_scores)
        dv_ref[part, :] += matmul(jnp.concatenate(low_weights, axis=1), grad)
        dk_ref[part, :] += matmul(jnp.concatenate(low_grads, axis=1), queries)
    dq = jnp.concatenate(totals, axis=0).T * 0.125
    here = pl.ds(pl.multiple_of(block * BLOCK, BLOCK), BLOCK)
    g_ref[here, :TWO] = turn(dq, cos_ref[...], -sin_ref[...]).astype(jnp.bfloat16)

    @pl.when(block == pl.num_programs(0) - 1)
    def _():
        turned = turn(dk_ref[...], cos_all_ref[...], -sin_all_ref[...])
        g_ref[:, TWO:2 * TWO] = turned.astype(jnp.bfloat16)
        g_ref[:, 2 * TWO:] = dv_ref[...].astype(jnp.bfloat16)


def attend_back(q, member, grad, att, log_total, cosine, sine, k, kt, v):
    frames = q.shape[0]
    return pl.pallas_call(
        attend_back_kernel,
        grid=(frames // BLOCK,),
        in_specs=[block_spec(TWO), block_spec(TWO), block_spec(TWO), block_spec(TWO),
                  pl.BlockSpec((8, BLOCK), lambda i: (0, i)), block_spec(TWO), block_spec(TWO),
                  whole_spec(frames, TWO), whole_spec(frames, TWO),
                  whole_spec(frames, 2 * TWO), whole_spec(TWO, frames), whole_spec(frames, TWO)],
        out_specs=whole_spec(frames, 3 * TWO),
        out_shape=jax.ShapeDtypeStruct((frames, 3 * TWO), jnp.bfloat16),
        scratch_shapes=[pltpu.VMEM((frames, TWO), jnp.float32),
                        pltpu.VMEM((frames, TWO), jnp.float32)],
        compiler_params=params(VMEM_MIB),
        cost_estimate=cost(27),
        name="attend_back",
    )(q, member, grad, att, log_total, cosine, sine, cosine, sine, k, kt, v)


def three_terms(values):
    high = lax.reduce_precision(values, 8, 7)
    middle = lax.reduce_precision(values - high, 8, 7)
    return [high, middle, values - high - middle]


def standardize(rows):
    centered = rows - jnp.mean(rows, axis=1, keepdims=True)
    inverse = lax.rsqrt(jnp.mean(centered * centered, axis=1, keepdims=True) + 1e-06)
    return centered * inverse, inverse


def sum_of_clips(clip_ref, values):
    ids = lax.broadcasted_iota(jnp.int32, (CLIPS, clip_ref.shape[1]), 0)
    chosen = jnp.where(clip_ref[...] == ids, 1.0, 0.0).astype(jnp.bfloat16)
    high = values.astype(jnp.bfloat16)
    rest = values - high.astype(jnp.float32)
    middle = rest.astype(jnp.bfloat16)
    last = (rest - middle.astype(jnp.float32)).astype(jnp.bfloat16)
    return matmul(chosen, high) + matmul(chosen, middle) + matmul(chosen, last)


def beside(ref, tiles, rows):
    return jnp.concatenate([ref[tile, rows, :] for tile in tiles], axis=1)


def tile_index(away, apart):
    return 16 * (away % 2) + 8 * (away // 2) + 4 * (apart % 2) + apart // 2


def middle_kernel(mine_ref, x_ref, cot_ref, member_ref, clip_ref, emb_ref, *refs):
    *tile_refs, result_ref, grad_middle_ref, grad_att_ref, grad_emb_ref, left_ref, right_ref = refs[:-9]
    out_ref, up_ref, down_ref, sems, branch_ref, low_ref, act_ref, slope_ref, wide_ref = refs[-9:]
    low = jnp.bfloat16
    act_t_ref, ffn_t_ref = left_ref.at[:2 * D], left_ref.at[2 * D:3 * D]
    mine_t_ref = left_ref.at[3 * D:]
    g_ffn_ref, g_attn_ref = right_ref.at[:, :D], right_ref.at[:, 3 * D:]
    g_hidden_ref = right_ref.at[:, D:3 * D]
    pieces = ((out_ref, 0, 256), (up_ref, 256, 512), (down_ref, 768, 512))
    for i, (ref, start, size) in enumerate(pieces):
        first = 0
        for tile_ref in tile_refs:
            count = tile_ref.shape[0]
            pltpu.make_async_copy(
                tile_ref.at[:, pl.ds(start, size), :], ref.at[pl.ds(first, count)], sems.at[i]
            ).start()
            first += count
    copies = [
        pltpu.make_async_copy(ref, ref, sems.at[i]) for i, (ref, _, _) in enumerate(pieces)
    ]

    def tile(b, s):
        return SEQ * b + s

    member = member_ref[...]

    def modulation(index):
        return matmul(member, emb_ref[:, index * D:(index + 1) * D])

    def cols(n, width=256):
        return pl.ds(pl.multiple_of(n * width, width), width)

    every = slice(None)
    mine = jnp.concatenate([mine_ref[j] for j in range(SEQ)], axis=1)
    low_ref[...] = mine
    mine_t_ref[...] = mine.T
    gate_attn = modulation(2)
    copies[0].wait()

    @pl.loop(0, 4)
    def _(n):
        total = jnp.zeros((ROWS, 256), jnp.float32)
        for b in range(REPLICAS):
            weight = beside(out_ref, [tile(b, 2 * n), tile(b, 2 * n + 1)], every)
            total = total + matmul(low_ref[:, 256 * b:256 * b + 256], weight)
        branch_ref[:, cols(n)] = total

    branch = branch_ref[...]
    middle = x_ref[...].astype(jnp.float32) + gate_attn * branch
    normed, inverse = standardize(middle)
    scale_ffn = modulation(4)
    ffn_input = normed * (1.0 + scale_ffn) + modulation(3)
    low_ref[...] = ffn_input.astype(low)
    ffn_t_ref[...] = ffn_input.T.astype(low)
    gate_ffn = modulation(5)
    cot = cot_ref[...].astype(jnp.float32)
    g_ffn_ref[...] = (cot * gate_ffn).astype(low)
    copies[1].wait()

    @pl.loop(0, 8)
    def _(n):
        hidden = jnp.zeros((ROWS, 256), jnp.float32)
        for b in range(REPLICAS):
            index = tile(b, n)
            weight = jnp.concatenate([up_ref[index, :256, :], up_ref[index, 256:, :]], axis=1)
            hidden = hidden + matmul(low_ref[:, 256 * b:256 * b + 256], weight)
        root = math.sqrt(2.0 / math.pi)
        squared = hidden * hidden
        bent = jnp.tanh(root * (hidden + 0.044715 * (squared * hidden)))
        half = 0.5 * (1.0 + bent)
        activated = hidden * half
        slope = half + 0.5 * hidden * (1.0 - bent * bent) * (
            root * (1.0 + (3.0 * 0.044715) * squared)
        )
        act_ref[:, cols(n)] = activated.astype(low)
        act_t_ref[cols(n), :] = activated.T.astype(low)
        slope_ref[:, cols(n)] = slope

    copies[2].wait()

    @pl.loop(0, 4)
    def _(n):
        total = jnp.zeros((ROWS, 256), jnp.float32)
        for b in range(REPLICAS):
            weight = beside(down_ref, [tile(b, 2 * n), tile(b, 2 * n + 1)], every)
            total = total + matmul(act_ref[:, 512 * b:512 * b + 512], weight)
        wide_ref[:, cols(n)] = total

    ffn_branch = wide_ref[...]
    result_ref[...] = (middle + gate_ffn * ffn_branch).astype(low)
    grad_emb_ref[:, 3 * D:] = sum_of_clips(clip_ref, cot * ffn_branch)

    @pl.loop(0, REPLICAS)
    def _(b):
        weight = beside(down_ref, [tile(b, s) for s in range(SEQ)], every)
        grad = dot_t(g_ffn_ref[...], weight)
        here = cols(b, 512)
        g_hidden_ref[:, here] = (grad * slope_ref[:, here]).astype(low)

    @pl.loop(0, REPLICAS)
    def _(b):
        weight = jnp.concatenate(
            [up_ref[tile(b, s), 256 * k:256 * k + 256, :] for s in range(SEQ) for k in range(2)],
            axis=1,
        )
        wide_ref[:, cols(b)] = dot_t(g_hidden_ref[...], weight)

    grad_ffn_input = wide_ref[...]
    grad_emb_ref[:, D:2 * D] = sum_of_clips(clip_ref, grad_ffn_input)
    grad_emb_ref[:, 2 * D:3 * D] = sum_of_clips(clip_ref, grad_ffn_input * normed)
    spread = grad_ffn_input * (1.0 + scale_ffn)
    grad_middle = cot + inverse * (
        spread
        - jnp.mean(spread, axis=1, keepdims=True)
        - normed * jnp.mean(spread * normed, axis=1, keepdims=True)
    )
    grad_middle_ref[...] = grad_middle
    grad_emb_ref[:, :D] = sum_of_clips(clip_ref, grad_middle * branch)
    g_attn_ref[...] = (grad_middle * gate_attn).astype(low)

    @pl.loop(0, REPLICAS)
    def _(b):
        weight = beside(out_ref, [tile(b, s) for s in range(SEQ)], every)
        grad = dot_t(g_attn_ref[...], weight).astype(low)
        grad_att_ref[2 * b] = grad[:, :TWO]
        grad_att_ref[2 * b + 1] = grad[:, TWO:]


def middle_part(mine, x, cot, member, clip_row, emb, tiles):
    low = jnp.bfloat16
    shapes = [
        ((ROWS, D), low), ((ROWS, D), jnp.float32), ((SEQ, ROWS, TWO), low),
        ((CLIPS, 4 * D), jnp.float32),
        ((4 * D, ROWS), low), ((ROWS, 4 * D), low),
    ]
    vmem = pl.BlockSpec(memory_space=pltpu.VMEM)
    return pl.pallas_call(
        middle_kernel,
        in_specs=[vmem] * 6 + [pl.BlockSpec(memory_space=pl.ANY)] * len(tiles),
        out_specs=[vmem] * len(shapes),
        out_shape=[jax.ShapeDtypeStruct(shape, dtype) for shape, dtype in shapes],
        scratch_shapes=[
            pltpu.VMEM((32, 256, 128), low),
            pltpu.VMEM((32, 512, 128), low),
            pltpu.VMEM((32, 512, 128), low),
            pltpu.SemaphoreType.DMA((3,)),
            pltpu.VMEM((ROWS, D), jnp.float32),
            pltpu.VMEM((ROWS, D), low),
            pltpu.VMEM((ROWS, 2 * D), low),
            pltpu.VMEM((ROWS, 2 * D), jnp.float32),
            pltpu.VMEM((ROWS, D), jnp.float32),
        ],
        compiler_params=pltpu.CompilerParams(vmem_limit_bytes=VMEM_MIB * 1024 * 1024),
        cost_estimate=cost(20),
        name="middle",
    )(mine, x, cot, member, clip_row, emb, *tiles)


def weight_grads_kernel(place_ref, down_l, up_l, out_l, right_ref, down_o, up_o, out_o, other_ref,
                        away_d_ref, keep_d_ref, away_u_ref, keep_u_ref):
    low = jnp.bfloat16
    z, y = place_ref[2] // 2, place_ref[2] % 2
    lefts = [
        jnp.concatenate([mine[...], other[...]], axis=1)
        for mine, other in ((down_l, down_o), (up_l, up_o), (out_l, out_o))
    ]

    def product(left, first, block):
        here = pl.ds(pl.multiple_of(first + 256 * block, 256), 256)
        right = jnp.concatenate([right_ref[:, here], other_ref[:, here]], axis=0)
        return matmul(left, right).astype(low)

    def fill(ref):
        for k in range(4):
            block = z ^ k
            for left, first, rows in ((lefts[0], 0, slice(0, 512)), (lefts[2], 3 * D, slice(512, 768))):
                grad = product(left, first, block)
                ref[4 * y + k, rows, :] = grad[:, :128]
                ref[4 - 4 * y + k, rows, :] = grad[:, 128:]
            for side, up_ref in enumerate((keep_u_ref, away_u_ref)):
                grad = product(lefts[1], D, 2 * block + (y ^ side))
                up_ref[0, k, :256, :] = grad[:, :128]
                up_ref[0, k, 256:, :] = grad[:, 128:]

    @pl.when(pl.program_id(0) == 0)
    def _():
        fill(away_d_ref)

    @pl.when(pl.program_id(0) == 1)
    def _():
        fill(keep_d_ref)


def weight_grads(place, left, right, other_left, other_right):
    low = jnp.bfloat16

    def target(i, p):
        return 2 * jnp.where(i == 0, 1 - p[0], p[0]) + p[1]

    down = pl.BlockSpec((512, ROWS), lambda i, p: (target(i, p), 0))
    up = pl.BlockSpec((256, ROWS), lambda i, p: (8 + target(i, p), 0))
    out = pl.BlockSpec((256, ROWS), lambda i, p: (12 + target(i, p), 0))
    wide = pl.BlockSpec((ROWS, 4 * D), lambda i, p: (0, 0))
    whole = pl.BlockSpec((SEQ, 768, 128), lambda i, p: (0, 0, 0))
    part = pl.BlockSpec((1, 4, 512, 128), lambda i, p: (1 - i, 0, 0, 0))
    return pl.pallas_call(
        weight_grads_kernel,
        grid_spec=pltpu.PrefetchScalarGridSpec(
            num_scalar_prefetch=1,
            grid=(2,),
            in_specs=[down, up, out, wide] * 2,
            out_specs=[whole, whole, part, part],
        ),
        out_shape=[jax.ShapeDtypeStruct((SEQ, 768, 128), low)] * 2
        + [jax.ShapeDtypeStruct((2, 4, 512, 128), low)] * 2,
        compiler_params=params(VMEM_MIB),
        cost_estimate=cost(9),
        name="weight_grads",
    )(place, left, left, left, right, other_left, other_left, other_left, other_right)


def clip_grads_kernel(place_ref, x_ref, clip_ref, g_ref, w_ref, out_ref):
    @pl.when(pl.program_id(0) == 0)
    def _():
        out_ref[...] = jnp.zeros_like(out_ref)

    normed, _ = standardize(x_ref[...].astype(jnp.float32))
    grad = jnp.concatenate(
        [dot_t(g_ref[...], w_ref[b ^ place_ref[1]]) for b in range(REPLICAS)], axis=1
    )
    out_ref[:, :D] += sum_of_clips(clip_ref, grad)
    out_ref[:, D:] += sum_of_clips(clip_ref, grad * normed)


def clip_grads(places, x, clip_row, g_heads, heads_w):
    frames = x.shape[0]
    return pl.pallas_call(
        clip_grads_kernel,
        grid=(frames // ROWS,),
        in_specs=[pl.BlockSpec(memory_space=pltpu.SMEM), rows_spec(D), cols_spec(1),
                  rows_spec(3 * TWO),
                  pl.BlockSpec((REPLICAS, ROWS, 3 * TWO), lambda i: (0, 0, 0))],
        out_specs=whole_spec(CLIPS, 2 * D),
        out_shape=jax.ShapeDtypeStruct((CLIPS, 2 * D), jnp.float32),
        compiler_params=params(VMEM_MIB),
        cost_estimate=cost(9),
        name="clip_grads",
    )(places, x, clip_row, g_heads, heads_w)


def last_kernel(place_ref, own_ref, x_ref, grad_middle_ref, member_ref, emb_ref, *refs):
    *tile_refs, out_ref, wide_ref = refs
    grads = jnp.concatenate([own_ref[place_ref[2] ^ s] for s in range(SEQ)], axis=1)

    def tile(away, apart):
        index = tile_index(away, apart)
        for ref in tile_refs:
            if index < ref.shape[0]:
                return ref[index, ref.shape[1] - 768:, :]
            index -= ref.shape[0]

    for away in range(REPLICAS):
        weight = jnp.concatenate(
            [
                tile(away, s)[256 * k:256 * k + 256, :]
                for s in range(SEQ)
                for k in range(3)
            ],
            axis=1,
        )
        b = (2 * place_ref[0] + place_ref[1]) ^ away
        wide_ref[:, pl.ds(pl.multiple_of(b * 256, 256), 256)] = dot_t(grads, weight)

    normed, inverse = standardize(x_ref[...].astype(jnp.float32))
    spread = wide_ref[...] * (1.0 + matmul(member_ref[...], emb_ref[:, D:2 * D]))
    grad = grad_middle_ref[...] + inverse * (
        spread
        - jnp.mean(spread, axis=1, keepdims=True)
        - normed * jnp.mean(spread * normed, axis=1, keepdims=True)
    )
    out_ref[...] = grad.astype(jnp.bfloat16)


def last_part(place, own, x, grad_middle, member, emb, tiles):
    vmem = pl.BlockSpec(memory_space=pltpu.VMEM)
    return pl.pallas_call(
        last_kernel,
        in_specs=[pl.BlockSpec(memory_space=pltpu.SMEM)] + [vmem] * (5 + len(tiles)),
        out_specs=vmem,
        out_shape=jax.ShapeDtypeStruct((ROWS, D), jnp.bfloat16),
        scratch_shapes=[pltpu.VMEM((ROWS, D), jnp.float32)],
        compiler_params=pltpu.CompilerParams(vmem_limit_bytes=30 * 1024 * 1024),
        cost_estimate=cost(4),
        name="last",
    )(place, own, x, grad_middle, member, emb, *tiles)


def after(value, *others):
    return lax.optimization_barrier((value,) + others)[0]


def together(*values):
    return lax.optimization_barrier(values)


def plus(*terms):
    total = terms[0].astype(jnp.float32)
    for term in terms[1:]:
        total = total + term.astype(jnp.float32)
    return total


def clip_lanes(clip, terms):
    lane = jnp.arange(TWO, dtype=jnp.int32)[None, :]
    return (clip[:, None] == lane % CLIPS) & (lane < terms * CLIPS)


def body_fast(
    tokens, w_query, w_key, w_value, w_out, w_ada, w_up, w_down,
    segments, validity, timesteps, cotangent,
):
    highest = lax.Precision.HIGHEST
    low = jnp.bfloat16
    wide = jnp.float32
    replica = lax.axis_index("batch")
    x = tokens[0]
    frame_count = x.shape[0]
    frames = frame_count * SEQ
    segment = segments[0]

    seat = lax.axis_index("seq").astype(jnp.int32)
    z, y = seat // 2, seat % 2
    place = jnp.stack([replica // 2, replica % 2, seat]).astype(jnp.int32)
    mine_w = jnp.concatenate([w_out, w_up[:, :128], w_up[:, 128:], w_down], axis=0).astype(low)

    z1, z2, y0 = swap(x, "seq", 2), swap(x, "seq", 4), swap(x, "seq", 1)
    times = lax.all_gather(timesteps[0], "batch", axis=0, tiled=True)
    silu_all = jax.nn.silu(time_embedding(times)).astype(low)
    depth = w_ada.shape[0]
    silu_part = lax.dynamic_slice_in_dim(silu_all, replica * depth, depth, 1)
    emb_part = matmul(silu_part, w_ada.astype(low)).reshape(REPLICAS, CLIPS, -1)
    emb_cols = lax.all_to_all(emb_part, "batch", 0, 0, tiled=True)
    emb_cols = jnp.sum(emb_cols, axis=0)
    own_codes = (segment * 2 + (validity[0] == 1)).astype(wide)
    cols = emb_cols.shape[1]
    own_codes = jnp.pad(own_codes, (0, 8 * cols - frame_count)).reshape(8, cols)
    packed = jnp.concatenate([emb_cols, own_codes])
    packed = jnp.broadcast_to(packed[None], (SEQ,) + packed.shape)
    heads_w = jnp.concatenate([w_query, w_key, w_value], axis=1).astype(low)
    heads_w = jnp.stack([heads_w, swap(heads_w, "batch", 1)])
    z1, z2, y0, packed, heads_w, mine_w = together(z1, z2, y0, packed, heads_w, mine_w)
    tiles_w = (lax.all_gather(mine_w, ("batch", "seq"), axis=0),)
    packed = exchange(packed)
    z3 = swap(z2, "seq", 2)
    y1, y2 = swap(z1, "seq", 1), swap(z2, "seq", 1)
    heads_x = swap(heads_w, "batch", 2)
    z3, heads_x = together(z3, heads_x)
    y3 = swap(z3, "seq", 1)
    mine_h = jnp.concatenate([w_query, w_key, w_value], axis=0).astype(low)
    mine_h = after(mine_h, z3)
    h_z1, h_z2 = swap(mine_h, "seq", 2), swap(mine_h, "seq", 4)
    heads_w = jnp.concatenate([heads_w, heads_x])
    emb = packed[:, :CLIPS]
    codes = packed[:, CLIPS:].reshape(SEQ, -1)[:, :frame_count].reshape(frames).astype(jnp.int32)
    clip = codes // 2
    clip_row = clip[None, :]
    tri = jnp.arange(frame_count)[:, None] > jnp.arange(frame_count)[None, :]
    ids = jnp.arange(CLIPS, dtype=jnp.int32)
    one_hot = (clip.reshape(SEQ, frame_count)[:, :, None] == ids).astype(low)
    within = jnp.einsum("ij,njc->nic", tri.astype(low), one_hot, preferred_element_type=wide)
    counts = jnp.sum(one_hot.astype(wide), axis=1)
    offsets = jnp.cumsum(counts, axis=0) - counts
    position = jnp.sum(one_hot.astype(wide) * (within + offsets[:, None, :]), axis=2)
    half = HEAD // 2
    frequency = jnp.exp(-math.log(10000.0) * jnp.arange(half, dtype=wide) / half)
    angle = position.reshape(frames)[:, None] * jnp.tile(frequency, 4)[None, :]
    cosine, sine = jnp.cos(angle), jnp.sin(angle)
    member = clip_lanes(clip, 3).astype(low)
    allowed = clip_lanes(jnp.where(codes % 2 == 1, clip, -1), 1)
    inside = jnp.arange(TWO, dtype=jnp.int32)[None, :] < CLIPS
    bar = jnp.where(inside & ~allowed, -BIG, 0.0).astype(low)
    emb, y1, y2 = together(after(emb, heads_w, member, cosine), y1, y2)
    emb = emb.transpose(1, 0, 2).reshape(CLIPS, -1)
    emb = jnp.concatenate(
        [t.astype(low) for t in three_terms(emb)] + [jnp.zeros((TWO - 3 * CLIPS, 6 * D), low)],
        axis=0,
    )

    tables = (member, bar, cosine, sine, emb, heads_w)
    places = jnp.stack([seat, replica.astype(jnp.int32)])
    earlier = project(places, 0, (x, z1, z2, z3), *tables, ())
    y3, h_z1, h_z2, earlier = together(y3, h_z1, h_z2, earlier)
    h_z3 = swap(h_z2, "seq", 2)
    x_all, attn_input, q, k, kt, v, vt = project(places, 1, (y0, y1, y2, y3), *tables, earlier)
    attended, attended_low, log_total = attend(q, member, k, vt)
    attended_low, h_z3 = together(attended_low, h_z3)
    mine = exchange(attended_low.reshape(SEQ, frame_count, TWO))
    h_z = jnp.stack([mine_h, h_z1, h_z2, h_z3])
    mine, h_z = together(mine, h_z)
    h_y, h_x = swap(h_z, "seq", 1), swap(h_z, "batch", 2)

    own_member = clip_lanes(segment, 3).astype(low)
    result, grad_middle, grad_att, grad_emb, left, right = middle_part(
        mine, x, cotangent[0], own_member, segment[None, :], emb, tiles_w
    )
    left, h_y, h_x = together(left, h_y, h_x)
    other_left, other_right = swap(left, "batch", 1), swap(right, "batch", 1)
    h_first = jnp.concatenate([h_z, h_y, h_x])
    other_left, other_right, h_first = together(other_left, other_right, h_first)
    away_d, keep_d, away_u, keep_u = weight_grads(place, left, right, other_left, other_right)
    grad_heads = exchange(grad_att).reshape(frames, TWO)
    grad_heads, away_d, away_u = together(grad_heads, away_d, away_u)
    from_x = swap(away_d, "batch", 2)
    from_y = swap(away_u, "seq", 1)

    g_heads = attend_back(
        q, member, grad_heads, attended, log_total, cosine, sine, k, kt, v
    )
    own = exchange(g_heads.reshape(SEQ, frame_count, 3 * TWO))
    from_y = after(from_y, g_heads)
    to_x_u = plus(keep_u[1], from_y[1]).astype(low)
    from_x_u = swap(to_x_u, "batch", 2)
    from_x = after(from_x, to_x_u)
    to_y_d = plus(keep_d[4:], from_x[4:]).astype(low)
    from_y_d = swap(to_y_d, "seq", 1)
    h_yx = swap(after(h_y, to_y_d), "batch", 2)
    h_first_core = swap(after(h_first, to_x_u), "batch", 1)
    g_heads = after(g_heads, to_y_d, to_x_u)
    late = clip_grads(places, x_all, clip_row, g_heads, heads_w)
    grad_heads_w = matmul(attn_input.T, g_heads).astype(low).reshape(2, 2, ROWS, 3 * TWO)
    late, grad_heads_w, from_y_d, from_x_u, h_first_core = together(
        late, grad_heads_w, from_y_d, from_x_u, h_first_core
    )
    part = jnp.concatenate(
        [
            plus(keep_u[0], from_y[0], from_x_u).astype(low),
            plus(keep_d[:4], from_x[:4], from_y_d).astype(low),
        ],
        axis=1,
    )
    late, own = together(late, own)
    grad_emb = jnp.concatenate([late, grad_emb], axis=1)
    grad_emb = grad_emb.reshape(CLIPS, 4, 2, -1).transpose(2, 1, 0, 3)
    keep_e = lax.dynamic_index_in_dim(grad_emb, y, 0, False)
    other_e = swap(lax.dynamic_index_in_dim(grad_emb, 1 - y, 0, False), "seq", 1)
    x_place, core_place = replica // 2, replica % 2
    grad_emb = keep_e + other_e
    from_z_e = [
        swap(lax.dynamic_index_in_dim(grad_emb, z ^ k, 0, False), "seq", 2 * k) for k in range(1, 4)
    ]
    grad_emb = plus(lax.dynamic_index_in_dim(grad_emb, z, 0, False), *from_z_e)
    keep_h = lax.dynamic_index_in_dim(grad_heads_w, core_place, 1, False)
    other_h = swap(lax.dynamic_index_in_dim(grad_heads_w, 1 - core_place, 1, False), "batch", 1)
    h_yx_core = swap(after(h_yx, part), "batch", 1)
    from_z = [swap(part[k], "seq", 2 * k) for k in range(1, 4)]
    both_h = plus(keep_h, other_h).astype(low)
    away_h = swap(lax.dynamic_index_in_dim(both_h, 1 - x_place, 0, False), "batch", 2)

    grad_tokens = last_part(place, own, x, grad_middle, own_member, emb,
        (h_first, h_yx, h_first_core, h_yx_core),
    )
    grad_emb = lax.all_gather(grad_emb, "batch", axis=0, tiled=True)
    final_a = jnp.dot(silu_part.astype(wide).T, grad_emb, precision=highest)
    grad_tokens, final_a, away_h, *from_z = together(grad_tokens, final_a, away_h, *from_z)
    final_heads = plus(lax.dynamic_index_in_dim(both_h, x_place, 0, False), away_h)
    total = plus(part[0], *from_z)
    final_u = jnp.concatenate([total[:256], total[256:512]], axis=1)
    final_d, final_o = total[512:1024], total[1024:]
    width = w_query.shape[1]
    return (
        result[None],
        grad_tokens[None],
        final_heads[:, :width],
        final_heads[:, width:2 * width],
        final_heads[:, 2 * width:],
        final_o,
        final_a,
        final_u,
        final_d,
    )


def solution(mesh):
    fits = mesh.shape["seq"] == SEQ and mesh.shape["batch"] == REPLICAS
    chosen = body_fast if fits else body
    return jax.shard_map(
        chosen,
        mesh=mesh,
        in_specs=(
            P("batch", "seq", None),
            P("batch", "seq"),
            P("batch", "seq"),
            P("batch", "seq"),
            P("batch", "seq"),
            P("batch", "seq"),
            P("batch", "seq"),
            P("batch", "seq"),
            P("batch", "seq"),
            P("batch", "seq"),
            P("batch", None),
            P("batch", "seq", None),
        ),
        out_specs=(
            P("batch", "seq", None),
            P("batch", "seq", None),
            P("batch", "seq"),
            P("batch", "seq"),
            P("batch", "seq"),
            P("batch", "seq"),
            P("batch", "seq"),
            P("batch", "seq"),
            P("batch", "seq"),
        ),
        check_vma=False,
    )
```

```python
from functools import partial
import math

import jax
import jax.numpy as jnp
from jax import lax
from jax.experimental import pallas as pl
from jax.experimental.pallas import tpu as pltpu
from jax.sharding import PartitionSpec as P

D = 1024
HEADS = 16
HEAD = 64
CLIPS = 16


def carried_in(part, axis, combine, identity):
    place = lax.axis_index(axis)
    gathered = lax.all_gather(part, axis)
    state = jnp.zeros_like(part) + jnp.asarray(identity, part.dtype)

    def one(step, state):
        return combine(state, lax.dynamic_index_in_dim(gathered, step, 0, False))

    return lax.fori_loop(0, place, one, state)


def matmul(left, right):
    return jnp.dot(left, right, preferred_element_type=jnp.float32)


def time_embedding(timestep_row):
    half_width = D // 2
    frequency = jnp.exp(-math.log(10000.0) * jnp.arange(half_width, dtype=jnp.float32) / half_width)
    angle = timestep_row.astype(jnp.float32)[:, None] * frequency[None, :]
    return jnp.concatenate([jnp.sin(angle), jnp.cos(angle)], axis=1)


def rotate_pairs(vectors, position, direction):
    half_size = vectors.shape[-1] // 2
    frequency = jnp.exp(-math.log(10000.0) * jnp.arange(half_size, dtype=jnp.float32) / half_size)
    angle = position[:, None] * frequency[None, :]
    cosine = jnp.cos(angle)[:, None, :]
    sine = jnp.sin(angle)[:, None, :] * direction
    first_half = vectors[..., :half_size]
    second_half = vectors[..., half_size:]
    return jnp.concatenate(
        [first_half * cosine - second_half * sine, second_half * cosine + first_half * sine],
        axis=-1,
    )


def normalize(inputs):
    centered = inputs - jnp.mean(inputs, axis=-1, keepdims=True)
    inverse = lax.rsqrt(jnp.mean(centered * centered, axis=-1, keepdims=True) + 1e-06)
    return (centered * inverse, inverse)


def norm_backward(grad_normed, normed, inverse):
    mean_grad = jnp.mean(grad_normed, axis=-1, keepdims=True)
    mean_mixed = jnp.mean(grad_normed * normed, axis=-1, keepdims=True)
    return inverse * (grad_normed - mean_grad - normed * mean_mixed)


def add_counts(earlier, later):
    return earlier + later


def block_rows_for(row_count):
    chosen = 1
    for candidate in range(1, 513):
        if row_count % candidate == 0:
            chosen = candidate
    return chosen


def stack_blocks(shard_piece):
    row_count = shard_piece[0].shape[0]
    block_rows = block_rows_for(row_count)
    block_count = row_count // block_rows
    return (
        shard_piece[0].reshape(block_count, block_rows, HEADS, HEAD),
        shard_piece[1].reshape(block_count, block_rows, HEADS, HEAD),
        shard_piece[2].reshape(block_count, block_rows),
    )


def forward_block(carried, key_block, queries, query_codes):
    running_max, running_sum, accumulated = carried
    key_rows, values, key_codes = key_block
    scores = (
        jnp.einsum("qhe,khe->hqk", queries, key_rows, preferred_element_type=jnp.float32) * 0.125
    )
    allowed = (query_codes[:, None] == key_codes.astype(jnp.float32)[None, :])[None]
    masked = jnp.where(allowed, scores, -1e30)
    new_max = jnp.maximum(running_max, jnp.max(masked, axis=2))
    rescale = jnp.exp(running_max - new_max)
    weights = jnp.where(allowed, jnp.exp(masked - new_max[:, :, None]), 0.0)
    running_sum = running_sum * rescale + jnp.sum(weights, axis=2)
    product = jnp.einsum(
        "hqk,khe->qhe", weights, values.astype(jnp.float32), precision=lax.Precision.HIGHEST
    )
    accumulated = accumulated * rescale.T[:, :, None] + product
    return (new_max, running_sum, accumulated)


def block_grads(key_block, queries, query_codes, grad_attn, log_total, delta_rows):
    key_rows, values, key_codes = key_block
    scores = (
        jnp.einsum("qhe,khe->hqk", queries, key_rows, preferred_element_type=jnp.float32) * 0.125
    )
    allowed = (query_codes[:, None] == key_codes.astype(jnp.float32)[None, :])[None]
    probabilities = jnp.exp(jnp.where(allowed, scores, -1e30) - log_total[:, :, None])
    grad_probs = jnp.einsum("qhe,khe->hqk", grad_attn, values, preferred_element_type=jnp.float32)
    grad_scores = (probabilities * (grad_probs - delta_rows[:, :, None])).astype(jnp.bfloat16)
    return (probabilities, grad_scores)


def body(
    tokens,
    w_query,
    w_key,
    w_value,
    w_out,
    w_ada,
    w_up,
    w_down,
    segments,
    validity,
    timesteps,
    cotangent,
):
    inputs = tokens[0].astype(jnp.float32)
    segment = segments[0]
    valid_row = validity[0]
    timestep_row = timesteps[0]
    grad_output = cotangent[0].astype(jnp.float32)
    frame_count = inputs.shape[0]
    highest = lax.Precision.HIGHEST
    cols_q, cols_k, cols_v, cols_o, cols_a, cols_u, cols_d = (
        lax.all_gather(w_query.astype(jnp.bfloat16), "seq", axis=1, tiled=True),
        lax.all_gather(w_key.astype(jnp.bfloat16), "seq", axis=1, tiled=True),
        lax.all_gather(w_value.astype(jnp.bfloat16), "seq", axis=1, tiled=True),
        lax.all_gather(w_out.astype(jnp.bfloat16), "seq", axis=1, tiled=True),
        lax.all_gather(w_ada.astype(jnp.bfloat16), "seq", axis=1, tiled=True),
        lax.all_gather(w_up.astype(jnp.bfloat16), "seq", axis=1, tiled=True),
        lax.all_gather(w_down.astype(jnp.bfloat16), "seq", axis=1, tiled=True),
    )
    full_q, full_k, full_v, full_o, full_a, full_u, full_d = (
        lax.all_gather(cols_q, "batch", axis=0, tiled=True),
        lax.all_gather(cols_k, "batch", axis=0, tiled=True),
        lax.all_gather(cols_v, "batch", axis=0, tiled=True),
        lax.all_gather(cols_o, "batch", axis=0, tiled=True),
        lax.all_gather(cols_a, "batch", axis=0, tiled=True),
        lax.all_gather(cols_u, "batch", axis=0, tiled=True),
        lax.all_gather(cols_d, "batch", axis=0, tiled=True),
    )
    silu_time = jax.nn.silu(time_embedding(timestep_row)).astype(jnp.bfloat16)
    emb_rows = matmul(silu_time, full_a)
    member = segment[:, None] == jnp.arange(CLIPS, dtype=jnp.int32)[None, :]
    one_hot = member.astype(jnp.float32)
    counted = member.astype(jnp.int32)
    modulation = jnp.dot(one_hot, emb_rows, precision=highest)
    shift_attn, scale_attn, gate_attn, shift_ffn, scale_ffn, gate_ffn = jnp.split(
        modulation, 6, axis=1
    )
    offsets = carried_in(
        jnp.sum(counted, axis=0), "seq", add_counts, jnp.zeros((CLIPS,), jnp.int32)
    )
    before = jnp.cumsum(counted, axis=0) - counted + offsets[None, :]
    position = jnp.sum(before * counted, axis=1).astype(jnp.float32)
    normed, inverse = normalize(inputs)
    attn_input = (normed * (1.0 + scale_attn) + shift_attn).astype(jnp.bfloat16)
    queries = rotate_pairs(
        matmul(attn_input, full_q).reshape(frame_count, HEADS, HEAD), position, 1.0
    ).astype(jnp.bfloat16)
    key_flat = (
        rotate_pairs(matmul(attn_input, full_k).reshape(frame_count, HEADS, HEAD), position, 1.0)
        .astype(jnp.bfloat16)
        .reshape(frame_count, D)
    )
    value_flat = matmul(attn_input, full_v).astype(jnp.bfloat16)
    key_codes = jnp.where(valid_row == 1, segment, -1).astype(jnp.bfloat16)
    query_codes = segment.astype(jnp.float32)
    start_state = (
        jnp.full((HEADS, frame_count), -1e30, jnp.float32),
        jnp.zeros((HEADS, frame_count), jnp.float32),
        jnp.zeros((frame_count, HEADS, HEAD), jnp.float32),
    )

    def step(state, key_block):
        return (forward_block(state, key_block, queries, query_codes), None)

    running_max, running_sum, accumulated = lax.scan(
        step,
        start_state,
        stack_blocks(
            (
                lax.all_gather(key_flat, "seq", axis=0, tiled=True),
                lax.all_gather(value_flat, "seq", axis=0, tiled=True),
                lax.all_gather(key_codes, "seq", axis=0, tiled=True),
            )
        ),
    )[0]
    attended = accumulated / running_sum.T[:, :, None]
    log_total = running_max + jnp.log(running_sum)
    attended_low = attended.reshape(frame_count, D).astype(jnp.bfloat16)
    attn_branch = matmul(attended_low, full_o)
    middle = inputs + gate_attn * attn_branch
    normed_mid, inverse_mid = normalize(middle)
    ffn_input = (normed_mid * (1.0 + scale_ffn) + shift_ffn).astype(jnp.bfloat16)
    hidden = matmul(ffn_input, full_u)
    activated, gelu_pull = jax.vjp(partial(jax.nn.gelu, approximate=True), hidden)
    activated_low = activated.astype(jnp.bfloat16)
    ffn_branch = matmul(activated_low, full_d)
    result = middle + gate_ffn * ffn_branch
    back_q, back_k, back_v, back_o, back_u, back_d = (
        full_q,
        full_k,
        full_v,
        full_o,
        full_u,
        full_d,
    )
    grad_gate_ffn = grad_output * ffn_branch
    g_ffn = (grad_output * gate_ffn).astype(jnp.bfloat16)
    grad_down_local = matmul(activated_low.T, g_ffn)
    grad_activated = matmul(g_ffn, back_d.T)
    g_hidden = gelu_pull(grad_activated)[0].astype(jnp.bfloat16)
    grad_up_local = matmul(ffn_input.T, g_hidden)
    grad_ffn_input = matmul(g_hidden, back_u.T)
    grad_middle = grad_output + norm_backward(
        grad_ffn_input * (1.0 + scale_ffn), normed_mid, inverse_mid
    )
    grad_scale_ffn = grad_ffn_input * normed_mid
    grad_gate_attn = grad_middle * attn_branch
    g_attn = (grad_middle * gate_attn).astype(jnp.bfloat16)
    grad_out_local = matmul(attended_low.T, g_attn)
    grad_attn = matmul(g_attn, back_o.T).astype(jnp.bfloat16).reshape(frame_count, HEADS, HEAD)
    delta_rows = jnp.einsum("qhe,qhe->hq", grad_attn.astype(jnp.float32), attended)
    zero_query = jnp.zeros((frame_count, HEADS, HEAD), jnp.float32)
    gathered = (
        lax.all_gather(key_flat, "seq", axis=0, tiled=True),
        lax.all_gather(value_flat, "seq", axis=0, tiled=True),
        lax.all_gather(key_codes, "seq", axis=0, tiled=True),
    )
    pack_rows = gathered[0].shape[0]
    grad_attn_wide = grad_attn.astype(jnp.float32)

    def joint_step(total_grad, key_block):
        probabilities, grad_scores = block_grads(
            key_block, queries, query_codes, grad_attn, log_total, delta_rows
        )
        total_grad = total_grad + 0.125 * jnp.einsum(
            "hqk,khe->qhe", grad_scores, key_block[0], preferred_element_type=jnp.float32
        )
        grad_keys = 0.125 * jnp.einsum(
            "hqk,qhe->khe", grad_scores, queries, preferred_element_type=jnp.float32
        )
        grad_values = jnp.einsum("hqk,qhe->khe", probabilities, grad_attn_wide, precision=highest)
        return (total_grad, (grad_keys, grad_values))

    grad_queries_rot, both_grads = lax.scan(joint_step, zero_query, stack_blocks(gathered))
    key_value_terms = jnp.concatenate(
        [both_grads[0].reshape(pack_rows, D), both_grads[1].reshape(pack_rows, D)], axis=1
    )
    key_value_grad = lax.psum_scatter(key_value_terms, "seq", scatter_dimension=0, tiled=True)
    g_query = (
        rotate_pairs(grad_queries_rot, position, -1.0).reshape(frame_count, D).astype(jnp.bfloat16)
    )
    g_key = (
        rotate_pairs(key_value_grad[:, :D].reshape(frame_count, HEADS, HEAD), position, -1.0)
        .reshape(frame_count, D)
        .astype(jnp.bfloat16)
    )
    g_value = key_value_grad[:, D:].astype(jnp.bfloat16)
    grad_query_local = matmul(attn_input.T, g_query)
    grad_key_local = matmul(attn_input.T, g_key)
    grad_value_local = matmul(attn_input.T, g_value)
    grad_attn_input = (
        matmul(g_query, back_q.T) + matmul(g_key, back_k.T) + matmul(g_value, back_v.T)
    )
    grad_inputs = grad_middle + norm_backward(grad_attn_input * (1.0 + scale_attn), normed, inverse)
    grad_modulation = jnp.concatenate(
        [
            grad_attn_input,
            grad_attn_input * normed,
            grad_gate_attn,
            grad_ffn_input,
            grad_scale_ffn,
            grad_gate_ffn,
        ],
        axis=1,
    )
    grad_emb = jnp.dot(one_hot.T, grad_modulation, precision=highest)
    grad_ada_local = jnp.dot(silu_time.astype(jnp.float32).T, grad_emb, precision=highest)
    part_q, part_k, part_v, part_o, part_a, part_u, part_d = (
        lax.psum_scatter(grad_query_local, "seq", scatter_dimension=1, tiled=True),
        lax.psum_scatter(grad_key_local, "seq", scatter_dimension=1, tiled=True),
        lax.psum_scatter(grad_value_local, "seq", scatter_dimension=1, tiled=True),
        lax.psum_scatter(grad_out_local, "seq", scatter_dimension=1, tiled=True),
        lax.psum_scatter(grad_ada_local, "seq", scatter_dimension=1, tiled=True),
        lax.psum_scatter(grad_up_local, "seq", scatter_dimension=1, tiled=True),
        lax.psum_scatter(grad_down_local, "seq", scatter_dimension=1, tiled=True),
    )
    final_q, final_k, final_v, final_o, final_a, final_u, final_d = (
        lax.psum_scatter(
            part_q.astype(jnp.bfloat16), "batch", scatter_dimension=0, tiled=True
        ).astype(jnp.float32),
        lax.psum_scatter(
            part_k.astype(jnp.bfloat16), "batch", scatter_dimension=0, tiled=True
        ).astype(jnp.float32),
        lax.psum_scatter(
            part_v.astype(jnp.bfloat16), "batch", scatter_dimension=0, tiled=True
        ).astype(jnp.float32),
        lax.psum_scatter(
            part_o.astype(jnp.bfloat16), "batch", scatter_dimension=0, tiled=True
        ).astype(jnp.float32),
        lax.psum_scatter(
            part_a.astype(jnp.bfloat16), "batch", scatter_dimension=0, tiled=True
        ).astype(jnp.float32),
        lax.psum_scatter(
            part_u.astype(jnp.bfloat16), "batch", scatter_dimension=0, tiled=True
        ).astype(jnp.float32),
        lax.psum_scatter(
            part_d.astype(jnp.bfloat16), "batch", scatter_dimension=0, tiled=True
        ).astype(jnp.float32),
    )
    return (
        result.astype(jnp.bfloat16)[None],
        grad_inputs.astype(jnp.bfloat16)[None],
        final_q,
        final_k,
        final_v,
        final_o,
        final_a,
        final_u,
        final_d,
    )


TWO = 2 * HEAD
ROWS = 256
BIG = 1e30
SEQ = 8
REPLICAS = 4
VMEM_MIB = 60
BLOCK = 256


def swap(part, axis, distance):
    size = SEQ if axis == "seq" else REPLICAS
    return lax.ppermute(part, axis, [(i, i ^ distance) for i in range(size)])


def exchange(blocks):
    return lax.all_to_all(blocks, "seq", 0, 0, tiled=True)


def turn(vectors, cosine, sine):
    lane = lax.broadcasted_iota(jnp.int32, vectors.shape, 1)
    first = (lane % HEAD) < HEAD // 2
    partner = jnp.where(
        first,
        pltpu.roll(vectors, TWO - HEAD // 2, 1),
        pltpu.roll(vectors, HEAD // 2, 1),
    )
    return vectors * cosine + partner * jnp.where(first, -sine, sine)


def of_head(vectors, head):
    lane = lax.broadcasted_iota(jnp.int32, vectors.shape, 1)
    return jnp.where(lane // HEAD == head, vectors, jnp.zeros_like(vectors))


def dot_t(left, right):
    return lax.dot_general(
        left, right, (((1,), (1,)), ((), ())), preferred_element_type=jnp.float32
    )


def project_kernel(place_ref, a_ref, b_ref, c_ref, d_ref, member_ref, bar_ref, cos_ref, sin_ref,
                   emb_ref, w_ref, *refs):
    x_ref, input_ref, q_ref, k_ref, kt_ref, v_ref, vt_ref, chunk_ref = refs[-8:]
    for step, ref in enumerate((a_ref, b_ref, c_ref, d_ref)):

        @pl.when(pl.program_id(0) == step)
        def _():
            chunk_ref[...] = ref[...]

    chunk = chunk_ref[...]
    x_ref[...] = chunk
    normed, _ = standardize(chunk.astype(jnp.float32))
    modulation = matmul(member_ref[...], emb_ref[...])
    low = (normed * (1.0 + modulation[:, D:]) + modulation[:, :D]).astype(jnp.bfloat16)
    input_ref[...] = low
    weight = jnp.concatenate([w_ref[b ^ place_ref[1]] for b in range(REPLICAS)], axis=0)
    product = matmul(low, weight)
    cosine, sine = cos_ref[...], sin_ref[...]
    keys = turn(product[:, TWO:2 * TWO], cosine, sine)
    values = product[:, 2 * TWO:]
    q_ref[...] = turn(product[:, :TWO], cosine, sine).astype(jnp.bfloat16)
    k_ref[:, :TWO] = keys.astype(jnp.bfloat16)
    k_ref[:, TWO:] = bar_ref[...]
    kt_ref[...] = keys.T.astype(jnp.bfloat16)
    v_ref[...] = values.astype(jnp.bfloat16)
    vt_ref[...] = values.T.astype(jnp.bfloat16)


def rows_spec(width):
    return pl.BlockSpec((ROWS, width), lambda i: (i, 0))


def cols_spec(height):
    return pl.BlockSpec((height, ROWS), lambda i: (0, i))


def whole_spec(height, width):
    return pl.BlockSpec((height, width), lambda i: (0, 0))


def params(mib):
    return pltpu.CompilerParams(
        dimension_semantics=("arbitrary",), vmem_limit_bytes=mib * 1024 * 1024
    )


def cost(micros):
    return pl.CostEstimate(
        flops=int(micros * 1e9), bytes_accessed=int(micros * 3e6), transcendentals=0
    )


def project(place, odd, chunks, member, bar, cosine, sine, emb, weights, earlier):
    frames = member.shape[0]
    low = jnp.bfloat16

    def rows(width):
        return pl.BlockSpec((ROWS, width), lambda i, p: ((2 * i + odd) ^ p[0], 0))

    def cols(height):
        return pl.BlockSpec((height, ROWS), lambda i, p: (0, (2 * i + odd) ^ p[0]))

    def whole(height, width):
        return pl.BlockSpec((height, width), lambda i, p: (0, 0))

    inputs = [place, *chunks, member, bar, cosine, sine, emb, weights, *earlier]
    first = len(inputs) - len(earlier)
    return pl.pallas_call(
        project_kernel,
        grid_spec=pltpu.PrefetchScalarGridSpec(
            num_scalar_prefetch=1,
            grid=(4,),
            in_specs=[whole(ROWS, D)] * 4 + [rows(TWO)] * 4
            + [whole(TWO, 2 * D),
               pl.BlockSpec((REPLICAS, ROWS, 3 * TWO), lambda i, p: (0, 0, 0))]
            + [pl.BlockSpec(memory_space=pl.ANY)] * len(earlier),
            out_specs=[rows(D), rows(D), rows(TWO), rows(2 * TWO), cols(TWO), rows(TWO),
                       cols(TWO)],
            scratch_shapes=[pltpu.VMEM((ROWS, D), low)],
        ),
        out_shape=[
            jax.ShapeDtypeStruct((frames, D), low),
            jax.ShapeDtypeStruct((frames, D), low),
            jax.ShapeDtypeStruct((frames, TWO), low),
            jax.ShapeDtypeStruct((frames, 2 * TWO), low),
            jax.ShapeDtypeStruct((TWO, frames), low),
            jax.ShapeDtypeStruct((frames, TWO), low),
            jax.ShapeDtypeStruct((TWO, frames), low),
        ],
        input_output_aliases={first + i: i for i in range(len(earlier))},
        compiler_params=params(30),
        cost_estimate=cost(2),
        name="project",
    )(*inputs)


def attend_kernel(q_ref, member_ref, k_ref, vt_ref, att_ref, low_ref, log_ref, *score_refs):
    frames = k_ref.shape[0]
    step = min(frames, 1024)
    queries = q_ref[...] * 0.125
    member = member_ref[...]
    bests, halves = [], []
    for head, score_ref in enumerate(score_refs):
        wide = jnp.concatenate([of_head(queries, head), member], axis=1)
        largest = jnp.full((1, BLOCK), -BIG, jnp.float32)
        for start in range(0, frames, step):
            scores = dot_t(k_ref[start:start + step, :], wide)
            score_ref[start:start + step, :] = scores
            largest = jnp.maximum(largest, jnp.max(scores, axis=0, keepdims=True))
        bests.append(largest)
    for head, score_ref in enumerate(score_refs):
        total = jnp.zeros((1, BLOCK), jnp.float32)
        out = jnp.zeros((TWO, BLOCK), jnp.float32)
        for start in range(0, frames, step):
            weights = jnp.exp(score_ref[start:start + step, :] - bests[head])
            total = total + jnp.sum(weights, axis=0, keepdims=True)
            out = out + matmul(vt_ref[:, start:start + step], weights.astype(jnp.bfloat16))
        halves.append(out[head * HEAD:(head + 1) * HEAD, :] / total)
        log_ref[head:head + 1, :] = bests[head] + jnp.log(total)
    attended = jnp.concatenate(halves, axis=0).T
    att_ref[...] = attended
    low_ref[...] = attended.astype(jnp.bfloat16)


def block_spec(width):
    return pl.BlockSpec((BLOCK, width), lambda i: (i, 0))


def attend(q, member, k, vt):
    frames = q.shape[0]
    return pl.pallas_call(
        attend_kernel,
        grid=(frames // BLOCK,),
        in_specs=[block_spec(TWO), block_spec(TWO), whole_spec(frames, 2 * TWO),
                  whole_spec(TWO, frames)],
        out_specs=[block_spec(TWO), block_spec(TWO), pl.BlockSpec((8, BLOCK), lambda i: (0, i))],
        out_shape=[
            jax.ShapeDtypeStruct((frames, TWO), jnp.float32),
            jax.ShapeDtypeStruct((frames, TWO), jnp.bfloat16),
            jax.ShapeDtypeStruct((8, frames), jnp.float32),
        ],
        scratch_shapes=[pltpu.VMEM((frames, BLOCK), jnp.float32)] * 2,
        compiler_params=params(26),
        cost_estimate=cost(18),
        name="attend",
    )(q, member, k, vt)


def attend_back_kernel(q_ref, member_ref, grad_ref, att_ref, log_ref, cos_ref, sin_ref, cos_all_ref,
                       sin_all_ref, k_ref, kt_ref, v_ref, g_ref, dk_ref, dv_ref):
    block = pl.program_id(0)
    frames = k_ref.shape[0]
    step = min(frames, 512)

    @pl.when(block == 0)
    def _():
        dk_ref[...] = jnp.zeros_like(dk_ref)
        dv_ref[...] = jnp.zeros_like(dv_ref)

    queries = q_ref[...] * 0.125
    member = member_ref[...]
    grad = grad_ref[...]
    mixed = (grad.astype(jnp.float32) * att_ref[...]).T
    halves = []
    wides, grads, deltas = [], [], []
    for head in range(2):
        wides.append(jnp.concatenate([of_head(queries, head), member], axis=1))
        grads.append(of_head(grad, head))
        deltas.append(jnp.sum(mixed[head * HEAD:(head + 1) * HEAD, :], axis=0, keepdims=True))
    totals = [jnp.zeros((TWO, ROWS), jnp.float32) for _ in range(2)]
    for start in range(0, frames, step):
        part = slice(start, start + step)
        dk = dk_ref[part, :]
        dv = dv_ref[part, :]
        for head in range(2):
            scores = dot_t(k_ref[part, :], wides[head])
            weights = jnp.exp(scores - log_ref[head:head + 1, :])
            grad_weights = dot_t(v_ref[part, :], grads[head])
            grad_scores = (weights * (grad_weights - deltas[head])).astype(jnp.bfloat16)
            dv = dv + matmul(weights.astype(jnp.bfloat16), grads[head])
            dk = dk + matmul(grad_scores, wides[head][:, :TWO])
            totals[head] = totals[head] + matmul(kt_ref[:, part], grad_scores)
        dk_ref[part, :] = dk
        dv_ref[part, :] = dv
    dq = jnp.concatenate([totals[0][:HEAD, :], totals[1][HEAD:, :]], axis=0).T * 0.125
    here = pl.ds(pl.multiple_of(block * ROWS, ROWS), ROWS)
    g_ref[here, :TWO] = turn(dq, cos_ref[...], -sin_ref[...]).astype(jnp.bfloat16)

    @pl.when(block == pl.num_programs(0) - 1)
    def _():
        turned = turn(dk_ref[...], cos_all_ref[...], -sin_all_ref[...])
        g_ref[:, TWO:2 * TWO] = turned.astype(jnp.bfloat16)
        g_ref[:, 2 * TWO:] = dv_ref[...].astype(jnp.bfloat16)


def attend_back(q, member, grad, att, log_total, cosine, sine, k, kt, v):
    frames = q.shape[0]
    return pl.pallas_call(
        attend_back_kernel,
        grid=(frames // ROWS,),
        in_specs=[rows_spec(TWO), rows_spec(TWO), rows_spec(TWO), rows_spec(TWO), cols_spec(8),
                  rows_spec(TWO), rows_spec(TWO), whole_spec(frames, TWO), whole_spec(frames, TWO),
                  whole_spec(frames, 2 * TWO), whole_spec(TWO, frames), whole_spec(frames, TWO)],
        out_specs=whole_spec(frames, 3 * TWO),
        out_shape=jax.ShapeDtypeStruct((frames, 3 * TWO), jnp.bfloat16),
        scratch_shapes=[pltpu.VMEM((frames, TWO), jnp.float32),
                        pltpu.VMEM((frames, TWO), jnp.float32)],
        compiler_params=params(VMEM_MIB),
        cost_estimate=cost(27),
        name="attend_back",
    )(q, member, grad, att, log_total, cosine, sine, cosine, sine, k, kt, v)


def three_terms(values):
    high = lax.reduce_precision(values, 8, 7)
    middle = lax.reduce_precision(values - high, 8, 7)
    return [high, middle, values - high - middle]


def standardize(rows):
    centered = rows - jnp.mean(rows, axis=1, keepdims=True)
    inverse = lax.rsqrt(jnp.mean(centered * centered, axis=1, keepdims=True) + 1e-06)
    return centered * inverse, inverse


def sum_of_clips(clip_ref, values):
    ids = lax.broadcasted_iota(jnp.int32, (CLIPS, clip_ref.shape[1]), 0)
    chosen = jnp.where(clip_ref[...] == ids, 1.0, 0.0).astype(jnp.bfloat16)
    high = values.astype(jnp.bfloat16)
    rest = values - high.astype(jnp.float32)
    middle = rest.astype(jnp.bfloat16)
    last = (rest - middle.astype(jnp.float32)).astype(jnp.bfloat16)
    return matmul(chosen, high) + matmul(chosen, middle) + matmul(chosen, last)


def beside(ref, tiles, rows):
    return jnp.concatenate([ref[tile, rows, :] for tile in tiles], axis=1)


def tile_index(away, apart):
    return 16 * (away % 2) + 8 * (away // 2) + 4 * (apart % 2) + apart // 2


def middle_kernel(mine_ref, x_ref, cot_ref, member_ref, clip_ref, emb_ref, *refs):
    *tile_refs, result_ref, grad_middle_ref, grad_att_ref, grad_emb_ref, left_ref, right_ref = refs[:-9]
    out_ref, up_ref, down_ref, sems, branch_ref, low_ref, act_ref, slope_ref, wide_ref = refs[-9:]
    low = jnp.bfloat16
    act_t_ref, ffn_t_ref = left_ref.at[:2 * D], left_ref.at[2 * D:3 * D]
    mine_t_ref = left_ref.at[3 * D:]
    g_ffn_ref, g_attn_ref = right_ref.at[:, :D], right_ref.at[:, 3 * D:]
    g_hidden_ref = right_ref.at[:, D:3 * D]
    pieces = ((out_ref, 0, 256), (up_ref, 256, 512), (down_ref, 768, 512))
    for i, (ref, start, size) in enumerate(pieces):
        first = 0
        for tile_ref in tile_refs:
            count = tile_ref.shape[0]
            pltpu.make_async_copy(
                tile_ref.at[:, pl.ds(start, size), :], ref.at[pl.ds(first, count)], sems.at[i]
            ).start()
            first += count
    copies = [
        pltpu.make_async_copy(ref, ref, sems.at[i]) for i, (ref, _, _) in enumerate(pieces)
    ]

    def tile(b, s):
        return SEQ * b + s

    member = member_ref[...]

    def modulation(index):
        return matmul(member, emb_ref[:, index * D:(index + 1) * D])

    def cols(n, width=256):
        return pl.ds(pl.multiple_of(n * width, width), width)

    every = slice(None)
    mine = jnp.concatenate([mine_ref[j] for j in range(SEQ)], axis=1)
    low_ref[...] = mine
    mine_t_ref[...] = mine.T
    gate_attn = modulation(2)
    copies[0].wait()

    @pl.loop(0, 4)
    def _(n):
        total = jnp.zeros((ROWS, 256), jnp.float32)
        for b in range(REPLICAS):
            weight = beside(out_ref, [tile(b, 2 * n), tile(b, 2 * n + 1)], every)
            total = total + matmul(low_ref[:, 256 * b:256 * b + 256], weight)
        branch_ref[:, cols(n)] = total

    branch = branch_ref[...]
    middle = x_ref[...].astype(jnp.float32) + gate_attn * branch
    normed, inverse = standardize(middle)
    scale_ffn = modulation(4)
    ffn_input = normed * (1.0 + scale_ffn) + modulation(3)
    low_ref[...] = ffn_input.astype(low)
    ffn_t_ref[...] = ffn_input.T.astype(low)
    gate_ffn = modulation(5)
    cot = cot_ref[...].astype(jnp.float32)
    g_ffn_ref[...] = (cot * gate_ffn).astype(low)
    copies[1].wait()

    @pl.loop(0, 8)
    def _(n):
        hidden = jnp.zeros((ROWS, 256), jnp.float32)
        for b in range(REPLICAS):
            index = tile(b, n)
            weight = jnp.concatenate([up_ref[index, :256, :], up_ref[index, 256:, :]], axis=1)
            hidden = hidden + matmul(low_ref[:, 256 * b:256 * b + 256], weight)
        root = math.sqrt(2.0 / math.pi)
        squared = hidden * hidden
        bent = jnp.tanh(root * (hidden + 0.044715 * (squared * hidden)))
        half = 0.5 * (1.0 + bent)
        activated = hidden * half
        slope = half + 0.5 * hidden * (1.0 - bent * bent) * (
            root * (1.0 + (3.0 * 0.044715) * squared)
        )
        act_ref[:, cols(n)] = activated.astype(low)
        act_t_ref[cols(n), :] = activated.T.astype(low)
        slope_ref[:, cols(n)] = slope

    copies[2].wait()

    @pl.loop(0, 4)
    def _(n):
        total = jnp.zeros((ROWS, 256), jnp.float32)
        for b in range(REPLICAS):
            weight = beside(down_ref, [tile(b, 2 * n), tile(b, 2 * n + 1)], every)
            total = total + matmul(act_ref[:, 512 * b:512 * b + 512], weight)
        wide_ref[:, cols(n)] = total

    ffn_branch = wide_ref[...]
    result_ref[...] = (middle + gate_ffn * ffn_branch).astype(low)
    grad_emb_ref[:, 3 * D:] = sum_of_clips(clip_ref, cot * ffn_branch)

    @pl.loop(0, REPLICAS)
    def _(b):
        weight = beside(down_ref, [tile(b, s) for s in range(SEQ)], every)
        grad = dot_t(g_ffn_ref[...], weight)
        here = cols(b, 512)
        g_hidden_ref[:, here] = (grad * slope_ref[:, here]).astype(low)

    @pl.loop(0, REPLICAS)
    def _(b):
        weight = jnp.concatenate(
            [up_ref[tile(b, s), 256 * k:256 * k + 256, :] for s in range(SEQ) for k in range(2)],
            axis=1,
        )
        wide_ref[:, cols(b)] = dot_t(g_hidden_ref[...], weight)

    grad_ffn_input = wide_ref[...]
    grad_emb_ref[:, D:2 * D] = sum_of_clips(clip_ref, grad_ffn_input)
    grad_emb_ref[:, 2 * D:3 * D] = sum_of_clips(clip_ref, grad_ffn_input * normed)
    spread = grad_ffn_input * (1.0 + scale_ffn)
    grad_middle = cot + inverse * (
        spread
        - jnp.mean(spread, axis=1, keepdims=True)
        - normed * jnp.mean(spread * normed, axis=1, keepdims=True)
    )
    grad_middle_ref[...] = grad_middle
    grad_emb_ref[:, :D] = sum_of_clips(clip_ref, grad_middle * branch)
    g_attn_ref[...] = (grad_middle * gate_attn).astype(low)

    @pl.loop(0, REPLICAS)
    def _(b):
        weight = beside(out_ref, [tile(b, s) for s in range(SEQ)], every)
        grad = dot_t(g_attn_ref[...], weight).astype(low)
        grad_att_ref[2 * b] = grad[:, :TWO]
        grad_att_ref[2 * b + 1] = grad[:, TWO:]


def middle_part(mine, x, cot, member, clip_row, emb, tiles):
    low = jnp.bfloat16
    shapes = [
        ((ROWS, D), low), ((ROWS, D), jnp.float32), ((SEQ, ROWS, TWO), low),
        ((CLIPS, 4 * D), jnp.float32),
        ((4 * D, ROWS), low), ((ROWS, 4 * D), low),
    ]
    vmem = pl.BlockSpec(memory_space=pltpu.VMEM)
    return pl.pallas_call(
        middle_kernel,
        in_specs=[vmem] * 6 + [pl.BlockSpec(memory_space=pl.ANY)] * len(tiles),
        out_specs=[vmem] * len(shapes),
        out_shape=[jax.ShapeDtypeStruct(shape, dtype) for shape, dtype in shapes],
        scratch_shapes=[
            pltpu.VMEM((32, 256, 128), low),
            pltpu.VMEM((32, 512, 128), low),
            pltpu.VMEM((32, 512, 128), low),
            pltpu.SemaphoreType.DMA((3,)),
            pltpu.VMEM((ROWS, D), jnp.float32),
            pltpu.VMEM((ROWS, D), low),
            pltpu.VMEM((ROWS, 2 * D), low),
            pltpu.VMEM((ROWS, 2 * D), jnp.float32),
            pltpu.VMEM((ROWS, D), jnp.float32),
        ],
        compiler_params=pltpu.CompilerParams(vmem_limit_bytes=VMEM_MIB * 1024 * 1024),
        cost_estimate=cost(20),
        name="middle",
    )(mine, x, cot, member, clip_row, emb, *tiles)


def weight_grads_kernel(place_ref, down_l, up_l, out_l, right_ref, down_o, up_o, out_o, other_ref,
                        away_d_ref, keep_d_ref, away_u_ref, keep_u_ref):
    low = jnp.bfloat16
    z, y = place_ref[2] // 2, place_ref[2] % 2
    lefts = [
        jnp.concatenate([mine[...], other[...]], axis=1)
        for mine, other in ((down_l, down_o), (up_l, up_o), (out_l, out_o))
    ]

    def product(left, first, block):
        here = pl.ds(pl.multiple_of(first + 256 * block, 256), 256)
        right = jnp.concatenate([right_ref[:, here], other_ref[:, here]], axis=0)
        return matmul(left, right).astype(low)

    def fill(ref):
        @pl.loop(0, 4)
        def _(k):
            block = z ^ k
            for left, first, rows in ((lefts[0], 0, slice(0, 512)), (lefts[2], 3 * D, slice(512, 768))):
                grad = product(left, first, block)
                ref[4 * y + k, rows, :] = grad[:, :128]
                ref[4 - 4 * y + k, rows, :] = grad[:, 128:]
            for side, up_ref in enumerate((keep_u_ref, away_u_ref)):
                grad = product(lefts[1], D, 2 * block + (y ^ side))
                up_ref[0, k, :256, :] = grad[:, :128]
                up_ref[0, k, 256:, :] = grad[:, 128:]

    @pl.when(pl.program_id(0) == 0)
    def _():
        fill(away_d_ref)

    @pl.when(pl.program_id(0) == 1)
    def _():
        fill(keep_d_ref)


def weight_grads(place, left, right, other_left, other_right):
    low = jnp.bfloat16

    def target(i, p):
        return 2 * jnp.where(i == 0, 1 - p[0], p[0]) + p[1]

    down = pl.BlockSpec((512, ROWS), lambda i, p: (target(i, p), 0))
    up = pl.BlockSpec((256, ROWS), lambda i, p: (8 + target(i, p), 0))
    out = pl.BlockSpec((256, ROWS), lambda i, p: (12 + target(i, p), 0))
    wide = pl.BlockSpec((ROWS, 4 * D), lambda i, p: (0, 0))
    whole = pl.BlockSpec((SEQ, 768, 128), lambda i, p: (0, 0, 0))
    part = pl.BlockSpec((1, 4, 512, 128), lambda i, p: (1 - i, 0, 0, 0))
    return pl.pallas_call(
        weight_grads_kernel,
        grid_spec=pltpu.PrefetchScalarGridSpec(
            num_scalar_prefetch=1,
            grid=(2,),
            in_specs=[down, up, out, wide] * 2,
            out_specs=[whole, whole, part, part],
        ),
        out_shape=[jax.ShapeDtypeStruct((SEQ, 768, 128), low)] * 2
        + [jax.ShapeDtypeStruct((2, 4, 512, 128), low)] * 2,
        compiler_params=params(VMEM_MIB),
        cost_estimate=cost(9),
        name="weight_grads",
    )(place, left, left, left, right, other_left, other_left, other_left, other_right)


def clip_grads_kernel(place_ref, x_ref, clip_ref, g_ref, w_ref, out_ref):
    @pl.when(pl.program_id(0) == 0)
    def _():
        out_ref[...] = jnp.zeros_like(out_ref)

    normed, _ = standardize(x_ref[...].astype(jnp.float32))
    grad = jnp.concatenate(
        [dot_t(g_ref[...], w_ref[b ^ place_ref[1]]) for b in range(REPLICAS)], axis=1
    )
    out_ref[:, :D] += sum_of_clips(clip_ref, grad)
    out_ref[:, D:] += sum_of_clips(clip_ref, grad * normed)


def clip_grads(places, x, clip_row, g_heads, heads_w):
    frames = x.shape[0]
    return pl.pallas_call(
        clip_grads_kernel,
        grid=(frames // ROWS,),
        in_specs=[pl.BlockSpec(memory_space=pltpu.SMEM), rows_spec(D), cols_spec(1),
                  rows_spec(3 * TWO),
                  pl.BlockSpec((REPLICAS, ROWS, 3 * TWO), lambda i: (0, 0, 0))],
        out_specs=whole_spec(CLIPS, 2 * D),
        out_shape=jax.ShapeDtypeStruct((CLIPS, 2 * D), jnp.float32),
        compiler_params=params(VMEM_MIB),
        cost_estimate=cost(9),
        name="clip_grads",
    )(places, x, clip_row, g_heads, heads_w)


def last_kernel(place_ref, own_ref, x_ref, grad_middle_ref, member_ref, emb_ref, *refs):
    *tile_refs, out_ref, wide_ref = refs
    grads = jnp.concatenate([own_ref[place_ref[2] ^ s] for s in range(SEQ)], axis=1)

    def tile(away, apart):
        index = tile_index(away, apart)
        for ref in tile_refs:
            if index < ref.shape[0]:
                return ref[index, ref.shape[1] - 768:, :]
            index -= ref.shape[0]

    for away in range(REPLICAS):
        weight = jnp.concatenate(
            [
                tile(away, s)[256 * k:256 * k + 256, :]
                for s in range(SEQ)
                for k in range(3)
            ],
            axis=1,
        )
        b = (2 * place_ref[0] + place_ref[1]) ^ away
        wide_ref[:, pl.ds(pl.multiple_of(b * 256, 256), 256)] = dot_t(grads, weight)

    normed, inverse = standardize(x_ref[...].astype(jnp.float32))
    spread = wide_ref[...] * (1.0 + matmul(member_ref[...], emb_ref[:, D:2 * D]))
    grad = grad_middle_ref[...] + inverse * (
        spread
        - jnp.mean(spread, axis=1, keepdims=True)
        - normed * jnp.mean(spread * normed, axis=1, keepdims=True)
    )
    out_ref[...] = grad.astype(jnp.bfloat16)


def last_part(place, own, x, grad_middle, member, emb, tiles):
    vmem = pl.BlockSpec(memory_space=pltpu.VMEM)
    return pl.pallas_call(
        last_kernel,
        in_specs=[pl.BlockSpec(memory_space=pltpu.SMEM)] + [vmem] * (5 + len(tiles)),
        out_specs=vmem,
        out_shape=jax.ShapeDtypeStruct((ROWS, D), jnp.bfloat16),
        scratch_shapes=[pltpu.VMEM((ROWS, D), jnp.float32)],
        compiler_params=pltpu.CompilerParams(vmem_limit_bytes=30 * 1024 * 1024),
        cost_estimate=cost(4),
        name="last",
    )(place, own, x, grad_middle, member, emb, *tiles)


def after(value, *others):
    return lax.optimization_barrier((value,) + others)[0]


def together(*values):
    return lax.optimization_barrier(values)


def plus(*terms):
    total = terms[0].astype(jnp.float32)
    for term in terms[1:]:
        total = total + term.astype(jnp.float32)
    return total


def clip_lanes(clip, terms):
    lane = jnp.arange(TWO, dtype=jnp.int32)[None, :]
    return (clip[:, None] == lane % CLIPS) & (lane < terms * CLIPS)


def body_fast(
    tokens, w_query, w_key, w_value, w_out, w_ada, w_up, w_down,
    segments, validity, timesteps, cotangent,
):
    highest = lax.Precision.HIGHEST
    low = jnp.bfloat16
    wide = jnp.float32
    replica = lax.axis_index("batch")
    x = tokens[0]
    frame_count = x.shape[0]
    frames = frame_count * SEQ
    segment = segments[0]

    seat = lax.axis_index("seq").astype(jnp.int32)
    z, y = seat // 2, seat % 2
    place = jnp.stack([replica // 2, replica % 2, seat]).astype(jnp.int32)
    mine_w = jnp.concatenate([w_out, w_up[:, :128], w_up[:, 128:], w_down], axis=0).astype(low)

    z1, z2, y0 = swap(x, "seq", 2), swap(x, "seq", 4), swap(x, "seq", 1)
    times = lax.all_gather(timesteps[0], "batch", axis=0, tiled=True)
    silu_all = jax.nn.silu(time_embedding(times)).astype(low)
    depth = w_ada.shape[0]
    silu_part = lax.dynamic_slice_in_dim(silu_all, replica * depth, depth, 1)
    emb_part = matmul(silu_part, w_ada.astype(low)).reshape(REPLICAS, CLIPS, -1)
    emb_cols = lax.all_to_all(emb_part, "batch", 0, 0, tiled=True)
    emb_cols = jnp.sum(emb_cols, axis=0)
    own_codes = (segment * 2 + (validity[0] == 1)).astype(wide)
    cols = emb_cols.shape[1]
    own_codes = jnp.pad(own_codes, (0, 8 * cols - frame_count)).reshape(8, cols)
    packed = jnp.concatenate([emb_cols, own_codes])
    packed = jnp.broadcast_to(packed[None], (SEQ,) + packed.shape)
    heads_w = jnp.concatenate([w_query, w_key, w_value], axis=1).astype(low)
    heads_w = jnp.stack([heads_w, swap(heads_w, "batch", 1)])
    z1, z2, y0, packed, heads_w, mine_w = together(z1, z2, y0, packed, heads_w, mine_w)
    tiles_w = (lax.all_gather(mine_w, ("batch", "seq"), axis=0),)
    packed = exchange(packed)
    z3 = swap(z2, "seq", 2)
    y1, y2 = swap(z1, "seq", 1), swap(z2, "seq", 1)
    heads_x = swap(heads_w, "batch", 2)
    z3, heads_x = together(z3, heads_x)
    y3 = swap(z3, "seq", 1)
    mine_h = jnp.concatenate([w_query, w_key, w_value], axis=0).astype(low)
    mine_h = after(mine_h, z3)
    h_z1, h_z2 = swap(mine_h, "seq", 2), swap(mine_h, "seq", 4)
    heads_w = jnp.concatenate([heads_w, heads_x])
    emb = packed[:, :CLIPS]
    codes = packed[:, CLIPS:].reshape(SEQ, -1)[:, :frame_count].reshape(frames).astype(jnp.int32)
    clip = codes // 2
    clip_row = clip[None, :]
    tri = jnp.arange(frame_count)[:, None] > jnp.arange(frame_count)[None, :]
    ids = jnp.arange(CLIPS, dtype=jnp.int32)
    one_hot = (clip.reshape(SEQ, frame_count)[:, :, None] == ids).astype(low)
    within = jnp.einsum("ij,njc->nic", tri.astype(low), one_hot, preferred_element_type=wide)
    counts = jnp.sum(one_hot.astype(wide), axis=1)
    offsets = jnp.cumsum(counts, axis=0) - counts
    position = jnp.sum(one_hot.astype(wide) * (within + offsets[:, None, :]), axis=2)
    half = HEAD // 2
    frequency = jnp.exp(-math.log(10000.0) * jnp.arange(half, dtype=wide) / half)
    angle = position.reshape(frames)[:, None] * jnp.tile(frequency, 4)[None, :]
    cosine, sine = jnp.cos(angle), jnp.sin(angle)
    member = clip_lanes(clip, 3).astype(low)
    allowed = clip_lanes(jnp.where(codes % 2 == 1, clip, -1), 1)
    inside = jnp.arange(TWO, dtype=jnp.int32)[None, :] < CLIPS
    bar = jnp.where(inside & ~allowed, -BIG, 0.0).astype(low)
    emb, y1, y2 = together(after(emb, heads_w, member, cosine), y1, y2)
    emb = emb.transpose(1, 0, 2).reshape(CLIPS, -1)
    emb = jnp.concatenate(
        [t.astype(low) for t in three_terms(emb)] + [jnp.zeros((TWO - 3 * CLIPS, 6 * D), low)],
        axis=0,
    )

    tables = (member, bar, cosine, sine, emb, heads_w)
    places = jnp.stack([seat, replica.astype(jnp.int32)])
    earlier = project(places, 0, (x, z1, z2, z3), *tables, ())
    y3, h_z1, h_z2, earlier = together(y3, h_z1, h_z2, earlier)
    h_z3 = swap(h_z2, "seq", 2)
    x_all, attn_input, q, k, kt, v, vt = project(places, 1, (y0, y1, y2, y3), *tables, earlier)
    attended, attended_low, log_total = attend(q, member, k, vt)
    attended_low, h_z3 = together(attended_low, h_z3)
    mine = exchange(attended_low.reshape(SEQ, frame_count, TWO))
    h_z = jnp.stack([mine_h, h_z1, h_z2, h_z3])
    mine, h_z = together(mine, h_z)
    h_y, h_x = swap(h_z, "seq", 1), swap(h_z, "batch", 2)

    own_member = clip_lanes(segment, 3).astype(low)
    result, grad_middle, grad_att, grad_emb, left, right = middle_part(
        mine, x, cotangent[0], own_member, segment[None, :], emb, tiles_w
    )
    left, h_y, h_x = together(left, h_y, h_x)
    other_left, other_right = swap(left, "batch", 1), swap(right, "batch", 1)
    h_first = jnp.concatenate([h_z, h_y, h_x])
    other_left, other_right, h_first = together(other_left, other_right, h_first)
    away_d, keep_d, away_u, keep_u = weight_grads(place, left, right, other_left, other_right)
    grad_heads = exchange(grad_att).reshape(frames, TWO)
    grad_heads, away_d, away_u = together(grad_heads, away_d, away_u)
    from_x = swap(away_d, "batch", 2)
    from_y = swap(away_u, "seq", 1)

    g_heads = attend_back(
        q, member, grad_heads, attended, log_total, cosine, sine, k, kt, v
    )
    own = exchange(g_heads.reshape(SEQ, frame_count, 3 * TWO))
    from_y = after(from_y, g_heads)
    to_x_u = plus(keep_u[1], from_y[1]).astype(low)
    from_x_u = swap(to_x_u, "batch", 2)
    from_x = after(from_x, to_x_u)
    to_y_d = plus(keep_d[4:], from_x[4:]).astype(low)
    from_y_d = swap(to_y_d, "seq", 1)
    h_yx = swap(after(h_y, to_y_d), "batch", 2)
    h_first_core = swap(after(h_first, to_x_u), "batch", 1)
    g_heads = after(g_heads, to_y_d, to_x_u)
    late = clip_grads(places, x_all, clip_row, g_heads, heads_w)
    grad_heads_w = matmul(attn_input.T, g_heads).astype(low).reshape(2, 2, ROWS, 3 * TWO)
    late, grad_heads_w, from_y_d, from_x_u, h_first_core = together(
        late, grad_heads_w, from_y_d, from_x_u, h_first_core
    )
    part = jnp.concatenate(
        [
            plus(keep_u[0], from_y[0], from_x_u).astype(low),
            plus(keep_d[:4], from_x[:4], from_y_d).astype(low),
        ],
        axis=1,
    )
    late, own = together(late, own)
    grad_emb = jnp.concatenate([late, grad_emb], axis=1)
    grad_emb = grad_emb.reshape(CLIPS, 4, 2, -1).transpose(2, 1, 0, 3)
    keep_e = lax.dynamic_index_in_dim(grad_emb, y, 0, False)
    other_e = swap(lax.dynamic_index_in_dim(grad_emb, 1 - y, 0, False), "seq", 1)
    x_place, core_place = replica // 2, replica % 2
    grad_emb = keep_e + other_e
    from_z_e = [
        swap(lax.dynamic_index_in_dim(grad_emb, z ^ k, 0, False), "seq", 2 * k) for k in range(1, 4)
    ]
    grad_emb = plus(lax.dynamic_index_in_dim(grad_emb, z, 0, False), *from_z_e)
    keep_h = lax.dynamic_index_in_dim(grad_heads_w, core_place, 1, False)
    other_h = swap(lax.dynamic_index_in_dim(grad_heads_w, 1 - core_place, 1, False), "batch", 1)
    h_yx_core = swap(after(h_yx, part), "batch", 1)
    from_z = [swap(part[k], "seq", 2 * k) for k in range(1, 4)]
    both_h = plus(keep_h, other_h).astype(low)
    away_h = swap(lax.dynamic_index_in_dim(both_h, 1 - x_place, 0, False), "batch", 2)

    grad_tokens = last_part(place, own, x, grad_middle, own_member, emb,
        (h_first, h_yx, h_first_core, h_yx_core),
    )
    grad_emb = lax.all_gather(grad_emb, "batch", axis=0, tiled=True)
    final_a = jnp.dot(silu_part.astype(wide).T, grad_emb, precision=highest)
    grad_tokens, final_a, away_h, *from_z = together(grad_tokens, final_a, away_h, *from_z)
    final_heads = plus(lax.dynamic_index_in_dim(both_h, x_place, 0, False), away_h)
    total = plus(part[0], *from_z)
    final_u = jnp.concatenate([total[:256], total[256:512]], axis=1)
    final_d, final_o = total[512:1024], total[1024:]
    width = w_query.shape[1]
    return (
        result[None],
        grad_tokens[None],
        final_heads[:, :width],
        final_heads[:, width:2 * width],
        final_heads[:, 2 * width:],
        final_o,
        final_a,
        final_u,
        final_d,
    )


def solution(mesh):
    fits = mesh.shape["seq"] == SEQ and mesh.shape["batch"] == REPLICAS
    chosen = body_fast if fits else body
    return jax.shard_map(
        chosen,
        mesh=mesh,
        in_specs=(
            P("batch", "seq", None),
            P("batch", "seq"),
            P("batch", "seq"),
            P("batch", "seq"),
            P("batch", "seq"),
            P("batch", "seq"),
            P("batch", "seq"),
            P("batch", "seq"),
            P("batch", "seq"),
            P("batch", "seq"),
            P("batch", None),
            P("batch", "seq", None),
        ),
        out_specs=(
            P("batch", "seq", None),
            P("batch", "seq", None),
            P("batch", "seq"),
            P("batch", "seq"),
            P("batch", "seq"),
            P("batch", "seq"),
            P("batch", "seq"),
            P("batch", "seq"),
            P("batch", "seq"),
        ),
        check_vma=False,
    )
```

```python
from functools import partial
import math

import jax
import jax.numpy as jnp
from jax import lax
from jax.experimental import pallas as pl
from jax.experimental.pallas import tpu as pltpu
from jax.sharding import PartitionSpec as P

D = 1024
HEADS = 16
HEAD = 64
CLIPS = 16


def carried_in(part, axis, combine, identity):
    place = lax.axis_index(axis)
    gathered = lax.all_gather(part, axis)
    state = jnp.zeros_like(part) + jnp.asarray(identity, part.dtype)

    def one(step, state):
        return combine(state, lax.dynamic_index_in_dim(gathered, step, 0, False))

    return lax.fori_loop(0, place, one, state)


def matmul(left, right):
    return jnp.dot(left, right, preferred_element_type=jnp.float32)


def time_embedding(timestep_row):
    half_width = D // 2
    frequency = jnp.exp(-math.log(10000.0) * jnp.arange(half_width, dtype=jnp.float32) / half_width)
    angle = timestep_row.astype(jnp.float32)[:, None] * frequency[None, :]
    return jnp.concatenate([jnp.sin(angle), jnp.cos(angle)], axis=1)


def rotate_pairs(vectors, position, direction):
    half_size = vectors.shape[-1] // 2
    frequency = jnp.exp(-math.log(10000.0) * jnp.arange(half_size, dtype=jnp.float32) / half_size)
    angle = position[:, None] * frequency[None, :]
    cosine = jnp.cos(angle)[:, None, :]
    sine = jnp.sin(angle)[:, None, :] * direction
    first_half = vectors[..., :half_size]
    second_half = vectors[..., half_size:]
    return jnp.concatenate(
        [first_half * cosine - second_half * sine, second_half * cosine + first_half * sine],
        axis=-1,
    )


def normalize(inputs):
    centered = inputs - jnp.mean(inputs, axis=-1, keepdims=True)
    inverse = lax.rsqrt(jnp.mean(centered * centered, axis=-1, keepdims=True) + 1e-06)
    return (centered * inverse, inverse)


def norm_backward(grad_normed, normed, inverse):
    mean_grad = jnp.mean(grad_normed, axis=-1, keepdims=True)
    mean_mixed = jnp.mean(grad_normed * normed, axis=-1, keepdims=True)
    return inverse * (grad_normed - mean_grad - normed * mean_mixed)


def add_counts(earlier, later):
    return earlier + later


def block_rows_for(row_count):
    chosen = 1
    for candidate in range(1, 513):
        if row_count % candidate == 0:
            chosen = candidate
    return chosen


def stack_blocks(shard_piece):
    row_count = shard_piece[0].shape[0]
    block_rows = block_rows_for(row_count)
    block_count = row_count // block_rows
    return (
        shard_piece[0].reshape(block_count, block_rows, HEADS, HEAD),
        shard_piece[1].reshape(block_count, block_rows, HEADS, HEAD),
        shard_piece[2].reshape(block_count, block_rows),
    )


def forward_block(carried, key_block, queries, query_codes):
    running_max, running_sum, accumulated = carried
    key_rows, values, key_codes = key_block
    scores = (
        jnp.einsum("qhe,khe->hqk", queries, key_rows, preferred_element_type=jnp.float32) * 0.125
    )
    allowed = (query_codes[:, None] == key_codes.astype(jnp.float32)[None, :])[None]
    masked = jnp.where(allowed, scores, -1e30)
    new_max = jnp.maximum(running_max, jnp.max(masked, axis=2))
    rescale = jnp.exp(running_max - new_max)
    weights = jnp.where(allowed, jnp.exp(masked - new_max[:, :, None]), 0.0)
    running_sum = running_sum * rescale + jnp.sum(weights, axis=2)
    product = jnp.einsum(
        "hqk,khe->qhe", weights, values.astype(jnp.float32), precision=lax.Precision.HIGHEST
    )
    accumulated = accumulated * rescale.T[:, :, None] + product
    return (new_max, running_sum, accumulated)


def block_grads(key_block, queries, query_codes, grad_attn, log_total, delta_rows):
    key_rows, values, key_codes = key_block
    scores = (
        jnp.einsum("qhe,khe->hqk", queries, key_rows, preferred_element_type=jnp.float32) * 0.125
    )
    allowed = (query_codes[:, None] == key_codes.astype(jnp.float32)[None, :])[None]
    probabilities = jnp.exp(jnp.where(allowed, scores, -1e30) - log_total[:, :, None])
    grad_probs = jnp.einsum("qhe,khe->hqk", grad_attn, values, preferred_element_type=jnp.float32)
    grad_scores = (probabilities * (grad_probs - delta_rows[:, :, None])).astype(jnp.bfloat16)
    return (probabilities, grad_scores)


def body(
    tokens,
    w_query,
    w_key,
    w_value,
    w_out,
    w_ada,
    w_up,
    w_down,
    segments,
    validity,
    timesteps,
    cotangent,
):
    inputs = tokens[0].astype(jnp.float32)
    segment = segments[0]
    valid_row = validity[0]
    timestep_row = timesteps[0]
    grad_output = cotangent[0].astype(jnp.float32)
    frame_count = inputs.shape[0]
    highest = lax.Precision.HIGHEST
    cols_q, cols_k, cols_v, cols_o, cols_a, cols_u, cols_d = (
        lax.all_gather(w_query.astype(jnp.bfloat16), "seq", axis=1, tiled=True),
        lax.all_gather(w_key.astype(jnp.bfloat16), "seq", axis=1, tiled=True),
        lax.all_gather(w_value.astype(jnp.bfloat16), "seq", axis=1, tiled=True),
        lax.all_gather(w_out.astype(jnp.bfloat16), "seq", axis=1, tiled=True),
        lax.all_gather(w_ada.astype(jnp.bfloat16), "seq", axis=1, tiled=True),
        lax.all_gather(w_up.astype(jnp.bfloat16), "seq", axis=1, tiled=True),
        lax.all_gather(w_down.astype(jnp.bfloat16), "seq", axis=1, tiled=True),
    )
    full_q, full_k, full_v, full_o, full_a, full_u, full_d = (
        lax.all_gather(cols_q, "batch", axis=0, tiled=True),
        lax.all_gather(cols_k, "batch", axis=0, tiled=True),
        lax.all_gather(cols_v, "batch", axis=0, tiled=True),
        lax.all_gather(cols_o, "batch", axis=0, tiled=True),
        lax.all_gather(cols_a, "batch", axis=0, tiled=True),
        lax.all_gather(cols_u, "batch", axis=0, tiled=True),
        lax.all_gather(cols_d, "batch", axis=0, tiled=True),
    )
    silu_time = jax.nn.silu(time_embedding(timestep_row)).astype(jnp.bfloat16)
    emb_rows = matmul(silu_time, full_a)
    member = segment[:, None] == jnp.arange(CLIPS, dtype=jnp.int32)[None, :]
    one_hot = member.astype(jnp.float32)
    counted = member.astype(jnp.int32)
    modulation = jnp.dot(one_hot, emb_rows, precision=highest)
    shift_attn, scale_attn, gate_attn, shift_ffn, scale_ffn, gate_ffn = jnp.split(
        modulation, 6, axis=1
    )
    offsets = carried_in(
        jnp.sum(counted, axis=0), "seq", add_counts, jnp.zeros((CLIPS,), jnp.int32)
    )
    before = jnp.cumsum(counted, axis=0) - counted + offsets[None, :]
    position = jnp.sum(before * counted, axis=1).astype(jnp.float32)
    normed, inverse = normalize(inputs)
    attn_input = (normed * (1.0 + scale_attn) + shift_attn).astype(jnp.bfloat16)
    queries = rotate_pairs(
        matmul(attn_input, full_q).reshape(frame_count, HEADS, HEAD), position, 1.0
    ).astype(jnp.bfloat16)
    key_flat = (
        rotate_pairs(matmul(attn_input, full_k).reshape(frame_count, HEADS, HEAD), position, 1.0)
        .astype(jnp.bfloat16)
        .reshape(frame_count, D)
    )
    value_flat = matmul(attn_input, full_v).astype(jnp.bfloat16)
    key_codes = jnp.where(valid_row == 1, segment, -1).astype(jnp.bfloat16)
    query_codes = segment.astype(jnp.float32)
    start_state = (
        jnp.full((HEADS, frame_count), -1e30, jnp.float32),
        jnp.zeros((HEADS, frame_count), jnp.float32),
        jnp.zeros((frame_count, HEADS, HEAD), jnp.float32),
    )

    def step(state, key_block):
        return (forward_block(state, key_block, queries, query_codes), None)

    running_max, running_sum, accumulated = lax.scan(
        step,
        start_state,
        stack_blocks(
            (
                lax.all_gather(key_flat, "seq", axis=0, tiled=True),
                lax.all_gather(value_flat, "seq", axis=0, tiled=True),
                lax.all_gather(key_codes, "seq", axis=0, tiled=True),
            )
        ),
    )[0]
    attended = accumulated / running_sum.T[:, :, None]
    log_total = running_max + jnp.log(running_sum)
    attended_low = attended.reshape(frame_count, D).astype(jnp.bfloat16)
    attn_branch = matmul(attended_low, full_o)
    middle = inputs + gate_attn * attn_branch
    normed_mid, inverse_mid = normalize(middle)
    ffn_input = (normed_mid * (1.0 + scale_ffn) + shift_ffn).astype(jnp.bfloat16)
    hidden = matmul(ffn_input, full_u)
    activated, gelu_pull = jax.vjp(partial(jax.nn.gelu, approximate=True), hidden)
    activated_low = activated.astype(jnp.bfloat16)
    ffn_branch = matmul(activated_low, full_d)
    result = middle + gate_ffn * ffn_branch
    back_q, back_k, back_v, back_o, back_u, back_d = (
        full_q,
        full_k,
        full_v,
        full_o,
        full_u,
        full_d,
    )
    grad_gate_ffn = grad_output * ffn_branch
    g_ffn = (grad_output * gate_ffn).astype(jnp.bfloat16)
    grad_down_local = matmul(activated_low.T, g_ffn)
    grad_activated = matmul(g_ffn, back_d.T)
    g_hidden = gelu_pull(grad_activated)[0].astype(jnp.bfloat16)
    grad_up_local = matmul(ffn_input.T, g_hidden)
    grad_ffn_input = matmul(g_hidden, back_u.T)
    grad_middle = grad_output + norm_backward(
        grad_ffn_input * (1.0 + scale_ffn), normed_mid, inverse_mid
    )
    grad_scale_ffn = grad_ffn_input * normed_mid
    grad_gate_attn = grad_middle * attn_branch
    g_attn = (grad_middle * gate_attn).astype(jnp.bfloat16)
    grad_out_local = matmul(attended_low.T, g_attn)
    grad_attn = matmul(g_attn, back_o.T).astype(jnp.bfloat16).reshape(frame_count, HEADS, HEAD)
    delta_rows = jnp.einsum("qhe,qhe->hq", grad_attn.astype(jnp.float32), attended)
    zero_query = jnp.zeros((frame_count, HEADS, HEAD), jnp.float32)
    gathered = (
        lax.all_gather(key_flat, "seq", axis=0, tiled=True),
        lax.all_gather(value_flat, "seq", axis=0, tiled=True),
        lax.all_gather(key_codes, "seq", axis=0, tiled=True),
    )
    pack_rows = gathered[0].shape[0]
    grad_attn_wide = grad_attn.astype(jnp.float32)

    def joint_step(total_grad, key_block):
        probabilities, grad_scores = block_grads(
            key_block, queries, query_codes, grad_attn, log_total, delta_rows
        )
        total_grad = total_grad + 0.125 * jnp.einsum(
            "hqk,khe->qhe", grad_scores, key_block[0], preferred_element_type=jnp.float32
        )
        grad_keys = 0.125 * jnp.einsum(
            "hqk,qhe->khe", grad_scores, queries, preferred_element_type=jnp.float32
        )
        grad_values = jnp.einsum("hqk,qhe->khe", probabilities, grad_attn_wide, precision=highest)
        return (total_grad, (grad_keys, grad_values))

    grad_queries_rot, both_grads = lax.scan(joint_step, zero_query, stack_blocks(gathered))
    key_value_terms = jnp.concatenate(
        [both_grads[0].reshape(pack_rows, D), both_grads[1].reshape(pack_rows, D)], axis=1
    )
    key_value_grad = lax.psum_scatter(key_value_terms, "seq", scatter_dimension=0, tiled=True)
    g_query = (
        rotate_pairs(grad_queries_rot, position, -1.0).reshape(frame_count, D).astype(jnp.bfloat16)
    )
    g_key = (
        rotate_pairs(key_value_grad[:, :D].reshape(frame_count, HEADS, HEAD), position, -1.0)
        .reshape(frame_count, D)
        .astype(jnp.bfloat16)
    )
    g_value = key_value_grad[:, D:].astype(jnp.bfloat16)
    grad_query_local = matmul(attn_input.T, g_query)
    grad_key_local = matmul(attn_input.T, g_key)
    grad_value_local = matmul(attn_input.T, g_value)
    grad_attn_input = (
        matmul(g_query, back_q.T) + matmul(g_key, back_k.T) + matmul(g_value, back_v.T)
    )
    grad_inputs = grad_middle + norm_backward(grad_attn_input * (1.0 + scale_attn), normed, inverse)
    grad_modulation = jnp.concatenate(
        [
            grad_attn_input,
            grad_attn_input * normed,
            grad_gate_attn,
            grad_ffn_input,
            grad_scale_ffn,
            grad_gate_ffn,
        ],
        axis=1,
    )
    grad_emb = jnp.dot(one_hot.T, grad_modulation, precision=highest)
    grad_ada_local = jnp.dot(silu_time.astype(jnp.float32).T, grad_emb, precision=highest)
    part_q, part_k, part_v, part_o, part_a, part_u, part_d = (
        lax.psum_scatter(grad_query_local, "seq", scatter_dimension=1, tiled=True),
        lax.psum_scatter(grad_key_local, "seq", scatter_dimension=1, tiled=True),
        lax.psum_scatter(grad_value_local, "seq", scatter_dimension=1, tiled=True),
        lax.psum_scatter(grad_out_local, "seq", scatter_dimension=1, tiled=True),
        lax.psum_scatter(grad_ada_local, "seq", scatter_dimension=1, tiled=True),
        lax.psum_scatter(grad_up_local, "seq", scatter_dimension=1, tiled=True),
        lax.psum_scatter(grad_down_local, "seq", scatter_dimension=1, tiled=True),
    )
    final_q, final_k, final_v, final_o, final_a, final_u, final_d = (
        lax.psum_scatter(
            part_q.astype(jnp.bfloat16), "batch", scatter_dimension=0, tiled=True
        ).astype(jnp.float32),
        lax.psum_scatter(
            part_k.astype(jnp.bfloat16), "batch", scatter_dimension=0, tiled=True
        ).astype(jnp.float32),
        lax.psum_scatter(
            part_v.astype(jnp.bfloat16), "batch", scatter_dimension=0, tiled=True
        ).astype(jnp.float32),
        lax.psum_scatter(
            part_o.astype(jnp.bfloat16), "batch", scatter_dimension=0, tiled=True
        ).astype(jnp.float32),
        lax.psum_scatter(
            part_a.astype(jnp.bfloat16), "batch", scatter_dimension=0, tiled=True
        ).astype(jnp.float32),
        lax.psum_scatter(
            part_u.astype(jnp.bfloat16), "batch", scatter_dimension=0, tiled=True
        ).astype(jnp.float32),
        lax.psum_scatter(
            part_d.astype(jnp.bfloat16), "batch", scatter_dimension=0, tiled=True
        ).astype(jnp.float32),
    )
    return (
        result.astype(jnp.bfloat16)[None],
        grad_inputs.astype(jnp.bfloat16)[None],
        final_q,
        final_k,
        final_v,
        final_o,
        final_a,
        final_u,
        final_d,
    )


TWO = 2 * HEAD
ROWS = 256
BIG = 1e30
SEQ = 8
REPLICAS = 4
VMEM_MIB = 60
BLOCK = 256


def swap(part, axis, distance):
    size = SEQ if axis == "seq" else REPLICAS
    return lax.ppermute(part, axis, [(i, i ^ distance) for i in range(size)])


def exchange(blocks):
    return lax.all_to_all(blocks, "seq", 0, 0, tiled=True)


def turn(vectors, cosine, sine):
    lane = lax.broadcasted_iota(jnp.int32, vectors.shape, 1)
    first = (lane % HEAD) < HEAD // 2
    partner = jnp.where(
        first,
        pltpu.roll(vectors, TWO - HEAD // 2, 1),
        pltpu.roll(vectors, HEAD // 2, 1),
    )
    return vectors * cosine + partner * jnp.where(first, -sine, sine)


def of_head(vectors, head):
    lane = lax.broadcasted_iota(jnp.int32, vectors.shape, 1)
    return jnp.where(lane // HEAD == head, vectors, jnp.zeros_like(vectors))


def dot_t(left, right):
    return lax.dot_general(
        left, right, (((1,), (1,)), ((), ())), preferred_element_type=jnp.float32
    )


def project_kernel(place_ref, a_ref, b_ref, c_ref, d_ref, member_ref, bar_ref, cos_ref, sin_ref,
                   emb_ref, w_ref, *refs):
    x_ref, input_ref, q_ref, k_ref, kt_ref, v_ref, vt_ref, chunk_ref = refs[-8:]
    for step, ref in enumerate((a_ref, b_ref, c_ref, d_ref)):

        @pl.when(pl.program_id(0) == step)
        def _():
            chunk_ref[...] = ref[...]

    chunk = chunk_ref[...]
    x_ref[...] = chunk
    normed, _ = standardize(chunk.astype(jnp.float32))
    modulation = matmul(member_ref[...], emb_ref[...])
    low = (normed * (1.0 + modulation[:, D:]) + modulation[:, :D]).astype(jnp.bfloat16)
    input_ref[...] = low
    weight = jnp.concatenate([w_ref[b ^ place_ref[1]] for b in range(REPLICAS)], axis=0)
    product = matmul(low, weight)
    cosine, sine = cos_ref[...], sin_ref[...]
    keys = turn(product[:, TWO:2 * TWO], cosine, sine)
    values = product[:, 2 * TWO:]
    q_ref[...] = turn(product[:, :TWO], cosine, sine).astype(jnp.bfloat16)
    k_ref[:, :TWO] = keys.astype(jnp.bfloat16)
    k_ref[:, TWO:] = bar_ref[...]
    kt_ref[...] = keys.T.astype(jnp.bfloat16)
    v_ref[...] = values.astype(jnp.bfloat16)
    vt_ref[...] = values.T.astype(jnp.bfloat16)


def rows_spec(width):
    return pl.BlockSpec((ROWS, width), lambda i: (i, 0))


def cols_spec(height):
    return pl.BlockSpec((height, ROWS), lambda i: (0, i))


def whole_spec(height, width):
    return pl.BlockSpec((height, width), lambda i: (0, 0))


def params(mib):
    return pltpu.CompilerParams(
        dimension_semantics=("arbitrary",), vmem_limit_bytes=mib * 1024 * 1024
    )


def cost(micros):
    return pl.CostEstimate(
        flops=int(micros * 1e9), bytes_accessed=int(micros * 3e6), transcendentals=0
    )


def project(place, odd, chunks, member, bar, cosine, sine, emb, weights, earlier):
    frames = member.shape[0]
    low = jnp.bfloat16

    def rows(width):
        return pl.BlockSpec((ROWS, width), lambda i, p: ((2 * i + odd) ^ p[0], 0))

    def cols(height):
        return pl.BlockSpec((height, ROWS), lambda i, p: (0, (2 * i + odd) ^ p[0]))

    def whole(height, width):
        return pl.BlockSpec((height, width), lambda i, p: (0, 0))

    inputs = [place, *chunks, member, bar, cosine, sine, emb, weights, *earlier]
    first = len(inputs) - len(earlier)
    return pl.pallas_call(
        project_kernel,
        grid_spec=pltpu.PrefetchScalarGridSpec(
            num_scalar_prefetch=1,
            grid=(4,),
            in_specs=[whole(ROWS, D)] * 4 + [rows(TWO)] * 4
            + [whole(TWO, 2 * D),
               pl.BlockSpec((REPLICAS, ROWS, 3 * TWO), lambda i, p: (0, 0, 0))]
            + [pl.BlockSpec(memory_space=pl.ANY)] * len(earlier),
            out_specs=[rows(D), rows(D), rows(TWO), rows(2 * TWO), cols(TWO), rows(TWO),
                       cols(TWO)],
            scratch_shapes=[pltpu.VMEM((ROWS, D), low)],
        ),
        out_shape=[
            jax.ShapeDtypeStruct((frames, D), low),
            jax.ShapeDtypeStruct((frames, D), low),
            jax.ShapeDtypeStruct((frames, TWO), low),
            jax.ShapeDtypeStruct((frames, 2 * TWO), low),
            jax.ShapeDtypeStruct((TWO, frames), low),
            jax.ShapeDtypeStruct((frames, TWO), low),
            jax.ShapeDtypeStruct((TWO, frames), low),
        ],
        input_output_aliases={first + i: i for i in range(len(earlier))},
        compiler_params=params(30),
        cost_estimate=cost(2),
        name="project",
    )(*inputs)


def attend_kernel(q_ref, member_ref, k_ref, vt_ref, att_ref, low_ref, log_ref, *score_refs):
    frames = k_ref.shape[0]
    step = min(frames, 1024)
    queries = q_ref[...] * 0.125
    member = member_ref[...]
    bests, halves = [], []
    for head, score_ref in enumerate(score_refs):
        wide = jnp.concatenate([of_head(queries, head), member], axis=1)
        largest = jnp.full((1, BLOCK), -BIG, jnp.float32)
        for start in range(0, frames, step):
            scores = dot_t(k_ref[start:start + step, :], wide)
            score_ref[start:start + step, :] = scores
            largest = jnp.maximum(largest, jnp.max(scores, axis=0, keepdims=True))
        bests.append(largest)
    for head, score_ref in enumerate(score_refs):
        total = jnp.zeros((1, BLOCK), jnp.float32)
        out = jnp.zeros((TWO, BLOCK), jnp.float32)
        for start in range(0, frames, step):
            weights = jnp.exp(score_ref[start:start + step, :] - bests[head])
            total = total + jnp.sum(weights, axis=0, keepdims=True)
            out = out + matmul(vt_ref[:, start:start + step], weights.astype(jnp.bfloat16))
        halves.append(out[head * HEAD:(head + 1) * HEAD, :] / total)
        log_ref[head:head + 1, :] = bests[head] + jnp.log(total)
    attended = jnp.concatenate(halves, axis=0).T
    att_ref[...] = attended
    low_ref[...] = attended.astype(jnp.bfloat16)


def block_spec(width):
    return pl.BlockSpec((BLOCK, width), lambda i: (i, 0))


def attend(q, member, k, vt):
    frames = q.shape[0]
    return pl.pallas_call(
        attend_kernel,
        grid=(frames // BLOCK,),
        in_specs=[block_spec(TWO), block_spec(TWO), whole_spec(frames, 2 * TWO),
                  whole_spec(TWO, frames)],
        out_specs=[block_spec(TWO), block_spec(TWO), pl.BlockSpec((8, BLOCK), lambda i: (0, i))],
        out_shape=[
            jax.ShapeDtypeStruct((frames, TWO), jnp.float32),
            jax.ShapeDtypeStruct((frames, TWO), jnp.bfloat16),
            jax.ShapeDtypeStruct((8, frames), jnp.float32),
        ],
        scratch_shapes=[pltpu.VMEM((frames, BLOCK), jnp.float32)] * 2,
        compiler_params=params(26),
        cost_estimate=cost(18),
        name="attend",
    )(q, member, k, vt)


def attend_back_kernel(q_ref, member_ref, grad_ref, att_ref, log_ref, cos_ref, sin_ref, cos_all_ref,
                       sin_all_ref, k_ref, kt_ref, v_ref, g_ref, dk_ref, dv_ref):
    block = pl.program_id(0)
    frames = k_ref.shape[0]
    step = min(frames, 512)

    @pl.when(block == 0)
    def _():
        dk_ref[...] = jnp.zeros_like(dk_ref)
        dv_ref[...] = jnp.zeros_like(dv_ref)

    queries = q_ref[...] * 0.125
    member = member_ref[...]
    grad = grad_ref[...]
    mixed = (grad.astype(jnp.float32) * att_ref[...]).T
    halves = []
    wides, grads, deltas = [], [], []
    for head in range(2):
        wides.append(jnp.concatenate([of_head(queries, head), member], axis=1))
        grads.append(of_head(grad, head))
        deltas.append(jnp.sum(mixed[head * HEAD:(head + 1) * HEAD, :], axis=0, keepdims=True))
    totals = [jnp.zeros((TWO, ROWS), jnp.float32) for _ in range(2)]
    for start in range(0, frames, step):
        part = slice(start, start + step)
        dk = dk_ref[part, :]
        dv = dv_ref[part, :]
        for head in range(2):
            scores = dot_t(k_ref[part, :], wides[head])
            weights = jnp.exp(scores - log_ref[head:head + 1, :])
            grad_weights = dot_t(v_ref[part, :], grads[head])
            grad_scores = (weights * (grad_weights - deltas[head])).astype(jnp.bfloat16)
            dv = dv + matmul(weights.astype(jnp.bfloat16), grads[head])
            dk = dk + matmul(grad_scores, wides[head][:, :TWO])
            totals[head] = totals[head] + matmul(kt_ref[:, part], grad_scores)
        dk_ref[part, :] = dk
        dv_ref[part, :] = dv
    dq = jnp.concatenate([totals[0][:HEAD, :], totals[1][HEAD:, :]], axis=0).T * 0.125
    here = pl.ds(pl.multiple_of(block * ROWS, ROWS), ROWS)
    g_ref[here, :TWO] = turn(dq, cos_ref[...], -sin_ref[...]).astype(jnp.bfloat16)

    @pl.when(block == pl.num_programs(0) - 1)
    def _():
        turned = turn(dk_ref[...], cos_all_ref[...], -sin_all_ref[...])
        g_ref[:, TWO:2 * TWO] = turned.astype(jnp.bfloat16)
        g_ref[:, 2 * TWO:] = dv_ref[...].astype(jnp.bfloat16)


def attend_back(q, member, grad, att, log_total, cosine, sine, k, kt, v):
    frames = q.shape[0]
    return pl.pallas_call(
        attend_back_kernel,
        grid=(frames // ROWS,),
        in_specs=[rows_spec(TWO), rows_spec(TWO), rows_spec(TWO), rows_spec(TWO), cols_spec(8),
                  rows_spec(TWO), rows_spec(TWO), whole_spec(frames, TWO), whole_spec(frames, TWO),
                  whole_spec(frames, 2 * TWO), whole_spec(TWO, frames), whole_spec(frames, TWO)],
        out_specs=whole_spec(frames, 3 * TWO),
        out_shape=jax.ShapeDtypeStruct((frames, 3 * TWO), jnp.bfloat16),
        scratch_shapes=[pltpu.VMEM((frames, TWO), jnp.float32),
                        pltpu.VMEM((frames, TWO), jnp.float32)],
        compiler_params=params(VMEM_MIB),
        cost_estimate=cost(27),
        name="attend_back",
    )(q, member, grad, att, log_total, cosine, sine, cosine, sine, k, kt, v)


def three_terms(values):
    high = lax.reduce_precision(values, 8, 7)
    middle = lax.reduce_precision(values - high, 8, 7)
    return [high, middle, values - high - middle]


def standardize(rows):
    centered = rows - jnp.mean(rows, axis=1, keepdims=True)
    inverse = lax.rsqrt(jnp.mean(centered * centered, axis=1, keepdims=True) + 1e-06)
    return centered * inverse, inverse


def sum_of_clips(clip_ref, values):
    ids = lax.broadcasted_iota(jnp.int32, (CLIPS, clip_ref.shape[1]), 0)
    chosen = jnp.where(clip_ref[...] == ids, 1.0, 0.0).astype(jnp.bfloat16)
    high = values.astype(jnp.bfloat16)
    rest = values - high.astype(jnp.float32)
    middle = rest.astype(jnp.bfloat16)
    last = (rest - middle.astype(jnp.float32)).astype(jnp.bfloat16)
    return matmul(chosen, high) + matmul(chosen, middle) + matmul(chosen, last)


def beside(ref, tiles, rows):
    return jnp.concatenate([ref[tile, rows, :] for tile in tiles], axis=1)


def tile_index(away, apart):
    return 16 * (away % 2) + 8 * (away // 2) + 4 * (apart % 2) + apart // 2


def middle_kernel(mine_ref, x_ref, member_ref, clip_ref, cot_any, emb_any, tiles_ref,
                  result_any, grad_middle_ref, grad_att_ref, grad_emb_ref, left_any, right_any,
                  out_ref, up_ref, down_ref, cot_ref, emb_ref, result_ref, left_ref, right_ref,
                  sems, branch_ref, low_ref, act_ref, slope_ref, wide_ref):
    low = jnp.bfloat16
    act_t_ref, ffn_t_ref = left_ref.at[:2 * D], left_ref.at[2 * D:3 * D]
    mine_t_ref = left_ref.at[3 * D:]
    g_ffn_ref, g_attn_ref = right_ref.at[:, :D], right_ref.at[:, 3 * D:]
    g_hidden_ref = right_ref.at[:, D:3 * D]
    copies = [
        pltpu.make_async_copy(source, target, sems.at[i])
        for i, (source, target) in enumerate((
            (tiles_ref.at[:, pl.ds(0, 256), :], out_ref),
            (emb_any, emb_ref),
            (cot_any, cot_ref),
            (tiles_ref.at[:, pl.ds(256, 512), :], up_ref),
            (tiles_ref.at[:, pl.ds(768, 512), :], down_ref),
        ))
    ]
    for copy in copies:
        copy.start()
    stores = [
        pltpu.make_async_copy(source, target, sems.at[len(copies) + i])
        for i, (source, target) in enumerate((
            (mine_t_ref, left_any.at[3 * D:]),
            (ffn_t_ref, left_any.at[2 * D:3 * D]),
            (g_ffn_ref, right_any.at[:, :D]),
            (act_t_ref, left_any.at[:2 * D]),
            (result_ref, result_any),
            (g_hidden_ref, right_any.at[:, D:3 * D]),
            (g_attn_ref, right_any.at[:, 3 * D:]),
        ))
    ]

    def tile(b, s):
        return SEQ * b + s

    member = member_ref[...]

    def modulation(index):
        return matmul(member, emb_ref[:, index * D:(index + 1) * D])

    def cols(n, width=256):
        return pl.ds(pl.multiple_of(n * width, width), width)

    every = slice(None)
    mine = jnp.concatenate([mine_ref[j] for j in range(SEQ)], axis=1)
    low_ref[...] = mine
    mine_t_ref[...] = mine.T
    stores[0].start()
    copies[0].wait()

    @pl.loop(0, 4)
    def _(n):
        total = jnp.zeros((ROWS, 256), jnp.float32)
        for b in range(REPLICAS):
            weight = beside(out_ref, [tile(b, 2 * n), tile(b, 2 * n + 1)], every)
            total = total + matmul(low_ref[:, 256 * b:256 * b + 256], weight)
        branch_ref[:, cols(n)] = total

    copies[1].wait()
    gate_attn = modulation(2)
    branch = branch_ref[...]
    middle = x_ref[...].astype(jnp.float32) + gate_attn * branch
    normed, inverse = standardize(middle)
    scale_ffn = modulation(4)
    ffn_input = normed * (1.0 + scale_ffn) + modulation(3)
    low_ref[...] = ffn_input.astype(low)
    ffn_t_ref[...] = ffn_input.T.astype(low)
    gate_ffn = modulation(5)
    copies[2].wait()
    cot = cot_ref[...].astype(jnp.float32)
    g_ffn_ref[...] = (cot * gate_ffn).astype(low)
    stores[1].start()
    stores[2].start()
    copies[3].wait()

    @pl.loop(0, 8)
    def _(n):
        hidden = jnp.zeros((ROWS, 256), jnp.float32)
        for b in range(REPLICAS):
            index = tile(b, n)
            weight = jnp.concatenate([up_ref[index, :256, :], up_ref[index, 256:, :]], axis=1)
            hidden = hidden + matmul(low_ref[:, 256 * b:256 * b + 256], weight)
        root = math.sqrt(2.0 / math.pi)
        squared = hidden * hidden
        bent = jnp.tanh(root * (hidden + 0.044715 * (squared * hidden)))
        half = 0.5 * (1.0 + bent)
        activated = hidden * half
        slope = half + 0.5 * hidden * (1.0 - bent * bent) * (
            root * (1.0 + (3.0 * 0.044715) * squared)
        )
        act_ref[:, cols(n)] = activated.astype(low)
        act_t_ref[cols(n), :] = activated.T.astype(low)
        slope_ref[:, cols(n)] = slope

    stores[3].start()
    copies[4].wait()

    @pl.loop(0, 4)
    def _(n):
        total = jnp.zeros((ROWS, 256), jnp.float32)
        for b in range(REPLICAS):
            weight = beside(down_ref, [tile(b, 2 * n), tile(b, 2 * n + 1)], every)
            total = total + matmul(act_ref[:, 512 * b:512 * b + 512], weight)
        wide_ref[:, cols(n)] = total

    ffn_branch = wide_ref[...]
    result_ref[...] = (middle + gate_ffn * ffn_branch).astype(low)
    stores[4].start()
    grad_emb_ref[:, 3 * D:] = sum_of_clips(clip_ref, cot * ffn_branch)

    @pl.loop(0, REPLICAS)
    def _(b):
        weight = beside(down_ref, [tile(b, s) for s in range(SEQ)], every)
        grad = dot_t(g_ffn_ref[...], weight)
        here = cols(b, 512)
        g_hidden_ref[:, here] = (grad * slope_ref[:, here]).astype(low)

    stores[5].start()

    @pl.loop(0, REPLICAS)
    def _(b):
        weight = jnp.concatenate(
            [up_ref[tile(b, s), 256 * k:256 * k + 256, :] for s in range(SEQ) for k in range(2)],
            axis=1,
        )
        wide_ref[:, cols(b)] = dot_t(g_hidden_ref[...], weight)

    grad_ffn_input = wide_ref[...]
    grad_emb_ref[:, D:2 * D] = sum_of_clips(clip_ref, grad_ffn_input)
    grad_emb_ref[:, 2 * D:3 * D] = sum_of_clips(clip_ref, grad_ffn_input * normed)
    spread = grad_ffn_input * (1.0 + scale_ffn)
    grad_middle = cot + inverse * (
        spread
        - jnp.mean(spread, axis=1, keepdims=True)
        - normed * jnp.mean(spread * normed, axis=1, keepdims=True)
    )
    grad_middle_ref[...] = grad_middle
    grad_emb_ref[:, :D] = sum_of_clips(clip_ref, grad_middle * branch)
    g_attn_ref[...] = (grad_middle * gate_attn).astype(low)
    stores[6].start()

    @pl.loop(0, REPLICAS)
    def _(b):
        weight = beside(out_ref, [tile(b, s) for s in range(SEQ)], every)
        grad = dot_t(g_attn_ref[...], weight).astype(low)
        grad_att_ref[2 * b] = grad[:, :TWO]
        grad_att_ref[2 * b + 1] = grad[:, TWO:]

    for store in stores:
        store.wait()


def middle_part(mine, x, cot, member, clip_row, emb, tiles):
    low = jnp.bfloat16
    shapes = [
        ((ROWS, D), low), ((ROWS, D), jnp.float32), ((SEQ, ROWS, TWO), low),
        ((CLIPS, 4 * D), jnp.float32), ((4 * D, ROWS), low), ((ROWS, 4 * D), low),
    ]
    vmem, anywhere = pl.BlockSpec(memory_space=pltpu.VMEM), pl.BlockSpec(memory_space=pl.ANY)
    return pl.pallas_call(
        middle_kernel,
        in_specs=[vmem] * 4 + [anywhere] * 3,
        out_specs=[anywhere, vmem, vmem, vmem, anywhere, anywhere],
        out_shape=[jax.ShapeDtypeStruct(shape, dtype) for shape, dtype in shapes],
        scratch_shapes=[
            pltpu.VMEM((32, 256, 128), low),
            pltpu.VMEM((32, 512, 128), low),
            pltpu.VMEM((32, 512, 128), low),
            pltpu.VMEM((ROWS, D), low),
            pltpu.VMEM((TWO, 6 * D), low),
            pltpu.VMEM((ROWS, D), low),
            pltpu.VMEM((4 * D, ROWS), low),
            pltpu.VMEM((ROWS, 4 * D), low),
            pltpu.SemaphoreType.DMA((12,)),
            pltpu.VMEM((ROWS, D), jnp.float32),
            pltpu.VMEM((ROWS, D), low),
            pltpu.VMEM((ROWS, 2 * D), low),
            pltpu.VMEM((ROWS, 2 * D), jnp.float32),
            pltpu.VMEM((ROWS, D), jnp.float32),
        ],
        compiler_params=pltpu.CompilerParams(vmem_limit_bytes=VMEM_MIB * 1024 * 1024),
        cost_estimate=cost(20),
        name="middle",
    )(mine, x, member, clip_row, cot, emb, *tiles)


def weight_grads_kernel(place_ref, down_l, up_l, out_l, right_ref, down_o, up_o, out_o, other_ref,
                        away_d_ref, keep_d_ref, away_u_ref, keep_u_ref):
    low = jnp.bfloat16
    z, y = place_ref[2] // 2, place_ref[2] % 2
    lefts = [
        jnp.concatenate([mine[...], other[...]], axis=1)
        for mine, other in ((down_l, down_o), (up_l, up_o), (out_l, out_o))
    ]

    def product(left, first, block):
        here = pl.ds(pl.multiple_of(first + 256 * block, 256), 256)
        right = jnp.concatenate([right_ref[:, here], other_ref[:, here]], axis=0)
        return matmul(left, right).astype(low)

    def fill(ref):
        @pl.loop(0, 4)
        def _(k):
            block = z ^ k
            for left, first, rows in ((lefts[0], 0, slice(0, 512)), (lefts[2], 3 * D, slice(512, 768))):
                grad = product(left, first, block)
                ref[4 * y + k, rows, :] = grad[:, :128]
                ref[4 - 4 * y + k, rows, :] = grad[:, 128:]
            for side, up_ref in enumerate((keep_u_ref, away_u_ref)):
                grad = product(lefts[1], D, 2 * block + (y ^ side))
                up_ref[0, k, :256, :] = grad[:, :128]
                up_ref[0, k, 256:, :] = grad[:, 128:]

    @pl.when(pl.program_id(0) == 0)
    def _():
        fill(away_d_ref)

    @pl.when(pl.program_id(0) == 1)
    def _():
        fill(keep_d_ref)


def weight_grads(place, left, right, other_left, other_right):
    low = jnp.bfloat16

    def target(i, p):
        return 2 * jnp.where(i == 0, 1 - p[0], p[0]) + p[1]

    down = pl.BlockSpec((512, ROWS), lambda i, p: (target(i, p), 0))
    up = pl.BlockSpec((256, ROWS), lambda i, p: (8 + target(i, p), 0))
    out = pl.BlockSpec((256, ROWS), lambda i, p: (12 + target(i, p), 0))
    wide = pl.BlockSpec((ROWS, 4 * D), lambda i, p: (0, 0))
    whole = pl.BlockSpec((SEQ, 768, 128), lambda i, p: (0, 0, 0))
    part = pl.BlockSpec((1, 4, 512, 128), lambda i, p: (1 - i, 0, 0, 0))
    return pl.pallas_call(
        weight_grads_kernel,
        grid_spec=pltpu.PrefetchScalarGridSpec(
            num_scalar_prefetch=1,
            grid=(2,),
            in_specs=[down, up, out, wide] * 2,
            out_specs=[whole, whole, part, part],
        ),
        out_shape=[jax.ShapeDtypeStruct((SEQ, 768, 128), low)] * 2
        + [jax.ShapeDtypeStruct((2, 4, 512, 128), low)] * 2,
        compiler_params=params(VMEM_MIB),
        cost_estimate=cost(9),
        name="weight_grads",
    )(place, left, left, left, right, other_left, other_left, other_left, other_right)


def clip_grads_kernel(place_ref, x_ref, clip_ref, g_ref, w_ref, out_ref):
    @pl.when(pl.program_id(0) == 0)
    def _():
        out_ref[...] = jnp.zeros_like(out_ref)

    normed, _ = standardize(x_ref[...].astype(jnp.float32))
    grad = jnp.concatenate(
        [dot_t(g_ref[...], w_ref[b ^ place_ref[1]]) for b in range(REPLICAS)], axis=1
    )
    out_ref[:, :D] += sum_of_clips(clip_ref, grad)
    out_ref[:, D:] += sum_of_clips(clip_ref, grad * normed)


def clip_grads(places, x, clip_row, g_heads, heads_w):
    frames = x.shape[0]
    return pl.pallas_call(
        clip_grads_kernel,
        grid=(frames // ROWS,),
        in_specs=[pl.BlockSpec(memory_space=pltpu.SMEM), rows_spec(D), cols_spec(1),
                  rows_spec(3 * TWO),
                  pl.BlockSpec((REPLICAS, ROWS, 3 * TWO), lambda i: (0, 0, 0))],
        out_specs=whole_spec(CLIPS, 2 * D),
        out_shape=jax.ShapeDtypeStruct((CLIPS, 2 * D), jnp.float32),
        compiler_params=params(VMEM_MIB),
        cost_estimate=cost(9),
        name="clip_grads",
    )(places, x, clip_row, g_heads, heads_w)


def last_kernel(place_ref, own_ref, x_ref, grad_middle_ref, member_ref, emb_ref, *refs):
    *tile_refs, out_ref, wide_ref = refs
    grads = jnp.concatenate([own_ref[place_ref[2] ^ s] for s in range(SEQ)], axis=1)

    def tile(away, apart):
        index = tile_index(away, apart)
        for ref in tile_refs:
            if index < ref.shape[0]:
                return ref[index, ref.shape[1] - 768:, :]
            index -= ref.shape[0]

    for away in range(REPLICAS):
        weight = jnp.concatenate(
            [
                tile(away, s)[256 * k:256 * k + 256, :]
                for s in range(SEQ)
                for k in range(3)
            ],
            axis=1,
        )
        b = (2 * place_ref[0] + place_ref[1]) ^ away
        wide_ref[:, pl.ds(pl.multiple_of(b * 256, 256), 256)] = dot_t(grads, weight)

    normed, inverse = standardize(x_ref[...].astype(jnp.float32))
    spread = wide_ref[...] * (1.0 + matmul(member_ref[...], emb_ref[:, D:2 * D]))
    grad = grad_middle_ref[...] + inverse * (
        spread
        - jnp.mean(spread, axis=1, keepdims=True)
        - normed * jnp.mean(spread * normed, axis=1, keepdims=True)
    )
    out_ref[...] = grad.astype(jnp.bfloat16)


def last_part(place, own, x, grad_middle, member, emb, tiles):
    vmem = pl.BlockSpec(memory_space=pltpu.VMEM)
    return pl.pallas_call(
        last_kernel,
        in_specs=[pl.BlockSpec(memory_space=pltpu.SMEM)] + [vmem] * (5 + len(tiles)),
        out_specs=vmem,
        out_shape=jax.ShapeDtypeStruct((ROWS, D), jnp.bfloat16),
        scratch_shapes=[pltpu.VMEM((ROWS, D), jnp.float32)],
        compiler_params=pltpu.CompilerParams(vmem_limit_bytes=30 * 1024 * 1024),
        cost_estimate=cost(4),
        name="last",
    )(place, own, x, grad_middle, member, emb, *tiles)


def after(value, *others):
    return lax.optimization_barrier((value,) + others)[0]


def together(*values):
    return lax.optimization_barrier(values)


def plus(*terms):
    total = terms[0].astype(jnp.float32)
    for term in terms[1:]:
        total = total + term.astype(jnp.float32)
    return total


def clip_lanes(clip, terms):
    lane = jnp.arange(TWO, dtype=jnp.int32)[None, :]
    return (clip[:, None] == lane % CLIPS) & (lane < terms * CLIPS)


def body_fast(
    tokens, w_query, w_key, w_value, w_out, w_ada, w_up, w_down,
    segments, validity, timesteps, cotangent,
):
    highest = lax.Precision.HIGHEST
    low = jnp.bfloat16
    wide = jnp.float32
    replica = lax.axis_index("batch")
    x = tokens[0]
    frame_count = x.shape[0]
    frames = frame_count * SEQ
    segment = segments[0]

    seat = lax.axis_index("seq").astype(jnp.int32)
    z, y = seat // 2, seat % 2
    place = jnp.stack([replica // 2, replica % 2, seat]).astype(jnp.int32)
    mine_w = jnp.concatenate([w_out, w_up[:, :128], w_up[:, 128:], w_down], axis=0).astype(low)

    z1, z2, y0 = swap(x, "seq", 2), swap(x, "seq", 4), swap(x, "seq", 1)
    times = lax.all_gather(timesteps[0], "batch", axis=0, tiled=True)
    silu_all = jax.nn.silu(time_embedding(times)).astype(low)
    depth = w_ada.shape[0]
    silu_part = lax.dynamic_slice_in_dim(silu_all, replica * depth, depth, 1)
    emb_part = matmul(silu_part, w_ada.astype(low)).reshape(REPLICAS, CLIPS, -1)
    emb_cols = lax.all_to_all(emb_part, "batch", 0, 0, tiled=True)
    emb_cols = jnp.sum(emb_cols, axis=0)
    own_codes = (segment * 2 + (validity[0] == 1)).astype(wide)
    cols = emb_cols.shape[1]
    own_codes = jnp.pad(own_codes, (0, 8 * cols - frame_count)).reshape(8, cols)
    packed = jnp.concatenate([emb_cols, own_codes])
    packed = jnp.broadcast_to(packed[None], (SEQ,) + packed.shape)
    heads_w = jnp.concatenate([w_query, w_key, w_value], axis=1).astype(low)
    heads_w = jnp.stack([heads_w, swap(heads_w, "batch", 1)])
    z1, z2, y0, packed, heads_w, mine_w = together(z1, z2, y0, packed, heads_w, mine_w)
    tiles_w = (lax.all_gather(mine_w, ("batch", "seq"), axis=0),)
    packed = exchange(packed)
    z3 = swap(z2, "seq", 2)
    y1, y2 = swap(z1, "seq", 1), swap(z2, "seq", 1)
    heads_x = swap(heads_w, "batch", 2)
    z3, heads_x = together(z3, heads_x)
    y3 = swap(z3, "seq", 1)
    mine_h = jnp.concatenate([w_query, w_key, w_value], axis=0).astype(low)
    mine_h = after(mine_h, z3)
    h_z1, h_z2 = swap(mine_h, "seq", 2), swap(mine_h, "seq", 4)
    heads_w = jnp.concatenate([heads_w, heads_x])
    emb = packed[:, :CLIPS]
    codes = packed[:, CLIPS:].reshape(SEQ, -1)[:, :frame_count].reshape(frames).astype(jnp.int32)
    clip = codes // 2
    clip_row = clip[None, :]
    tri = jnp.arange(frame_count)[:, None] > jnp.arange(frame_count)[None, :]
    ids = jnp.arange(CLIPS, dtype=jnp.int32)
    one_hot = (clip.reshape(SEQ, frame_count)[:, :, None] == ids).astype(low)
    within = jnp.einsum("ij,njc->nic", tri.astype(low), one_hot, preferred_element_type=wide)
    counts = jnp.sum(one_hot.astype(wide), axis=1)
    offsets = jnp.cumsum(counts, axis=0) - counts
    position = jnp.sum(one_hot.astype(wide) * (within + offsets[:, None, :]), axis=2)
    half = HEAD // 2
    frequency = jnp.exp(-math.log(10000.0) * jnp.arange(half, dtype=wide) / half)
    angle = position.reshape(frames)[:, None] * jnp.tile(frequency, 4)[None, :]
    cosine, sine = jnp.cos(angle), jnp.sin(angle)
    member = clip_lanes(clip, 3).astype(low)
    allowed = clip_lanes(jnp.where(codes % 2 == 1, clip, -1), 1)
    inside = jnp.arange(TWO, dtype=jnp.int32)[None, :] < CLIPS
    bar = jnp.where(inside & ~allowed, -BIG, 0.0).astype(low)
    emb, y1, y2 = together(after(emb, heads_w, member, cosine), y1, y2)
    emb = emb.transpose(1, 0, 2).reshape(CLIPS, -1)
    emb = jnp.concatenate(
        [t.astype(low) for t in three_terms(emb)] + [jnp.zeros((TWO - 3 * CLIPS, 6 * D), low)],
        axis=0,
    )

    tables = (member, bar, cosine, sine, emb, heads_w)
    places = jnp.stack([seat, replica.astype(jnp.int32)])
    earlier = project(places, 0, (x, z1, z2, z3), *tables, ())
    y3, h_z1, h_z2, earlier = together(y3, h_z1, h_z2, earlier)
    h_z3 = swap(h_z2, "seq", 2)
    x_all, attn_input, q, k, kt, v, vt = project(places, 1, (y0, y1, y2, y3), *tables, earlier)
    attended, attended_low, log_total = attend(q, member, k, vt)
    attended_low, h_z3 = together(attended_low, h_z3)
    mine = exchange(attended_low.reshape(SEQ, frame_count, TWO))
    h_z = jnp.stack([mine_h, h_z1, h_z2, h_z3])
    mine, h_z = together(mine, h_z)
    h_y, h_x = swap(h_z, "seq", 1), swap(h_z, "batch", 2)

    own_member = clip_lanes(segment, 3).astype(low)
    result, grad_middle, grad_att, grad_emb, left, right = middle_part(
        mine, x, cotangent[0], own_member, segment[None, :], emb, tiles_w
    )
    left, h_y, h_x = together(left, h_y, h_x)
    other_left, other_right = swap(left, "batch", 1), swap(right, "batch", 1)
    h_first = jnp.concatenate([h_z, h_y, h_x])
    other_left, other_right, h_first = together(other_left, other_right, h_first)
    away_d, keep_d, away_u, keep_u = weight_grads(place, left, right, other_left, other_right)
    grad_heads = exchange(grad_att).reshape(frames, TWO)
    from_x = swap(away_d, "batch", 2)
    from_y = swap(away_u, "seq", 1)
    grad_heads = after(grad_heads, away_d, away_u)

    g_heads = attend_back(
        q, member, grad_heads, attended, log_total, cosine, sine, k, kt, v
    )
    own = exchange(g_heads.reshape(SEQ, frame_count, 3 * TWO))
    from_y = after(from_y, g_heads)
    to_x_u = plus(keep_u[1], from_y[1]).astype(low)
    from_x_u = swap(to_x_u, "batch", 2)
    from_x = after(from_x, to_x_u)
    to_y_d = plus(keep_d[4:], from_x[4:]).astype(low)
    from_y_d = swap(to_y_d, "seq", 1)
    h_yx = swap(after(h_y, to_y_d), "batch", 2)
    h_first_core = swap(after(h_first, to_x_u), "batch", 1)
    g_heads = after(g_heads, to_y_d, to_x_u)
    late = clip_grads(places, x_all, clip_row, g_heads, heads_w)
    grad_heads_w = matmul(attn_input.T, g_heads).astype(low).reshape(2, 2, ROWS, 3 * TWO)
    late, grad_heads_w, from_y_d, from_x_u, h_first_core = together(
        late, grad_heads_w, from_y_d, from_x_u, h_first_core
    )
    part = jnp.concatenate(
        [
            plus(keep_u[0], from_y[0], from_x_u).astype(low),
            plus(keep_d[:4], from_x[:4], from_y_d).astype(low),
        ],
        axis=1,
    )
    late, own = together(late, own)
    grad_emb = jnp.concatenate([late, grad_emb], axis=1)
    grad_emb = grad_emb.reshape(CLIPS, 4, 2, -1).transpose(2, 1, 0, 3)
    keep_e = lax.dynamic_index_in_dim(grad_emb, y, 0, False)
    other_e = swap(lax.dynamic_index_in_dim(grad_emb, 1 - y, 0, False), "seq", 1)
    x_place, core_place = replica // 2, replica % 2
    grad_emb = keep_e + other_e
    from_z_e = [
        swap(lax.dynamic_index_in_dim(grad_emb, z ^ k, 0, False), "seq", 2 * k) for k in range(1, 4)
    ]
    grad_emb = plus(lax.dynamic_index_in_dim(grad_emb, z, 0, False), *from_z_e)
    keep_h = lax.dynamic_index_in_dim(grad_heads_w, core_place, 1, False)
    other_h = swap(lax.dynamic_index_in_dim(grad_heads_w, 1 - core_place, 1, False), "batch", 1)
    h_yx_core = swap(after(h_yx, part), "batch", 1)
    from_z = [swap(part[k], "seq", 2 * k) for k in range(1, 4)]
    both_h = plus(keep_h, other_h).astype(low)
    away_h = swap(lax.dynamic_index_in_dim(both_h, 1 - x_place, 0, False), "batch", 2)

    grad_tokens = last_part(place, own, x, grad_middle, own_member, emb,
        (h_first, h_yx, h_first_core, h_yx_core),
    )
    grad_emb = lax.all_gather(grad_emb, "batch", axis=0, tiled=True)
    final_a = jnp.dot(silu_part.astype(wide).T, grad_emb, precision=highest)
    grad_tokens, final_a, away_h, *from_z = together(grad_tokens, final_a, away_h, *from_z)
    final_heads = plus(lax.dynamic_index_in_dim(both_h, x_place, 0, False), away_h)
    total = plus(part[0], *from_z)
    final_u = jnp.concatenate([total[:256], total[256:512]], axis=1)
    final_d, final_o = total[512:1024], total[1024:]
    width = w_query.shape[1]
    return (
        result[None],
        grad_tokens[None],
        final_heads[:, :width],
        final_heads[:, width:2 * width],
        final_heads[:, 2 * width:],
        final_o,
        final_a,
        final_u,
        final_d,
    )


def solution(mesh):
    fits = mesh.shape["seq"] == SEQ and mesh.shape["batch"] == REPLICAS
    chosen = body_fast if fits else body
    return jax.shard_map(
        chosen,
        mesh=mesh,
        in_specs=(
            P("batch", "seq", None),
            P("batch", "seq"),
            P("batch", "seq"),
            P("batch", "seq"),
            P("batch", "seq"),
            P("batch", "seq"),
            P("batch", "seq"),
            P("batch", "seq"),
            P("batch", "seq"),
            P("batch", "seq"),
            P("batch", None),
            P("batch", "seq", None),
        ),
        out_specs=(
            P("batch", "seq", None),
            P("batch", "seq", None),
            P("batch", "seq"),
            P("batch", "seq"),
            P("batch", "seq"),
            P("batch", "seq"),
            P("batch", "seq"),
            P("batch", "seq"),
            P("batch", "seq"),
        ),
        check_vma=False,
    )
```

```python
from functools import partial
import math

import jax
import jax.numpy as jnp
from jax import lax
from jax.experimental import pallas as pl
from jax.experimental.pallas import tpu as pltpu
from jax.sharding import PartitionSpec as P

D = 1024
HEADS = 16
HEAD = 64
CLIPS = 16


def carried_in(part, axis, combine, identity):
    place = lax.axis_index(axis)
    gathered = lax.all_gather(part, axis)
    state = jnp.zeros_like(part) + jnp.asarray(identity, part.dtype)

    def one(step, state):
        return combine(state, lax.dynamic_index_in_dim(gathered, step, 0, False))

    return lax.fori_loop(0, place, one, state)


def matmul(left, right):
    return jnp.dot(left, right, preferred_element_type=jnp.float32)


def time_embedding(timestep_row):
    half_width = D // 2
    frequency = jnp.exp(-math.log(10000.0) * jnp.arange(half_width, dtype=jnp.float32) / half_width)
    angle = timestep_row.astype(jnp.float32)[:, None] * frequency[None, :]
    return jnp.concatenate([jnp.sin(angle), jnp.cos(angle)], axis=1)


def rotate_pairs(vectors, position, direction):
    half_size = vectors.shape[-1] // 2
    frequency = jnp.exp(-math.log(10000.0) * jnp.arange(half_size, dtype=jnp.float32) / half_size)
    angle = position[:, None] * frequency[None, :]
    cosine = jnp.cos(angle)[:, None, :]
    sine = jnp.sin(angle)[:, None, :] * direction
    first_half = vectors[..., :half_size]
    second_half = vectors[..., half_size:]
    return jnp.concatenate(
        [first_half * cosine - second_half * sine, second_half * cosine + first_half * sine],
        axis=-1,
    )


def normalize(inputs):
    centered = inputs - jnp.mean(inputs, axis=-1, keepdims=True)
    inverse = lax.rsqrt(jnp.mean(centered * centered, axis=-1, keepdims=True) + 1e-06)
    return (centered * inverse, inverse)


def norm_backward(grad_normed, normed, inverse):
    mean_grad = jnp.mean(grad_normed, axis=-1, keepdims=True)
    mean_mixed = jnp.mean(grad_normed * normed, axis=-1, keepdims=True)
    return inverse * (grad_normed - mean_grad - normed * mean_mixed)


def add_counts(earlier, later):
    return earlier + later


def block_rows_for(row_count):
    chosen = 1
    for candidate in range(1, 513):
        if row_count % candidate == 0:
            chosen = candidate
    return chosen


def stack_blocks(shard_piece):
    row_count = shard_piece[0].shape[0]
    block_rows = block_rows_for(row_count)
    block_count = row_count // block_rows
    return (
        shard_piece[0].reshape(block_count, block_rows, HEADS, HEAD),
        shard_piece[1].reshape(block_count, block_rows, HEADS, HEAD),
        shard_piece[2].reshape(block_count, block_rows),
    )


def forward_block(carried, key_block, queries, query_codes):
    running_max, running_sum, accumulated = carried
    key_rows, values, key_codes = key_block
    scores = (
        jnp.einsum("qhe,khe->hqk", queries, key_rows, preferred_element_type=jnp.float32) * 0.125
    )
    allowed = (query_codes[:, None] == key_codes.astype(jnp.float32)[None, :])[None]
    masked = jnp.where(allowed, scores, -1e30)
    new_max = jnp.maximum(running_max, jnp.max(masked, axis=2))
    rescale = jnp.exp(running_max - new_max)
    weights = jnp.where(allowed, jnp.exp(masked - new_max[:, :, None]), 0.0)
    running_sum = running_sum * rescale + jnp.sum(weights, axis=2)
    product = jnp.einsum(
        "hqk,khe->qhe", weights, values.astype(jnp.float32), precision=lax.Precision.HIGHEST
    )
    accumulated = accumulated * rescale.T[:, :, None] + product
    return (new_max, running_sum, accumulated)


def block_grads(key_block, queries, query_codes, grad_attn, log_total, delta_rows):
    key_rows, values, key_codes = key_block
    scores = (
        jnp.einsum("qhe,khe->hqk", queries, key_rows, preferred_element_type=jnp.float32) * 0.125
    )
    allowed = (query_codes[:, None] == key_codes.astype(jnp.float32)[None, :])[None]
    probabilities = jnp.exp(jnp.where(allowed, scores, -1e30) - log_total[:, :, None])
    grad_probs = jnp.einsum("qhe,khe->hqk", grad_attn, values, preferred_element_type=jnp.float32)
    grad_scores = (probabilities * (grad_probs - delta_rows[:, :, None])).astype(jnp.bfloat16)
    return (probabilities, grad_scores)


def body(
    tokens,
    w_query,
    w_key,
    w_value,
    w_out,
    w_ada,
    w_up,
    w_down,
    segments,
    validity,
    timesteps,
    cotangent,
):
    inputs = tokens[0].astype(jnp.float32)
    segment = segments[0]
    valid_row = validity[0]
    timestep_row = timesteps[0]
    grad_output = cotangent[0].astype(jnp.float32)
    frame_count = inputs.shape[0]
    highest = lax.Precision.HIGHEST
    cols_q, cols_k, cols_v, cols_o, cols_a, cols_u, cols_d = (
        lax.all_gather(w_query.astype(jnp.bfloat16), "seq", axis=1, tiled=True),
        lax.all_gather(w_key.astype(jnp.bfloat16), "seq", axis=1, tiled=True),
        lax.all_gather(w_value.astype(jnp.bfloat16), "seq", axis=1, tiled=True),
        lax.all_gather(w_out.astype(jnp.bfloat16), "seq", axis=1, tiled=True),
        lax.all_gather(w_ada.astype(jnp.bfloat16), "seq", axis=1, tiled=True),
        lax.all_gather(w_up.astype(jnp.bfloat16), "seq", axis=1, tiled=True),
        lax.all_gather(w_down.astype(jnp.bfloat16), "seq", axis=1, tiled=True),
    )
    full_q, full_k, full_v, full_o, full_a, full_u, full_d = (
        lax.all_gather(cols_q, "batch", axis=0, tiled=True),
        lax.all_gather(cols_k, "batch", axis=0, tiled=True),
        lax.all_gather(cols_v, "batch", axis=0, tiled=True),
        lax.all_gather(cols_o, "batch", axis=0, tiled=True),
        lax.all_gather(cols_a, "batch", axis=0, tiled=True),
        lax.all_gather(cols_u, "batch", axis=0, tiled=True),
        lax.all_gather(cols_d, "batch", axis=0, tiled=True),
    )
    silu_time = jax.nn.silu(time_embedding(timestep_row)).astype(jnp.bfloat16)
    emb_rows = matmul(silu_time, full_a)
    member = segment[:, None] == jnp.arange(CLIPS, dtype=jnp.int32)[None, :]
    one_hot = member.astype(jnp.float32)
    counted = member.astype(jnp.int32)
    modulation = jnp.dot(one_hot, emb_rows, precision=highest)
    shift_attn, scale_attn, gate_attn, shift_ffn, scale_ffn, gate_ffn = jnp.split(
        modulation, 6, axis=1
    )
    offsets = carried_in(
        jnp.sum(counted, axis=0), "seq", add_counts, jnp.zeros((CLIPS,), jnp.int32)
    )
    before = jnp.cumsum(counted, axis=0) - counted + offsets[None, :]
    position = jnp.sum(before * counted, axis=1).astype(jnp.float32)
    normed, inverse = normalize(inputs)
    attn_input = (normed * (1.0 + scale_attn) + shift_attn).astype(jnp.bfloat16)
    queries = rotate_pairs(
        matmul(attn_input, full_q).reshape(frame_count, HEADS, HEAD), position, 1.0
    ).astype(jnp.bfloat16)
    key_flat = (
        rotate_pairs(matmul(attn_input, full_k).reshape(frame_count, HEADS, HEAD), position, 1.0)
        .astype(jnp.bfloat16)
        .reshape(frame_count, D)
    )
    value_flat = matmul(attn_input, full_v).astype(jnp.bfloat16)
    key_codes = jnp.where(valid_row == 1, segment, -1).astype(jnp.bfloat16)
    query_codes = segment.astype(jnp.float32)
    start_state = (
        jnp.full((HEADS, frame_count), -1e30, jnp.float32),
        jnp.zeros((HEADS, frame_count), jnp.float32),
        jnp.zeros((frame_count, HEADS, HEAD), jnp.float32),
    )

    def step(state, key_block):
        return (forward_block(state, key_block, queries, query_codes), None)

    running_max, running_sum, accumulated = lax.scan(
        step,
        start_state,
        stack_blocks(
            (
                lax.all_gather(key_flat, "seq", axis=0, tiled=True),
                lax.all_gather(value_flat, "seq", axis=0, tiled=True),
                lax.all_gather(key_codes, "seq", axis=0, tiled=True),
            )
        ),
    )[0]
    attended = accumulated / running_sum.T[:, :, None]
    log_total = running_max + jnp.log(running_sum)
    attended_low = attended.reshape(frame_count, D).astype(jnp.bfloat16)
    attn_branch = matmul(attended_low, full_o)
    middle = inputs + gate_attn * attn_branch
    normed_mid, inverse_mid = normalize(middle)
    ffn_input = (normed_mid * (1.0 + scale_ffn) + shift_ffn).astype(jnp.bfloat16)
    hidden = matmul(ffn_input, full_u)
    activated, gelu_pull = jax.vjp(partial(jax.nn.gelu, approximate=True), hidden)
    activated_low = activated.astype(jnp.bfloat16)
    ffn_branch = matmul(activated_low, full_d)
    result = middle + gate_ffn * ffn_branch
    back_q, back_k, back_v, back_o, back_u, back_d = (
        full_q,
        full_k,
        full_v,
        full_o,
        full_u,
        full_d,
    )
    grad_gate_ffn = grad_output * ffn_branch
    g_ffn = (grad_output * gate_ffn).astype(jnp.bfloat16)
    grad_down_local = matmul(activated_low.T, g_ffn)
    grad_activated = matmul(g_ffn, back_d.T)
    g_hidden = gelu_pull(grad_activated)[0].astype(jnp.bfloat16)
    grad_up_local = matmul(ffn_input.T, g_hidden)
    grad_ffn_input = matmul(g_hidden, back_u.T)
    grad_middle = grad_output + norm_backward(
        grad_ffn_input * (1.0 + scale_ffn), normed_mid, inverse_mid
    )
    grad_scale_ffn = grad_ffn_input * normed_mid
    grad_gate_attn = grad_middle * attn_branch
    g_attn = (grad_middle * gate_attn).astype(jnp.bfloat16)
    grad_out_local = matmul(attended_low.T, g_attn)
    grad_attn = matmul(g_attn, back_o.T).astype(jnp.bfloat16).reshape(frame_count, HEADS, HEAD)
    delta_rows = jnp.einsum("qhe,qhe->hq", grad_attn.astype(jnp.float32), attended)
    zero_query = jnp.zeros((frame_count, HEADS, HEAD), jnp.float32)
    gathered = (
        lax.all_gather(key_flat, "seq", axis=0, tiled=True),
        lax.all_gather(value_flat, "seq", axis=0, tiled=True),
        lax.all_gather(key_codes, "seq", axis=0, tiled=True),
    )
    pack_rows = gathered[0].shape[0]
    grad_attn_wide = grad_attn.astype(jnp.float32)

    def joint_step(total_grad, key_block):
        probabilities, grad_scores = block_grads(
            key_block, queries, query_codes, grad_attn, log_total, delta_rows
        )
        total_grad = total_grad + 0.125 * jnp.einsum(
            "hqk,khe->qhe", grad_scores, key_block[0], preferred_element_type=jnp.float32
        )
        grad_keys = 0.125 * jnp.einsum(
            "hqk,qhe->khe", grad_scores, queries, preferred_element_type=jnp.float32
        )
        grad_values = jnp.einsum("hqk,qhe->khe", probabilities, grad_attn_wide, precision=highest)
        return (total_grad, (grad_keys, grad_values))

    grad_queries_rot, both_grads = lax.scan(joint_step, zero_query, stack_blocks(gathered))
    key_value_terms = jnp.concatenate(
        [both_grads[0].reshape(pack_rows, D), both_grads[1].reshape(pack_rows, D)], axis=1
    )
    key_value_grad = lax.psum_scatter(key_value_terms, "seq", scatter_dimension=0, tiled=True)
    g_query = (
        rotate_pairs(grad_queries_rot, position, -1.0).reshape(frame_count, D).astype(jnp.bfloat16)
    )
    g_key = (
        rotate_pairs(key_value_grad[:, :D].reshape(frame_count, HEADS, HEAD), position, -1.0)
        .reshape(frame_count, D)
        .astype(jnp.bfloat16)
    )
    g_value = key_value_grad[:, D:].astype(jnp.bfloat16)
    grad_query_local = matmul(attn_input.T, g_query)
    grad_key_local = matmul(attn_input.T, g_key)
    grad_value_local = matmul(attn_input.T, g_value)
    grad_attn_input = (
        matmul(g_query, back_q.T) + matmul(g_key, back_k.T) + matmul(g_value, back_v.T)
    )
    grad_inputs = grad_middle + norm_backward(grad_attn_input * (1.0 + scale_attn), normed, inverse)
    grad_modulation = jnp.concatenate(
        [
            grad_attn_input,
            grad_attn_input * normed,
            grad_gate_attn,
            grad_ffn_input,
            grad_scale_ffn,
            grad_gate_ffn,
        ],
        axis=1,
    )
    grad_emb = jnp.dot(one_hot.T, grad_modulation, precision=highest)
    grad_ada_local = jnp.dot(silu_time.astype(jnp.float32).T, grad_emb, precision=highest)
    part_q, part_k, part_v, part_o, part_a, part_u, part_d = (
        lax.psum_scatter(grad_query_local, "seq", scatter_dimension=1, tiled=True),
        lax.psum_scatter(grad_key_local, "seq", scatter_dimension=1, tiled=True),
        lax.psum_scatter(grad_value_local, "seq", scatter_dimension=1, tiled=True),
        lax.psum_scatter(grad_out_local, "seq", scatter_dimension=1, tiled=True),
        lax.psum_scatter(grad_ada_local, "seq", scatter_dimension=1, tiled=True),
        lax.psum_scatter(grad_up_local, "seq", scatter_dimension=1, tiled=True),
        lax.psum_scatter(grad_down_local, "seq", scatter_dimension=1, tiled=True),
    )
    final_q, final_k, final_v, final_o, final_a, final_u, final_d = (
        lax.psum_scatter(
            part_q.astype(jnp.bfloat16), "batch", scatter_dimension=0, tiled=True
        ).astype(jnp.float32),
        lax.psum_scatter(
            part_k.astype(jnp.bfloat16), "batch", scatter_dimension=0, tiled=True
        ).astype(jnp.float32),
        lax.psum_scatter(
            part_v.astype(jnp.bfloat16), "batch", scatter_dimension=0, tiled=True
        ).astype(jnp.float32),
        lax.psum_scatter(
            part_o.astype(jnp.bfloat16), "batch", scatter_dimension=0, tiled=True
        ).astype(jnp.float32),
        lax.psum_scatter(
            part_a.astype(jnp.bfloat16), "batch", scatter_dimension=0, tiled=True
        ).astype(jnp.float32),
        lax.psum_scatter(
            part_u.astype(jnp.bfloat16), "batch", scatter_dimension=0, tiled=True
        ).astype(jnp.float32),
        lax.psum_scatter(
            part_d.astype(jnp.bfloat16), "batch", scatter_dimension=0, tiled=True
        ).astype(jnp.float32),
    )
    return (
        result.astype(jnp.bfloat16)[None],
        grad_inputs.astype(jnp.bfloat16)[None],
        final_q,
        final_k,
        final_v,
        final_o,
        final_a,
        final_u,
        final_d,
    )


TWO = 2 * HEAD
ROWS = 256
BIG = 1e30
SEQ = 8
REPLICAS = 4
VMEM_MIB = 60
BLOCK = 256


def swap(part, axis, distance):
    size = SEQ if axis == "seq" else REPLICAS
    return lax.ppermute(part, axis, [(i, i ^ distance) for i in range(size)])


def exchange(blocks):
    return lax.all_to_all(blocks, "seq", 0, 0, tiled=True)


def turn(vectors, cosine, sine):
    lane = lax.broadcasted_iota(jnp.int32, vectors.shape, 1)
    first = (lane % HEAD) < HEAD // 2
    partner = jnp.where(
        first,
        pltpu.roll(vectors, TWO - HEAD // 2, 1),
        pltpu.roll(vectors, HEAD // 2, 1),
    )
    return vectors * cosine + partner * jnp.where(first, -sine, sine)


def of_head(vectors, head):
    lane = lax.broadcasted_iota(jnp.int32, vectors.shape, 1)
    return jnp.where(lane // HEAD == head, vectors, jnp.zeros_like(vectors))


def dot_t(left, right):
    return lax.dot_general(
        left, right, (((1,), (1,)), ((), ())), preferred_element_type=jnp.float32
    )


def project_kernel(place_ref, a_ref, b_ref, c_ref, d_ref, member_ref, bar_ref, cos_ref, sin_ref,
                   emb_ref, w_ref, *refs):
    x_ref, input_ref, q_ref, k_ref, kt_ref, v_ref, vt_ref, chunk_ref = refs[-8:]
    for step, ref in enumerate((a_ref, b_ref, c_ref, d_ref)):

        @pl.when(pl.program_id(0) == step)
        def _():
            chunk_ref[...] = ref[...]

    chunk = chunk_ref[...]
    x_ref[...] = chunk
    normed, _ = standardize(chunk.astype(jnp.float32))
    modulation = matmul(member_ref[...], emb_ref[...])
    low = (normed * (1.0 + modulation[:, D:]) + modulation[:, :D]).astype(jnp.bfloat16)
    input_ref[...] = low
    weight = jnp.concatenate([w_ref[b ^ place_ref[1]] for b in range(REPLICAS)], axis=0)
    product = matmul(low, weight)
    cosine, sine = cos_ref[...], sin_ref[...]
    keys = turn(product[:, TWO:2 * TWO], cosine, sine)
    values = product[:, 2 * TWO:]
    q_ref[...] = turn(product[:, :TWO], cosine, sine).astype(jnp.bfloat16)
    k_ref[:, :TWO] = keys.astype(jnp.bfloat16)
    k_ref[:, TWO:] = bar_ref[...]
    kt_ref[...] = keys.T.astype(jnp.bfloat16)
    v_ref[...] = values.astype(jnp.bfloat16)
    vt_ref[...] = values.T.astype(jnp.bfloat16)


def rows_spec(width):
    return pl.BlockSpec((ROWS, width), lambda i: (i, 0))


def cols_spec(height):
    return pl.BlockSpec((height, ROWS), lambda i: (0, i))


def whole_spec(height, width):
    return pl.BlockSpec((height, width), lambda i: (0, 0))


def params(mib):
    return pltpu.CompilerParams(
        dimension_semantics=("arbitrary",), vmem_limit_bytes=mib * 1024 * 1024
    )


def cost(micros):
    return pl.CostEstimate(
        flops=int(micros * 1e9), bytes_accessed=int(micros * 3e6), transcendentals=0
    )


def project(place, odd, chunks, member, bar, cosine, sine, emb, weights, earlier):
    frames = member.shape[0]
    low = jnp.bfloat16

    def rows(width):
        return pl.BlockSpec((ROWS, width), lambda i, p: ((2 * i + odd) ^ p[0], 0))

    def cols(height):
        return pl.BlockSpec((height, ROWS), lambda i, p: (0, (2 * i + odd) ^ p[0]))

    def whole(height, width):
        return pl.BlockSpec((height, width), lambda i, p: (0, 0))

    inputs = [place, *chunks, member, bar, cosine, sine, emb, weights, *earlier]
    first = len(inputs) - len(earlier)
    return pl.pallas_call(
        project_kernel,
        grid_spec=pltpu.PrefetchScalarGridSpec(
            num_scalar_prefetch=1,
            grid=(4,),
            in_specs=[whole(ROWS, D)] * 4 + [rows(TWO)] * 4
            + [whole(TWO, 2 * D),
               pl.BlockSpec((REPLICAS, ROWS, 3 * TWO), lambda i, p: (0, 0, 0))]
            + [pl.BlockSpec(memory_space=pl.ANY)] * len(earlier),
            out_specs=[rows(D), rows(D), rows(TWO), rows(2 * TWO), cols(TWO), rows(TWO),
                       cols(TWO)],
            scratch_shapes=[pltpu.VMEM((ROWS, D), low)],
        ),
        out_shape=[
            jax.ShapeDtypeStruct((frames, D), low),
            jax.ShapeDtypeStruct((frames, D), low),
            jax.ShapeDtypeStruct((frames, TWO), low),
            jax.ShapeDtypeStruct((frames, 2 * TWO), low),
            jax.ShapeDtypeStruct((TWO, frames), low),
            jax.ShapeDtypeStruct((frames, TWO), low),
            jax.ShapeDtypeStruct((TWO, frames), low),
        ],
        input_output_aliases={first + i: i for i in range(len(earlier))},
        compiler_params=params(30),
        cost_estimate=cost(2),
        name="project",
    )(*inputs)


def attend_kernel(q_ref, member_ref, k_ref, vt_ref, att_ref, low_ref, log_ref, *score_refs):
    frames = k_ref.shape[0]
    step = min(frames, 1024)
    queries = q_ref[...] * 0.125
    member = member_ref[...]
    bests, halves = [], []
    for head, score_ref in enumerate(score_refs):
        wide = jnp.concatenate([of_head(queries, head), member], axis=1)
        largest = jnp.full((1, BLOCK), -BIG, jnp.float32)
        for start in range(0, frames, step):
            scores = dot_t(k_ref[start:start + step, :], wide)
            score_ref[start:start + step, :] = scores
            largest = jnp.maximum(largest, jnp.max(scores, axis=0, keepdims=True))
        bests.append(largest)
    for head, score_ref in enumerate(score_refs):
        total = jnp.zeros((1, BLOCK), jnp.float32)
        out = jnp.zeros((TWO, BLOCK), jnp.float32)
        for start in range(0, frames, step):
            weights = jnp.exp(score_ref[start:start + step, :] - bests[head])
            total = total + jnp.sum(weights, axis=0, keepdims=True)
            out = out + matmul(vt_ref[:, start:start + step], weights.astype(jnp.bfloat16))
        halves.append(out[head * HEAD:(head + 1) * HEAD, :] / total)
        log_ref[head:head + 1, :] = bests[head] + jnp.log(total)
    attended = jnp.concatenate(halves, axis=0).T
    att_ref[...] = attended
    low_ref[...] = attended.astype(jnp.bfloat16)


def block_spec(width):
    return pl.BlockSpec((BLOCK, width), lambda i: (i, 0))


def attend(q, member, k, vt):
    frames = q.shape[0]
    return pl.pallas_call(
        attend_kernel,
        grid=(frames // BLOCK,),
        in_specs=[block_spec(TWO), block_spec(TWO), whole_spec(frames, 2 * TWO),
                  whole_spec(TWO, frames)],
        out_specs=[block_spec(TWO), block_spec(TWO), pl.BlockSpec((8, BLOCK), lambda i: (0, i))],
        out_shape=[
            jax.ShapeDtypeStruct((frames, TWO), jnp.float32),
            jax.ShapeDtypeStruct((frames, TWO), jnp.bfloat16),
            jax.ShapeDtypeStruct((8, frames), jnp.float32),
        ],
        scratch_shapes=[pltpu.VMEM((frames, BLOCK), jnp.float32)] * 2,
        compiler_params=params(26),
        cost_estimate=cost(18),
        name="attend",
    )(q, member, k, vt)


def attend_back_kernel(q_ref, member_ref, grad_ref, att_ref, log_ref, cos_ref, sin_ref, cos_all_ref,
                       sin_all_ref, k_ref, kt_ref, v_ref, g_ref, dk_ref, dv_ref):
    block = pl.program_id(0)
    frames = k_ref.shape[0]
    step = min(frames, 512)

    @pl.when(block == 0)
    def _():
        dk_ref[...] = jnp.zeros_like(dk_ref)
        dv_ref[...] = jnp.zeros_like(dv_ref)

    queries = q_ref[...] * 0.125
    member = member_ref[...]
    grad = grad_ref[...]
    mixed = (grad.astype(jnp.float32) * att_ref[...]).T
    halves = []
    wides, grads, deltas = [], [], []
    for head in range(2):
        wides.append(jnp.concatenate([of_head(queries, head), member], axis=1))
        grads.append(of_head(grad, head))
        deltas.append(jnp.sum(mixed[head * HEAD:(head + 1) * HEAD, :], axis=0, keepdims=True))
    totals = [jnp.zeros((TWO, ROWS), jnp.float32) for _ in range(2)]
    for start in range(0, frames, step):
        part = slice(start, start + step)
        dk = dk_ref[part, :]
        dv = dv_ref[part, :]
        for head in range(2):
            scores = dot_t(k_ref[part, :], wides[head])
            weights = jnp.exp(scores - log_ref[head:head + 1, :])
            grad_weights = dot_t(v_ref[part, :], grads[head])
            grad_scores = (weights * (grad_weights - deltas[head])).astype(jnp.bfloat16)
            dv = dv + matmul(weights.astype(jnp.bfloat16), grads[head])
            dk = dk + matmul(grad_scores, wides[head][:, :TWO])
            totals[head] = totals[head] + matmul(kt_ref[:, part], grad_scores)
        dk_ref[part, :] = dk
        dv_ref[part, :] = dv
    dq = jnp.concatenate([totals[0][:HEAD, :], totals[1][HEAD:, :]], axis=0).T * 0.125
    here = pl.ds(pl.multiple_of(block * ROWS, ROWS), ROWS)
    g_ref[here, :TWO] = turn(dq, cos_ref[...], -sin_ref[...]).astype(jnp.bfloat16)

    @pl.when(block == pl.num_programs(0) - 1)
    def _():
        turned = turn(dk_ref[...], cos_all_ref[...], -sin_all_ref[...])
        g_ref[:, TWO:2 * TWO] = turned.astype(jnp.bfloat16)
        g_ref[:, 2 * TWO:] = dv_ref[...].astype(jnp.bfloat16)


def attend_back(q, member, grad, att, log_total, cosine, sine, k, kt, v):
    frames = q.shape[0]
    return pl.pallas_call(
        attend_back_kernel,
        grid=(frames // ROWS,),
        in_specs=[rows_spec(TWO), rows_spec(TWO), rows_spec(TWO), rows_spec(TWO), cols_spec(8),
                  rows_spec(TWO), rows_spec(TWO), whole_spec(frames, TWO), whole_spec(frames, TWO),
                  whole_spec(frames, 2 * TWO), whole_spec(TWO, frames), whole_spec(frames, TWO)],
        out_specs=whole_spec(frames, 3 * TWO),
        out_shape=jax.ShapeDtypeStruct((frames, 3 * TWO), jnp.bfloat16),
        scratch_shapes=[pltpu.VMEM((frames, TWO), jnp.float32),
                        pltpu.VMEM((frames, TWO), jnp.float32)],
        compiler_params=params(VMEM_MIB),
        cost_estimate=cost(27),
        name="attend_back",
    )(q, member, grad, att, log_total, cosine, sine, cosine, sine, k, kt, v)


def three_terms(values):
    high = lax.reduce_precision(values, 8, 7)
    middle = lax.reduce_precision(values - high, 8, 7)
    return [high, middle, values - high - middle]


def standardize(rows):
    centered = rows - jnp.mean(rows, axis=1, keepdims=True)
    inverse = lax.rsqrt(jnp.mean(centered * centered, axis=1, keepdims=True) + 1e-06)
    return centered * inverse, inverse


def sum_of_clips(clip_ref, values):
    ids = lax.broadcasted_iota(jnp.int32, (CLIPS, clip_ref.shape[1]), 0)
    chosen = jnp.where(clip_ref[...] == ids, 1.0, 0.0).astype(jnp.bfloat16)
    high = values.astype(jnp.bfloat16)
    rest = values - high.astype(jnp.float32)
    middle = rest.astype(jnp.bfloat16)
    last = (rest - middle.astype(jnp.float32)).astype(jnp.bfloat16)
    return matmul(chosen, high) + matmul(chosen, middle) + matmul(chosen, last)


def beside(ref, tiles, rows):
    return jnp.concatenate([ref[tile, rows, :] for tile in tiles], axis=1)


def tile_index(away, apart):
    return 16 * (away % 2) + 8 * (away // 2) + 4 * (apart % 2) + apart // 2


def middle_kernel(mine_ref, x_ref, member_ref, clip_ref, cot_any, emb_any, tiles_ref,
                  result_any, grad_middle_ref, grad_att_ref, grad_emb_ref, left_any, right_any,
                  out_ref, up_ref, down_ref, cot_ref, emb_ref, result_ref, left_ref, right_ref,
                  sems, branch_ref, low_ref, act_ref, slope_ref, wide_ref):
    low = jnp.bfloat16
    act_t_ref, ffn_t_ref = left_ref.at[:2 * D], left_ref.at[2 * D:3 * D]
    mine_t_ref = left_ref.at[3 * D:]
    g_ffn_ref, g_attn_ref = right_ref.at[:, :D], right_ref.at[:, 3 * D:]
    g_hidden_ref = right_ref.at[:, D:3 * D]
    copies = [
        pltpu.make_async_copy(source, target, sems.at[i])
        for i, (source, target) in enumerate((
            (tiles_ref.at[:, pl.ds(0, 256), :], out_ref),
            (emb_any, emb_ref),
            (cot_any, cot_ref),
            (tiles_ref.at[:, pl.ds(256, 512), :], up_ref),
            (tiles_ref.at[:, pl.ds(768, 512), :], down_ref),
        ))
    ]
    for copy in copies:
        copy.start()
    stores = [
        pltpu.make_async_copy(source, target, sems.at[len(copies) + i])
        for i, (source, target) in enumerate((
            (mine_t_ref, left_any.at[3 * D:]),
            (ffn_t_ref, left_any.at[2 * D:3 * D]),
            (g_ffn_ref, right_any.at[:, :D]),
            (act_t_ref, left_any.at[:2 * D]),
            (result_ref, result_any),
            (g_hidden_ref, right_any.at[:, D:3 * D]),
            (g_attn_ref, right_any.at[:, 3 * D:]),
        ))
    ]

    def tile(b, s):
        return SEQ * b + s

    member = member_ref[...]

    def modulation(index):
        return matmul(member, emb_ref[:, index * D:(index + 1) * D])

    def cols(n, width=256):
        return pl.ds(pl.multiple_of(n * width, width), width)

    every = slice(None)
    mine = jnp.concatenate([mine_ref[j] for j in range(SEQ)], axis=1)
    low_ref[...] = mine
    mine_t_ref[...] = mine.T
    stores[0].start()
    copies[0].wait()

    @pl.loop(0, 4)
    def _(n):
        total = jnp.zeros((ROWS, 256), jnp.float32)
        for b in range(REPLICAS):
            weight = beside(out_ref, [tile(b, 2 * n), tile(b, 2 * n + 1)], every)
            total = total + matmul(low_ref[:, 256 * b:256 * b + 256], weight)
        branch_ref[:, cols(n)] = total

    copies[1].wait()
    gate_attn = modulation(2)
    branch = branch_ref[...]
    middle = x_ref[...].astype(jnp.float32) + gate_attn * branch
    normed, inverse = standardize(middle)
    scale_ffn = modulation(4)
    ffn_input = normed * (1.0 + scale_ffn) + modulation(3)
    low_ref[...] = ffn_input.astype(low)
    ffn_t_ref[...] = ffn_input.T.astype(low)
    gate_ffn = modulation(5)
    copies[2].wait()
    cot = cot_ref[...].astype(jnp.float32)
    g_ffn_ref[...] = (cot * gate_ffn).astype(low)
    stores[1].start()
    stores[2].start()
    copies[3].wait()

    @pl.loop(0, 8)
    def _(n):
        hidden = jnp.zeros((ROWS, 256), jnp.float32)
        for b in range(REPLICAS):
            index = tile(b, n)
            weight = jnp.concatenate([up_ref[index, :256, :], up_ref[index, 256:, :]], axis=1)
            hidden = hidden + matmul(low_ref[:, 256 * b:256 * b + 256], weight)
        root = math.sqrt(2.0 / math.pi)
        squared = hidden * hidden
        bent = jnp.tanh(root * (hidden + 0.044715 * (squared * hidden)))
        half = 0.5 * (1.0 + bent)
        activated = hidden * half
        slope = half + 0.5 * hidden * (1.0 - bent * bent) * (
            root * (1.0 + (3.0 * 0.044715) * squared)
        )
        act_ref[:, cols(n)] = activated.astype(low)
        act_t_ref[cols(n), :] = activated.T.astype(low)
        slope_ref[:, cols(n)] = slope

    stores[3].start()
    copies[4].wait()

    @pl.loop(0, 4)
    def _(n):
        total = jnp.zeros((ROWS, 256), jnp.float32)
        for b in range(REPLICAS):
            weight = beside(down_ref, [tile(b, 2 * n), tile(b, 2 * n + 1)], every)
            total = total + matmul(act_ref[:, 512 * b:512 * b + 512], weight)
        wide_ref[:, cols(n)] = total

    ffn_branch = wide_ref[...]
    result_ref[...] = (middle + gate_ffn * ffn_branch).astype(low)
    stores[4].start()
    grad_emb_ref[:, 3 * D:] = sum_of_clips(clip_ref, cot * ffn_branch)

    @pl.loop(0, REPLICAS)
    def _(b):
        weight = beside(down_ref, [tile(b, s) for s in range(SEQ)], every)
        grad = dot_t(g_ffn_ref[...], weight)
        here = cols(b, 512)
        g_hidden_ref[:, here] = (grad * slope_ref[:, here]).astype(low)

    stores[5].start()

    @pl.loop(0, REPLICAS)
    def _(b):
        weight = jnp.concatenate(
            [up_ref[tile(b, s), 256 * k:256 * k + 256, :] for s in range(SEQ) for k in range(2)],
            axis=1,
        )
        wide_ref[:, cols(b)] = dot_t(g_hidden_ref[...], weight)

    grad_ffn_input = wide_ref[...]
    grad_emb_ref[:, D:2 * D] = sum_of_clips(clip_ref, grad_ffn_input)
    grad_emb_ref[:, 2 * D:3 * D] = sum_of_clips(clip_ref, grad_ffn_input * normed)
    spread = grad_ffn_input * (1.0 + scale_ffn)
    grad_middle = cot + inverse * (
        spread
        - jnp.mean(spread, axis=1, keepdims=True)
        - normed * jnp.mean(spread * normed, axis=1, keepdims=True)
    )
    grad_middle_ref[...] = grad_middle
    grad_emb_ref[:, :D] = sum_of_clips(clip_ref, grad_middle * branch)
    g_attn_ref[...] = (grad_middle * gate_attn).astype(low)
    stores[6].start()

    @pl.loop(0, REPLICAS)
    def _(b):
        weight = beside(out_ref, [tile(b, s) for s in range(SEQ)], every)
        grad = dot_t(g_attn_ref[...], weight).astype(low)
        grad_att_ref[2 * b] = grad[:, :TWO]
        grad_att_ref[2 * b + 1] = grad[:, TWO:]

    for store in stores:
        store.wait()


def middle_part(mine, x, cot, member, clip_row, emb, tiles):
    low = jnp.bfloat16
    shapes = [
        ((ROWS, D), low), ((ROWS, D), jnp.float32), ((SEQ, ROWS, TWO), low),
        ((CLIPS, 4 * D), jnp.float32), ((4 * D, ROWS), low), ((ROWS, 4 * D), low),
    ]
    vmem, anywhere = pl.BlockSpec(memory_space=pltpu.VMEM), pl.BlockSpec(memory_space=pl.ANY)
    return pl.pallas_call(
        middle_kernel,
        in_specs=[vmem] * 4 + [anywhere] * 3,
        out_specs=[anywhere, vmem, vmem, vmem, anywhere, anywhere],
        out_shape=[jax.ShapeDtypeStruct(shape, dtype) for shape, dtype in shapes],
        scratch_shapes=[
            pltpu.VMEM((32, 256, 128), low),
            pltpu.VMEM((32, 512, 128), low),
            pltpu.VMEM((32, 512, 128), low),
            pltpu.VMEM((ROWS, D), low),
            pltpu.VMEM((TWO, 6 * D), low),
            pltpu.VMEM((ROWS, D), low),
            pltpu.VMEM((4 * D, ROWS), low),
            pltpu.VMEM((ROWS, 4 * D), low),
            pltpu.SemaphoreType.DMA((12,)),
            pltpu.VMEM((ROWS, D), jnp.float32),
            pltpu.VMEM((ROWS, D), low),
            pltpu.VMEM((ROWS, 2 * D), low),
            pltpu.VMEM((ROWS, 2 * D), jnp.float32),
            pltpu.VMEM((ROWS, D), jnp.float32),
        ],
        compiler_params=pltpu.CompilerParams(vmem_limit_bytes=VMEM_MIB * 1024 * 1024),
        cost_estimate=cost(20),
        name="middle",
    )(mine, x, member, clip_row, cot, emb, *tiles)


def weight_grads_kernel(place_ref, down_l, up_l, out_l, right_ref, down_o, up_o, out_o, other_ref,
                        away_d_ref, keep_d_ref, away_u_ref, keep_u_ref):
    low = jnp.bfloat16
    z, y = place_ref[2] // 2, place_ref[2] % 2
    lefts = [
        jnp.concatenate([mine[...], other[...]], axis=1)
        for mine, other in ((down_l, down_o), (up_l, up_o), (out_l, out_o))
    ]

    def product(left, first, block):
        here = pl.ds(pl.multiple_of(first + 256 * block, 256), 256)
        right = jnp.concatenate([right_ref[:, here], other_ref[:, here]], axis=0)
        return matmul(left, right).astype(low)

    def fill(ref):
        @pl.loop(0, 4)
        def _(k):
            block = z ^ k
            for left, first, rows in ((lefts[0], 0, slice(0, 512)), (lefts[2], 3 * D, slice(512, 768))):
                grad = product(left, first, block)
                ref[4 * y + k, rows, :] = grad[:, :128]
                ref[4 - 4 * y + k, rows, :] = grad[:, 128:]
            for side, up_ref in enumerate((keep_u_ref, away_u_ref)):
                grad = product(lefts[1], D, 2 * block + (y ^ side))
                up_ref[0, k, :256, :] = grad[:, :128]
                up_ref[0, k, 256:, :] = grad[:, 128:]

    @pl.when(pl.program_id(0) == 0)
    def _():
        fill(away_d_ref)

    @pl.when(pl.program_id(0) == 1)
    def _():
        fill(keep_d_ref)


def weight_grads(place, left, right, other_left, other_right):
    low = jnp.bfloat16

    def target(i, p):
        return 2 * jnp.where(i == 0, 1 - p[0], p[0]) + p[1]

    down = pl.BlockSpec((512, ROWS), lambda i, p: (target(i, p), 0))
    up = pl.BlockSpec((256, ROWS), lambda i, p: (8 + target(i, p), 0))
    out = pl.BlockSpec((256, ROWS), lambda i, p: (12 + target(i, p), 0))
    wide = pl.BlockSpec((ROWS, 4 * D), lambda i, p: (0, 0))
    whole = pl.BlockSpec((SEQ, 768, 128), lambda i, p: (0, 0, 0))
    part = pl.BlockSpec((1, 4, 512, 128), lambda i, p: (1 - i, 0, 0, 0))
    return pl.pallas_call(
        weight_grads_kernel,
        grid_spec=pltpu.PrefetchScalarGridSpec(
            num_scalar_prefetch=1,
            grid=(2,),
            in_specs=[down, up, out, wide] * 2,
            out_specs=[whole, whole, part, part],
        ),
        out_shape=[jax.ShapeDtypeStruct((SEQ, 768, 128), low)] * 2
        + [jax.ShapeDtypeStruct((2, 4, 512, 128), low)] * 2,
        compiler_params=params(VMEM_MIB),
        cost_estimate=cost(9),
        name="weight_grads",
    )(place, left, left, left, right, other_left, other_left, other_left, other_right)


def clip_grads_kernel(place_ref, x_ref, clip_ref, g_ref, w_ref, out_ref):
    @pl.when(pl.program_id(0) == 0)
    def _():
        out_ref[...] = jnp.zeros_like(out_ref)

    normed, _ = standardize(x_ref[...].astype(jnp.float32))
    grad = jnp.concatenate(
        [dot_t(g_ref[...], w_ref[b ^ place_ref[1]]) for b in range(REPLICAS)], axis=1
    )
    out_ref[:, :D] += sum_of_clips(clip_ref, grad)
    out_ref[:, D:] += sum_of_clips(clip_ref, grad * normed)


def clip_grads(places, x, clip_row, g_heads, heads_w):
    frames = x.shape[0]
    return pl.pallas_call(
        clip_grads_kernel,
        grid=(frames // ROWS,),
        in_specs=[pl.BlockSpec(memory_space=pltpu.SMEM), rows_spec(D), cols_spec(1),
                  rows_spec(3 * TWO),
                  pl.BlockSpec((REPLICAS, ROWS, 3 * TWO), lambda i: (0, 0, 0))],
        out_specs=whole_spec(CLIPS, 2 * D),
        out_shape=jax.ShapeDtypeStruct((CLIPS, 2 * D), jnp.float32),
        compiler_params=params(VMEM_MIB),
        cost_estimate=cost(9),
        name="clip_grads",
    )(places, x, clip_row, g_heads, heads_w)


def last_kernel(place_ref, own_ref, x_ref, grad_middle_ref, member_ref, emb_ref, *refs):
    *tile_refs, out_ref, wide_ref = refs
    grads = jnp.concatenate([own_ref[place_ref[2] ^ s] for s in range(SEQ)], axis=1)

    def tile(away, apart):
        index = tile_index(away, apart)
        for ref in tile_refs:
            if index < ref.shape[0]:
                return ref[index, ref.shape[1] - 768:, :]
            index -= ref.shape[0]

    for away in range(REPLICAS):
        weight = jnp.concatenate(
            [
                tile(away, s)[256 * k:256 * k + 256, :]
                for s in range(SEQ)
                for k in range(3)
            ],
            axis=1,
        )
        b = (2 * place_ref[0] + place_ref[1]) ^ away
        wide_ref[:, pl.ds(pl.multiple_of(b * 256, 256), 256)] = dot_t(grads, weight)

    normed, inverse = standardize(x_ref[...].astype(jnp.float32))
    spread = wide_ref[...] * (1.0 + matmul(member_ref[...], emb_ref[:, D:2 * D]))
    grad = grad_middle_ref[...] + inverse * (
        spread
        - jnp.mean(spread, axis=1, keepdims=True)
        - normed * jnp.mean(spread * normed, axis=1, keepdims=True)
    )
    out_ref[...] = grad.astype(jnp.bfloat16)


def last_part(place, own, x, grad_middle, member, emb, tiles):
    vmem = pl.BlockSpec(memory_space=pltpu.VMEM)
    return pl.pallas_call(
        last_kernel,
        in_specs=[pl.BlockSpec(memory_space=pltpu.SMEM)] + [vmem] * (5 + len(tiles)),
        out_specs=vmem,
        out_shape=jax.ShapeDtypeStruct((ROWS, D), jnp.bfloat16),
        scratch_shapes=[pltpu.VMEM((ROWS, D), jnp.float32)],
        compiler_params=pltpu.CompilerParams(vmem_limit_bytes=30 * 1024 * 1024),
        cost_estimate=cost(4),
        name="last",
    )(place, own, x, grad_middle, member, emb, *tiles)


def after(value, *others):
    return lax.optimization_barrier((value,) + others)[0]


def together(*values):
    return lax.optimization_barrier(values)


def plus(*terms):
    total = terms[0].astype(jnp.float32)
    for term in terms[1:]:
        total = total + term.astype(jnp.float32)
    return total


def clip_lanes(clip, terms):
    lane = jnp.arange(TWO, dtype=jnp.int32)[None, :]
    return (clip[:, None] == lane % CLIPS) & (lane < terms * CLIPS)


def body_fast(
    tokens, w_query, w_key, w_value, w_out, w_ada, w_up, w_down,
    segments, validity, timesteps, cotangent,
):
    highest = lax.Precision.HIGHEST
    low = jnp.bfloat16
    wide = jnp.float32
    replica = lax.axis_index("batch")
    x = tokens[0]
    frame_count = x.shape[0]
    frames = frame_count * SEQ
    segment = segments[0]

    seat = lax.axis_index("seq").astype(jnp.int32)
    z, y = seat // 2, seat % 2
    place = jnp.stack([replica // 2, replica % 2, seat]).astype(jnp.int32)
    mine_w = jnp.concatenate([w_out, w_up[:, :128], w_up[:, 128:], w_down], axis=0).astype(low)

    z1, z2, y0 = swap(x, "seq", 2), swap(x, "seq", 4), swap(x, "seq", 1)
    times = lax.all_gather(timesteps[0], "batch", axis=0, tiled=True)
    silu_all = jax.nn.silu(time_embedding(times)).astype(low)
    depth = w_ada.shape[0]
    silu_part = lax.dynamic_slice_in_dim(silu_all, replica * depth, depth, 1)
    emb_part = matmul(silu_part, w_ada.astype(low)).reshape(REPLICAS, CLIPS, -1)
    emb_cols = lax.all_to_all(emb_part, "batch", 0, 0, tiled=True)
    emb_cols = jnp.sum(emb_cols, axis=0)
    own_codes = (segment * 2 + (validity[0] == 1)).astype(wide)
    cols = emb_cols.shape[1]
    own_codes = jnp.pad(own_codes, (0, 8 * cols - frame_count)).reshape(8, cols)
    packed = jnp.concatenate([emb_cols, own_codes])
    packed = jnp.broadcast_to(packed[None], (SEQ,) + packed.shape)
    heads_w = jnp.concatenate([w_query, w_key, w_value], axis=1).astype(low)
    heads_w = jnp.stack([heads_w, swap(heads_w, "batch", 1)])
    z1, z2, y0, packed, heads_w, mine_w = together(z1, z2, y0, packed, heads_w, mine_w)
    tiles_w = (lax.all_gather(mine_w, ("batch", "seq"), axis=0),)
    packed = exchange(packed)
    z3 = swap(z2, "seq", 2)
    y1, y2 = swap(z1, "seq", 1), swap(z2, "seq", 1)
    heads_x = swap(heads_w, "batch", 2)
    z3, heads_x = together(z3, heads_x)
    y3 = swap(z3, "seq", 1)
    mine_h = jnp.concatenate([w_query, w_key, w_value], axis=0).astype(low)
    mine_h = after(mine_h, z3)
    h_z1, h_z2 = swap(mine_h, "seq", 2), swap(mine_h, "seq", 4)
    heads_w = jnp.concatenate([heads_w, heads_x])
    emb = packed[:, :CLIPS]
    codes = packed[:, CLIPS:].reshape(SEQ, -1)[:, :frame_count].reshape(frames).astype(jnp.int32)
    clip = codes // 2
    clip_row = clip[None, :]
    tri = jnp.arange(frame_count)[:, None] > jnp.arange(frame_count)[None, :]
    ids = jnp.arange(CLIPS, dtype=jnp.int32)
    one_hot = (clip.reshape(SEQ, frame_count)[:, :, None] == ids).astype(low)
    within = jnp.einsum("ij,njc->nic", tri.astype(low), one_hot, preferred_element_type=wide)
    counts = jnp.sum(one_hot.astype(wide), axis=1)
    offsets = jnp.cumsum(counts, axis=0) - counts
    position = jnp.sum(one_hot.astype(wide) * (within + offsets[:, None, :]), axis=2)
    half = HEAD // 2
    frequency = jnp.exp(-math.log(10000.0) * jnp.arange(half, dtype=wide) / half)
    angle = position.reshape(frames)[:, None] * jnp.tile(frequency, 4)[None, :]
    cosine, sine = jnp.cos(angle), jnp.sin(angle)
    member = clip_lanes(clip, 3).astype(low)
    allowed = clip_lanes(jnp.where(codes % 2 == 1, clip, -1), 1)
    inside = jnp.arange(TWO, dtype=jnp.int32)[None, :] < CLIPS
    bar = jnp.where(inside & ~allowed, -BIG, 0.0).astype(low)
    emb, y1, y2 = together(after(emb, heads_w, member, cosine), y1, y2)
    emb = emb.transpose(1, 0, 2).reshape(CLIPS, -1)
    emb = jnp.concatenate(
        [t.astype(low) for t in three_terms(emb)] + [jnp.zeros((TWO - 3 * CLIPS, 6 * D), low)],
        axis=0,
    )

    tables = (member, bar, cosine, sine, emb, heads_w)
    places = jnp.stack([seat, replica.astype(jnp.int32)])
    earlier = project(places, 0, (x, z1, z2, z3), *tables, ())
    y3, h_z1, h_z2, earlier = together(y3, h_z1, h_z2, earlier)
    h_z3 = swap(h_z2, "seq", 2)
    x_all, attn_input, q, k, kt, v, vt = project(places, 1, (y0, y1, y2, y3), *tables, earlier)
    attended, attended_low, log_total = attend(q, member, k, vt)
    attended_low, h_z3 = together(attended_low, h_z3)
    mine = exchange(attended_low.reshape(SEQ, frame_count, TWO))
    h_z = jnp.stack([mine_h, h_z1, h_z2, h_z3])
    mine, h_z = together(mine, h_z)
    h_y, h_x = swap(h_z, "seq", 1), swap(h_z, "batch", 2)

    own_member = clip_lanes(segment, 3).astype(low)
    result, grad_middle, grad_att, grad_emb, left, right = middle_part(
        mine, x, cotangent[0], own_member, segment[None, :], emb, tiles_w
    )
    left, h_y, h_x = together(left, h_y, h_x)
    other_left, other_right = swap(left, "batch", 1), swap(right, "batch", 1)
    h_first = jnp.concatenate([h_z, h_y, h_x])
    other_left, other_right, h_first = together(other_left, other_right, h_first)
    away_d, keep_d, away_u, keep_u = weight_grads(place, left, right, other_left, other_right)
    grad_heads = exchange(grad_att).reshape(frames, TWO)
    from_x = swap(away_d, "batch", 2)
    from_y = swap(away_u, "seq", 1)
    grad_heads = after(grad_heads, away_d, away_u)

    g_heads = attend_back(
        q, member, grad_heads, attended, log_total, cosine, sine, k, kt, v
    )
    own = exchange(g_heads.reshape(SEQ, frame_count, 3 * TWO))
    from_y = after(from_y, g_heads)
    to_x_u = plus(keep_u[1], from_y[1]).astype(low)
    from_x_u = swap(to_x_u, "batch", 2)
    from_x = after(from_x, to_x_u)
    to_y_d = plus(keep_d[4:], from_x[4:]).astype(low)
    from_y_d = swap(to_y_d, "seq", 1)
    h_yx = swap(after(h_y, to_y_d), "batch", 2)
    h_first_core = swap(after(h_first, to_x_u), "batch", 1)
    g_heads = after(g_heads, to_y_d, to_x_u)
    late = clip_grads(places, x_all, clip_row, g_heads, heads_w)
    grad_heads_w = matmul(attn_input.T, g_heads).astype(low).reshape(2, 2, ROWS, 3 * TWO)
    late, grad_heads_w, from_y_d, from_x_u, h_first_core = together(
        late, grad_heads_w, from_y_d, from_x_u, h_first_core
    )
    part = jnp.concatenate(
        [
            plus(keep_u[0], from_y[0], from_x_u).astype(low),
            plus(keep_d[:4], from_x[:4], from_y_d).astype(low),
        ],
        axis=1,
    )
    late, own = together(late, own)
    grad_emb = jnp.concatenate([late, grad_emb], axis=1)
    grad_emb = exchange(grad_emb.reshape(CLIPS, SEQ, -1).transpose(1, 0, 2))
    grad_emb = jnp.sum(grad_emb, axis=0)
    x_place, core_place = replica // 2, replica % 2
    keep_h = lax.dynamic_index_in_dim(grad_heads_w, core_place, 1, False)
    other_h = swap(lax.dynamic_index_in_dim(grad_heads_w, 1 - core_place, 1, False), "batch", 1)
    h_yx_core = swap(after(h_yx, part), "batch", 1)
    from_z = [swap(part[k], "seq", 2 * k) for k in range(1, 4)]
    both_h = plus(keep_h, other_h).astype(low)
    away_h = swap(lax.dynamic_index_in_dim(both_h, 1 - x_place, 0, False), "batch", 2)

    grad_tokens = last_part(place, own, x, grad_middle, own_member, emb,
        (h_first, h_yx, h_first_core, h_yx_core),
    )
    grad_emb = lax.all_gather(grad_emb, "batch", axis=0, tiled=True)
    final_a = jnp.dot(silu_part.astype(wide).T, grad_emb, precision=highest)
    grad_tokens, final_a, away_h, *from_z = together(grad_tokens, final_a, away_h, *from_z)
    final_heads = plus(lax.dynamic_index_in_dim(both_h, x_place, 0, False), away_h)
    total = plus(part[0], *from_z)
    final_u = jnp.concatenate([total[:256], total[256:512]], axis=1)
    final_d, final_o = total[512:1024], total[1024:]
    width = w_query.shape[1]
    return (
        result[None],
        grad_tokens[None],
        final_heads[:, :width],
        final_heads[:, width:2 * width],
        final_heads[:, 2 * width:],
        final_o,
        final_a,
        final_u,
        final_d,
    )


def solution(mesh):
    fits = mesh.shape["seq"] == SEQ and mesh.shape["batch"] == REPLICAS
    chosen = body_fast if fits else body
    return jax.shard_map(
        chosen,
        mesh=mesh,
        in_specs=(
            P("batch", "seq", None),
            P("batch", "seq"),
            P("batch", "seq"),
            P("batch", "seq"),
            P("batch", "seq"),
            P("batch", "seq"),
            P("batch", "seq"),
            P("batch", "seq"),
            P("batch", "seq"),
            P("batch", "seq"),
            P("batch", None),
            P("batch", "seq", None),
        ),
        out_specs=(
            P("batch", "seq", None),
            P("batch", "seq", None),
            P("batch", "seq"),
            P("batch", "seq"),
            P("batch", "seq"),
            P("batch", "seq"),
            P("batch", "seq"),
            P("batch", "seq"),
            P("batch", "seq"),
        ),
        check_vma=False,
    )
```

```python
from functools import partial
import math

import jax
import jax.numpy as jnp
from jax import lax
from jax.experimental import pallas as pl
from jax.experimental.pallas import tpu as pltpu
from jax.sharding import PartitionSpec as P

D = 1024
HEADS = 16
HEAD = 64
CLIPS = 16


def carried_in(part, axis, combine, identity):
    place = lax.axis_index(axis)
    gathered = lax.all_gather(part, axis)
    state = jnp.zeros_like(part) + jnp.asarray(identity, part.dtype)

    def one(step, state):
        return combine(state, lax.dynamic_index_in_dim(gathered, step, 0, False))

    return lax.fori_loop(0, place, one, state)


def matmul(left, right):
    return jnp.dot(left, right, preferred_element_type=jnp.float32)


def time_embedding(timestep_row):
    half_width = D // 2
    frequency = jnp.exp(-math.log(10000.0) * jnp.arange(half_width, dtype=jnp.float32) / half_width)
    angle = timestep_row.astype(jnp.float32)[:, None] * frequency[None, :]
    return jnp.concatenate([jnp.sin(angle), jnp.cos(angle)], axis=1)


def rotate_pairs(vectors, position, direction):
    half_size = vectors.shape[-1] // 2
    frequency = jnp.exp(-math.log(10000.0) * jnp.arange(half_size, dtype=jnp.float32) / half_size)
    angle = position[:, None] * frequency[None, :]
    cosine = jnp.cos(angle)[:, None, :]
    sine = jnp.sin(angle)[:, None, :] * direction
    first_half = vectors[..., :half_size]
    second_half = vectors[..., half_size:]
    return jnp.concatenate(
        [first_half * cosine - second_half * sine, second_half * cosine + first_half * sine],
        axis=-1,
    )


def normalize(inputs):
    centered = inputs - jnp.mean(inputs, axis=-1, keepdims=True)
    inverse = lax.rsqrt(jnp.mean(centered * centered, axis=-1, keepdims=True) + 1e-06)
    return (centered * inverse, inverse)


def norm_backward(grad_normed, normed, inverse):
    mean_grad = jnp.mean(grad_normed, axis=-1, keepdims=True)
    mean_mixed = jnp.mean(grad_normed * normed, axis=-1, keepdims=True)
    return inverse * (grad_normed - mean_grad - normed * mean_mixed)


def add_counts(earlier, later):
    return earlier + later


def block_rows_for(row_count):
    chosen = 1
    for candidate in range(1, 513):
        if row_count % candidate == 0:
            chosen = candidate
    return chosen


def stack_blocks(shard_piece):
    row_count = shard_piece[0].shape[0]
    block_rows = block_rows_for(row_count)
    block_count = row_count // block_rows
    return (
        shard_piece[0].reshape(block_count, block_rows, HEADS, HEAD),
        shard_piece[1].reshape(block_count, block_rows, HEADS, HEAD),
        shard_piece[2].reshape(block_count, block_rows),
    )


def forward_block(carried, key_block, queries, query_codes):
    running_max, running_sum, accumulated = carried
    key_rows, values, key_codes = key_block
    scores = (
        jnp.einsum("qhe,khe->hqk", queries, key_rows, preferred_element_type=jnp.float32) * 0.125
    )
    allowed = (query_codes[:, None] == key_codes.astype(jnp.float32)[None, :])[None]
    masked = jnp.where(allowed, scores, -1e30)
    new_max = jnp.maximum(running_max, jnp.max(masked, axis=2))
    rescale = jnp.exp(running_max - new_max)
    weights = jnp.where(allowed, jnp.exp(masked - new_max[:, :, None]), 0.0)
    running_sum = running_sum * rescale + jnp.sum(weights, axis=2)
    product = jnp.einsum(
        "hqk,khe->qhe", weights, values.astype(jnp.float32), precision=lax.Precision.HIGHEST
    )
    accumulated = accumulated * rescale.T[:, :, None] + product
    return (new_max, running_sum, accumulated)


def block_grads(key_block, queries, query_codes, grad_attn, log_total, delta_rows):
    key_rows, values, key_codes = key_block
    scores = (
        jnp.einsum("qhe,khe->hqk", queries, key_rows, preferred_element_type=jnp.float32) * 0.125
    )
    allowed = (query_codes[:, None] == key_codes.astype(jnp.float32)[None, :])[None]
    probabilities = jnp.exp(jnp.where(allowed, scores, -1e30) - log_total[:, :, None])
    grad_probs = jnp.einsum("qhe,khe->hqk", grad_attn, values, preferred_element_type=jnp.float32)
    grad_scores = (probabilities * (grad_probs - delta_rows[:, :, None])).astype(jnp.bfloat16)
    return (probabilities, grad_scores)


def body(
    tokens,
    w_query,
    w_key,
    w_value,
    w_out,
    w_ada,
    w_up,
    w_down,
    segments,
    validity,
    timesteps,
    cotangent,
):
    inputs = tokens[0].astype(jnp.float32)
    segment = segments[0]
    valid_row = validity[0]
    timestep_row = timesteps[0]
    grad_output = cotangent[0].astype(jnp.float32)
    frame_count = inputs.shape[0]
    highest = lax.Precision.HIGHEST
    cols_q, cols_k, cols_v, cols_o, cols_a, cols_u, cols_d = (
        lax.all_gather(w_query.astype(jnp.bfloat16), "seq", axis=1, tiled=True),
        lax.all_gather(w_key.astype(jnp.bfloat16), "seq", axis=1, tiled=True),
        lax.all_gather(w_value.astype(jnp.bfloat16), "seq", axis=1, tiled=True),
        lax.all_gather(w_out.astype(jnp.bfloat16), "seq", axis=1, tiled=True),
        lax.all_gather(w_ada.astype(jnp.bfloat16), "seq", axis=1, tiled=True),
        lax.all_gather(w_up.astype(jnp.bfloat16), "seq", axis=1, tiled=True),
        lax.all_gather(w_down.astype(jnp.bfloat16), "seq", axis=1, tiled=True),
    )
    full_q, full_k, full_v, full_o, full_a, full_u, full_d = (
        lax.all_gather(cols_q, "batch", axis=0, tiled=True),
        lax.all_gather(cols_k, "batch", axis=0, tiled=True),
        lax.all_gather(cols_v, "batch", axis=0, tiled=True),
        lax.all_gather(cols_o, "batch", axis=0, tiled=True),
        lax.all_gather(cols_a, "batch", axis=0, tiled=True),
        lax.all_gather(cols_u, "batch", axis=0, tiled=True),
        lax.all_gather(cols_d, "batch", axis=0, tiled=True),
    )
    silu_time = jax.nn.silu(time_embedding(timestep_row)).astype(jnp.bfloat16)
    emb_rows = matmul(silu_time, full_a)
    member = segment[:, None] == jnp.arange(CLIPS, dtype=jnp.int32)[None, :]
    one_hot = member.astype(jnp.float32)
    counted = member.astype(jnp.int32)
    modulation = jnp.dot(one_hot, emb_rows, precision=highest)
    shift_attn, scale_attn, gate_attn, shift_ffn, scale_ffn, gate_ffn = jnp.split(
        modulation, 6, axis=1
    )
    offsets = carried_in(
        jnp.sum(counted, axis=0), "seq", add_counts, jnp.zeros((CLIPS,), jnp.int32)
    )
    before = jnp.cumsum(counted, axis=0) - counted + offsets[None, :]
    position = jnp.sum(before * counted, axis=1).astype(jnp.float32)
    normed, inverse = normalize(inputs)
    attn_input = (normed * (1.0 + scale_attn) + shift_attn).astype(jnp.bfloat16)
    queries = rotate_pairs(
        matmul(attn_input, full_q).reshape(frame_count, HEADS, HEAD), position, 1.0
    ).astype(jnp.bfloat16)
    key_flat = (
        rotate_pairs(matmul(attn_input, full_k).reshape(frame_count, HEADS, HEAD), position, 1.0)
        .astype(jnp.bfloat16)
        .reshape(frame_count, D)
    )
    value_flat = matmul(attn_input, full_v).astype(jnp.bfloat16)
    key_codes = jnp.where(valid_row == 1, segment, -1).astype(jnp.bfloat16)
    query_codes = segment.astype(jnp.float32)
    start_state = (
        jnp.full((HEADS, frame_count), -1e30, jnp.float32),
        jnp.zeros((HEADS, frame_count), jnp.float32),
        jnp.zeros((frame_count, HEADS, HEAD), jnp.float32),
    )

    def step(state, key_block):
        return (forward_block(state, key_block, queries, query_codes), None)

    running_max, running_sum, accumulated = lax.scan(
        step,
        start_state,
        stack_blocks(
            (
                lax.all_gather(key_flat, "seq", axis=0, tiled=True),
                lax.all_gather(value_flat, "seq", axis=0, tiled=True),
                lax.all_gather(key_codes, "seq", axis=0, tiled=True),
            )
        ),
    )[0]
    attended = accumulated / running_sum.T[:, :, None]
    log_total = running_max + jnp.log(running_sum)
    attended_low = attended.reshape(frame_count, D).astype(jnp.bfloat16)
    attn_branch = matmul(attended_low, full_o)
    middle = inputs + gate_attn * attn_branch
    normed_mid, inverse_mid = normalize(middle)
    ffn_input = (normed_mid * (1.0 + scale_ffn) + shift_ffn).astype(jnp.bfloat16)
    hidden = matmul(ffn_input, full_u)
    activated, gelu_pull = jax.vjp(partial(jax.nn.gelu, approximate=True), hidden)
    activated_low = activated.astype(jnp.bfloat16)
    ffn_branch = matmul(activated_low, full_d)
    result = middle + gate_ffn * ffn_branch
    back_q, back_k, back_v, back_o, back_u, back_d = (
        full_q,
        full_k,
        full_v,
        full_o,
        full_u,
        full_d,
    )
    grad_gate_ffn = grad_output * ffn_branch
    g_ffn = (grad_output * gate_ffn).astype(jnp.bfloat16)
    grad_down_local = matmul(activated_low.T, g_ffn)
    grad_activated = matmul(g_ffn, back_d.T)
    g_hidden = gelu_pull(grad_activated)[0].astype(jnp.bfloat16)
    grad_up_local = matmul(ffn_input.T, g_hidden)
    grad_ffn_input = matmul(g_hidden, back_u.T)
    grad_middle = grad_output + norm_backward(
        grad_ffn_input * (1.0 + scale_ffn), normed_mid, inverse_mid
    )
    grad_scale_ffn = grad_ffn_input * normed_mid
    grad_gate_attn = grad_middle * attn_branch
    g_attn = (grad_middle * gate_attn).astype(jnp.bfloat16)
    grad_out_local = matmul(attended_low.T, g_attn)
    grad_attn = matmul(g_attn, back_o.T).astype(jnp.bfloat16).reshape(frame_count, HEADS, HEAD)
    delta_rows = jnp.einsum("qhe,qhe->hq", grad_attn.astype(jnp.float32), attended)
    zero_query = jnp.zeros((frame_count, HEADS, HEAD), jnp.float32)
    gathered = (
        lax.all_gather(key_flat, "seq", axis=0, tiled=True),
        lax.all_gather(value_flat, "seq", axis=0, tiled=True),
        lax.all_gather(key_codes, "seq", axis=0, tiled=True),
    )
    pack_rows = gathered[0].shape[0]
    grad_attn_wide = grad_attn.astype(jnp.float32)

    def joint_step(total_grad, key_block):
        probabilities, grad_scores = block_grads(
            key_block, queries, query_codes, grad_attn, log_total, delta_rows
        )
        total_grad = total_grad + 0.125 * jnp.einsum(
            "hqk,khe->qhe", grad_scores, key_block[0], preferred_element_type=jnp.float32
        )
        grad_keys = 0.125 * jnp.einsum(
            "hqk,qhe->khe", grad_scores, queries, preferred_element_type=jnp.float32
        )
        grad_values = jnp.einsum("hqk,qhe->khe", probabilities, grad_attn_wide, precision=highest)
        return (total_grad, (grad_keys, grad_values))

    grad_queries_rot, both_grads = lax.scan(joint_step, zero_query, stack_blocks(gathered))
    key_value_terms = jnp.concatenate(
        [both_grads[0].reshape(pack_rows, D), both_grads[1].reshape(pack_rows, D)], axis=1
    )
    key_value_grad = lax.psum_scatter(key_value_terms, "seq", scatter_dimension=0, tiled=True)
    g_query = (
        rotate_pairs(grad_queries_rot, position, -1.0).reshape(frame_count, D).astype(jnp.bfloat16)
    )
    g_key = (
        rotate_pairs(key_value_grad[:, :D].reshape(frame_count, HEADS, HEAD), position, -1.0)
        .reshape(frame_count, D)
        .astype(jnp.bfloat16)
    )
    g_value = key_value_grad[:, D:].astype(jnp.bfloat16)
    grad_query_local = matmul(attn_input.T, g_query)
    grad_key_local = matmul(attn_input.T, g_key)
    grad_value_local = matmul(attn_input.T, g_value)
    grad_attn_input = (
        matmul(g_query, back_q.T) + matmul(g_key, back_k.T) + matmul(g_value, back_v.T)
    )
    grad_inputs = grad_middle + norm_backward(grad_attn_input * (1.0 + scale_attn), normed, inverse)
    grad_modulation = jnp.concatenate(
        [
            grad_attn_input,
            grad_attn_input * normed,
            grad_gate_attn,
            grad_ffn_input,
            grad_scale_ffn,
            grad_gate_ffn,
        ],
        axis=1,
    )
    grad_emb = jnp.dot(one_hot.T, grad_modulation, precision=highest)
    grad_ada_local = jnp.dot(silu_time.astype(jnp.float32).T, grad_emb, precision=highest)
    part_q, part_k, part_v, part_o, part_a, part_u, part_d = (
        lax.psum_scatter(grad_query_local, "seq", scatter_dimension=1, tiled=True),
        lax.psum_scatter(grad_key_local, "seq", scatter_dimension=1, tiled=True),
        lax.psum_scatter(grad_value_local, "seq", scatter_dimension=1, tiled=True),
        lax.psum_scatter(grad_out_local, "seq", scatter_dimension=1, tiled=True),
        lax.psum_scatter(grad_ada_local, "seq", scatter_dimension=1, tiled=True),
        lax.psum_scatter(grad_up_local, "seq", scatter_dimension=1, tiled=True),
        lax.psum_scatter(grad_down_local, "seq", scatter_dimension=1, tiled=True),
    )
    final_q, final_k, final_v, final_o, final_a, final_u, final_d = (
        lax.psum_scatter(
            part_q.astype(jnp.bfloat16), "batch", scatter_dimension=0, tiled=True
        ).astype(jnp.float32),
        lax.psum_scatter(
            part_k.astype(jnp.bfloat16), "batch", scatter_dimension=0, tiled=True
        ).astype(jnp.float32),
        lax.psum_scatter(
            part_v.astype(jnp.bfloat16), "batch", scatter_dimension=0, tiled=True
        ).astype(jnp.float32),
        lax.psum_scatter(
            part_o.astype(jnp.bfloat16), "batch", scatter_dimension=0, tiled=True
        ).astype(jnp.float32),
        lax.psum_scatter(
            part_a.astype(jnp.bfloat16), "batch", scatter_dimension=0, tiled=True
        ).astype(jnp.float32),
        lax.psum_scatter(
            part_u.astype(jnp.bfloat16), "batch", scatter_dimension=0, tiled=True
        ).astype(jnp.float32),
        lax.psum_scatter(
            part_d.astype(jnp.bfloat16), "batch", scatter_dimension=0, tiled=True
        ).astype(jnp.float32),
    )
    return (
        result.astype(jnp.bfloat16)[None],
        grad_inputs.astype(jnp.bfloat16)[None],
        final_q,
        final_k,
        final_v,
        final_o,
        final_a,
        final_u,
        final_d,
    )


TWO = 2 * HEAD
ROWS = 256
BIG = 1e30
SEQ = 8
REPLICAS = 4
VMEM_MIB = 60
BLOCK = 256


def swap(part, axis, distance):
    size = SEQ if axis == "seq" else REPLICAS
    return lax.ppermute(part, axis, [(i, i ^ distance) for i in range(size)])


def exchange(blocks):
    return lax.all_to_all(blocks, "seq", 0, 0, tiled=True)


def turn(vectors, cosine, sine):
    lane = lax.broadcasted_iota(jnp.int32, vectors.shape, 1)
    first = (lane % HEAD) < HEAD // 2
    partner = jnp.where(
        first,
        pltpu.roll(vectors, TWO - HEAD // 2, 1),
        pltpu.roll(vectors, HEAD // 2, 1),
    )
    return vectors * cosine + partner * jnp.where(first, -sine, sine)


def of_head(vectors, head):
    lane = lax.broadcasted_iota(jnp.int32, vectors.shape, 1)
    return jnp.where(lane // HEAD == head, vectors, jnp.zeros_like(vectors))


def dot_t(left, right):
    return lax.dot_general(
        left, right, (((1,), (1,)), ((), ())), preferred_element_type=jnp.float32
    )


def project_kernel(place_ref, a_ref, b_ref, c_ref, d_ref, member_ref, bar_ref, cos_ref, sin_ref,
                   emb_ref, w_ref, *refs):
    x_ref, input_ref, q_ref, k_ref, kt_ref, v_ref, vt_ref, chunk_ref = refs[-8:]
    for step, ref in enumerate((a_ref, b_ref, c_ref, d_ref)):

        @pl.when(pl.program_id(0) == step)
        def _():
            chunk_ref[...] = ref[...]

    chunk = chunk_ref[...]
    x_ref[...] = chunk
    normed, _ = standardize(chunk.astype(jnp.float32))
    modulation = matmul(member_ref[...], emb_ref[...])
    low = (normed * (1.0 + modulation[:, D:]) + modulation[:, :D]).astype(jnp.bfloat16)
    input_ref[...] = low
    weight = jnp.concatenate([w_ref[b ^ place_ref[1]] for b in range(REPLICAS)], axis=0)
    product = matmul(low, weight)
    cosine, sine = cos_ref[...], sin_ref[...]
    keys = turn(product[:, TWO:2 * TWO], cosine, sine)
    values = product[:, 2 * TWO:]
    q_ref[...] = turn(product[:, :TWO], cosine, sine).astype(jnp.bfloat16)
    k_ref[:, :TWO] = keys.astype(jnp.bfloat16)
    k_ref[:, TWO:] = bar_ref[...]
    kt_ref[...] = keys.T.astype(jnp.bfloat16)
    v_ref[...] = values.astype(jnp.bfloat16)
    vt_ref[...] = values.T.astype(jnp.bfloat16)


def rows_spec(width):
    return pl.BlockSpec((ROWS, width), lambda i: (i, 0))


def cols_spec(height):
    return pl.BlockSpec((height, ROWS), lambda i: (0, i))


def whole_spec(height, width):
    return pl.BlockSpec((height, width), lambda i: (0, 0))


def params(mib):
    return pltpu.CompilerParams(
        dimension_semantics=("arbitrary",), vmem_limit_bytes=mib * 1024 * 1024
    )


def cost(micros):
    return pl.CostEstimate(
        flops=int(micros * 1e9), bytes_accessed=int(micros * 3e6), transcendentals=0
    )


def project(place, odd, chunks, member, bar, cosine, sine, emb, weights, earlier):
    frames = member.shape[0]
    low = jnp.bfloat16

    def rows(width):
        return pl.BlockSpec((ROWS, width), lambda i, p: ((2 * i + odd) ^ p[0], 0))

    def cols(height):
        return pl.BlockSpec((height, ROWS), lambda i, p: (0, (2 * i + odd) ^ p[0]))

    def whole(height, width):
        return pl.BlockSpec((height, width), lambda i, p: (0, 0))

    inputs = [place, *chunks, member, bar, cosine, sine, emb, weights, *earlier]
    first = len(inputs) - len(earlier)
    return pl.pallas_call(
        project_kernel,
        grid_spec=pltpu.PrefetchScalarGridSpec(
            num_scalar_prefetch=1,
            grid=(4,),
            in_specs=[whole(ROWS, D)] * 4 + [rows(TWO)] * 4
            + [whole(TWO, 2 * D),
               pl.BlockSpec((REPLICAS, ROWS, 3 * TWO), lambda i, p: (0, 0, 0))]
            + [pl.BlockSpec(memory_space=pl.ANY)] * len(earlier),
            out_specs=[rows(D), rows(D), rows(TWO), rows(2 * TWO), cols(TWO), rows(TWO),
                       cols(TWO)],
            scratch_shapes=[pltpu.VMEM((ROWS, D), low)],
        ),
        out_shape=[
            jax.ShapeDtypeStruct((frames, D), low),
            jax.ShapeDtypeStruct((frames, D), low),
            jax.ShapeDtypeStruct((frames, TWO), low),
            jax.ShapeDtypeStruct((frames, 2 * TWO), low),
            jax.ShapeDtypeStruct((TWO, frames), low),
            jax.ShapeDtypeStruct((frames, TWO), low),
            jax.ShapeDtypeStruct((TWO, frames), low),
        ],
        input_output_aliases={first + i: i for i in range(len(earlier))},
        compiler_params=params(30),
        cost_estimate=cost(2),
        name="project",
    )(*inputs)


def attend_kernel(q_ref, member_ref, k_ref, vt_ref, att_ref, low_ref, log_ref, *score_refs):
    frames = k_ref.shape[0]
    step = min(frames, 1024)
    queries = q_ref[...] * 0.125
    member = member_ref[...]
    bests, halves = [], []
    for head, score_ref in enumerate(score_refs):
        wide = jnp.concatenate([of_head(queries, head), member], axis=1)
        largest = jnp.full((1, BLOCK), -BIG, jnp.float32)
        for start in range(0, frames, step):
            scores = dot_t(k_ref[start:start + step, :], wide)
            score_ref[start:start + step, :] = scores
            largest = jnp.maximum(largest, jnp.max(scores, axis=0, keepdims=True))
        bests.append(largest)
    for head, score_ref in enumerate(score_refs):
        total = jnp.zeros((1, BLOCK), jnp.float32)
        out = jnp.zeros((TWO, BLOCK), jnp.float32)
        for start in range(0, frames, step):
            weights = jnp.exp(score_ref[start:start + step, :] - bests[head])
            total = total + jnp.sum(weights, axis=0, keepdims=True)
            out = out + matmul(vt_ref[:, start:start + step], weights.astype(jnp.bfloat16))
        halves.append(out[head * HEAD:(head + 1) * HEAD, :] / total)
        log_ref[head:head + 1, :] = bests[head] + jnp.log(total)
    attended = jnp.concatenate(halves, axis=0).T
    att_ref[...] = attended
    low_ref[...] = attended.astype(jnp.bfloat16)


def block_spec(width):
    return pl.BlockSpec((BLOCK, width), lambda i: (i, 0))


def attend(q, member, k, vt):
    frames = q.shape[0]
    return pl.pallas_call(
        attend_kernel,
        grid=(frames // BLOCK,),
        in_specs=[block_spec(TWO), block_spec(TWO), whole_spec(frames, 2 * TWO),
                  whole_spec(TWO, frames)],
        out_specs=[block_spec(TWO), block_spec(TWO), pl.BlockSpec((8, BLOCK), lambda i: (0, i))],
        out_shape=[
            jax.ShapeDtypeStruct((frames, TWO), jnp.float32),
            jax.ShapeDtypeStruct((frames, TWO), jnp.bfloat16),
            jax.ShapeDtypeStruct((8, frames), jnp.float32),
        ],
        scratch_shapes=[pltpu.VMEM((frames, BLOCK), jnp.float32)] * 2,
        compiler_params=params(26),
        cost_estimate=cost(18),
        name="attend",
    )(q, member, k, vt)


def attend_back_kernel(q_ref, member_ref, grad_ref, att_ref, log_ref, cos_ref, sin_ref, cos_all_ref,
                       sin_all_ref, k_ref, kt_ref, v_ref, g_ref, dk_ref, dv_ref):
    block = pl.program_id(0)
    frames = k_ref.shape[0]
    step = min(frames, 512)

    @pl.when(block == 0)
    def _():
        dk_ref[...] = jnp.zeros_like(dk_ref)
        dv_ref[...] = jnp.zeros_like(dv_ref)

    queries = q_ref[...] * 0.125
    member = member_ref[...]
    grad = grad_ref[...]
    mixed = (grad.astype(jnp.float32) * att_ref[...]).T
    halves = []
    wides, grads, deltas = [], [], []
    for head in range(2):
        wides.append(jnp.concatenate([of_head(queries, head), member], axis=1))
        grads.append(of_head(grad, head))
        deltas.append(jnp.sum(mixed[head * HEAD:(head + 1) * HEAD, :], axis=0, keepdims=True))
    totals = [jnp.zeros((TWO, ROWS), jnp.float32) for _ in range(2)]
    for start in range(0, frames, step):
        part = slice(start, start + step)
        dk = dk_ref[part, :]
        dv = dv_ref[part, :]
        for head in range(2):
            scores = dot_t(k_ref[part, :], wides[head])
            weights = jnp.exp(scores - log_ref[head:head + 1, :])
            grad_weights = dot_t(v_ref[part, :], grads[head])
            grad_scores = (weights * (grad_weights - deltas[head])).astype(jnp.bfloat16)
            dv = dv + matmul(weights.astype(jnp.bfloat16), grads[head])
            dk = dk + matmul(grad_scores, wides[head][:, :TWO])
            totals[head] = totals[head] + matmul(kt_ref[:, part], grad_scores)
        dk_ref[part, :] = dk
        dv_ref[part, :] = dv
    dq = jnp.concatenate([totals[0][:HEAD, :], totals[1][HEAD:, :]], axis=0).T * 0.125
    here = pl.ds(pl.multiple_of(block * ROWS, ROWS), ROWS)
    g_ref[here, :TWO] = turn(dq, cos_ref[...], -sin_ref[...]).astype(jnp.bfloat16)

    @pl.when(block == pl.num_programs(0) - 1)
    def _():
        turned = turn(dk_ref[...], cos_all_ref[...], -sin_all_ref[...])
        g_ref[:, TWO:2 * TWO] = turned.astype(jnp.bfloat16)
        g_ref[:, 2 * TWO:] = dv_ref[...].astype(jnp.bfloat16)


def attend_back(q, member, grad, att, log_total, cosine, sine, k, kt, v):
    frames = q.shape[0]
    return pl.pallas_call(
        attend_back_kernel,
        grid=(frames // ROWS,),
        in_specs=[rows_spec(TWO), rows_spec(TWO), rows_spec(TWO), rows_spec(TWO), cols_spec(8),
                  rows_spec(TWO), rows_spec(TWO), whole_spec(frames, TWO), whole_spec(frames, TWO),
                  whole_spec(frames, 2 * TWO), whole_spec(TWO, frames), whole_spec(frames, TWO)],
        out_specs=whole_spec(frames, 3 * TWO),
        out_shape=jax.ShapeDtypeStruct((frames, 3 * TWO), jnp.bfloat16),
        scratch_shapes=[pltpu.VMEM((frames, TWO), jnp.float32),
                        pltpu.VMEM((frames, TWO), jnp.float32)],
        compiler_params=params(VMEM_MIB),
        cost_estimate=cost(27),
        name="attend_back",
    )(q, member, grad, att, log_total, cosine, sine, cosine, sine, k, kt, v)


def three_terms(values):
    high = lax.reduce_precision(values, 8, 7)
    middle = lax.reduce_precision(values - high, 8, 7)
    return [high, middle, values - high - middle]


def standardize(rows):
    centered = rows - jnp.mean(rows, axis=1, keepdims=True)
    inverse = lax.rsqrt(jnp.mean(centered * centered, axis=1, keepdims=True) + 1e-06)
    return centered * inverse, inverse


def sum_of_clips(clip_ref, values):
    ids = lax.broadcasted_iota(jnp.int32, (CLIPS, clip_ref.shape[1]), 0)
    chosen = jnp.where(clip_ref[...] == ids, 1.0, 0.0).astype(jnp.bfloat16)
    high = values.astype(jnp.bfloat16)
    rest = values - high.astype(jnp.float32)
    middle = rest.astype(jnp.bfloat16)
    last = (rest - middle.astype(jnp.float32)).astype(jnp.bfloat16)
    return matmul(chosen, high) + matmul(chosen, middle) + matmul(chosen, last)


def beside(ref, tiles, rows):
    return jnp.concatenate([ref[tile, rows, :] for tile in tiles], axis=1)


def tile_index(away, apart):
    return 16 * (away % 2) + 8 * (away // 2) + 4 * (apart % 2) + apart // 2


def middle_kernel(mine_ref, x_ref, member_ref, clip_ref, cot_any, emb_any, tiles_ref,
                  result_any, grad_middle_ref, grad_att_ref, grad_emb_ref, left_any, right_any,
                  out_ref, up_ref, down_ref, cot_ref, emb_ref, result_ref, left_ref, right_ref,
                  sems, branch_ref, low_ref, act_ref, slope_ref, wide_ref):
    low = jnp.bfloat16
    act_t_ref, ffn_t_ref = left_ref.at[:2 * D], left_ref.at[2 * D:3 * D]
    mine_t_ref = left_ref.at[3 * D:]
    g_ffn_ref, g_attn_ref = right_ref.at[:, :D], right_ref.at[:, 3 * D:]
    g_hidden_ref = right_ref.at[:, D:3 * D]
    copies = [
        pltpu.make_async_copy(source, target, sems.at[i])
        for i, (source, target) in enumerate((
            (tiles_ref.at[:, pl.ds(0, 256), :], out_ref),
            (emb_any, emb_ref),
            (cot_any, cot_ref),
            (tiles_ref.at[:, pl.ds(256, 512), :], up_ref),
            (tiles_ref.at[:, pl.ds(768, 512), :], down_ref),
        ))
    ]
    for copy in copies:
        copy.start()
    stores = [
        pltpu.make_async_copy(source, target, sems.at[len(copies) + i])
        for i, (source, target) in enumerate((
            (mine_t_ref, left_any.at[3 * D:]),
            (ffn_t_ref, left_any.at[2 * D:3 * D]),
            (g_ffn_ref, right_any.at[:, :D]),
            (act_t_ref, left_any.at[:2 * D]),
            (result_ref, result_any),
            (g_hidden_ref, right_any.at[:, D:3 * D]),
            (g_attn_ref, right_any.at[:, 3 * D:]),
        ))
    ]

    def tile(b, s):
        return SEQ * b + s

    member = member_ref[...]

    def modulation(index):
        return matmul(member, emb_ref[:, index * D:(index + 1) * D])

    def cols(n, width=256):
        return pl.ds(pl.multiple_of(n * width, width), width)

    every = slice(None)
    mine = jnp.concatenate([mine_ref[j] for j in range(SEQ)], axis=1)
    low_ref[...] = mine
    mine_t_ref[...] = mine.T
    stores[0].start()
    copies[0].wait()

    @pl.loop(0, 4)
    def _(n):
        total = jnp.zeros((ROWS, 256), jnp.float32)
        for b in range(REPLICAS):
            weight = beside(out_ref, [tile(b, 2 * n), tile(b, 2 * n + 1)], every)
            total = total + matmul(low_ref[:, 256 * b:256 * b + 256], weight)
        branch_ref[:, cols(n)] = total

    copies[1].wait()
    gate_attn = modulation(2)
    branch = branch_ref[...]
    middle = x_ref[...].astype(jnp.float32) + gate_attn * branch
    normed, inverse = standardize(middle)
    scale_ffn = modulation(4)
    ffn_input = normed * (1.0 + scale_ffn) + modulation(3)
    low_ref[...] = ffn_input.astype(low)
    ffn_t_ref[...] = ffn_input.T.astype(low)
    gate_ffn = modulation(5)
    copies[2].wait()
    cot = cot_ref[...].astype(jnp.float32)
    g_ffn_ref[...] = (cot * gate_ffn).astype(low)
    stores[1].start()
    stores[2].start()
    copies[3].wait()

    @pl.loop(0, 8)
    def _(n):
        hidden = jnp.zeros((ROWS, 256), jnp.float32)
        for b in range(REPLICAS):
            index = tile(b, n)
            weight = jnp.concatenate([up_ref[index, :256, :], up_ref[index, 256:, :]], axis=1)
            hidden = hidden + matmul(low_ref[:, 256 * b:256 * b + 256], weight)
        root = math.sqrt(2.0 / math.pi)
        squared = hidden * hidden
        bent = jnp.tanh(root * (hidden + 0.044715 * (squared * hidden)))
        half = 0.5 * (1.0 + bent)
        activated = hidden * half
        slope = half + 0.5 * hidden * (1.0 - bent * bent) * (
            root * (1.0 + (3.0 * 0.044715) * squared)
        )
        act_ref[:, cols(n)] = activated.astype(low)
        act_t_ref[cols(n), :] = activated.T.astype(low)
        slope_ref[:, cols(n)] = slope

    stores[3].start()
    copies[4].wait()

    @pl.loop(0, 4)
    def _(n):
        total = jnp.zeros((ROWS, 256), jnp.float32)
        for b in range(REPLICAS):
            weight = beside(down_ref, [tile(b, 2 * n), tile(b, 2 * n + 1)], every)
            total = total + matmul(act_ref[:, 512 * b:512 * b + 512], weight)
        wide_ref[:, cols(n)] = total

    ffn_branch = wide_ref[...]
    result_ref[...] = (middle + gate_ffn * ffn_branch).astype(low)
    stores[4].start()
    grad_emb_ref[:, 3 * D:] = sum_of_clips(clip_ref, cot * ffn_branch)

    @pl.loop(0, REPLICAS)
    def _(b):
        weight = beside(down_ref, [tile(b, s) for s in range(SEQ)], every)
        grad = dot_t(g_ffn_ref[...], weight)
        here = cols(b, 512)
        g_hidden_ref[:, here] = (grad * slope_ref[:, here]).astype(low)

    stores[5].start()

    @pl.loop(0, REPLICAS)
    def _(b):
        weight = jnp.concatenate(
            [up_ref[tile(b, s), 256 * k:256 * k + 256, :] for s in range(SEQ) for k in range(2)],
            axis=1,
        )
        wide_ref[:, cols(b)] = dot_t(g_hidden_ref[...], weight)

    grad_ffn_input = wide_ref[...]
    grad_emb_ref[:, D:2 * D] = sum_of_clips(clip_ref, grad_ffn_input)
    grad_emb_ref[:, 2 * D:3 * D] = sum_of_clips(clip_ref, grad_ffn_input * normed)
    spread = grad_ffn_input * (1.0 + scale_ffn)
    grad_middle = cot + inverse * (
        spread
        - jnp.mean(spread, axis=1, keepdims=True)
        - normed * jnp.mean(spread * normed, axis=1, keepdims=True)
    )
    grad_middle_ref[...] = grad_middle
    grad_emb_ref[:, :D] = sum_of_clips(clip_ref, grad_middle * branch)
    g_attn_ref[...] = (grad_middle * gate_attn).astype(low)
    stores[6].start()

    @pl.loop(0, REPLICAS)
    def _(b):
        weight = beside(out_ref, [tile(b, s) for s in range(SEQ)], every)
        grad = dot_t(g_attn_ref[...], weight).astype(low)
        grad_att_ref[2 * b] = grad[:, :TWO]
        grad_att_ref[2 * b + 1] = grad[:, TWO:]

    for store in stores:
        store.wait()


def middle_part(mine, x, cot, member, clip_row, emb, tiles):
    low = jnp.bfloat16
    shapes = [
        ((ROWS, D), low), ((ROWS, D), jnp.float32), ((SEQ, ROWS, TWO), low),
        ((CLIPS, 4 * D), jnp.float32), ((4 * D, ROWS), low), ((ROWS, 4 * D), low),
    ]
    vmem, anywhere = pl.BlockSpec(memory_space=pltpu.VMEM), pl.BlockSpec(memory_space=pl.ANY)
    return pl.pallas_call(
        middle_kernel,
        in_specs=[vmem] * 4 + [anywhere] * 3,
        out_specs=[anywhere, vmem, vmem, vmem, anywhere, anywhere],
        out_shape=[jax.ShapeDtypeStruct(shape, dtype) for shape, dtype in shapes],
        scratch_shapes=[
            pltpu.VMEM((32, 256, 128), low),
            pltpu.VMEM((32, 512, 128), low),
            pltpu.VMEM((32, 512, 128), low),
            pltpu.VMEM((ROWS, D), low),
            pltpu.VMEM((TWO, 6 * D), low),
            pltpu.VMEM((ROWS, D), low),
            pltpu.VMEM((4 * D, ROWS), low),
            pltpu.VMEM((ROWS, 4 * D), low),
            pltpu.SemaphoreType.DMA((12,)),
            pltpu.VMEM((ROWS, D), jnp.float32),
            pltpu.VMEM((ROWS, D), low),
            pltpu.VMEM((ROWS, 2 * D), low),
            pltpu.VMEM((ROWS, 2 * D), jnp.float32),
            pltpu.VMEM((ROWS, D), jnp.float32),
        ],
        compiler_params=pltpu.CompilerParams(vmem_limit_bytes=VMEM_MIB * 1024 * 1024),
        cost_estimate=cost(20),
        name="middle",
    )(mine, x, member, clip_row, cot, emb, *tiles)


def weight_grads_kernel(place_ref, down_l, up_l, out_l, right_ref, down_o, up_o, out_o, other_ref,
                        away_d_ref, keep_d_ref, away_u_ref, keep_u_ref):
    low = jnp.bfloat16
    z, y = place_ref[2] // 2, place_ref[2] % 2
    lefts = [
        jnp.concatenate([mine[...], other[...]], axis=1)
        for mine, other in ((down_l, down_o), (up_l, up_o), (out_l, out_o))
    ]

    def product(left, first, block):
        here = pl.ds(pl.multiple_of(first + 256 * block, 256), 256)
        right = jnp.concatenate([right_ref[:, here], other_ref[:, here]], axis=0)
        return matmul(left, right).astype(low)

    def fill(ref):
        @pl.loop(0, 4)
        def _(k):
            block = z ^ k
            for left, first, rows in ((lefts[0], 0, slice(0, 512)), (lefts[2], 3 * D, slice(512, 768))):
                grad = product(left, first, block)
                ref[4 * y + k, rows, :] = grad[:, :128]
                ref[4 - 4 * y + k, rows, :] = grad[:, 128:]
            for side, up_ref in enumerate((keep_u_ref, away_u_ref)):
                grad = product(lefts[1], D, 2 * block + (y ^ side))
                up_ref[0, k, :256, :] = grad[:, :128]
                up_ref[0, k, 256:, :] = grad[:, 128:]

    @pl.when(pl.program_id(0) == 0)
    def _():
        fill(away_d_ref)

    @pl.when(pl.program_id(0) == 1)
    def _():
        fill(keep_d_ref)


def weight_grads(place, left, right, other_left, other_right):
    low = jnp.bfloat16

    def target(i, p):
        return 2 * jnp.where(i == 0, 1 - p[0], p[0]) + p[1]

    down = pl.BlockSpec((512, ROWS), lambda i, p: (target(i, p), 0))
    up = pl.BlockSpec((256, ROWS), lambda i, p: (8 + target(i, p), 0))
    out = pl.BlockSpec((256, ROWS), lambda i, p: (12 + target(i, p), 0))
    wide = pl.BlockSpec((ROWS, 4 * D), lambda i, p: (0, 0))
    whole = pl.BlockSpec((SEQ, 768, 128), lambda i, p: (0, 0, 0))
    part = pl.BlockSpec((1, 4, 512, 128), lambda i, p: (1 - i, 0, 0, 0))
    return pl.pallas_call(
        weight_grads_kernel,
        grid_spec=pltpu.PrefetchScalarGridSpec(
            num_scalar_prefetch=1,
            grid=(2,),
            in_specs=[down, up, out, wide] * 2,
            out_specs=[whole, whole, part, part],
        ),
        out_shape=[jax.ShapeDtypeStruct((SEQ, 768, 128), low)] * 2
        + [jax.ShapeDtypeStruct((2, 4, 512, 128), low)] * 2,
        compiler_params=params(VMEM_MIB),
        cost_estimate=cost(9),
        name="weight_grads",
    )(place, left, left, left, right, other_left, other_left, other_left, other_right)


def clip_grads_kernel(place_ref, x_ref, clip_ref, g_ref, w_ref, out_ref):
    @pl.when(pl.program_id(0) == 0)
    def _():
        out_ref[...] = jnp.zeros_like(out_ref)

    normed, _ = standardize(x_ref[...].astype(jnp.float32))
    grad = jnp.concatenate(
        [dot_t(g_ref[...], w_ref[b ^ place_ref[1]]) for b in range(REPLICAS)], axis=1
    )
    out_ref[:, :D] += sum_of_clips(clip_ref, grad)
    out_ref[:, D:] += sum_of_clips(clip_ref, grad * normed)


def clip_grads(places, x, clip_row, g_heads, heads_w):
    frames = x.shape[0]
    return pl.pallas_call(
        clip_grads_kernel,
        grid=(frames // ROWS,),
        in_specs=[pl.BlockSpec(memory_space=pltpu.SMEM), rows_spec(D), cols_spec(1),
                  rows_spec(3 * TWO),
                  pl.BlockSpec((REPLICAS, ROWS, 3 * TWO), lambda i: (0, 0, 0))],
        out_specs=whole_spec(CLIPS, 2 * D),
        out_shape=jax.ShapeDtypeStruct((CLIPS, 2 * D), jnp.float32),
        compiler_params=params(VMEM_MIB),
        cost_estimate=cost(9),
        name="clip_grads",
    )(places, x, clip_row, g_heads, heads_w)


def last_kernel(place_ref, own_ref, x_ref, grad_middle_ref, member_ref, emb_ref, *refs):
    *tile_refs, out_ref, wide_ref = refs
    grads = jnp.concatenate([own_ref[place_ref[2] ^ s] for s in range(SEQ)], axis=1)

    def tile(away, apart):
        index = tile_index(away, apart)
        for ref in tile_refs:
            if index < ref.shape[0]:
                return ref[index, ref.shape[1] - 768:, :]
            index -= ref.shape[0]

    for away in range(REPLICAS):
        weight = jnp.concatenate(
            [
                tile(away, s)[256 * k:256 * k + 256, :]
                for s in range(SEQ)
                for k in range(3)
            ],
            axis=1,
        )
        b = (2 * place_ref[0] + place_ref[1]) ^ away
        wide_ref[:, pl.ds(pl.multiple_of(b * 256, 256), 256)] = dot_t(grads, weight)

    normed, inverse = standardize(x_ref[...].astype(jnp.float32))
    spread = wide_ref[...] * (1.0 + matmul(member_ref[...], emb_ref[:, D:2 * D]))
    grad = grad_middle_ref[...] + inverse * (
        spread
        - jnp.mean(spread, axis=1, keepdims=True)
        - normed * jnp.mean(spread * normed, axis=1, keepdims=True)
    )
    out_ref[...] = grad.astype(jnp.bfloat16)


def last_part(place, own, x, grad_middle, member, emb, tiles):
    vmem = pl.BlockSpec(memory_space=pltpu.VMEM)
    return pl.pallas_call(
        last_kernel,
        in_specs=[pl.BlockSpec(memory_space=pltpu.SMEM)] + [vmem] * (5 + len(tiles)),
        out_specs=vmem,
        out_shape=jax.ShapeDtypeStruct((ROWS, D), jnp.bfloat16),
        scratch_shapes=[pltpu.VMEM((ROWS, D), jnp.float32)],
        compiler_params=pltpu.CompilerParams(vmem_limit_bytes=30 * 1024 * 1024),
        cost_estimate=cost(4),
        name="last",
    )(place, own, x, grad_middle, member, emb, *tiles)


def after(value, *others):
    return lax.optimization_barrier((value,) + others)[0]


def together(*values):
    return lax.optimization_barrier(values)


def plus(*terms):
    total = terms[0].astype(jnp.float32)
    for term in terms[1:]:
        total = total + term.astype(jnp.float32)
    return total


def clip_lanes(clip, terms):
    lane = jnp.arange(TWO, dtype=jnp.int32)[None, :]
    return (clip[:, None] == lane % CLIPS) & (lane < terms * CLIPS)


def body_fast(
    tokens, w_query, w_key, w_value, w_out, w_ada, w_up, w_down,
    segments, validity, timesteps, cotangent,
):
    highest = lax.Precision.HIGHEST
    low = jnp.bfloat16
    wide = jnp.float32
    replica = lax.axis_index("batch")
    x = tokens[0]
    frame_count = x.shape[0]
    frames = frame_count * SEQ
    segment = segments[0]

    seat = lax.axis_index("seq").astype(jnp.int32)
    z, y = seat // 2, seat % 2
    place = jnp.stack([replica // 2, replica % 2, seat]).astype(jnp.int32)
    mine_w = jnp.concatenate([w_out, w_up[:, :128], w_up[:, 128:], w_down], axis=0).astype(low)

    z1, z2, y0 = swap(x, "seq", 2), swap(x, "seq", 4), swap(x, "seq", 1)
    times = lax.all_gather(timesteps[0], "batch", axis=0, tiled=True)
    silu_all = jax.nn.silu(time_embedding(times)).astype(low)
    depth = w_ada.shape[0]
    silu_part = lax.dynamic_slice_in_dim(silu_all, replica * depth, depth, 1)
    emb_part = matmul(silu_part, w_ada.astype(low)).reshape(REPLICAS, CLIPS, -1)
    emb_cols = lax.all_to_all(emb_part, "batch", 0, 0, tiled=True)
    emb_cols = jnp.sum(emb_cols, axis=0)
    own_codes = (segment * 2 + (validity[0] == 1)).astype(wide)
    cols = emb_cols.shape[1]
    own_codes = jnp.pad(own_codes, (0, 8 * cols - frame_count)).reshape(8, cols)
    packed = jnp.concatenate([emb_cols, own_codes])
    packed = jnp.broadcast_to(packed[None], (SEQ,) + packed.shape)
    heads_w = jnp.concatenate([w_query, w_key, w_value], axis=1).astype(low)
    heads_w = jnp.stack([heads_w, swap(heads_w, "batch", 1)])
    z1, z2, y0, packed, heads_w, mine_w = together(z1, z2, y0, packed, heads_w, mine_w)
    tiles_w = (lax.all_gather(mine_w, ("batch", "seq"), axis=0),)
    packed = exchange(packed)
    z3 = swap(z2, "seq", 2)
    y1, y2 = swap(z1, "seq", 1), swap(z2, "seq", 1)
    heads_x = swap(heads_w, "batch", 2)
    z3, heads_x = together(z3, heads_x)
    y3 = swap(z3, "seq", 1)
    mine_h = jnp.concatenate([w_query, w_key, w_value], axis=0).astype(low)
    mine_h = after(mine_h, z3)
    h_z1, h_z2 = swap(mine_h, "seq", 2), swap(mine_h, "seq", 4)
    heads_w = jnp.concatenate([heads_w, heads_x])
    emb = packed[:, :CLIPS]
    codes = packed[:, CLIPS:].reshape(SEQ, -1)[:, :frame_count].reshape(frames).astype(jnp.int32)
    clip = codes // 2
    clip_row = clip[None, :]
    tri = jnp.arange(frame_count)[:, None] > jnp.arange(frame_count)[None, :]
    ids = jnp.arange(CLIPS, dtype=jnp.int32)
    one_hot = (clip.reshape(SEQ, frame_count)[:, :, None] == ids).astype(low)
    within = jnp.einsum("ij,njc->nic", tri.astype(low), one_hot, preferred_element_type=wide)
    counts = jnp.sum(one_hot.astype(wide), axis=1)
    offsets = jnp.cumsum(counts, axis=0) - counts
    position = jnp.sum(one_hot.astype(wide) * (within + offsets[:, None, :]), axis=2)
    half = HEAD // 2
    frequency = jnp.exp(-math.log(10000.0) * jnp.arange(half, dtype=wide) / half)
    angle = position.reshape(frames)[:, None] * jnp.tile(frequency, 4)[None, :]
    cosine, sine = jnp.cos(angle), jnp.sin(angle)
    member = clip_lanes(clip, 3).astype(low)
    allowed = clip_lanes(jnp.where(codes % 2 == 1, clip, -1), 1)
    inside = jnp.arange(TWO, dtype=jnp.int32)[None, :] < CLIPS
    bar = jnp.where(inside & ~allowed, -BIG, 0.0).astype(low)
    emb, y1, y2 = together(after(emb, heads_w, member, cosine), y1, y2)
    emb = emb.transpose(1, 0, 2).reshape(CLIPS, -1)
    emb = jnp.concatenate(
        [t.astype(low) for t in three_terms(emb)] + [jnp.zeros((TWO - 3 * CLIPS, 6 * D), low)],
        axis=0,
    )

    tables = (member, bar, cosine, sine, emb, heads_w)
    places = jnp.stack([seat, replica.astype(jnp.int32)])
    earlier = project(places, 0, (x, z1, z2, z3), *tables, ())
    y3, h_z1, h_z2, earlier = together(y3, h_z1, h_z2, earlier)
    h_z3 = swap(h_z2, "seq", 2)
    x_all, attn_input, q, k, kt, v, vt = project(places, 1, (y0, y1, y2, y3), *tables, earlier)
    attended, attended_low, log_total = attend(q, member, k, vt)
    attended_low, h_z3 = together(attended_low, h_z3)
    mine = exchange(attended_low.reshape(SEQ, frame_count, TWO))
    h_z = jnp.stack([mine_h, h_z1, h_z2, h_z3])
    mine, h_z = together(mine, h_z)
    h_y, h_x = swap(h_z, "seq", 1), swap(h_z, "batch", 2)

    own_member = clip_lanes(segment, 3).astype(low)
    result, grad_middle, grad_att, grad_emb, left, right = middle_part(
        mine, x, cotangent[0], own_member, segment[None, :], emb, tiles_w
    )
    left, h_y, h_x = together(left, h_y, h_x)
    other_left, other_right = swap(left, "batch", 1), swap(right, "batch", 1)
    h_first = jnp.concatenate([h_z, h_y, h_x])
    other_left, other_right, h_first = together(other_left, other_right, h_first)
    away_d, keep_d, away_u, keep_u = weight_grads(place, left, right, other_left, other_right)
    grad_heads = exchange(grad_att).reshape(frames, TWO)
    from_x = swap(away_d, "batch", 2)
    from_y = swap(away_u, "seq", 1)
    grad_heads = after(grad_heads, away_d, away_u)

    g_heads = attend_back(
        q, member, grad_heads, attended, log_total, cosine, sine, k, kt, v
    )
    own = exchange(g_heads.reshape(SEQ, frame_count, 3 * TWO))
    from_y = after(from_y, g_heads)
    to_x_u = plus(keep_u[1], from_y[1]).astype(low)
    from_x_u = swap(to_x_u, "batch", 2)
    from_x = after(from_x, to_x_u)
    to_y_d = plus(keep_d[4:], from_x[4:]).astype(low)
    from_y_d = swap(to_y_d, "seq", 1)
    h_yx = swap(after(h_y, to_y_d), "batch", 2)
    h_first_core = swap(after(h_first, to_x_u), "batch", 1)
    g_heads = after(g_heads, to_y_d, to_x_u)
    grad_heads_w = matmul(attn_input.T, g_heads).astype(low).reshape(2, 2, ROWS, 3 * TWO)
    grad_heads_w, from_x_u = together(grad_heads_w, from_x_u)
    part_u = plus(keep_u[0], from_y[0], from_x_u).astype(low)
    from_z_u = [swap(part_u[k], "seq", 2 * k) for k in range(1, 4)]
    late = clip_grads(places, x_all, clip_row, after(g_heads, part_u), heads_w)
    late, from_y_d, h_first_core = together(late, from_y_d, h_first_core)
    part = plus(keep_d[:4], from_x[:4], from_y_d).astype(low)
    late, own = together(late, own)
    grad_emb = jnp.concatenate([late, grad_emb], axis=1)
    grad_emb = exchange(grad_emb.reshape(CLIPS, SEQ, -1).transpose(1, 0, 2))
    grad_emb, *from_z_u = together(grad_emb, *from_z_u)
    grad_emb = jnp.sum(grad_emb, axis=0)
    x_place, core_place = replica // 2, replica % 2
    keep_h = lax.dynamic_index_in_dim(grad_heads_w, core_place, 1, False)
    other_h = swap(lax.dynamic_index_in_dim(grad_heads_w, 1 - core_place, 1, False), "batch", 1)
    h_yx_core = swap(after(h_yx, part), "batch", 1)
    from_z = [swap(part[k], "seq", 2 * k) for k in range(1, 4)]
    both_h = plus(keep_h, other_h).astype(low)
    away_h = swap(lax.dynamic_index_in_dim(both_h, 1 - x_place, 0, False), "batch", 2)

    grad_tokens = last_part(place, own, x, grad_middle, own_member, emb,
        (h_first, h_yx, h_first_core, h_yx_core),
    )
    grad_emb = lax.all_gather(grad_emb, "batch", axis=0, tiled=True)
    final_a = jnp.dot(silu_part.astype(wide).T, grad_emb, precision=highest)
    grad_tokens, final_a, away_h, *from_z = together(grad_tokens, final_a, away_h, *from_z)
    final_heads = plus(lax.dynamic_index_in_dim(both_h, x_place, 0, False), away_h)
    total = plus(part[0], *from_z)
    final_d, final_o = total[:512], total[512:]
    total = plus(part_u[0], *from_z_u)
    final_u = jnp.concatenate([total[:256], total[256:]], axis=1)
    width = w_query.shape[1]
    return (
        result[None],
        grad_tokens[None],
        final_heads[:, :width],
        final_heads[:, width:2 * width],
        final_heads[:, 2 * width:],
        final_o,
        final_a,
        final_u,
        final_d,
    )


def solution(mesh):
    fits = mesh.shape["seq"] == SEQ and mesh.shape["batch"] == REPLICAS
    chosen = body_fast if fits else body
    return jax.shard_map(
        chosen,
        mesh=mesh,
        in_specs=(
            P("batch", "seq", None),
            P("batch", "seq"),
            P("batch", "seq"),
            P("batch", "seq"),
            P("batch", "seq"),
            P("batch", "seq"),
            P("batch", "seq"),
            P("batch", "seq"),
            P("batch", "seq"),
            P("batch", "seq"),
            P("batch", None),
            P("batch", "seq", None),
        ),
        out_specs=(
            P("batch", "seq", None),
            P("batch", "seq", None),
            P("batch", "seq"),
            P("batch", "seq"),
            P("batch", "seq"),
            P("batch", "seq"),
            P("batch", "seq"),
            P("batch", "seq"),
            P("batch", "seq"),
        ),
        check_vma=False,
    )
```

```python
from functools import partial
import math

import jax
import jax.numpy as jnp
from jax import lax
from jax.experimental import pallas as pl
from jax.experimental.pallas import tpu as pltpu
from jax.sharding import PartitionSpec as P

D = 1024
HEADS = 16
HEAD = 64
CLIPS = 16


def carried_in(part, axis, combine, identity):
    place = lax.axis_index(axis)
    gathered = lax.all_gather(part, axis)
    state = jnp.zeros_like(part) + jnp.asarray(identity, part.dtype)

    def one(step, state):
        return combine(state, lax.dynamic_index_in_dim(gathered, step, 0, False))

    return lax.fori_loop(0, place, one, state)


def matmul(left, right):
    return jnp.dot(left, right, preferred_element_type=jnp.float32)


def time_embedding(timestep_row):
    half_width = D // 2
    frequency = jnp.exp(-math.log(10000.0) * jnp.arange(half_width, dtype=jnp.float32) / half_width)
    angle = timestep_row.astype(jnp.float32)[:, None] * frequency[None, :]
    return jnp.concatenate([jnp.sin(angle), jnp.cos(angle)], axis=1)


def rotate_pairs(vectors, position, direction):
    half_size = vectors.shape[-1] // 2
    frequency = jnp.exp(-math.log(10000.0) * jnp.arange(half_size, dtype=jnp.float32) / half_size)
    angle = position[:, None] * frequency[None, :]
    cosine = jnp.cos(angle)[:, None, :]
    sine = jnp.sin(angle)[:, None, :] * direction
    first_half = vectors[..., :half_size]
    second_half = vectors[..., half_size:]
    return jnp.concatenate(
        [first_half * cosine - second_half * sine, second_half * cosine + first_half * sine],
        axis=-1,
    )


def normalize(inputs):
    centered = inputs - jnp.mean(inputs, axis=-1, keepdims=True)
    inverse = lax.rsqrt(jnp.mean(centered * centered, axis=-1, keepdims=True) + 1e-06)
    return (centered * inverse, inverse)


def norm_backward(grad_normed, normed, inverse):
    mean_grad = jnp.mean(grad_normed, axis=-1, keepdims=True)
    mean_mixed = jnp.mean(grad_normed * normed, axis=-1, keepdims=True)
    return inverse * (grad_normed - mean_grad - normed * mean_mixed)


def add_counts(earlier, later):
    return earlier + later


def block_rows_for(row_count):
    chosen = 1
    for candidate in range(1, 513):
        if row_count % candidate == 0:
            chosen = candidate
    return chosen


def stack_blocks(shard_piece):
    row_count = shard_piece[0].shape[0]
    block_rows = block_rows_for(row_count)
    block_count = row_count // block_rows
    return (
        shard_piece[0].reshape(block_count, block_rows, HEADS, HEAD),
        shard_piece[1].reshape(block_count, block_rows, HEADS, HEAD),
        shard_piece[2].reshape(block_count, block_rows),
    )


def forward_block(carried, key_block, queries, query_codes):
    running_max, running_sum, accumulated = carried
    key_rows, values, key_codes = key_block
    scores = (
        jnp.einsum("qhe,khe->hqk", queries, key_rows, preferred_element_type=jnp.float32) * 0.125
    )
    allowed = (query_codes[:, None] == key_codes.astype(jnp.float32)[None, :])[None]
    masked = jnp.where(allowed, scores, -1e30)
    new_max = jnp.maximum(running_max, jnp.max(masked, axis=2))
    rescale = jnp.exp(running_max - new_max)
    weights = jnp.where(allowed, jnp.exp(masked - new_max[:, :, None]), 0.0)
    running_sum = running_sum * rescale + jnp.sum(weights, axis=2)
    product = jnp.einsum(
        "hqk,khe->qhe", weights, values.astype(jnp.float32), precision=lax.Precision.HIGHEST
    )
    accumulated = accumulated * rescale.T[:, :, None] + product
    return (new_max, running_sum, accumulated)


def block_grads(key_block, queries, query_codes, grad_attn, log_total, delta_rows):
    key_rows, values, key_codes = key_block
    scores = (
        jnp.einsum("qhe,khe->hqk", queries, key_rows, preferred_element_type=jnp.float32) * 0.125
    )
    allowed = (query_codes[:, None] == key_codes.astype(jnp.float32)[None, :])[None]
    probabilities = jnp.exp(jnp.where(allowed, scores, -1e30) - log_total[:, :, None])
    grad_probs = jnp.einsum("qhe,khe->hqk", grad_attn, values, preferred_element_type=jnp.float32)
    grad_scores = (probabilities * (grad_probs - delta_rows[:, :, None])).astype(jnp.bfloat16)
    return (probabilities, grad_scores)


def body(
    tokens,
    w_query,
    w_key,
    w_value,
    w_out,
    w_ada,
    w_up,
    w_down,
    segments,
    validity,
    timesteps,
    cotangent,
):
    inputs = tokens[0].astype(jnp.float32)
    segment = segments[0]
    valid_row = validity[0]
    timestep_row = timesteps[0]
    grad_output = cotangent[0].astype(jnp.float32)
    frame_count = inputs.shape[0]
    highest = lax.Precision.HIGHEST
    cols_q, cols_k, cols_v, cols_o, cols_a, cols_u, cols_d = (
        lax.all_gather(w_query.astype(jnp.bfloat16), "seq", axis=1, tiled=True),
        lax.all_gather(w_key.astype(jnp.bfloat16), "seq", axis=1, tiled=True),
        lax.all_gather(w_value.astype(jnp.bfloat16), "seq", axis=1, tiled=True),
        lax.all_gather(w_out.astype(jnp.bfloat16), "seq", axis=1, tiled=True),
        lax.all_gather(w_ada.astype(jnp.bfloat16), "seq", axis=1, tiled=True),
        lax.all_gather(w_up.astype(jnp.bfloat16), "seq", axis=1, tiled=True),
        lax.all_gather(w_down.astype(jnp.bfloat16), "seq", axis=1, tiled=True),
    )
    full_q, full_k, full_v, full_o, full_a, full_u, full_d = (
        lax.all_gather(cols_q, "batch", axis=0, tiled=True),
        lax.all_gather(cols_k, "batch", axis=0, tiled=True),
        lax.all_gather(cols_v, "batch", axis=0, tiled=True),
        lax.all_gather(cols_o, "batch", axis=0, tiled=True),
        lax.all_gather(cols_a, "batch", axis=0, tiled=True),
        lax.all_gather(cols_u, "batch", axis=0, tiled=True),
        lax.all_gather(cols_d, "batch", axis=0, tiled=True),
    )
    silu_time = jax.nn.silu(time_embedding(timestep_row)).astype(jnp.bfloat16)
    emb_rows = matmul(silu_time, full_a)
    member = segment[:, None] == jnp.arange(CLIPS, dtype=jnp.int32)[None, :]
    one_hot = member.astype(jnp.float32)
    counted = member.astype(jnp.int32)
    modulation = jnp.dot(one_hot, emb_rows, precision=highest)
    shift_attn, scale_attn, gate_attn, shift_ffn, scale_ffn, gate_ffn = jnp.split(
        modulation, 6, axis=1
    )
    offsets = carried_in(
        jnp.sum(counted, axis=0), "seq", add_counts, jnp.zeros((CLIPS,), jnp.int32)
    )
    before = jnp.cumsum(counted, axis=0) - counted + offsets[None, :]
    position = jnp.sum(before * counted, axis=1).astype(jnp.float32)
    normed, inverse = normalize(inputs)
    attn_input = (normed * (1.0 + scale_attn) + shift_attn).astype(jnp.bfloat16)
    queries = rotate_pairs(
        matmul(attn_input, full_q).reshape(frame_count, HEADS, HEAD), position, 1.0
    ).astype(jnp.bfloat16)
    key_flat = (
        rotate_pairs(matmul(attn_input, full_k).reshape(frame_count, HEADS, HEAD), position, 1.0)
        .astype(jnp.bfloat16)
        .reshape(frame_count, D)
    )
    value_flat = matmul(attn_input, full_v).astype(jnp.bfloat16)
    key_codes = jnp.where(valid_row == 1, segment, -1).astype(jnp.bfloat16)
    query_codes = segment.astype(jnp.float32)
    start_state = (
        jnp.full((HEADS, frame_count), -1e30, jnp.float32),
        jnp.zeros((HEADS, frame_count), jnp.float32),
        jnp.zeros((frame_count, HEADS, HEAD), jnp.float32),
    )

    def step(state, key_block):
        return (forward_block(state, key_block, queries, query_codes), None)

    running_max, running_sum, accumulated = lax.scan(
        step,
        start_state,
        stack_blocks(
            (
                lax.all_gather(key_flat, "seq", axis=0, tiled=True),
                lax.all_gather(value_flat, "seq", axis=0, tiled=True),
                lax.all_gather(key_codes, "seq", axis=0, tiled=True),
            )
        ),
    )[0]
    attended = accumulated / running_sum.T[:, :, None]
    log_total = running_max + jnp.log(running_sum)
    attended_low = attended.reshape(frame_count, D).astype(jnp.bfloat16)
    attn_branch = matmul(attended_low, full_o)
    middle = inputs + gate_attn * attn_branch
    normed_mid, inverse_mid = normalize(middle)
    ffn_input = (normed_mid * (1.0 + scale_ffn) + shift_ffn).astype(jnp.bfloat16)
    hidden = matmul(ffn_input, full_u)
    activated, gelu_pull = jax.vjp(partial(jax.nn.gelu, approximate=True), hidden)
    activated_low = activated.astype(jnp.bfloat16)
    ffn_branch = matmul(activated_low, full_d)
    result = middle + gate_ffn * ffn_branch
    back_q, back_k, back_v, back_o, back_u, back_d = (
        full_q,
        full_k,
        full_v,
        full_o,
        full_u,
        full_d,
    )
    grad_gate_ffn = grad_output * ffn_branch
    g_ffn = (grad_output * gate_ffn).astype(jnp.bfloat16)
    grad_down_local = matmul(activated_low.T, g_ffn)
    grad_activated = matmul(g_ffn, back_d.T)
    g_hidden = gelu_pull(grad_activated)[0].astype(jnp.bfloat16)
    grad_up_local = matmul(ffn_input.T, g_hidden)
    grad_ffn_input = matmul(g_hidden, back_u.T)
    grad_middle = grad_output + norm_backward(
        grad_ffn_input * (1.0 + scale_ffn), normed_mid, inverse_mid
    )
    grad_scale_ffn = grad_ffn_input * normed_mid
    grad_gate_attn = grad_middle * attn_branch
    g_attn = (grad_middle * gate_attn).astype(jnp.bfloat16)
    grad_out_local = matmul(attended_low.T, g_attn)
    grad_attn = matmul(g_attn, back_o.T).astype(jnp.bfloat16).reshape(frame_count, HEADS, HEAD)
    delta_rows = jnp.einsum("qhe,qhe->hq", grad_attn.astype(jnp.float32), attended)
    zero_query = jnp.zeros((frame_count, HEADS, HEAD), jnp.float32)
    gathered = (
        lax.all_gather(key_flat, "seq", axis=0, tiled=True),
        lax.all_gather(value_flat, "seq", axis=0, tiled=True),
        lax.all_gather(key_codes, "seq", axis=0, tiled=True),
    )
    pack_rows = gathered[0].shape[0]
    grad_attn_wide = grad_attn.astype(jnp.float32)

    def joint_step(total_grad, key_block):
        probabilities, grad_scores = block_grads(
            key_block, queries, query_codes, grad_attn, log_total, delta_rows
        )
        total_grad = total_grad + 0.125 * jnp.einsum(
            "hqk,khe->qhe", grad_scores, key_block[0], preferred_element_type=jnp.float32
        )
        grad_keys = 0.125 * jnp.einsum(
            "hqk,qhe->khe", grad_scores, queries, preferred_element_type=jnp.float32
        )
        grad_values = jnp.einsum("hqk,qhe->khe", probabilities, grad_attn_wide, precision=highest)
        return (total_grad, (grad_keys, grad_values))

    grad_queries_rot, both_grads = lax.scan(joint_step, zero_query, stack_blocks(gathered))
    key_value_terms = jnp.concatenate(
        [both_grads[0].reshape(pack_rows, D), both_grads[1].reshape(pack_rows, D)], axis=1
    )
    key_value_grad = lax.psum_scatter(key_value_terms, "seq", scatter_dimension=0, tiled=True)
    g_query = (
        rotate_pairs(grad_queries_rot, position, -1.0).reshape(frame_count, D).astype(jnp.bfloat16)
    )
    g_key = (
        rotate_pairs(key_value_grad[:, :D].reshape(frame_count, HEADS, HEAD), position, -1.0)
        .reshape(frame_count, D)
        .astype(jnp.bfloat16)
    )
    g_value = key_value_grad[:, D:].astype(jnp.bfloat16)
    grad_query_local = matmul(attn_input.T, g_query)
    grad_key_local = matmul(attn_input.T, g_key)
    grad_value_local = matmul(attn_input.T, g_value)
    grad_attn_input = (
        matmul(g_query, back_q.T) + matmul(g_key, back_k.T) + matmul(g_value, back_v.T)
    )
    grad_inputs = grad_middle + norm_backward(grad_attn_input * (1.0 + scale_attn), normed, inverse)
    grad_modulation = jnp.concatenate(
        [
            grad_attn_input,
            grad_attn_input * normed,
            grad_gate_attn,
            grad_ffn_input,
            grad_scale_ffn,
            grad_gate_ffn,
        ],
        axis=1,
    )
    grad_emb = jnp.dot(one_hot.T, grad_modulation, precision=highest)
    grad_ada_local = jnp.dot(silu_time.astype(jnp.float32).T, grad_emb, precision=highest)
    part_q, part_k, part_v, part_o, part_a, part_u, part_d = (
        lax.psum_scatter(grad_query_local, "seq", scatter_dimension=1, tiled=True),
        lax.psum_scatter(grad_key_local, "seq", scatter_dimension=1, tiled=True),
        lax.psum_scatter(grad_value_local, "seq", scatter_dimension=1, tiled=True),
        lax.psum_scatter(grad_out_local, "seq", scatter_dimension=1, tiled=True),
        lax.psum_scatter(grad_ada_local, "seq", scatter_dimension=1, tiled=True),
        lax.psum_scatter(grad_up_local, "seq", scatter_dimension=1, tiled=True),
        lax.psum_scatter(grad_down_local, "seq", scatter_dimension=1, tiled=True),
    )
    final_q, final_k, final_v, final_o, final_a, final_u, final_d = (
        lax.psum_scatter(
            part_q.astype(jnp.bfloat16), "batch", scatter_dimension=0, tiled=True
        ).astype(jnp.float32),
        lax.psum_scatter(
            part_k.astype(jnp.bfloat16), "batch", scatter_dimension=0, tiled=True
        ).astype(jnp.float32),
        lax.psum_scatter(
            part_v.astype(jnp.bfloat16), "batch", scatter_dimension=0, tiled=True
        ).astype(jnp.float32),
        lax.psum_scatter(
            part_o.astype(jnp.bfloat16), "batch", scatter_dimension=0, tiled=True
        ).astype(jnp.float32),
        lax.psum_scatter(
            part_a.astype(jnp.bfloat16), "batch", scatter_dimension=0, tiled=True
        ).astype(jnp.float32),
        lax.psum_scatter(
            part_u.astype(jnp.bfloat16), "batch", scatter_dimension=0, tiled=True
        ).astype(jnp.float32),
        lax.psum_scatter(
            part_d.astype(jnp.bfloat16), "batch", scatter_dimension=0, tiled=True
        ).astype(jnp.float32),
    )
    return (
        result.astype(jnp.bfloat16)[None],
        grad_inputs.astype(jnp.bfloat16)[None],
        final_q,
        final_k,
        final_v,
        final_o,
        final_a,
        final_u,
        final_d,
    )


TWO = 2 * HEAD
ROWS = 256
BIG = 1e30
SEQ = 8
REPLICAS = 4
VMEM_MIB = 60
BLOCK = 256


def swap(part, axis, distance):
    size = SEQ if axis == "seq" else REPLICAS
    return lax.ppermute(part, axis, [(i, i ^ distance) for i in range(size)])


def exchange(blocks):
    return lax.all_to_all(blocks, "seq", 0, 0, tiled=True)


def turn(vectors, cosine, sine):
    lane = lax.broadcasted_iota(jnp.int32, vectors.shape, 1)
    first = (lane % HEAD) < HEAD // 2
    partner = jnp.where(
        first,
        pltpu.roll(vectors, TWO - HEAD // 2, 1),
        pltpu.roll(vectors, HEAD // 2, 1),
    )
    return vectors * cosine + partner * jnp.where(first, -sine, sine)


def of_head(vectors, head):
    lane = lax.broadcasted_iota(jnp.int32, vectors.shape, 1)
    return jnp.where(lane // HEAD == head, vectors, jnp.zeros_like(vectors))


def dot_t(left, right):
    return lax.dot_general(
        left, right, (((1,), (1,)), ((), ())), preferred_element_type=jnp.float32
    )


def project_kernel(place_ref, a_ref, b_ref, c_ref, d_ref, member_ref, bar_ref, cos_ref, sin_ref,
                   emb_ref, w_ref, *refs):
    x_ref, input_ref, q_ref, k_ref, kt_ref, v_ref, vt_ref, chunk_ref = refs[-8:]
    for step, ref in enumerate((a_ref, b_ref, c_ref, d_ref)):

        @pl.when(pl.program_id(0) == step)
        def _():
            chunk_ref[...] = ref[...]

    chunk = chunk_ref[...]
    x_ref[...] = chunk
    normed, _ = standardize(chunk.astype(jnp.float32))
    modulation = matmul(member_ref[...], emb_ref[...])
    low = (normed * (1.0 + modulation[:, D:]) + modulation[:, :D]).astype(jnp.bfloat16)
    input_ref[...] = low
    weight = jnp.concatenate([w_ref[b ^ place_ref[1]] for b in range(REPLICAS)], axis=0)
    product = matmul(low, weight)
    cosine, sine = cos_ref[...], sin_ref[...]
    keys = turn(product[:, TWO:2 * TWO], cosine, sine)
    values = product[:, 2 * TWO:]
    q_ref[...] = turn(product[:, :TWO], cosine, sine).astype(jnp.bfloat16)
    k_ref[:, :TWO] = keys.astype(jnp.bfloat16)
    k_ref[:, TWO:] = bar_ref[...]
    kt_ref[...] = keys.T.astype(jnp.bfloat16)
    v_ref[...] = values.astype(jnp.bfloat16)
    vt_ref[...] = values.T.astype(jnp.bfloat16)


def rows_spec(width):
    return pl.BlockSpec((ROWS, width), lambda i: (i, 0))


def cols_spec(height):
    return pl.BlockSpec((height, ROWS), lambda i: (0, i))


def whole_spec(height, width):
    return pl.BlockSpec((height, width), lambda i: (0, 0))


def params(mib):
    return pltpu.CompilerParams(
        dimension_semantics=("arbitrary",), vmem_limit_bytes=mib * 1024 * 1024
    )


def cost(micros):
    return pl.CostEstimate(
        flops=int(micros * 1e9), bytes_accessed=int(micros * 3e6), transcendentals=0
    )


def project(place, odd, chunks, member, bar, cosine, sine, emb, weights, earlier):
    frames = member.shape[0]
    low = jnp.bfloat16

    def rows(width):
        return pl.BlockSpec((ROWS, width), lambda i, p: ((2 * i + odd) ^ p[0], 0))

    def cols(height):
        return pl.BlockSpec((height, ROWS), lambda i, p: (0, (2 * i + odd) ^ p[0]))

    def whole(height, width):
        return pl.BlockSpec((height, width), lambda i, p: (0, 0))

    inputs = [place, *chunks, member, bar, cosine, sine, emb, weights, *earlier]
    first = len(inputs) - len(earlier)
    return pl.pallas_call(
        project_kernel,
        grid_spec=pltpu.PrefetchScalarGridSpec(
            num_scalar_prefetch=1,
            grid=(4,),
            in_specs=[whole(ROWS, D)] * 4 + [rows(TWO)] * 4
            + [whole(TWO, 2 * D),
               pl.BlockSpec((REPLICAS, ROWS, 3 * TWO), lambda i, p: (0, 0, 0))]
            + [pl.BlockSpec(memory_space=pl.ANY)] * len(earlier),
            out_specs=[rows(D), rows(D), rows(TWO), rows(2 * TWO), cols(TWO), rows(TWO),
                       cols(TWO)],
            scratch_shapes=[pltpu.VMEM((ROWS, D), low)],
        ),
        out_shape=[
            jax.ShapeDtypeStruct((frames, D), low),
            jax.ShapeDtypeStruct((frames, D), low),
            jax.ShapeDtypeStruct((frames, TWO), low),
            jax.ShapeDtypeStruct((frames, 2 * TWO), low),
            jax.ShapeDtypeStruct((TWO, frames), low),
            jax.ShapeDtypeStruct((frames, TWO), low),
            jax.ShapeDtypeStruct((TWO, frames), low),
        ],
        input_output_aliases={first + i: i for i in range(len(earlier))},
        compiler_params=params(30),
        cost_estimate=cost(2),
        name="project",
    )(*inputs)


def attend_kernel(q_ref, member_ref, k_ref, vt_ref, att_ref, low_ref, log_ref, *score_refs):
    frames = k_ref.shape[0]
    step = min(frames, 1024)
    queries = q_ref[...] * 0.125
    member = member_ref[...]
    bests, halves = [], []
    for head, score_ref in enumerate(score_refs):
        wide = jnp.concatenate([of_head(queries, head), member], axis=1)
        largest = jnp.full((1, BLOCK), -BIG, jnp.float32)
        for start in range(0, frames, step):
            scores = dot_t(k_ref[start:start + step, :], wide)
            score_ref[start:start + step, :] = scores
            largest = jnp.maximum(largest, jnp.max(scores, axis=0, keepdims=True))
        bests.append(largest)
    for head, score_ref in enumerate(score_refs):
        total = jnp.zeros((1, BLOCK), jnp.float32)
        out = jnp.zeros((TWO, BLOCK), jnp.float32)
        for start in range(0, frames, step):
            weights = jnp.exp(score_ref[start:start + step, :] - bests[head])
            total = total + jnp.sum(weights, axis=0, keepdims=True)
            out = out + matmul(vt_ref[:, start:start + step], weights.astype(jnp.bfloat16))
        halves.append(out[head * HEAD:(head + 1) * HEAD, :] / total)
        log_ref[head:head + 1, :] = bests[head] + jnp.log(total)
    attended = jnp.concatenate(halves, axis=0).T
    att_ref[...] = attended
    low_ref[...] = attended.astype(jnp.bfloat16)


def block_spec(width):
    return pl.BlockSpec((BLOCK, width), lambda i: (i, 0))


def attend(q, member, k, vt):
    frames = q.shape[0]
    return pl.pallas_call(
        attend_kernel,
        grid=(frames // BLOCK,),
        in_specs=[block_spec(TWO), block_spec(TWO), whole_spec(frames, 2 * TWO),
                  whole_spec(TWO, frames)],
        out_specs=[block_spec(TWO), block_spec(TWO), pl.BlockSpec((8, BLOCK), lambda i: (0, i))],
        out_shape=[
            jax.ShapeDtypeStruct((frames, TWO), jnp.float32),
            jax.ShapeDtypeStruct((frames, TWO), jnp.bfloat16),
            jax.ShapeDtypeStruct((8, frames), jnp.float32),
        ],
        scratch_shapes=[pltpu.VMEM((frames, BLOCK), jnp.float32)] * 2,
        compiler_params=params(26),
        cost_estimate=cost(18),
        name="attend",
    )(q, member, k, vt)


def attend_back_kernel(q_ref, member_ref, grad_ref, att_ref, log_ref, cos_ref, sin_ref, cos_all_ref,
                       sin_all_ref, k_ref, kt_ref, v_ref, g_ref, dk_ref, dv_ref):
    block = pl.program_id(0)
    frames = k_ref.shape[0]
    step = min(frames, 512)

    @pl.when(block == 0)
    def _():
        dk_ref[...] = jnp.zeros_like(dk_ref)
        dv_ref[...] = jnp.zeros_like(dv_ref)

    queries = q_ref[...] * 0.125
    member = member_ref[...]
    grad = grad_ref[...]
    mixed = (grad.astype(jnp.float32) * att_ref[...]).T
    halves = []
    wides, grads, deltas = [], [], []
    for head in range(2):
        wides.append(jnp.concatenate([of_head(queries, head), member], axis=1))
        grads.append(of_head(grad, head))
        deltas.append(jnp.sum(mixed[head * HEAD:(head + 1) * HEAD, :], axis=0, keepdims=True))
    totals = [jnp.zeros((TWO, ROWS), jnp.float32) for _ in range(2)]
    for start in range(0, frames, step):
        part = slice(start, start + step)
        dk = dk_ref[part, :]
        dv = dv_ref[part, :]
        for head in range(2):
            scores = dot_t(k_ref[part, :], wides[head])
            weights = jnp.exp(scores - log_ref[head:head + 1, :])
            grad_weights = dot_t(v_ref[part, :], grads[head])
            grad_scores = (weights * (grad_weights - deltas[head])).astype(jnp.bfloat16)
            dv = dv + matmul(weights.astype(jnp.bfloat16), grads[head])
            dk = dk + matmul(grad_scores, wides[head][:, :TWO])
            totals[head] = totals[head] + matmul(kt_ref[:, part], grad_scores)
        dk_ref[part, :] = dk
        dv_ref[part, :] = dv
    dq = jnp.concatenate([totals[0][:HEAD, :], totals[1][HEAD:, :]], axis=0).T * 0.125
    here = pl.ds(pl.multiple_of(block * ROWS, ROWS), ROWS)
    g_ref[here, :TWO] = turn(dq, cos_ref[...], -sin_ref[...]).astype(jnp.bfloat16)

    @pl.when(block == pl.num_programs(0) - 1)
    def _():
        turned = turn(dk_ref[...], cos_all_ref[...], -sin_all_ref[...])
        g_ref[:, TWO:2 * TWO] = turned.astype(jnp.bfloat16)
        g_ref[:, 2 * TWO:] = dv_ref[...].astype(jnp.bfloat16)


def attend_back(q, member, grad, att, log_total, cosine, sine, k, kt, v):
    frames = q.shape[0]
    return pl.pallas_call(
        attend_back_kernel,
        grid=(frames // ROWS,),
        in_specs=[rows_spec(TWO), rows_spec(TWO), rows_spec(TWO), rows_spec(TWO), cols_spec(8),
                  rows_spec(TWO), rows_spec(TWO), whole_spec(frames, TWO), whole_spec(frames, TWO),
                  whole_spec(frames, 2 * TWO), whole_spec(TWO, frames), whole_spec(frames, TWO)],
        out_specs=whole_spec(frames, 3 * TWO),
        out_shape=jax.ShapeDtypeStruct((frames, 3 * TWO), jnp.bfloat16),
        scratch_shapes=[pltpu.VMEM((frames, TWO), jnp.float32),
                        pltpu.VMEM((frames, TWO), jnp.float32)],
        compiler_params=params(VMEM_MIB),
        cost_estimate=cost(27),
        name="attend_back",
    )(q, member, grad, att, log_total, cosine, sine, cosine, sine, k, kt, v)


def three_terms(values):
    high = lax.reduce_precision(values, 8, 7)
    middle = lax.reduce_precision(values - high, 8, 7)
    return [high, middle, values - high - middle]


def standardize(rows):
    centered = rows - jnp.mean(rows, axis=1, keepdims=True)
    inverse = lax.rsqrt(jnp.mean(centered * centered, axis=1, keepdims=True) + 1e-06)
    return centered * inverse, inverse


def sum_of_clips(clip_ref, values):
    ids = lax.broadcasted_iota(jnp.int32, (CLIPS, clip_ref.shape[1]), 0)
    chosen = jnp.where(clip_ref[...] == ids, 1.0, 0.0).astype(jnp.bfloat16)
    high = values.astype(jnp.bfloat16)
    rest = values - high.astype(jnp.float32)
    middle = rest.astype(jnp.bfloat16)
    last = (rest - middle.astype(jnp.float32)).astype(jnp.bfloat16)
    return matmul(chosen, high) + matmul(chosen, middle) + matmul(chosen, last)


def beside(ref, tiles, rows):
    return jnp.concatenate([ref[tile, rows, :] for tile in tiles], axis=1)


def tile_index(away, apart):
    return 16 * (away % 2) + 8 * (away // 2) + 4 * (apart % 2) + apart // 2


def middle_kernel(mine_ref, x_ref, member_ref, clip_ref, cot_any, emb_any, tiles_ref,
                  result_any, grad_middle_ref, grad_att_ref, grad_emb_ref, left_any, right_any,
                  out_ref, up_ref, down_ref, cot_ref, emb_ref, result_ref, left_ref, right_ref,
                  sems, branch_ref, low_ref, act_ref, slope_ref, wide_ref):
    low = jnp.bfloat16
    act_t_ref, ffn_t_ref = left_ref.at[:2 * D], left_ref.at[2 * D:3 * D]
    mine_t_ref = left_ref.at[3 * D:]
    g_ffn_ref, g_attn_ref = right_ref.at[:, :D], right_ref.at[:, 3 * D:]
    g_hidden_ref = right_ref.at[:, D:3 * D]
    copies = [
        pltpu.make_async_copy(source, target, sems.at[i])
        for i, (source, target) in enumerate((
            (tiles_ref.at[:, pl.ds(0, 256), :], out_ref),
            (emb_any, emb_ref),
            (cot_any, cot_ref),
            (tiles_ref.at[:, pl.ds(256, 512), :], up_ref),
            (tiles_ref.at[:, pl.ds(768, 512), :], down_ref),
        ))
    ]
    for copy in copies:
        copy.start()
    stores = [
        pltpu.make_async_copy(source, target, sems.at[len(copies) + i])
        for i, (source, target) in enumerate((
            (mine_t_ref, left_any.at[3 * D:]),
            (ffn_t_ref, left_any.at[2 * D:3 * D]),
            (g_ffn_ref, right_any.at[:, :D]),
            (act_t_ref, left_any.at[:2 * D]),
            (result_ref, result_any),
            (g_hidden_ref, right_any.at[:, D:3 * D]),
            (g_attn_ref, right_any.at[:, 3 * D:]),
        ))
    ]

    def tile(b, s):
        return SEQ * b + s

    member = member_ref[...]

    def modulation(index):
        return matmul(member, emb_ref[:, index * D:(index + 1) * D])

    def cols(n, width=256):
        return pl.ds(pl.multiple_of(n * width, width), width)

    every = slice(None)
    mine = jnp.concatenate([mine_ref[j] for j in range(SEQ)], axis=1)
    low_ref[...] = mine
    mine_t_ref[...] = mine.T
    stores[0].start()
    copies[0].wait()

    @pl.loop(0, 4)
    def _(n):
        total = jnp.zeros((ROWS, 256), jnp.float32)
        for b in range(REPLICAS):
            weight = beside(out_ref, [tile(b, 2 * n), tile(b, 2 * n + 1)], every)
            total = total + matmul(low_ref[:, 256 * b:256 * b + 256], weight)
        branch_ref[:, cols(n)] = total

    copies[1].wait()
    gate_attn = modulation(2)
    branch = branch_ref[...]
    middle = x_ref[...].astype(jnp.float32) + gate_attn * branch
    normed, inverse = standardize(middle)
    scale_ffn = modulation(4)
    ffn_input = normed * (1.0 + scale_ffn) + modulation(3)
    low_ref[...] = ffn_input.astype(low)
    ffn_t_ref[...] = ffn_input.T.astype(low)
    gate_ffn = modulation(5)
    copies[2].wait()
    cot = cot_ref[...].astype(jnp.float32)
    g_ffn_ref[...] = (cot * gate_ffn).astype(low)
    stores[1].start()
    stores[2].start()
    copies[3].wait()

    @pl.loop(0, 8)
    def _(n):
        hidden = jnp.zeros((ROWS, 256), jnp.float32)
        for b in range(REPLICAS):
            index = tile(b, n)
            weight = jnp.concatenate([up_ref[index, :256, :], up_ref[index, 256:, :]], axis=1)
            hidden = hidden + matmul(low_ref[:, 256 * b:256 * b + 256], weight)
        root = math.sqrt(2.0 / math.pi)
        squared = hidden * hidden
        bent = jnp.tanh(root * (hidden + 0.044715 * (squared * hidden)))
        half = 0.5 * (1.0 + bent)
        activated = hidden * half
        slope = half + 0.5 * hidden * (1.0 - bent * bent) * (
            root * (1.0 + (3.0 * 0.044715) * squared)
        )
        act_ref[:, cols(n)] = activated.astype(low)
        act_t_ref[cols(n), :] = activated.T.astype(low)
        slope_ref[:, cols(n)] = slope

    stores[3].start()
    copies[4].wait()

    @pl.loop(0, 4)
    def _(n):
        total = jnp.zeros((ROWS, 256), jnp.float32)
        for b in range(REPLICAS):
            weight = beside(down_ref, [tile(b, 2 * n), tile(b, 2 * n + 1)], every)
            total = total + matmul(act_ref[:, 512 * b:512 * b + 512], weight)
        wide_ref[:, cols(n)] = total

    ffn_branch = wide_ref[...]
    result_ref[...] = (middle + gate_ffn * ffn_branch).astype(low)
    stores[4].start()
    grad_emb_ref[:, 3 * D:] = sum_of_clips(clip_ref, cot * ffn_branch)

    @pl.loop(0, REPLICAS)
    def _(b):
        weight = beside(down_ref, [tile(b, s) for s in range(SEQ)], every)
        grad = dot_t(g_ffn_ref[...], weight)
        here = cols(b, 512)
        g_hidden_ref[:, here] = (grad * slope_ref[:, here]).astype(low)

    stores[5].start()

    @pl.loop(0, REPLICAS)
    def _(b):
        weight = jnp.concatenate(
            [up_ref[tile(b, s), 256 * k:256 * k + 256, :] for s in range(SEQ) for k in range(2)],
            axis=1,
        )
        wide_ref[:, cols(b)] = dot_t(g_hidden_ref[...], weight)

    grad_ffn_input = wide_ref[...]
    grad_emb_ref[:, D:2 * D] = sum_of_clips(clip_ref, grad_ffn_input)
    grad_emb_ref[:, 2 * D:3 * D] = sum_of_clips(clip_ref, grad_ffn_input * normed)
    spread = grad_ffn_input * (1.0 + scale_ffn)
    grad_middle = cot + inverse * (
        spread
        - jnp.mean(spread, axis=1, keepdims=True)
        - normed * jnp.mean(spread * normed, axis=1, keepdims=True)
    )
    grad_middle_ref[...] = grad_middle
    grad_emb_ref[:, :D] = sum_of_clips(clip_ref, grad_middle * branch)
    g_attn_ref[...] = (grad_middle * gate_attn).astype(low)
    stores[6].start()

    @pl.loop(0, REPLICAS)
    def _(b):
        weight = beside(out_ref, [tile(b, s) for s in range(SEQ)], every)
        grad = dot_t(g_attn_ref[...], weight).astype(low)
        grad_att_ref[2 * b] = grad[:, :TWO]
        grad_att_ref[2 * b + 1] = grad[:, TWO:]

    for store in stores:
        store.wait()


def middle_part(mine, x, cot, member, clip_row, emb, tiles):
    low = jnp.bfloat16
    shapes = [
        ((ROWS, D), low), ((ROWS, D), jnp.float32), ((SEQ, ROWS, TWO), low),
        ((CLIPS, 4 * D), jnp.float32), ((4 * D, ROWS), low), ((ROWS, 4 * D), low),
    ]
    vmem, anywhere = pl.BlockSpec(memory_space=pltpu.VMEM), pl.BlockSpec(memory_space=pl.ANY)
    return pl.pallas_call(
        middle_kernel,
        in_specs=[vmem] * 4 + [anywhere] * 3,
        out_specs=[anywhere, vmem, vmem, vmem, anywhere, anywhere],
        out_shape=[jax.ShapeDtypeStruct(shape, dtype) for shape, dtype in shapes],
        scratch_shapes=[
            pltpu.VMEM((32, 256, 128), low),
            pltpu.VMEM((32, 512, 128), low),
            pltpu.VMEM((32, 512, 128), low),
            pltpu.VMEM((ROWS, D), low),
            pltpu.VMEM((TWO, 6 * D), low),
            pltpu.VMEM((ROWS, D), low),
            pltpu.VMEM((4 * D, ROWS), low),
            pltpu.VMEM((ROWS, 4 * D), low),
            pltpu.SemaphoreType.DMA((12,)),
            pltpu.VMEM((ROWS, D), jnp.float32),
            pltpu.VMEM((ROWS, D), low),
            pltpu.VMEM((ROWS, 2 * D), low),
            pltpu.VMEM((ROWS, 2 * D), jnp.float32),
            pltpu.VMEM((ROWS, D), jnp.float32),
        ],
        compiler_params=pltpu.CompilerParams(vmem_limit_bytes=VMEM_MIB * 1024 * 1024),
        cost_estimate=cost(20),
        name="middle",
    )(mine, x, member, clip_row, cot, emb, *tiles)


def weight_grads_kernel(place_ref, down_l, up_l, out_l, right_ref, down_o, up_o, out_o, other_ref,
                        away_d_ref, keep_d_ref, away_u_ref, keep_u_ref):
    low = jnp.bfloat16
    z, y = place_ref[2] // 2, place_ref[2] % 2
    lefts = [
        jnp.concatenate([mine[...], other[...]], axis=1)
        for mine, other in ((down_l, down_o), (up_l, up_o), (out_l, out_o))
    ]

    def product(left, first, block):
        here = pl.ds(pl.multiple_of(first + 256 * block, 256), 256)
        right = jnp.concatenate([right_ref[:, here], other_ref[:, here]], axis=0)
        return matmul(left, right).astype(low)

    def fill(ref):
        @pl.loop(0, 4)
        def _(k):
            block = z ^ k
            for left, first, rows in ((lefts[0], 0, slice(0, 512)), (lefts[2], 3 * D, slice(512, 768))):
                grad = product(left, first, block)
                ref[4 * y + k, rows, :] = grad[:, :128]
                ref[4 - 4 * y + k, rows, :] = grad[:, 128:]
            for side, up_ref in enumerate((keep_u_ref, away_u_ref)):
                grad = product(lefts[1], D, 2 * block + (y ^ side))
                up_ref[0, k, :256, :] = grad[:, :128]
                up_ref[0, k, 256:, :] = grad[:, 128:]

    @pl.when(pl.program_id(0) == 0)
    def _():
        fill(away_d_ref)

    @pl.when(pl.program_id(0) == 1)
    def _():
        fill(keep_d_ref)


def weight_grads(place, left, right, other_left, other_right):
    low = jnp.bfloat16

    def target(i, p):
        return 2 * jnp.where(i == 0, 1 - p[0], p[0]) + p[1]

    down = pl.BlockSpec((512, ROWS), lambda i, p: (target(i, p), 0))
    up = pl.BlockSpec((256, ROWS), lambda i, p: (8 + target(i, p), 0))
    out = pl.BlockSpec((256, ROWS), lambda i, p: (12 + target(i, p), 0))
    wide = pl.BlockSpec((ROWS, 4 * D), lambda i, p: (0, 0))
    whole = pl.BlockSpec((SEQ, 768, 128), lambda i, p: (0, 0, 0))
    part = pl.BlockSpec((1, 4, 512, 128), lambda i, p: (1 - i, 0, 0, 0))
    return pl.pallas_call(
        weight_grads_kernel,
        grid_spec=pltpu.PrefetchScalarGridSpec(
            num_scalar_prefetch=1,
            grid=(2,),
            in_specs=[down, up, out, wide] * 2,
            out_specs=[whole, whole, part, part],
        ),
        out_shape=[jax.ShapeDtypeStruct((SEQ, 768, 128), low)] * 2
        + [jax.ShapeDtypeStruct((2, 4, 512, 128), low)] * 2,
        compiler_params=params(VMEM_MIB),
        cost_estimate=cost(9),
        name="weight_grads",
    )(place, left, left, left, right, other_left, other_left, other_left, other_right)


def clip_grads_kernel(place_ref, x_ref, clip_ref, g_ref, w_ref, out_ref):
    @pl.when(pl.program_id(0) == 0)
    def _():
        out_ref[...] = jnp.zeros_like(out_ref)

    normed, _ = standardize(x_ref[...].astype(jnp.float32))
    grad = jnp.concatenate(
        [dot_t(g_ref[...], w_ref[b ^ place_ref[1]]) for b in range(REPLICAS)], axis=1
    )
    out_ref[:, :D] += sum_of_clips(clip_ref, grad)
    out_ref[:, D:] += sum_of_clips(clip_ref, grad * normed)


def clip_grads(places, x, clip_row, g_heads, heads_w):
    frames = x.shape[0]
    return pl.pallas_call(
        clip_grads_kernel,
        grid=(frames // ROWS,),
        in_specs=[pl.BlockSpec(memory_space=pltpu.SMEM), rows_spec(D), cols_spec(1),
                  rows_spec(3 * TWO),
                  pl.BlockSpec((REPLICAS, ROWS, 3 * TWO), lambda i: (0, 0, 0))],
        out_specs=whole_spec(CLIPS, 2 * D),
        out_shape=jax.ShapeDtypeStruct((CLIPS, 2 * D), jnp.float32),
        compiler_params=params(VMEM_MIB),
        cost_estimate=cost(9),
        name="clip_grads",
    )(places, x, clip_row, g_heads, heads_w)


def last_kernel(place_ref, own_ref, x_ref, grad_middle_ref, member_ref, emb_ref, *refs):
    *tile_refs, out_ref, wide_ref = refs
    grads = jnp.concatenate([own_ref[place_ref[2] ^ s] for s in range(SEQ)], axis=1)

    def tile(away, apart):
        index = tile_index(away, apart)
        for ref in tile_refs:
            if index < ref.shape[0]:
                return ref[index, ref.shape[1] - 768:, :]
            index -= ref.shape[0]

    for away in range(REPLICAS):
        weight = jnp.concatenate(
            [
                tile(away, s)[256 * k:256 * k + 256, :]
                for s in range(SEQ)
                for k in range(3)
            ],
            axis=1,
        )
        b = (2 * place_ref[0] + place_ref[1]) ^ away
        wide_ref[:, pl.ds(pl.multiple_of(b * 256, 256), 256)] = dot_t(grads, weight)

    normed, inverse = standardize(x_ref[...].astype(jnp.float32))
    spread = wide_ref[...] * (1.0 + matmul(member_ref[...], emb_ref[:, D:2 * D]))
    grad = grad_middle_ref[...] + inverse * (
        spread
        - jnp.mean(spread, axis=1, keepdims=True)
        - normed * jnp.mean(spread * normed, axis=1, keepdims=True)
    )
    out_ref[...] = grad.astype(jnp.bfloat16)


def last_part(place, own, x, grad_middle, member, emb, tiles):
    vmem = pl.BlockSpec(memory_space=pltpu.VMEM)
    return pl.pallas_call(
        last_kernel,
        in_specs=[pl.BlockSpec(memory_space=pltpu.SMEM)] + [vmem] * (5 + len(tiles)),
        out_specs=vmem,
        out_shape=jax.ShapeDtypeStruct((ROWS, D), jnp.bfloat16),
        scratch_shapes=[pltpu.VMEM((ROWS, D), jnp.float32)],
        compiler_params=pltpu.CompilerParams(vmem_limit_bytes=30 * 1024 * 1024),
        cost_estimate=cost(4),
        name="last",
    )(place, own, x, grad_middle, member, emb, *tiles)


def after(value, *others):
    return lax.optimization_barrier((value,) + others)[0]


def together(*values):
    return lax.optimization_barrier(values)


def plus(*terms):
    total = terms[0].astype(jnp.float32)
    for term in terms[1:]:
        total = total + term.astype(jnp.float32)
    return total


def clip_lanes(clip, terms):
    lane = jnp.arange(TWO, dtype=jnp.int32)[None, :]
    return (clip[:, None] == lane % CLIPS) & (lane < terms * CLIPS)


def body_fast(
    tokens, w_query, w_key, w_value, w_out, w_ada, w_up, w_down,
    segments, validity, timesteps, cotangent,
):
    highest = lax.Precision.HIGHEST
    low = jnp.bfloat16
    wide = jnp.float32
    replica = lax.axis_index("batch")
    x = tokens[0]
    frame_count = x.shape[0]
    frames = frame_count * SEQ
    segment = segments[0]

    seat = lax.axis_index("seq").astype(jnp.int32)
    z, y = seat // 2, seat % 2
    place = jnp.stack([replica // 2, replica % 2, seat]).astype(jnp.int32)
    mine_w = jnp.concatenate([w_out, w_up[:, :128], w_up[:, 128:], w_down], axis=0).astype(low)

    z1, z2, y0 = swap(x, "seq", 2), swap(x, "seq", 4), swap(x, "seq", 1)
    times = lax.all_gather(timesteps[0], "batch", axis=0, tiled=True)
    silu_all = jax.nn.silu(time_embedding(times)).astype(low)
    depth = w_ada.shape[0]
    silu_part = lax.dynamic_slice_in_dim(silu_all, replica * depth, depth, 1)
    emb_part = matmul(silu_part, w_ada.astype(low)).reshape(REPLICAS, CLIPS, -1)
    emb_cols = lax.all_to_all(emb_part, "batch", 0, 0, tiled=True)
    emb_cols = jnp.sum(emb_cols, axis=0)
    own_codes = (segment * 2 + (validity[0] == 1)).astype(wide)
    cols = emb_cols.shape[1]
    own_codes = jnp.pad(own_codes, (0, 8 * cols - frame_count)).reshape(8, cols)
    packed = jnp.concatenate([emb_cols, own_codes])
    packed = jnp.broadcast_to(packed[None], (SEQ,) + packed.shape)
    heads_w = jnp.concatenate([w_query, w_key, w_value], axis=1).astype(low)
    heads_w = jnp.stack([heads_w, swap(heads_w, "batch", 1)])
    z1, z2, y0, packed, heads_w, mine_w = together(z1, z2, y0, packed, heads_w, mine_w)
    tiles_w = (lax.all_gather(mine_w, ("batch", "seq"), axis=0),)
    packed = exchange(packed)
    z3 = swap(z2, "seq", 2)
    y1, y2 = swap(z1, "seq", 1), swap(z2, "seq", 1)
    heads_x = swap(heads_w, "batch", 2)
    z3, heads_x = together(z3, heads_x)
    y3 = swap(z3, "seq", 1)
    mine_h = jnp.concatenate([w_query, w_key, w_value], axis=0).astype(low)
    mine_h = after(mine_h, z3)
    h_z1, h_z2 = swap(mine_h, "seq", 2), swap(mine_h, "seq", 4)
    heads_w = jnp.concatenate([heads_w, heads_x])
    emb = packed[:, :CLIPS]
    codes = packed[:, CLIPS:].reshape(SEQ, -1)[:, :frame_count].reshape(frames).astype(jnp.int32)
    clip = codes // 2
    clip_row = clip[None, :]
    tri = jnp.arange(frame_count)[:, None] > jnp.arange(frame_count)[None, :]
    ids = jnp.arange(CLIPS, dtype=jnp.int32)
    one_hot = (clip.reshape(SEQ, frame_count)[:, :, None] == ids).astype(low)
    within = jnp.einsum("ij,njc->nic", tri.astype(low), one_hot, preferred_element_type=wide)
    counts = jnp.sum(one_hot.astype(wide), axis=1)
    offsets = jnp.cumsum(counts, axis=0) - counts
    position = jnp.sum(one_hot.astype(wide) * (within + offsets[:, None, :]), axis=2)
    half = HEAD // 2
    frequency = jnp.exp(-math.log(10000.0) * jnp.arange(half, dtype=wide) / half)
    angle = position.reshape(frames)[:, None] * jnp.tile(frequency, 4)[None, :]
    cosine, sine = jnp.cos(angle), jnp.sin(angle)
    member = clip_lanes(clip, 3).astype(low)
    allowed = clip_lanes(jnp.where(codes % 2 == 1, clip, -1), 1)
    inside = jnp.arange(TWO, dtype=jnp.int32)[None, :] < CLIPS
    bar = jnp.where(inside & ~allowed, -BIG, 0.0).astype(low)
    emb, y1, y2 = together(after(emb, heads_w, member, cosine), y1, y2)
    emb = emb.transpose(1, 0, 2).reshape(CLIPS, -1)
    emb = jnp.concatenate(
        [t.astype(low) for t in three_terms(emb)] + [jnp.zeros((TWO - 3 * CLIPS, 6 * D), low)],
        axis=0,
    )

    tables = (member, bar, cosine, sine, emb, heads_w)
    places = jnp.stack([seat, replica.astype(jnp.int32)])
    earlier = project(places, 0, (x, z1, z2, z3), *tables, ())
    y3, h_z1, h_z2, earlier = together(y3, h_z1, h_z2, earlier)
    h_z3 = swap(h_z2, "seq", 2)
    x_all, attn_input, q, k, kt, v, vt = project(places, 1, (y0, y1, y2, y3), *tables, earlier)
    attended, attended_low, log_total = attend(q, member, k, vt)
    attended_low, h_z3 = together(attended_low, h_z3)
    mine = exchange(attended_low.reshape(SEQ, frame_count, TWO))
    h_z = jnp.stack([mine_h, h_z1, h_z2, h_z3])
    mine, h_z = together(mine, h_z)
    h_y, h_x = swap(h_z, "seq", 1), swap(h_z, "batch", 2)

    own_member = clip_lanes(segment, 3).astype(low)
    result, grad_middle, grad_att, grad_emb, left, right = middle_part(
        mine, x, cotangent[0], own_member, segment[None, :], emb, tiles_w
    )
    left, h_y, h_x = together(left, h_y, h_x)
    other_left, other_right = swap(left, "batch", 1), swap(right, "batch", 1)
    h_first = jnp.concatenate([h_z, h_y, h_x])
    other_left, other_right, h_first = together(other_left, other_right, h_first)
    away_d, keep_d, away_u, keep_u = weight_grads(place, left, right, other_left, other_right)
    grad_heads = exchange(grad_att).reshape(frames, TWO)
    from_x = swap(away_d, "batch", 2)
    from_y = swap(away_u, "seq", 1)
    grad_heads = after(grad_heads, away_d, away_u)

    g_heads = attend_back(
        q, member, grad_heads, attended, log_total, cosine, sine, k, kt, v
    )
    own = exchange(g_heads.reshape(SEQ, frame_count, 3 * TWO))
    from_y = after(from_y, g_heads)
    to_x_u = plus(keep_u[1], from_y[1]).astype(low)
    from_x_u = swap(to_x_u, "batch", 2)
    from_x = after(from_x, to_x_u)
    to_y_d = plus(keep_d[4:], from_x[4:]).astype(low)
    from_y_d = swap(to_y_d, "seq", 1)
    h_yx = swap(after(h_y, to_y_d), "batch", 2)
    h_first_core = swap(after(h_first, to_x_u), "batch", 1)
    g_heads = after(g_heads, to_y_d, to_x_u)
    grad_heads_w = matmul(attn_input.T, g_heads).astype(low).reshape(2, 2, ROWS, 3 * TWO)
    grad_heads_w, from_x_u = together(grad_heads_w, from_x_u)
    part_u = plus(keep_u[0], from_y[0], from_x_u).astype(low)
    from_z_u = [swap(part_u[k], "seq", 2 * k) for k in range(1, 4)]
    late = clip_grads(places, x_all, clip_row, after(g_heads, part_u), heads_w)
    late, from_y_d, h_first_core = together(late, from_y_d, h_first_core)
    part = plus(keep_d[:4], from_x[:4], from_y_d).astype(low)
    late, own = together(late, own)
    grad_emb = jnp.concatenate([late, grad_emb], axis=1)
    grad_emb = exchange(grad_emb.reshape(CLIPS, SEQ, -1).transpose(1, 0, 2))
    grad_emb, *from_z_u = together(grad_emb, *from_z_u)
    grad_emb = jnp.sum(grad_emb, axis=0)
    x_place, core_place = replica // 2, replica % 2
    keep_h = lax.dynamic_index_in_dim(grad_heads_w, core_place, 1, False)
    other_h = swap(lax.dynamic_index_in_dim(grad_heads_w, 1 - core_place, 1, False), "batch", 1)
    h_yx_core = swap(after(h_yx, part), "batch", 1)
    from_z = [swap(part[k], "seq", 2 * k) for k in range(1, 4)]
    both_h = plus(keep_h, other_h).astype(low)
    away_h = swap(lax.dynamic_index_in_dim(both_h, 1 - x_place, 0, False), "batch", 2)

    grad_tokens = last_part(place, own, x, grad_middle, own_member, emb,
        (h_first, h_yx, h_first_core, h_yx_core),
    )
    grad_emb = lax.all_gather(after(grad_emb, grad_tokens), "batch", axis=0, tiled=True)
    final_a = jnp.dot(silu_part.astype(wide).T, grad_emb, precision=highest)
    grad_tokens, final_a, away_h, *from_z = together(grad_tokens, final_a, away_h, *from_z)
    final_heads = plus(lax.dynamic_index_in_dim(both_h, x_place, 0, False), away_h)
    total = plus(part[0], *from_z)
    final_d, final_o = total[:512], total[512:]
    total = plus(part_u[0], *from_z_u)
    final_u = jnp.concatenate([total[:256], total[256:]], axis=1)
    width = w_query.shape[1]
    return (
        result[None],
        grad_tokens[None],
        final_heads[:, :width],
        final_heads[:, width:2 * width],
        final_heads[:, 2 * width:],
        final_o,
        final_a,
        final_u,
        final_d,
    )


def solution(mesh):
    fits = mesh.shape["seq"] == SEQ and mesh.shape["batch"] == REPLICAS
    chosen = body_fast if fits else body
    return jax.shard_map(
        chosen,
        mesh=mesh,
        in_specs=(
            P("batch", "seq", None),
            P("batch", "seq"),
            P("batch", "seq"),
            P("batch", "seq"),
            P("batch", "seq"),
            P("batch", "seq"),
            P("batch", "seq"),
            P("batch", "seq"),
            P("batch", "seq"),
            P("batch", "seq"),
            P("batch", None),
            P("batch", "seq", None),
        ),
        out_specs=(
            P("batch", "seq", None),
            P("batch", "seq", None),
            P("batch", "seq"),
            P("batch", "seq"),
            P("batch", "seq"),
            P("batch", "seq"),
            P("batch", "seq"),
            P("batch", "seq"),
            P("batch", "seq"),
        ),
        check_vma=False,
    )
```

```python
from functools import partial
import math

import jax
import jax.numpy as jnp
from jax import lax
from jax.experimental import pallas as pl
from jax.experimental.pallas import tpu as pltpu
from jax.sharding import PartitionSpec as P

D = 1024
HEADS = 16
HEAD = 64
CLIPS = 16


def carried_in(part, axis, combine, identity):
    place = lax.axis_index(axis)
    gathered = lax.all_gather(part, axis)
    state = jnp.zeros_like(part) + jnp.asarray(identity, part.dtype)

    def one(step, state):
        return combine(state, lax.dynamic_index_in_dim(gathered, step, 0, False))

    return lax.fori_loop(0, place, one, state)


def matmul(left, right):
    return jnp.dot(left, right, preferred_element_type=jnp.float32)


def time_embedding(timestep_row):
    half_width = D // 2
    frequency = jnp.exp(-math.log(10000.0) * jnp.arange(half_width, dtype=jnp.float32) / half_width)
    angle = timestep_row.astype(jnp.float32)[:, None] * frequency[None, :]
    return jnp.concatenate([jnp.sin(angle), jnp.cos(angle)], axis=1)


def rotate_pairs(vectors, position, direction):
    half_size = vectors.shape[-1] // 2
    frequency = jnp.exp(-math.log(10000.0) * jnp.arange(half_size, dtype=jnp.float32) / half_size)
    angle = position[:, None] * frequency[None, :]
    cosine = jnp.cos(angle)[:, None, :]
    sine = jnp.sin(angle)[:, None, :] * direction
    first_half = vectors[..., :half_size]
    second_half = vectors[..., half_size:]
    return jnp.concatenate(
        [first_half * cosine - second_half * sine, second_half * cosine + first_half * sine],
        axis=-1,
    )


def normalize(inputs):
    centered = inputs - jnp.mean(inputs, axis=-1, keepdims=True)
    inverse = lax.rsqrt(jnp.mean(centered * centered, axis=-1, keepdims=True) + 1e-06)
    return (centered * inverse, inverse)


def norm_backward(grad_normed, normed, inverse):
    mean_grad = jnp.mean(grad_normed, axis=-1, keepdims=True)
    mean_mixed = jnp.mean(grad_normed * normed, axis=-1, keepdims=True)
    return inverse * (grad_normed - mean_grad - normed * mean_mixed)


def add_counts(earlier, later):
    return earlier + later


def block_rows_for(row_count):
    chosen = 1
    for candidate in range(1, 513):
        if row_count % candidate == 0:
            chosen = candidate
    return chosen


def stack_blocks(shard_piece):
    row_count = shard_piece[0].shape[0]
    block_rows = block_rows_for(row_count)
    block_count = row_count // block_rows
    return (
        shard_piece[0].reshape(block_count, block_rows, HEADS, HEAD),
        shard_piece[1].reshape(block_count, block_rows, HEADS, HEAD),
        shard_piece[2].reshape(block_count, block_rows),
    )


def forward_block(carried, key_block, queries, query_codes):
    running_max, running_sum, accumulated = carried
    key_rows, values, key_codes = key_block
    scores = (
        jnp.einsum("qhe,khe->hqk", queries, key_rows, preferred_element_type=jnp.float32) * 0.125
    )
    allowed = (query_codes[:, None] == key_codes.astype(jnp.float32)[None, :])[None]
    masked = jnp.where(allowed, scores, -1e30)
    new_max = jnp.maximum(running_max, jnp.max(masked, axis=2))
    rescale = jnp.exp(running_max - new_max)
    weights = jnp.where(allowed, jnp.exp(masked - new_max[:, :, None]), 0.0)
    running_sum = running_sum * rescale + jnp.sum(weights, axis=2)
    product = jnp.einsum(
        "hqk,khe->qhe", weights, values.astype(jnp.float32), precision=lax.Precision.HIGHEST
    )
    accumulated = accumulated * rescale.T[:, :, None] + product
    return (new_max, running_sum, accumulated)


def block_grads(key_block, queries, query_codes, grad_attn, log_total, delta_rows):
    key_rows, values, key_codes = key_block
    scores = (
        jnp.einsum("qhe,khe->hqk", queries, key_rows, preferred_element_type=jnp.float32) * 0.125
    )
    allowed = (query_codes[:, None] == key_codes.astype(jnp.float32)[None, :])[None]
    probabilities = jnp.exp(jnp.where(allowed, scores, -1e30) - log_total[:, :, None])
    grad_probs = jnp.einsum("qhe,khe->hqk", grad_attn, values, preferred_element_type=jnp.float32)
    grad_scores = (probabilities * (grad_probs - delta_rows[:, :, None])).astype(jnp.bfloat16)
    return (probabilities, grad_scores)


def body(
    tokens,
    w_query,
    w_key,
    w_value,
    w_out,
    w_ada,
    w_up,
    w_down,
    segments,
    validity,
    timesteps,
    cotangent,
):
    inputs = tokens[0].astype(jnp.float32)
    segment = segments[0]
    valid_row = validity[0]
    timestep_row = timesteps[0]
    grad_output = cotangent[0].astype(jnp.float32)
    frame_count = inputs.shape[0]
    highest = lax.Precision.HIGHEST
    cols_q, cols_k, cols_v, cols_o, cols_a, cols_u, cols_d = (
        lax.all_gather(w_query.astype(jnp.bfloat16), "seq", axis=1, tiled=True),
        lax.all_gather(w_key.astype(jnp.bfloat16), "seq", axis=1, tiled=True),
        lax.all_gather(w_value.astype(jnp.bfloat16), "seq", axis=1, tiled=True),
        lax.all_gather(w_out.astype(jnp.bfloat16), "seq", axis=1, tiled=True),
        lax.all_gather(w_ada.astype(jnp.bfloat16), "seq", axis=1, tiled=True),
        lax.all_gather(w_up.astype(jnp.bfloat16), "seq", axis=1, tiled=True),
        lax.all_gather(w_down.astype(jnp.bfloat16), "seq", axis=1, tiled=True),
    )
    full_q, full_k, full_v, full_o, full_a, full_u, full_d = (
        lax.all_gather(cols_q, "batch", axis=0, tiled=True),
        lax.all_gather(cols_k, "batch", axis=0, tiled=True),
        lax.all_gather(cols_v, "batch", axis=0, tiled=True),
        lax.all_gather(cols_o, "batch", axis=0, tiled=True),
        lax.all_gather(cols_a, "batch", axis=0, tiled=True),
        lax.all_gather(cols_u, "batch", axis=0, tiled=True),
        lax.all_gather(cols_d, "batch", axis=0, tiled=True),
    )
    silu_time = jax.nn.silu(time_embedding(timestep_row)).astype(jnp.bfloat16)
    emb_rows = matmul(silu_time, full_a)
    member = segment[:, None] == jnp.arange(CLIPS, dtype=jnp.int32)[None, :]
    one_hot = member.astype(jnp.float32)
    counted = member.astype(jnp.int32)
    modulation = jnp.dot(one_hot, emb_rows, precision=highest)
    shift_attn, scale_attn, gate_attn, shift_ffn, scale_ffn, gate_ffn = jnp.split(
        modulation, 6, axis=1
    )
    offsets = carried_in(
        jnp.sum(counted, axis=0), "seq", add_counts, jnp.zeros((CLIPS,), jnp.int32)
    )
    before = jnp.cumsum(counted, axis=0) - counted + offsets[None, :]
    position = jnp.sum(before * counted, axis=1).astype(jnp.float32)
    normed, inverse = normalize(inputs)
    attn_input = (normed * (1.0 + scale_attn) + shift_attn).astype(jnp.bfloat16)
    queries = rotate_pairs(
        matmul(attn_input, full_q).reshape(frame_count, HEADS, HEAD), position, 1.0
    ).astype(jnp.bfloat16)
    key_flat = (
        rotate_pairs(matmul(attn_input, full_k).reshape(frame_count, HEADS, HEAD), position, 1.0)
        .astype(jnp.bfloat16)
        .reshape(frame_count, D)
    )
    value_flat = matmul(attn_input, full_v).astype(jnp.bfloat16)
    key_codes = jnp.where(valid_row == 1, segment, -1).astype(jnp.bfloat16)
    query_codes = segment.astype(jnp.float32)
    start_state = (
        jnp.full((HEADS, frame_count), -1e30, jnp.float32),
        jnp.zeros((HEADS, frame_count), jnp.float32),
        jnp.zeros((frame_count, HEADS, HEAD), jnp.float32),
    )

    def step(state, key_block):
        return (forward_block(state, key_block, queries, query_codes), None)

    running_max, running_sum, accumulated = lax.scan(
        step,
        start_state,
        stack_blocks(
            (
                lax.all_gather(key_flat, "seq", axis=0, tiled=True),
                lax.all_gather(value_flat, "seq", axis=0, tiled=True),
                lax.all_gather(key_codes, "seq", axis=0, tiled=True),
            )
        ),
    )[0]
    attended = accumulated / running_sum.T[:, :, None]
    log_total = running_max + jnp.log(running_sum)
    attended_low = attended.reshape(frame_count, D).astype(jnp.bfloat16)
    attn_branch = matmul(attended_low, full_o)
    middle = inputs + gate_attn * attn_branch
    normed_mid, inverse_mid = normalize(middle)
    ffn_input = (normed_mid * (1.0 + scale_ffn) + shift_ffn).astype(jnp.bfloat16)
    hidden = matmul(ffn_input, full_u)
    activated, gelu_pull = jax.vjp(partial(jax.nn.gelu, approximate=True), hidden)
    activated_low = activated.astype(jnp.bfloat16)
    ffn_branch = matmul(activated_low, full_d)
    result = middle + gate_ffn * ffn_branch
    back_q, back_k, back_v, back_o, back_u, back_d = (
        full_q,
        full_k,
        full_v,
        full_o,
        full_u,
        full_d,
    )
    grad_gate_ffn = grad_output * ffn_branch
    g_ffn = (grad_output * gate_ffn).astype(jnp.bfloat16)
    grad_down_local = matmul(activated_low.T, g_ffn)
    grad_activated = matmul(g_ffn, back_d.T)
    g_hidden = gelu_pull(grad_activated)[0].astype(jnp.bfloat16)
    grad_up_local = matmul(ffn_input.T, g_hidden)
    grad_ffn_input = matmul(g_hidden, back_u.T)
    grad_middle = grad_output + norm_backward(
        grad_ffn_input * (1.0 + scale_ffn), normed_mid, inverse_mid
    )
    grad_scale_ffn = grad_ffn_input * normed_mid
    grad_gate_attn = grad_middle * attn_branch
    g_attn = (grad_middle * gate_attn).astype(jnp.bfloat16)
    grad_out_local = matmul(attended_low.T, g_attn)
    grad_attn = matmul(g_attn, back_o.T).astype(jnp.bfloat16).reshape(frame_count, HEADS, HEAD)
    delta_rows = jnp.einsum("qhe,qhe->hq", grad_attn.astype(jnp.float32), attended)
    zero_query = jnp.zeros((frame_count, HEADS, HEAD), jnp.float32)
    gathered = (
        lax.all_gather(key_flat, "seq", axis=0, tiled=True),
        lax.all_gather(value_flat, "seq", axis=0, tiled=True),
        lax.all_gather(key_codes, "seq", axis=0, tiled=True),
    )
    pack_rows = gathered[0].shape[0]
    grad_attn_wide = grad_attn.astype(jnp.float32)

    def joint_step(total_grad, key_block):
        probabilities, grad_scores = block_grads(
            key_block, queries, query_codes, grad_attn, log_total, delta_rows
        )
        total_grad = total_grad + 0.125 * jnp.einsum(
            "hqk,khe->qhe", grad_scores, key_block[0], preferred_element_type=jnp.float32
        )
        grad_keys = 0.125 * jnp.einsum(
            "hqk,qhe->khe", grad_scores, queries, preferred_element_type=jnp.float32
        )
        grad_values = jnp.einsum("hqk,qhe->khe", probabilities, grad_attn_wide, precision=highest)
        return (total_grad, (grad_keys, grad_values))

    grad_queries_rot, both_grads = lax.scan(joint_step, zero_query, stack_blocks(gathered))
    key_value_terms = jnp.concatenate(
        [both_grads[0].reshape(pack_rows, D), both_grads[1].reshape(pack_rows, D)], axis=1
    )
    key_value_grad = lax.psum_scatter(key_value_terms, "seq", scatter_dimension=0, tiled=True)
    g_query = (
        rotate_pairs(grad_queries_rot, position, -1.0).reshape(frame_count, D).astype(jnp.bfloat16)
    )
    g_key = (
        rotate_pairs(key_value_grad[:, :D].reshape(frame_count, HEADS, HEAD), position, -1.0)
        .reshape(frame_count, D)
        .astype(jnp.bfloat16)
    )
    g_value = key_value_grad[:, D:].astype(jnp.bfloat16)
    grad_query_local = matmul(attn_input.T, g_query)
    grad_key_local = matmul(attn_input.T, g_key)
    grad_value_local = matmul(attn_input.T, g_value)
    grad_attn_input = (
        matmul(g_query, back_q.T) + matmul(g_key, back_k.T) + matmul(g_value, back_v.T)
    )
    grad_inputs = grad_middle + norm_backward(grad_attn_input * (1.0 + scale_attn), normed, inverse)
    grad_modulation = jnp.concatenate(
        [
            grad_attn_input,
            grad_attn_input * normed,
            grad_gate_attn,
            grad_ffn_input,
            grad_scale_ffn,
            grad_gate_ffn,
        ],
        axis=1,
    )
    grad_emb = jnp.dot(one_hot.T, grad_modulation, precision=highest)
    grad_ada_local = jnp.dot(silu_time.astype(jnp.float32).T, grad_emb, precision=highest)
    part_q, part_k, part_v, part_o, part_a, part_u, part_d = (
        lax.psum_scatter(grad_query_local, "seq", scatter_dimension=1, tiled=True),
        lax.psum_scatter(grad_key_local, "seq", scatter_dimension=1, tiled=True),
        lax.psum_scatter(grad_value_local, "seq", scatter_dimension=1, tiled=True),
        lax.psum_scatter(grad_out_local, "seq", scatter_dimension=1, tiled=True),
        lax.psum_scatter(grad_ada_local, "seq", scatter_dimension=1, tiled=True),
        lax.psum_scatter(grad_up_local, "seq", scatter_dimension=1, tiled=True),
        lax.psum_scatter(grad_down_local, "seq", scatter_dimension=1, tiled=True),
    )
    final_q, final_k, final_v, final_o, final_a, final_u, final_d = (
        lax.psum_scatter(
            part_q.astype(jnp.bfloat16), "batch", scatter_dimension=0, tiled=True
        ).astype(jnp.float32),
        lax.psum_scatter(
            part_k.astype(jnp.bfloat16), "batch", scatter_dimension=0, tiled=True
        ).astype(jnp.float32),
        lax.psum_scatter(
            part_v.astype(jnp.bfloat16), "batch", scatter_dimension=0, tiled=True
        ).astype(jnp.float32),
        lax.psum_scatter(
            part_o.astype(jnp.bfloat16), "batch", scatter_dimension=0, tiled=True
        ).astype(jnp.float32),
        lax.psum_scatter(
            part_a.astype(jnp.bfloat16), "batch", scatter_dimension=0, tiled=True
        ).astype(jnp.float32),
        lax.psum_scatter(
            part_u.astype(jnp.bfloat16), "batch", scatter_dimension=0, tiled=True
        ).astype(jnp.float32),
        lax.psum_scatter(
            part_d.astype(jnp.bfloat16), "batch", scatter_dimension=0, tiled=True
        ).astype(jnp.float32),
    )
    return (
        result.astype(jnp.bfloat16)[None],
        grad_inputs.astype(jnp.bfloat16)[None],
        final_q,
        final_k,
        final_v,
        final_o,
        final_a,
        final_u,
        final_d,
    )


TWO = 2 * HEAD
ROWS = 256
BIG = 1e30
SEQ = 8
REPLICAS = 4
VMEM_MIB = 60
BLOCK = 256


def swap(part, axis, distance):
    size = SEQ if axis == "seq" else REPLICAS
    return lax.ppermute(part, axis, [(i, i ^ distance) for i in range(size)])


def exchange(blocks):
    return lax.all_to_all(blocks, "seq", 0, 0, tiled=True)


def turn(vectors, cosine, sine):
    lane = lax.broadcasted_iota(jnp.int32, vectors.shape, 1)
    first = (lane % HEAD) < HEAD // 2
    partner = jnp.where(
        first,
        pltpu.roll(vectors, TWO - HEAD // 2, 1),
        pltpu.roll(vectors, HEAD // 2, 1),
    )
    return vectors * cosine + partner * jnp.where(first, -sine, sine)


def of_head(vectors, head):
    lane = lax.broadcasted_iota(jnp.int32, vectors.shape, 1)
    return jnp.where(lane // HEAD == head, vectors, jnp.zeros_like(vectors))


def dot_t(left, right):
    return lax.dot_general(
        left, right, (((1,), (1,)), ((), ())), preferred_element_type=jnp.float32
    )


def project_kernel(place_ref, a_ref, b_ref, c_ref, d_ref, member_ref, bar_ref, cos_ref, sin_ref,
                   emb_ref, w_ref, *refs):
    x_ref, input_ref, q_ref, k_ref, kt_ref, v_ref, vt_ref, chunk_ref = refs[-8:]
    for step, ref in enumerate((a_ref, b_ref, c_ref, d_ref)):

        @pl.when(pl.program_id(0) == step)
        def _():
            chunk_ref[...] = ref[...]

    chunk = chunk_ref[...]
    x_ref[...] = chunk
    normed, _ = standardize(chunk.astype(jnp.float32))
    modulation = matmul(member_ref[...], emb_ref[...])
    low = (normed * (1.0 + modulation[:, D:]) + modulation[:, :D]).astype(jnp.bfloat16)
    input_ref[...] = low
    weight = jnp.concatenate([w_ref[b ^ place_ref[1]] for b in range(REPLICAS)], axis=0)
    product = matmul(low, weight)
    cosine, sine = cos_ref[...], sin_ref[...]
    keys = turn(product[:, TWO:2 * TWO], cosine, sine)
    values = product[:, 2 * TWO:]
    q_ref[...] = turn(product[:, :TWO], cosine, sine).astype(jnp.bfloat16)
    k_ref[:, :TWO] = keys.astype(jnp.bfloat16)
    k_ref[:, TWO:] = bar_ref[...]
    kt_ref[...] = keys.T.astype(jnp.bfloat16)
    v_ref[...] = values.astype(jnp.bfloat16)
    vt_ref[...] = values.T.astype(jnp.bfloat16)


def rows_spec(width):
    return pl.BlockSpec((ROWS, width), lambda i: (i, 0))


def cols_spec(height):
    return pl.BlockSpec((height, ROWS), lambda i: (0, i))


def whole_spec(height, width):
    return pl.BlockSpec((height, width), lambda i: (0, 0))


def params(mib):
    return pltpu.CompilerParams(
        dimension_semantics=("arbitrary",), vmem_limit_bytes=mib * 1024 * 1024
    )


def cost(micros):
    return pl.CostEstimate(
        flops=int(micros * 1e9), bytes_accessed=int(micros * 3e6), transcendentals=0
    )


def project(place, odd, chunks, member, bar, cosine, sine, emb, weights, earlier):
    frames = member.shape[0]
    low = jnp.bfloat16

    def rows(width):
        return pl.BlockSpec((ROWS, width), lambda i, p: ((2 * i + odd) ^ p[0], 0))

    def cols(height):
        return pl.BlockSpec((height, ROWS), lambda i, p: (0, (2 * i + odd) ^ p[0]))

    def whole(height, width):
        return pl.BlockSpec((height, width), lambda i, p: (0, 0))

    inputs = [place, *chunks, member, bar, cosine, sine, emb, weights, *earlier]
    first = len(inputs) - len(earlier)
    return pl.pallas_call(
        project_kernel,
        grid_spec=pltpu.PrefetchScalarGridSpec(
            num_scalar_prefetch=1,
            grid=(4,),
            in_specs=[whole(ROWS, D)] * 4 + [rows(TWO)] * 4
            + [whole(TWO, 2 * D),
               pl.BlockSpec((REPLICAS, ROWS, 3 * TWO), lambda i, p: (0, 0, 0))]
            + [pl.BlockSpec(memory_space=pl.ANY)] * len(earlier),
            out_specs=[rows(D), rows(D), rows(TWO), rows(2 * TWO), cols(TWO), rows(TWO),
                       cols(TWO)],
            scratch_shapes=[pltpu.VMEM((ROWS, D), low)],
        ),
        out_shape=[
            jax.ShapeDtypeStruct((frames, D), low),
            jax.ShapeDtypeStruct((frames, D), low),
            jax.ShapeDtypeStruct((frames, TWO), low),
            jax.ShapeDtypeStruct((frames, 2 * TWO), low),
            jax.ShapeDtypeStruct((TWO, frames), low),
            jax.ShapeDtypeStruct((frames, TWO), low),
            jax.ShapeDtypeStruct((TWO, frames), low),
        ],
        input_output_aliases={first + i: i for i in range(len(earlier))},
        compiler_params=params(30),
        cost_estimate=cost(2),
        name="project",
    )(*inputs)


def attend_kernel(q_ref, member_ref, k_ref, vt_ref, att_ref, low_ref, log_ref, *score_refs):
    frames = k_ref.shape[0]
    step = min(frames, 1024)
    queries = q_ref[...] * 0.125
    member = member_ref[...]
    bests, halves = [], []
    for head, score_ref in enumerate(score_refs):
        wide = jnp.concatenate([of_head(queries, head), member], axis=1)
        largest = jnp.full((1, BLOCK), -BIG, jnp.float32)
        for start in range(0, frames, step):
            scores = dot_t(k_ref[start:start + step, :], wide)
            score_ref[start:start + step, :] = scores
            largest = jnp.maximum(largest, jnp.max(scores, axis=0, keepdims=True))
        bests.append(largest)
    for head, score_ref in enumerate(score_refs):
        total = jnp.zeros((1, BLOCK), jnp.float32)
        out = jnp.zeros((TWO, BLOCK), jnp.float32)
        for start in range(0, frames, step):
            weights = jnp.exp(score_ref[start:start + step, :] - bests[head])
            total = total + jnp.sum(weights, axis=0, keepdims=True)
            out = out + matmul(vt_ref[:, start:start + step], weights.astype(jnp.bfloat16))
        halves.append(out[head * HEAD:(head + 1) * HEAD, :] / total)
        log_ref[head:head + 1, :] = bests[head] + jnp.log(total)
    attended = jnp.concatenate(halves, axis=0).T
    att_ref[...] = attended
    low_ref[...] = attended.astype(jnp.bfloat16)


def block_spec(width):
    return pl.BlockSpec((BLOCK, width), lambda i: (i, 0))


def attend(q, member, k, vt):
    frames = q.shape[0]
    return pl.pallas_call(
        attend_kernel,
        grid=(frames // BLOCK,),
        in_specs=[block_spec(TWO), block_spec(TWO), whole_spec(frames, 2 * TWO),
                  whole_spec(TWO, frames)],
        out_specs=[block_spec(TWO), block_spec(TWO), pl.BlockSpec((8, BLOCK), lambda i: (0, i))],
        out_shape=[
            jax.ShapeDtypeStruct((frames, TWO), jnp.float32),
            jax.ShapeDtypeStruct((frames, TWO), jnp.bfloat16),
            jax.ShapeDtypeStruct((8, frames), jnp.float32),
        ],
        scratch_shapes=[pltpu.VMEM((frames, BLOCK), jnp.float32)] * 2,
        compiler_params=params(26),
        cost_estimate=cost(18),
        name="attend",
    )(q, member, k, vt)


def attend_back_kernel(q_ref, member_ref, grad_ref, att_ref, log_ref, cos_ref, sin_ref, cos_all_ref,
                       sin_all_ref, k_ref, kt_ref, v_ref, g_ref, dk_ref, dv_ref):
    block = pl.program_id(0)
    frames = k_ref.shape[0]
    step = min(frames, 512)

    @pl.when(block == 0)
    def _():
        dk_ref[...] = jnp.zeros_like(dk_ref)
        dv_ref[...] = jnp.zeros_like(dv_ref)

    queries = q_ref[...] * 0.125
    member = member_ref[...]
    grad = grad_ref[...]
    mixed = (grad.astype(jnp.float32) * att_ref[...]).T
    halves = []
    wides, grads, deltas = [], [], []
    for head in range(2):
        wides.append(jnp.concatenate([of_head(queries, head), member], axis=1))
        grads.append(of_head(grad, head))
        deltas.append(jnp.sum(mixed[head * HEAD:(head + 1) * HEAD, :], axis=0, keepdims=True))
    totals = [jnp.zeros((TWO, ROWS), jnp.float32) for _ in range(2)]
    for start in range(0, frames, step):
        part = slice(start, start + step)
        dk = dk_ref[part, :]
        dv = dv_ref[part, :]
        for head in range(2):
            scores = dot_t(k_ref[part, :], wides[head])
            weights = jnp.exp(scores - log_ref[head:head + 1, :])
            grad_weights = dot_t(v_ref[part, :], grads[head])
            grad_scores = (weights * (grad_weights - deltas[head])).astype(jnp.bfloat16)
            dv = dv + matmul(weights.astype(jnp.bfloat16), grads[head])
            dk = dk + matmul(grad_scores, wides[head][:, :TWO])
            totals[head] = totals[head] + matmul(kt_ref[:, part], grad_scores)
        dk_ref[part, :] = dk
        dv_ref[part, :] = dv
    dq = jnp.concatenate([totals[0][:HEAD, :], totals[1][HEAD:, :]], axis=0).T * 0.125
    here = pl.ds(pl.multiple_of(block * ROWS, ROWS), ROWS)
    g_ref[here, :TWO] = turn(dq, cos_ref[...], -sin_ref[...]).astype(jnp.bfloat16)

    @pl.when(block == pl.num_programs(0) - 1)
    def _():
        turned = turn(dk_ref[...], cos_all_ref[...], -sin_all_ref[...])
        g_ref[:, TWO:2 * TWO] = turned.astype(jnp.bfloat16)
        g_ref[:, 2 * TWO:] = dv_ref[...].astype(jnp.bfloat16)


def attend_back(q, member, grad, att, log_total, cosine, sine, k, kt, v):
    frames = q.shape[0]
    return pl.pallas_call(
        attend_back_kernel,
        grid=(frames // ROWS,),
        in_specs=[rows_spec(TWO), rows_spec(TWO), rows_spec(TWO), rows_spec(TWO), cols_spec(8),
                  rows_spec(TWO), rows_spec(TWO), whole_spec(frames, TWO), whole_spec(frames, TWO),
                  whole_spec(frames, 2 * TWO), whole_spec(TWO, frames), whole_spec(frames, TWO)],
        out_specs=whole_spec(frames, 3 * TWO),
        out_shape=jax.ShapeDtypeStruct((frames, 3 * TWO), jnp.bfloat16),
        scratch_shapes=[pltpu.VMEM((frames, TWO), jnp.float32),
                        pltpu.VMEM((frames, TWO), jnp.float32)],
        compiler_params=params(VMEM_MIB),
        cost_estimate=cost(27),
        name="attend_back",
    )(q, member, grad, att, log_total, cosine, sine, cosine, sine, k, kt, v)


def three_terms(values):
    high = lax.reduce_precision(values, 8, 7)
    middle = lax.reduce_precision(values - high, 8, 7)
    return [high, middle, values - high - middle]


def standardize(rows):
    centered = rows - jnp.mean(rows, axis=1, keepdims=True)
    inverse = lax.rsqrt(jnp.mean(centered * centered, axis=1, keepdims=True) + 1e-06)
    return centered * inverse, inverse


def sum_of_clips(clip_ref, values):
    ids = lax.broadcasted_iota(jnp.int32, (CLIPS, clip_ref.shape[1]), 0)
    chosen = jnp.where(clip_ref[...] == ids, 1.0, 0.0).astype(jnp.bfloat16)
    high = values.astype(jnp.bfloat16)
    rest = values - high.astype(jnp.float32)
    middle = rest.astype(jnp.bfloat16)
    last = (rest - middle.astype(jnp.float32)).astype(jnp.bfloat16)
    return matmul(chosen, high) + matmul(chosen, middle) + matmul(chosen, last)


def beside(ref, tiles, rows):
    return jnp.concatenate([ref[tile, rows, :] for tile in tiles], axis=1)


def tile_index(away, apart):
    return 16 * (away % 2) + 8 * (away // 2) + 4 * (apart % 2) + apart // 2


def middle_kernel(mine_ref, x_ref, member_ref, clip_ref, cot_any, emb_any, tiles_ref,
                  result_any, grad_middle_ref, grad_att_ref, grad_emb_ref, left_any, right_any,
                  out_ref, up_ref, down_ref, cot_ref, emb_ref, result_ref, left_ref, right_ref,
                  sems, branch_ref, low_ref, act_ref, slope_ref, wide_ref):
    low = jnp.bfloat16
    act_t_ref, ffn_t_ref = left_ref.at[:2 * D], left_ref.at[2 * D:3 * D]
    mine_t_ref = left_ref.at[3 * D:]
    g_ffn_ref, g_attn_ref = right_ref.at[:, :D], right_ref.at[:, 3 * D:]
    g_hidden_ref = right_ref.at[:, D:3 * D]
    copies = [
        pltpu.make_async_copy(source, target, sems.at[i])
        for i, (source, target) in enumerate((
            (tiles_ref.at[:, pl.ds(0, 256), :], out_ref),
            (emb_any, emb_ref),
            (cot_any, cot_ref),
            (tiles_ref.at[:, pl.ds(256, 512), :], up_ref),
            (tiles_ref.at[:, pl.ds(768, 512), :], down_ref),
        ))
    ]
    for copy in copies:
        copy.start()
    stores = [
        pltpu.make_async_copy(source, target, sems.at[len(copies) + i])
        for i, (source, target) in enumerate((
            (mine_t_ref, left_any.at[3 * D:]),
            (ffn_t_ref, left_any.at[2 * D:3 * D]),
            (g_ffn_ref, right_any.at[:, :D]),
            (act_t_ref, left_any.at[:2 * D]),
            (result_ref, result_any),
            (g_hidden_ref, right_any.at[:, D:3 * D]),
            (g_attn_ref, right_any.at[:, 3 * D:]),
        ))
    ]

    def tile(b, s):
        return SEQ * b + s

    member = member_ref[...]

    def modulation(index):
        return matmul(member, emb_ref[:, index * D:(index + 1) * D])

    def cols(n, width=256):
        return pl.ds(pl.multiple_of(n * width, width), width)

    every = slice(None)
    mine = jnp.concatenate([mine_ref[j] for j in range(SEQ)], axis=1)
    low_ref[...] = mine
    mine_t_ref[...] = mine.T
    stores[0].start()
    copies[0].wait()

    @pl.loop(0, 4)
    def _(n):
        total = jnp.zeros((ROWS, 256), jnp.float32)
        for b in range(REPLICAS):
            weight = beside(out_ref, [tile(b, 2 * n), tile(b, 2 * n + 1)], every)
            total = total + matmul(low_ref[:, 256 * b:256 * b + 256], weight)
        branch_ref[:, cols(n)] = total

    copies[1].wait()
    gate_attn = modulation(2)
    branch = branch_ref[...]
    middle = x_ref[...].astype(jnp.float32) + gate_attn * branch
    normed, inverse = standardize(middle)
    scale_ffn = modulation(4)
    ffn_input = normed * (1.0 + scale_ffn) + modulation(3)
    low_ref[...] = ffn_input.astype(low)
    ffn_t_ref[...] = ffn_input.T.astype(low)
    gate_ffn = modulation(5)
    copies[2].wait()
    cot = cot_ref[...].astype(jnp.float32)
    g_ffn_ref[...] = (cot * gate_ffn).astype(low)
    stores[1].start()
    stores[2].start()
    copies[3].wait()

    @pl.loop(0, 8)
    def _(n):
        hidden = jnp.zeros((ROWS, 256), jnp.float32)
        for b in range(REPLICAS):
            index = tile(b, n)
            weight = jnp.concatenate([up_ref[index, :256, :], up_ref[index, 256:, :]], axis=1)
            hidden = hidden + matmul(low_ref[:, 256 * b:256 * b + 256], weight)
        root = math.sqrt(2.0 / math.pi)
        squared = hidden * hidden
        bent = jnp.tanh(root * (hidden + 0.044715 * (squared * hidden)))
        half = 0.5 * (1.0 + bent)
        activated = hidden * half
        slope = half + 0.5 * hidden * (1.0 - bent * bent) * (
            root * (1.0 + (3.0 * 0.044715) * squared)
        )
        act_ref[:, cols(n)] = activated.astype(low)
        act_t_ref[cols(n), :] = activated.T.astype(low)
        slope_ref[:, cols(n)] = slope

    stores[3].start()
    copies[4].wait()

    @pl.loop(0, 4)
    def _(n):
        total = jnp.zeros((ROWS, 256), jnp.float32)
        for b in range(REPLICAS):
            weight = beside(down_ref, [tile(b, 2 * n), tile(b, 2 * n + 1)], every)
            total = total + matmul(act_ref[:, 512 * b:512 * b + 512], weight)
        wide_ref[:, cols(n)] = total

    ffn_branch = wide_ref[...]
    result_ref[...] = (middle + gate_ffn * ffn_branch).astype(low)
    stores[4].start()
    grad_emb_ref[:, 3 * D:] = sum_of_clips(clip_ref, cot * ffn_branch)

    @pl.loop(0, REPLICAS)
    def _(b):
        weight = beside(down_ref, [tile(b, s) for s in range(SEQ)], every)
        grad = dot_t(g_ffn_ref[...], weight)
        here = cols(b, 512)
        g_hidden_ref[:, here] = (grad * slope_ref[:, here]).astype(low)

    stores[5].start()

    @pl.loop(0, REPLICAS)
    def _(b):
        weight = jnp.concatenate(
            [up_ref[tile(b, s), 256 * k:256 * k + 256, :] for s in range(SEQ) for k in range(2)],
            axis=1,
        )
        wide_ref[:, cols(b)] = dot_t(g_hidden_ref[...], weight)

    grad_ffn_input = wide_ref[...]
    grad_emb_ref[:, D:2 * D] = sum_of_clips(clip_ref, grad_ffn_input)
    grad_emb_ref[:, 2 * D:3 * D] = sum_of_clips(clip_ref, grad_ffn_input * normed)
    spread = grad_ffn_input * (1.0 + scale_ffn)
    grad_middle = cot + inverse * (
        spread
        - jnp.mean(spread, axis=1, keepdims=True)
        - normed * jnp.mean(spread * normed, axis=1, keepdims=True)
    )
    grad_middle_ref[...] = grad_middle
    grad_emb_ref[:, :D] = sum_of_clips(clip_ref, grad_middle * branch)
    g_attn_ref[...] = (grad_middle * gate_attn).astype(low)
    stores[6].start()

    @pl.loop(0, REPLICAS)
    def _(b):
        weight = beside(out_ref, [tile(b, s) for s in range(SEQ)], every)
        grad = dot_t(g_attn_ref[...], weight).astype(low)
        grad_att_ref[2 * b] = grad[:, :TWO]
        grad_att_ref[2 * b + 1] = grad[:, TWO:]

    for store in stores:
        store.wait()


def middle_part(mine, x, cot, member, clip_row, emb, tiles):
    low = jnp.bfloat16
    shapes = [
        ((ROWS, D), low), ((ROWS, D), jnp.float32), ((SEQ, ROWS, TWO), low),
        ((CLIPS, 4 * D), jnp.float32), ((4 * D, ROWS), low), ((ROWS, 4 * D), low),
    ]
    vmem, anywhere = pl.BlockSpec(memory_space=pltpu.VMEM), pl.BlockSpec(memory_space=pl.ANY)
    return pl.pallas_call(
        middle_kernel,
        in_specs=[vmem] * 4 + [anywhere] * 3,
        out_specs=[anywhere, vmem, vmem, vmem, anywhere, anywhere],
        out_shape=[jax.ShapeDtypeStruct(shape, dtype) for shape, dtype in shapes],
        scratch_shapes=[
            pltpu.VMEM((32, 256, 128), low),
            pltpu.VMEM((32, 512, 128), low),
            pltpu.VMEM((32, 512, 128), low),
            pltpu.VMEM((ROWS, D), low),
            pltpu.VMEM((TWO, 6 * D), low),
            pltpu.VMEM((ROWS, D), low),
            pltpu.VMEM((4 * D, ROWS), low),
            pltpu.VMEM((ROWS, 4 * D), low),
            pltpu.SemaphoreType.DMA((12,)),
            pltpu.VMEM((ROWS, D), jnp.float32),
            pltpu.VMEM((ROWS, D), low),
            pltpu.VMEM((ROWS, 2 * D), low),
            pltpu.VMEM((ROWS, 2 * D), jnp.float32),
            pltpu.VMEM((ROWS, D), jnp.float32),
        ],
        compiler_params=pltpu.CompilerParams(vmem_limit_bytes=VMEM_MIB * 1024 * 1024),
        cost_estimate=cost(20),
        name="middle",
    )(mine, x, member, clip_row, cot, emb, *tiles)


def weight_grads_kernel(place_ref, down_l, up_l, out_l, right_ref, down_o, up_o, out_o, other_ref,
                        away_d_ref, keep_d_ref, away_u_ref, keep_u_ref):
    low = jnp.bfloat16
    z, y = place_ref[2] // 2, place_ref[2] % 2
    lefts = [
        jnp.concatenate([mine[...], other[...]], axis=1)
        for mine, other in ((down_l, down_o), (up_l, up_o), (out_l, out_o))
    ]

    def product(left, first, block):
        here = pl.ds(pl.multiple_of(first + 256 * block, 256), 256)
        right = jnp.concatenate([right_ref[:, here], other_ref[:, here]], axis=0)
        return matmul(left, right).astype(low)

    def fill(ref):
        @pl.loop(0, 4, unroll=2)
        def _(k):
            block = z ^ k
            for left, first, rows in ((lefts[0], 0, slice(0, 512)), (lefts[2], 3 * D, slice(512, 768))):
                grad = product(left, first, block)
                ref[4 * y + k, rows, :] = grad[:, :128]
                ref[4 - 4 * y + k, rows, :] = grad[:, 128:]
            for side, up_ref in enumerate((keep_u_ref, away_u_ref)):
                grad = product(lefts[1], D, 2 * block + (y ^ side))
                up_ref[0, k, :256, :] = grad[:, :128]
                up_ref[0, k, 256:, :] = grad[:, 128:]

    @pl.when(pl.program_id(0) == 0)
    def _():
        fill(away_d_ref)

    @pl.when(pl.program_id(0) == 1)
    def _():
        fill(keep_d_ref)


def weight_grads(place, left, right, other_left, other_right):
    low = jnp.bfloat16

    def target(i, p):
        return 2 * jnp.where(i == 0, 1 - p[0], p[0]) + p[1]

    down = pl.BlockSpec((512, ROWS), lambda i, p: (target(i, p), 0))
    up = pl.BlockSpec((256, ROWS), lambda i, p: (8 + target(i, p), 0))
    out = pl.BlockSpec((256, ROWS), lambda i, p: (12 + target(i, p), 0))
    wide = pl.BlockSpec((ROWS, 4 * D), lambda i, p: (0, 0))
    whole = pl.BlockSpec((SEQ, 768, 128), lambda i, p: (0, 0, 0))
    part = pl.BlockSpec((1, 4, 512, 128), lambda i, p: (1 - i, 0, 0, 0))
    return pl.pallas_call(
        weight_grads_kernel,
        grid_spec=pltpu.PrefetchScalarGridSpec(
            num_scalar_prefetch=1,
            grid=(2,),
            in_specs=[down, up, out, wide] * 2,
            out_specs=[whole, whole, part, part],
        ),
        out_shape=[jax.ShapeDtypeStruct((SEQ, 768, 128), low)] * 2
        + [jax.ShapeDtypeStruct((2, 4, 512, 128), low)] * 2,
        compiler_params=params(VMEM_MIB),
        cost_estimate=cost(9),
        name="weight_grads",
    )(place, left, left, left, right, other_left, other_left, other_left, other_right)


def clip_grads_kernel(place_ref, x_ref, clip_ref, g_ref, w_ref, out_ref):
    @pl.when(pl.program_id(0) == 0)
    def _():
        out_ref[...] = jnp.zeros_like(out_ref)

    normed, _ = standardize(x_ref[...].astype(jnp.float32))
    grad = jnp.concatenate(
        [dot_t(g_ref[...], w_ref[b ^ place_ref[1]]) for b in range(REPLICAS)], axis=1
    )
    out_ref[:, :D] += sum_of_clips(clip_ref, grad)
    out_ref[:, D:] += sum_of_clips(clip_ref, grad * normed)


def clip_grads(places, x, clip_row, g_heads, heads_w):
    frames = x.shape[0]
    return pl.pallas_call(
        clip_grads_kernel,
        grid=(frames // ROWS,),
        in_specs=[pl.BlockSpec(memory_space=pltpu.SMEM), rows_spec(D), cols_spec(1),
                  rows_spec(3 * TWO),
                  pl.BlockSpec((REPLICAS, ROWS, 3 * TWO), lambda i: (0, 0, 0))],
        out_specs=whole_spec(CLIPS, 2 * D),
        out_shape=jax.ShapeDtypeStruct((CLIPS, 2 * D), jnp.float32),
        compiler_params=params(VMEM_MIB),
        cost_estimate=cost(9),
        name="clip_grads",
    )(places, x, clip_row, g_heads, heads_w)


def last_kernel(place_ref, own_ref, x_ref, grad_middle_ref, member_ref, emb_ref, *refs):
    *tile_refs, out_ref, wide_ref = refs
    grads = jnp.concatenate([own_ref[place_ref[2] ^ s] for s in range(SEQ)], axis=1)

    def tile(away, apart):
        index = tile_index(away, apart)
        for ref in tile_refs:
            if index < ref.shape[0]:
                return ref[index, ref.shape[1] - 768:, :]
            index -= ref.shape[0]

    for away in range(REPLICAS):
        weight = jnp.concatenate(
            [
                tile(away, s)[256 * k:256 * k + 256, :]
                for s in range(SEQ)
                for k in range(3)
            ],
            axis=1,
        )
        b = (2 * place_ref[0] + place_ref[1]) ^ away
        wide_ref[:, pl.ds(pl.multiple_of(b * 256, 256), 256)] = dot_t(grads, weight)

    normed, inverse = standardize(x_ref[...].astype(jnp.float32))
    spread = wide_ref[...] * (1.0 + matmul(member_ref[...], emb_ref[:, D:2 * D]))
    grad = grad_middle_ref[...] + inverse * (
        spread
        - jnp.mean(spread, axis=1, keepdims=True)
        - normed * jnp.mean(spread * normed, axis=1, keepdims=True)
    )
    out_ref[...] = grad.astype(jnp.bfloat16)


def last_part(place, own, x, grad_middle, member, emb, tiles):
    vmem = pl.BlockSpec(memory_space=pltpu.VMEM)
    return pl.pallas_call(
        last_kernel,
        in_specs=[pl.BlockSpec(memory_space=pltpu.SMEM)] + [vmem] * (5 + len(tiles)),
        out_specs=vmem,
        out_shape=jax.ShapeDtypeStruct((ROWS, D), jnp.bfloat16),
        scratch_shapes=[pltpu.VMEM((ROWS, D), jnp.float32)],
        compiler_params=pltpu.CompilerParams(vmem_limit_bytes=30 * 1024 * 1024),
        cost_estimate=cost(4),
        name="last",
    )(place, own, x, grad_middle, member, emb, *tiles)


def after(value, *others):
    return lax.optimization_barrier((value,) + others)[0]


def together(*values):
    return lax.optimization_barrier(values)


def plus(*terms):
    total = terms[0].astype(jnp.float32)
    for term in terms[1:]:
        total = total + term.astype(jnp.float32)
    return total


def clip_lanes(clip, terms):
    lane = jnp.arange(TWO, dtype=jnp.int32)[None, :]
    return (clip[:, None] == lane % CLIPS) & (lane < terms * CLIPS)


def body_fast(
    tokens, w_query, w_key, w_value, w_out, w_ada, w_up, w_down,
    segments, validity, timesteps, cotangent,
):
    highest = lax.Precision.HIGHEST
    low = jnp.bfloat16
    wide = jnp.float32
    replica = lax.axis_index("batch")
    x = tokens[0]
    frame_count = x.shape[0]
    frames = frame_count * SEQ
    segment = segments[0]

    seat = lax.axis_index("seq").astype(jnp.int32)
    z, y = seat // 2, seat % 2
    place = jnp.stack([replica // 2, replica % 2, seat]).astype(jnp.int32)
    mine_w = jnp.concatenate([w_out, w_up[:, :128], w_up[:, 128:], w_down], axis=0).astype(low)

    z1, z2, y0 = swap(x, "seq", 2), swap(x, "seq", 4), swap(x, "seq", 1)
    times = lax.all_gather(timesteps[0], "batch", axis=0, tiled=True)
    silu_all = jax.nn.silu(time_embedding(times)).astype(low)
    depth = w_ada.shape[0]
    silu_part = lax.dynamic_slice_in_dim(silu_all, replica * depth, depth, 1)
    emb_part = matmul(silu_part, w_ada.astype(low)).reshape(REPLICAS, CLIPS, -1)
    emb_cols = lax.all_to_all(emb_part, "batch", 0, 0, tiled=True)
    emb_cols = jnp.sum(emb_cols, axis=0)
    own_codes = (segment * 2 + (validity[0] == 1)).astype(wide)
    cols = emb_cols.shape[1]
    own_codes = jnp.pad(own_codes, (0, 8 * cols - frame_count)).reshape(8, cols)
    packed = jnp.concatenate([emb_cols, own_codes])
    packed = jnp.broadcast_to(packed[None], (SEQ,) + packed.shape)
    heads_w = jnp.concatenate([w_query, w_key, w_value], axis=1).astype(low)
    heads_w = jnp.stack([heads_w, swap(heads_w, "batch", 1)])
    z1, z2, y0, packed, heads_w, mine_w = together(z1, z2, y0, packed, heads_w, mine_w)
    tiles_w = (lax.all_gather(mine_w, ("batch", "seq"), axis=0),)
    packed = exchange(packed)
    z3 = swap(z2, "seq", 2)
    y1, y2 = swap(z1, "seq", 1), swap(z2, "seq", 1)
    heads_x = swap(heads_w, "batch", 2)
    z3, heads_x = together(z3, heads_x)
    y3 = swap(z3, "seq", 1)
    mine_h = jnp.concatenate([w_query, w_key, w_value], axis=0).astype(low)
    mine_h = after(mine_h, z3)
    h_z1, h_z2 = swap(mine_h, "seq", 2), swap(mine_h, "seq", 4)
    heads_w = jnp.concatenate([heads_w, heads_x])
    emb = packed[:, :CLIPS]
    codes = packed[:, CLIPS:].reshape(SEQ, -1)[:, :frame_count].reshape(frames).astype(jnp.int32)
    clip = codes // 2
    clip_row = clip[None, :]
    tri = jnp.arange(frame_count)[:, None] > jnp.arange(frame_count)[None, :]
    ids = jnp.arange(CLIPS, dtype=jnp.int32)
    one_hot = (clip.reshape(SEQ, frame_count)[:, :, None] == ids).astype(low)
    within = jnp.einsum("ij,njc->nic", tri.astype(low), one_hot, preferred_element_type=wide)
    counts = jnp.sum(one_hot.astype(wide), axis=1)
    offsets = jnp.cumsum(counts, axis=0) - counts
    position = jnp.sum(one_hot.astype(wide) * (within + offsets[:, None, :]), axis=2)
    half = HEAD // 2
    frequency = jnp.exp(-math.log(10000.0) * jnp.arange(half, dtype=wide) / half)
    angle = position.reshape(frames)[:, None] * jnp.tile(frequency, 4)[None, :]
    cosine, sine = jnp.cos(angle), jnp.sin(angle)
    member = clip_lanes(clip, 3).astype(low)
    allowed = clip_lanes(jnp.where(codes % 2 == 1, clip, -1), 1)
    inside = jnp.arange(TWO, dtype=jnp.int32)[None, :] < CLIPS
    bar = jnp.where(inside & ~allowed, -BIG, 0.0).astype(low)
    emb, y1, y2 = together(after(emb, heads_w, member, cosine), y1, y2)
    emb = emb.transpose(1, 0, 2).reshape(CLIPS, -1)
    emb = jnp.concatenate(
        [t.astype(low) for t in three_terms(emb)] + [jnp.zeros((TWO - 3 * CLIPS, 6 * D), low)],
        axis=0,
    )

    tables = (member, bar, cosine, sine, emb, heads_w)
    places = jnp.stack([seat, replica.astype(jnp.int32)])
    earlier = project(places, 0, (x, z1, z2, z3), *tables, ())
    y3, h_z1, h_z2, earlier = together(y3, h_z1, h_z2, earlier)
    h_z3 = swap(h_z2, "seq", 2)
    x_all, attn_input, q, k, kt, v, vt = project(places, 1, (y0, y1, y2, y3), *tables, earlier)
    attended, attended_low, log_total = attend(q, member, k, vt)
    attended_low, h_z3 = together(attended_low, h_z3)
    mine = exchange(attended_low.reshape(SEQ, frame_count, TWO))
    h_z = jnp.stack([mine_h, h_z1, h_z2, h_z3])
    mine, h_z = together(mine, h_z)
    h_y, h_x = swap(h_z, "seq", 1), swap(h_z, "batch", 2)

    own_member = clip_lanes(segment, 3).astype(low)
    result, grad_middle, grad_att, grad_emb, left, right = middle_part(
        mine, x, cotangent[0], own_member, segment[None, :], emb, tiles_w
    )
    left, h_y, h_x = together(left, h_y, h_x)
    other_left, other_right = swap(left, "batch", 1), swap(right, "batch", 1)
    h_first = jnp.concatenate([h_z, h_y, h_x])
    other_left, other_right, h_first = together(other_left, other_right, h_first)
    away_d, keep_d, away_u, keep_u = weight_grads(place, left, right, other_left, other_right)
    grad_heads = exchange(grad_att).reshape(frames, TWO)
    from_x = swap(away_d, "batch", 2)
    from_y = swap(away_u, "seq", 1)
    grad_heads = after(grad_heads, away_d, away_u)

    g_heads = attend_back(
        q, member, grad_heads, attended, log_total, cosine, sine, k, kt, v
    )
    own = exchange(g_heads.reshape(SEQ, frame_count, 3 * TWO))
    from_y = after(from_y, g_heads)
    to_x_u = plus(keep_u[1], from_y[1]).astype(low)
    from_x_u = swap(to_x_u, "batch", 2)
    from_x = after(from_x, to_x_u)
    to_y_d = plus(keep_d[4:], from_x[4:]).astype(low)
    from_y_d = swap(to_y_d, "seq", 1)
    h_yx = swap(after(h_y, to_y_d), "batch", 2)
    h_first_core = swap(after(h_first, to_x_u), "batch", 1)
    g_heads = after(g_heads, to_y_d, to_x_u)
    grad_heads_w = matmul(attn_input.T, g_heads).astype(low).reshape(2, 2, ROWS, 3 * TWO)
    grad_heads_w, from_x_u = together(grad_heads_w, from_x_u)
    part_u = plus(keep_u[0], from_y[0], from_x_u).astype(low)
    from_z_u = [swap(part_u[k], "seq", 2 * k) for k in range(1, 4)]
    late = clip_grads(places, x_all, clip_row, after(g_heads, part_u), heads_w)
    late, from_y_d, h_first_core = together(late, from_y_d, h_first_core)
    part = plus(keep_d[:4], from_x[:4], from_y_d).astype(low)
    late, own = together(late, own)
    grad_emb = jnp.concatenate([late, grad_emb], axis=1)
    grad_emb = exchange(grad_emb.reshape(CLIPS, SEQ, -1).transpose(1, 0, 2))
    grad_emb, *from_z_u = together(grad_emb, *from_z_u)
    grad_emb = jnp.sum(grad_emb, axis=0)
    x_place, core_place = replica // 2, replica % 2
    keep_h = lax.dynamic_index_in_dim(grad_heads_w, core_place, 1, False)
    other_h = swap(lax.dynamic_index_in_dim(grad_heads_w, 1 - core_place, 1, False), "batch", 1)
    h_yx_core = swap(after(h_yx, part), "batch", 1)
    from_z = [swap(part[k], "seq", 2 * k) for k in range(1, 4)]
    both_h = plus(keep_h, other_h).astype(low)
    away_h = swap(lax.dynamic_index_in_dim(both_h, 1 - x_place, 0, False), "batch", 2)

    grad_tokens = last_part(place, own, x, grad_middle, own_member, emb,
        (h_first, h_yx, h_first_core, h_yx_core),
    )
    grad_emb = lax.all_gather(after(grad_emb, grad_tokens), "batch", axis=0, tiled=True)
    final_a = jnp.dot(silu_part.astype(wide).T, grad_emb, precision=highest)
    grad_tokens, final_a, away_h, *from_z = together(grad_tokens, final_a, away_h, *from_z)
    final_heads = plus(lax.dynamic_index_in_dim(both_h, x_place, 0, False), away_h)
    total = plus(part[0], *from_z)
    final_d, final_o = total[:512], total[512:]
    total = plus(part_u[0], *from_z_u)
    final_u = jnp.concatenate([total[:256], total[256:]], axis=1)
    width = w_query.shape[1]
    return (
        result[None],
        grad_tokens[None],
        final_heads[:, :width],
        final_heads[:, width:2 * width],
        final_heads[:, 2 * width:],
        final_o,
        final_a,
        final_u,
        final_d,
    )


def solution(mesh):
    fits = mesh.shape["seq"] == SEQ and mesh.shape["batch"] == REPLICAS
    chosen = body_fast if fits else body
    return jax.shard_map(
        chosen,
        mesh=mesh,
        in_specs=(
            P("batch", "seq", None),
            P("batch", "seq"),
            P("batch", "seq"),
            P("batch", "seq"),
            P("batch", "seq"),
            P("batch", "seq"),
            P("batch", "seq"),
            P("batch", "seq"),
            P("batch", "seq"),
            P("batch", "seq"),
            P("batch", None),
            P("batch", "seq", None),
        ),
        out_specs=(
            P("batch", "seq", None),
            P("batch", "seq", None),
            P("batch", "seq"),
            P("batch", "seq"),
            P("batch", "seq"),
            P("batch", "seq"),
            P("batch", "seq"),
            P("batch", "seq"),
            P("batch", "seq"),
        ),
        check_vma=False,
    )
```
